32 devices in a mesh: dp: 16 (over z, y, x), mp: 2 (over core).
Axes of the slice: x: 2, y: 2, z: 4, core: 2. Of those that a mesh axis runs over, the one named last changes fastest.
Arguments:
- variates: bfloat16 [45568, 512], P(('dp', 'mp')), may hold values from -6 to 6
- dataset: int32 [32], P('dp'), may hold values from 0 to 3
- w_qkv: bfloat16 [3, 512, 512], P(None, None, 'mp'), may hold values from -0.25 to 0.25
- b_qv: bfloat16 [2, 512], P(None, 'mp'), may hold values from -3 to 3
- w_out: bfloat16 [512, 512], P('mp'), may hold values from -0.75 to 0.75
- b_out: bfloat16 [512], replicated, may hold values from -2 to 2
- gain_one: bfloat16 [512], replicated, may hold values from 0.5 to 1.5
- shift_one: bfloat16 [512], replicated, may hold values from -2 to 2
- w_up: bfloat16 [512, 2048], P(None, 'mp'), may hold values from -0.25 to 0.25
- b_up: bfloat16 [2048], P('mp'), may hold values from -3 to 3
- w_down: bfloat16 [2048, 512], P('mp'), may hold values from -0.1875 to 0.1875
- b_down: bfloat16 [512], replicated, may hold values from -2 to 2
- gain_two: bfloat16 [512], replicated, may hold values from 0.5 to 1.5
- shift_two: bfloat16 [512], replicated, may hold values from -2 to 2
- cotangent: bfloat16 [45568, 512], P(('dp', 'mp')), may hold values from -6 to 6
Outputs:
- output: bfloat16 [45568, 512], P(('dp', 'mp'))
- grad_input: float32 [45568, 512], P(('dp', 'mp'))
- grad_w_qkv: float32 [3, 512, 512], P(None, None, 'mp')
- grad_b_qv: float32 [2, 512], P(None, 'mp')
- grad_w_out: float32 [512, 512], P('mp')
- grad_b_out: float32 [512], replicated
- grad_gain_one: float32 [512], replicated
- grad_shift_one: float32 [512], replicated
- grad_w_up: float32 [512, 2048], P(None, 'mp')
- grad_b_up: float32 [2048], P('mp')
- grad_w_down: float32 [2048, 512], P('mp')
- grad_b_down: float32 [512], replicated
- grad_gain_two: float32 [512], replicated
- grad_shift_two: float32 [512], replicated
The draws below stay inside these ranges and needn't reach their ends.
Inputs may be any that keep to these rules, and one draw needn't show every extreme that they name: dataset numbers 0, 1, 2, 3 stand for windows of 7, 21, 321 and 862 variates.
All inputs are finite; a program needn't handle non-finite values.
Results may differ from the reference program's by a relative error of at most 0.012.
Values may be sent and summed in bfloat16 or wider, within the bound.
No kernel may reach another device: no remote copies, remote signals or barrier semaphores. Data moves between devices by JAX's collectives and lax.ppermute only.
A program may use at most 256 MiB of HBM per device.

```python
from functools import partial
import jax
import jax.numpy as jnp
from jax import lax

D = 512
HEADS = 8
FF = 2048
HEAD_DIM = 64
SLOTS = 1424
WIN_ETT = 7
WIN_WEATHER = 21
WIN_ELEC = 321
WIN_TRAFFIC = 862
N_BUCKETS = 32
TOKENS = 45568


def set_ends(entries, rng, smallest, largest):
    shape = entries.shape
    place = [jax.random.randint(jax.random.fold_in(rng, axis), (), 0, shape[axis]) for axis in range(len(shape))]
    entries = entries.at[tuple(place)].set(smallest)
    longest = shape.index(max(shape))
    place[longest] = (place[longest] + 1) % shape[longest]
    return entries.at[tuple(place)].set(largest)


def levels(key, extent, shards, smallest, top_value):
    factor_of = 1.0
    for dim, parts in shards:
        heights = jax.random.uniform(jax.random.fold_in(jax.random.fold_in(key, 6), dim), (parts,), jnp.float32, smallest / len(shards), top_value / len(shards))
        factor_of = factor_of * jnp.repeat(jnp.exp(heights), extent[dim] // parts).reshape((-1,) + (1,) * (len(extent) - 1 - dim))
    return factor_of


def bell_draw(rng, dims, deviation, reach, cuts=(), held_as=jnp.bfloat16):
    result = deviation * jax.random.normal(rng, dims, jnp.float32)
    if cuts:
        result = result * levels(rng, dims, cuts, -0.22, 0.18)
    return jnp.clip(result, -reach, reach).astype(held_as)


def setup_inputs(seed: int = 0) -> dict:
    streams_of = jax.random.split(jax.random.key(seed), 16)
    return {
        "variates": bell_draw(streams_of[0], (TOKENS, D), 1.0, 6.0, ((0, 32),)),
        "dataset": set_ends(jax.random.randint(streams_of[1], (N_BUCKETS,), 0, 4), jax.random.fold_in(streams_of[1], 1), 0, 3).astype(jnp.int32),
        "w_qkv": bell_draw(streams_of[2], (3, D, D), D ** -0.5, 0.25, ((2, 2),)),
        "b_qv": bell_draw(streams_of[3], (2, D), 0.5, 3.0, ((1, 2),)),
        "w_out": bell_draw(streams_of[4], (D, D), (D // 8) ** -0.5, 0.75, ((0, 2),)),
        "b_out": bell_draw(streams_of[5], (D,), 0.3, 2.0),
        "gain_one": jnp.clip(1.0 + 0.1 * jax.random.normal(streams_of[6], (D,), jnp.float32), 0.5, 1.5).astype(jnp.bfloat16),
        "shift_one": bell_draw(streams_of[7], (D,), 0.3, 2.0),
        "w_up": bell_draw(streams_of[8], (D, FF), D ** -0.5, 0.25, ((1, 2),)),
        "b_up": bell_draw(streams_of[9], (FF,), 0.5, 3.0, ((0, 2),)),
        "w_down": bell_draw(streams_of[10], (FF, D), (FF // 2) ** -0.5, 0.1875, ((0, 2),)),
        "b_down": bell_draw(streams_of[11], (D,), 0.3, 2.0),
        "gain_two": jnp.clip(1.0 + 0.1 * jax.random.normal(streams_of[12], (D,), jnp.float32), 0.5, 1.5).astype(jnp.bfloat16),
        "shift_two": bell_draw(streams_of[13], (D,), 0.3, 2.0),
        "cotangent": bell_draw(streams_of[14], (TOKENS, D), 1.0, 6.0, ((0, 32),)),
    }


epsilon = 1e-05
highest = lax.Precision.HIGHEST

@jax.custom_vjp
def low(v):
    return lax.optimization_barrier(v.astype(jnp.bfloat16)).astype(jnp.float32)

@jax.custom_vjp
def low_back(v):
    return v

def low_keep(v):
    return (low(v), None)

def low_pass(kept, grad):
    return (grad,)

def back_keep(v):
    return (v, None)

def back_low(kept, grad):
    return (low(grad),)
low.defvjp(low_keep, low_pass)
low_back.defvjp(back_keep, back_low)

def window_layout(dataset):
    widths = jnp.array([WIN_ETT, WIN_WEATHER, WIN_ELEC, WIN_TRAFFIC], jnp.int32)
    chosen = (dataset[:, None] == jnp.arange(4, dtype=jnp.int32)[None, :]).astype(jnp.int32)
    window = lax.optimization_barrier(jnp.sum(chosen * widths[None, :], axis=1)).astype(jnp.int32)
    places = jnp.arange(SLOTS, dtype=jnp.int32)[None, :]
    filled = SLOTS // window * window
    occupied = places < filled[:, None]
    segment = jnp.where(occupied, places // window[:, None], -1).astype(jnp.int32)
    return (segment, occupied)

def matmul(left_op, right_op):
    return jnp.dot(left_op, right_op, precision=highest)

def normalize(matrix, gain_vec, shift_vec):
    centre = matrix - lax.optimization_barrier(jnp.mean(matrix, axis=1, keepdims=True))
    normed = centre * lax.rsqrt(lax.optimization_barrier(jnp.mean(centre * centre, axis=1, keepdims=True)) + epsilon)
    return normed * gain_vec + shift_vec

def attend(pieces):
    queries, key_rows, values, segment = pieces
    scores = low_back(jnp.einsum('qhd,khd->hqk', queries, key_rows, precision=highest) * HEAD_DIM ** (-0.5))
    allowed = (segment[:, None] == segment[None, :])[None, :, :]
    scores = jnp.where(allowed, scores, -jnp.inf)
    maxima = lax.optimization_barrier(jnp.max(scores, axis=2, keepdims=True))
    raised = jnp.exp(scores - maxima)
    probs = low(raised / lax.optimization_barrier(jnp.sum(raised, axis=2, keepdims=True)))
    mixed = jnp.einsum('hqk,khd->qhd', probs, values, precision=highest)
    return mixed.reshape(SLOTS, D)

def by_bucket(array_in):
    return array_in.reshape(array_in.shape[0] // SLOTS, SLOTS, HEADS, HEAD_DIM)

def forward(segment, variates, w_qkv, b_qv, w_out, b_out, gain_one, shift_one, w_up, b_up, w_down, b_down, gain_two, shift_two):
    queries = low(low_back(matmul(variates, w_qkv[0]) + b_qv[0]))
    key_rows = low(low_back(matmul(variates, w_qkv[1])))
    values = low(low_back(matmul(variates, w_qkv[2]) + b_qv[1]))
    mixed = lax.map(jax.checkpoint(attend), (by_bucket(queries), by_bucket(key_rows), by_bucket(values), segment))
    mixed = low(low_back(mixed.reshape(-1, D)))
    resid_one = variates + low_back(matmul(mixed, w_out)) + b_out
    hidden_one = normalize(resid_one, gain_one, shift_one)
    pre_act = low_back(matmul(low(hidden_one), w_up) + b_up)
    activated = low(jax.nn.gelu(pre_act, approximate=False))
    second = hidden_one + low_back(matmul(activated, w_down)) + b_down
    return normalize(second, gain_two, shift_two)

def reference(variates, dataset, w_qkv, b_qv, w_out, b_out, gain_one, shift_one, w_up, b_up, w_down, b_down, gain_two, shift_two, cotangent):
    segment, occupied = window_layout(dataset)
    inputs = tuple((array_in.astype(jnp.float32) for array_in in (variates, w_qkv, b_qv, w_out, b_out, gain_one, shift_one, w_up, b_up, w_down, b_down, gain_two, shift_two)))
    output, pullback = jax.vjp(partial(forward, segment), *inputs)
    grad_top = cotangent.astype(jnp.float32) * occupied.reshape(-1, 1).astype(jnp.float32)
    gradients = pullback(grad_top)
    return (output.astype(jnp.bfloat16), gradients[0], gradients[1], gradients[2], gradients[3], gradients[4], gradients[5], gradients[6], gradients[7], gradients[8], gradients[9], gradients[10], gradients[11], gradients[12])
```

```python
import jax
import jax.numpy as jnp
from jax import lax
from jax.experimental import pallas as pl
from jax.experimental.pallas import tpu as pltpu
from jax.sharding import PartitionSpec as P

HEAD_DIM = 64
SLOTS = 1424
WIDTHS = (7, 21, 321, 862)
LANES = 1536
CLASSES = 48
BIG = 1e30
EPS = 1e-05
MIB = 2**20

bf16 = jnp.bfloat16
f32 = jnp.float32


def mul(left, right, left_dim=1, right_dim=0):
    return lax.dot_general(
        left, right, (((left_dim,), (right_dim,)), ((), ())), preferred_element_type=f32
    )


def params(limit):
    return pltpu.CompilerParams(vmem_limit_bytes=limit * MIB)


def cover(width, start, stop, last):
    used = SLOTS // width * width
    low = start // width * width
    high = last if stop > used else -(-stop // width) * width
    return (low // 128 * 128, min(-(-min(high, last) // 128) * 128, LANES))


def groups_of(width, rows, step):
    found = []
    for start in range(0, rows, step):
        low, high = cover(width, start, min(start + step, rows), rows)
        if found and found[-1][2] == low and found[-1][2] + found[-1][3] == high:
            first, count = found[-1][:2]
            found[-1] = (first, count + step, low, high - low)
        else:
            found.append((start, step, low, high - low))
    return found


FORWARD = (
    [(128 * i, 128, max(128 * i - 128, 0), min(128 * i + 256, LANES) - max(128 * i - 128, 0)) for i in range(12)],
    groups_of(321, SLOTS, 128),
    [(768, 768, 768, 768), (0, 896, 0, 896)],
)
BACKWARD = (
    FORWARD[0],
    groups_of(321, 1284, 128),
    [(0, 896, 0, 896)],
)


def token_class(width):
    token = lax.broadcasted_iota(jnp.int32, (CLASSES, LANES), 1)
    numbers = token.astype(f32)
    held = jnp.floor((numbers + 0.5) * (1.0 / width)).astype(jnp.int32)
    held = jnp.where(token < SLOTS, held, (SLOTS - 1) // width + 1)
    row = lax.broadcasted_iota(jnp.int32, (CLASSES, LANES), 0)
    return held % CLASSES == row


def write_masks(set_ref, hot_ref, bar_ref):
    for number, width in enumerate(WIDTHS):

        @pl.when(set_ref[0] == number)
        def _():
            same = token_class(width)
            hot_ref[...] = jnp.where(same, 1.0, 0.0).astype(bf16)
            bar_ref[:CLASSES, :] = jnp.where(same, 0.0, -BIG).astype(bf16)

    row = lax.broadcasted_iota(jnp.int32, (16, LANES), 0)
    bar_ref[CLASSES:, :] = jnp.where(row < 3, 1.0, 0.0).astype(bf16)


def split_three(row):
    high = row.astype(bf16)
    rest = row - high.astype(f32)
    middle = rest.astype(bf16)
    low = (rest - middle.astype(f32)).astype(bf16)
    return high, middle, low


def extra_rows(row):
    parts = [p.astype(f32) for p in split_three(row)]
    number = lax.broadcasted_iota(jnp.int32, (16, row.shape[1]), 0)
    held = jnp.where(number == 0, parts[0], jnp.where(number == 1, parts[1], jnp.where(number == 2, parts[2], 0.0)))
    return held.astype(bf16)


def attend_forward(set_ref, x_ref, wa_ref, wb_ref, ba_ref, bb_ref, q_ref, k_ref, v_ref, o_ref, lse_ref, xt_ref, hot_ref, bar_ref):
    write_masks(set_ref, hot_ref, bar_ref)
    tail = jnp.zeros((LANES - SLOTS, x_ref.shape[1]), bf16)
    xt_ref[...] = jnp.concatenate([x_ref[...], tail], axis=0).T
    for side, (w_ref, b_ref) in enumerate(((wa_ref, ba_ref), (wb_ref, bb_ref))):
        for kind, out_ref in enumerate((q_ref, k_ref, v_ref)):
            weight = w_ref[kind].T
            rows = weight.shape[0]
            if kind != 1:
                row = b_ref[kind // 2 : kind // 2 + 1, :].astype(f32)
                column = jnp.broadcast_to(row, (128, rows)).T
                column = jnp.concatenate([column] * 4, axis=1)
            for start in range(0, LANES, 512):
                part = mul(weight, xt_ref[:, start : start + 512])
                if kind != 1:
                    part = part + column
                if kind == 0:
                    part = part * 0.125
                out_ref[side * rows : (side + 1) * rows, start : start + 512] = part.astype(bf16)

    def one_head(head, groups):
        rows = pl.ds(pl.multiple_of(head * 64, 64), 64)
        keep = None
        for q0, nq, k0, nk in groups:
            keys = jnp.concatenate([k_ref[rows, k0 : k0 + nk], bar_ref[:, k0 : k0 + nk]], axis=0).T
            ones = jnp.ones((16, nk), bf16)
            vals = jnp.concatenate([v_ref[rows, k0 : k0 + nk], ones], axis=0)
            for start in range(q0, q0 + nq, 256):
                size = min(256, q0 + nq - start)
                lanes = slice(start, start + size)
                zeros = jnp.zeros((16, size), bf16)
                quer = jnp.concatenate([q_ref[rows, lanes], hot_ref[:, lanes], zeros], axis=0)
                scores = mul(keys, quer)
                top = jnp.max(scores, axis=0, keepdims=True)
                raised = jnp.exp(scores - top).astype(bf16)
                total = mul(vals, raised)
                sums = total[64:65, :]
                mixed = (total[:64, :] * (1.0 / sums)).astype(bf16)
                logs = top + jnp.log(sums)
                if len(groups) == 2 and start == 768:
                    if q0 == 768:
                        keep = (mixed[:, :128], logs[:, :128])
                    else:
                        lane = lax.broadcasted_iota(jnp.int32, (64, 128), 1)
                        mixed = jnp.where(lane < WIDTHS[3] - 768, mixed.astype(f32), keep[0].astype(f32)).astype(bf16)
                        logs = jnp.where(lane[:1] < WIDTHS[3] - 768, logs, keep[1])
                o_ref[rows, lanes] = mixed
                lse_ref[pl.ds(pl.multiple_of(head * 16, 16), 16), lanes] = extra_rows(-logs)

    for group in range(3):
        chosen = (set_ref[0] < 2, set_ref[0] == 2, set_ref[0] == 3)[group]

        @pl.when(chosen)
        def _():
            def pair(number, carry):
                one_head(2 * number, FORWARD[group])
                one_head(2 * number + 1, FORWARD[group])
                return carry

            lax.fori_loop(0, q_ref.shape[0] // 128, pair, 0)


def attend_backward(set_ref, q_ref, k_ref, v_ref, g_ref, lse_ref, delta_ref, dq_ref, dk_ref, dv_ref, hot_ref, bar_ref, p_ref, s_ref, ka_ref, va_ref):
    write_masks(set_ref, hot_ref, bar_ref)

    def one_head(head, groups, slot):
        rows = pl.ds(pl.multiple_of(head * 64, 64), 64)
        more = pl.ds(pl.multiple_of(head * 16, 16), 16)
        single = len(groups) == 1
        if not single:
            ka_ref[...] = jnp.zeros_like(ka_ref)
            va_ref[...] = jnp.zeros_like(va_ref)
        for q0, nq, k0, nk in groups:
            span = slice(k0, k0 + nk)
            held = slice(q0, q0 + nq)
            keys = jnp.concatenate([k_ref[rows, span], bar_ref[:, span]], axis=0)
            vals = jnp.concatenate([v_ref[rows, span], bar_ref[CLASSES:, span]], axis=0)
            for start in range(q0, q0 + nq, 256):
                size = min(256, q0 + nq - start)
                lanes = slice(start, start + size)
                quer = jnp.concatenate(
                    [q_ref[rows, lanes], hot_ref[:, lanes], lse_ref[more, lanes]], axis=0
                )
                grad = jnp.concatenate([g_ref[rows, lanes], delta_ref[more, lanes]], axis=0)
                probs = jnp.exp(mul(quer, keys, 0, 0))
                slopes = probs * mul(grad, vals, 0, 0)
                p_ref[slot, start - q0 : start - q0 + size, :nk] = probs.astype(bf16)
                s_ref[slot, start - q0 : start - q0 + size, :nk] = slopes.astype(bf16)
            dv = mul(g_ref[rows, held], p_ref[slot, :nq, :nk])
            dk = mul(q_ref[rows, held], s_ref[slot, :nq, :nk])
            dq = mul(k_ref[rows, span], s_ref[slot, :nq, :nk], 1, 1)
            dq_ref[rows, held] = (dq * 0.125).astype(bf16)
            if single:
                dv_ref[rows, span] = dv.astype(bf16)
                dk_ref[rows, span] = dk.astype(bf16)
            else:
                va_ref[:, span] += dv
                ka_ref[:, span] += dk
        if single:
            rest = LANES - 896
            for out in (dq_ref, dk_ref, dv_ref):
                out[rows, 896:] = jnp.zeros((64, rest), bf16)
        else:
            dv_ref[rows, :] = va_ref[...].astype(bf16)
            dk_ref[rows, :] = ka_ref[...].astype(bf16)
            done = groups[-1][0] + groups[-1][1]
            if done < LANES:
                dq_ref[rows, done:] = jnp.zeros((64, LANES - done), bf16)

    for group in range(3):
        chosen = (set_ref[0] < 2, set_ref[0] == 2, set_ref[0] == 3)[group]

        @pl.when(chosen)
        def _():
            def pair(number, carry):
                one_head(2 * number, BACKWARD[group], 0)
                one_head(2 * number + 1, BACKWARD[group], 1)
                return carry

            lax.fori_loop(0, q_ref.shape[0] // 128, pair, 0)


TILES = [(i * 256, 256) for i in range(5)] + [(1280, 144)]


def over_tiles(step):
    def body(number, carry):
        step(pl.multiple_of(number * 256, 256), 256)
        return carry

    lax.fori_loop(0, 5, body, 0)
    step(1280, 144)


def mean_of(matrix):
    return jnp.sum(matrix, axis=1, keepdims=True) * (1.0 / matrix.shape[1])


def norm_parts(matrix):
    centre = matrix - mean_of(matrix)
    spread = lax.rsqrt(mean_of(centre * centre) + EPS)
    return centre * spread, spread


def norm_back(scaled, normed, spread):
    return spread * (scaled - mean_of(scaled) - normed * mean_of(scaled * normed))


def fold(matrix):
    return jnp.sum(matrix.reshape(matrix.shape[0] // 8, 8, matrix.shape[1]), axis=0)


def gelu_parts(pre):
    size = jnp.abs(pre)
    t = 1.0 / (1.0 + (0.3275911 * 2.0**-0.5) * size)
    bell = jnp.exp(-0.5 * pre * pre)
    poly = 0.5 * 1.061405429
    for factor in (-1.453152027, 1.421413741, -0.284496736, 0.254829592):
        poly = poly * t + 0.5 * factor
    tail = poly * t * bell
    phi = jnp.where(pre > 0, 1.0 - tail, tail)
    return pre * phi, phi + pre * (bell * (2.0 * jnp.pi) ** -0.5)


HIDDEN_STEP = 512


def feed_forward(
    set_ref, x_ref, o_ref, wo_a, wo_b, ua_ref, ub_ref, bup_ref, da_ref, db_ref, vec_ref, cot_ref,
    out_ref, hid_ref, res_ref, slope_ref, sec_ref, gd_a, gd_b, sums_ref, act_ref, low_ref,
):
    width = x_ref.shape[1]
    half = ua_ref.shape[1]
    used = jnp.where(set_ref[0] == 0, SLOTS // 7 * 7, jnp.where(set_ref[0] == 1, SLOTS // 21 * 21, jnp.where(set_ref[0] == 2, SLOTS // 321 * 321, 862)))
    sums_ref[...] = jnp.zeros_like(sums_ref)
    b_out, gain_one, shift_one, b_down, gain_two, shift_two = (vec_ref[i : i + 1, :].astype(f32) for i in range(6))

    def step(start, size):
        rows = pl.ds(start, size)
        lanes = pl.ds(start, 256)
        split = wo_a.shape[0]
        attn = mul(o_ref[:split, lanes], wo_a[...], 0, 0) + mul(o_ref[split:, lanes], wo_b[...], 0, 0)
        resid = x_ref[rows, :].astype(f32) + attn[:size] + b_out
        res_ref[rows, :] = resid
        normed, _ = norm_parts(resid)
        hidden = normed * gain_one + shift_one
        low = hidden.astype(bf16)
        hid_ref[rows, :] = low
        total = None
        for side, (u_ref, d_ref) in enumerate(((ua_ref, da_ref), (ub_ref, db_ref))):
            for at in range(0, half, HIDDEN_STEP):
                place = slice(side * half + at, side * half + at + HIDDEN_STEP)
                pre = mul(low, u_ref[:, at : at + HIDDEN_STEP]) + bup_ref[:, place].astype(f32)
                active, slope = gelu_parts(pre)
                active = active.astype(bf16)
                act_ref[rows, place] = active
                slope_ref[rows, place] = slope.astype(bf16)
                part = mul(active, d_ref[at : at + HIDDEN_STEP, :])
                total = part if total is None else total + part
        second = hidden + total + b_down
        normed, spread = norm_parts(second)
        out_ref[rows, :] = (normed * gain_two + shift_two).astype(bf16)
        row = start + lax.broadcasted_iota(jnp.int32, (size, width), 0)
        top = jnp.where(row < used, cot_ref[rows, :].astype(f32), 0.0)
        grad = norm_back(top * gain_two, normed, spread)
        sec_ref[rows, :] = grad
        low_ref[rows, :] = grad.astype(bf16)
        sums_ref[0:8, :] += fold(top * normed)
        sums_ref[8:16, :] += fold(top)
        sums_ref[16:24, :] += fold(grad)

    over_tiles(step)
    for side, g_ref in enumerate((gd_a, gd_b)):
        for at in range(0, half, 256):
            place = slice(side * half + at, side * half + at + 256)
            g_ref[at : at + 256, :] = mul(act_ref[:, place], low_ref[...], 0, 0).astype(g_ref.dtype)


def feed_backward(
    sec_ref, slope_ref, hid_ref, res_ref, o_ref, wo_a, wo_b, ua_ref, ub_ref, da_ref, db_ref, vec_ref,
    gr_ref, g_ref, delta_ref, gu_a, gu_b, go_a, go_b, sums_ref, bup_ref, pre_ref, mix_ref,
):
    half = ua_ref.shape[1]
    sums_ref[...] = jnp.zeros_like(sums_ref)
    bup_ref[...] = jnp.zeros_like(bup_ref)
    gain_one = vec_ref[1:2, :].astype(f32)
    mix_ref[SLOTS:, :] = jnp.zeros((LANES - SLOTS, mix_ref.shape[1]), bf16)

    def step(start, size):
        rows = pl.ds(start, size)
        second = sec_ref[rows, :]
        low = second.astype(bf16)
        total = None
        for side, (u_ref, d_ref) in enumerate(((ua_ref, da_ref), (ub_ref, db_ref))):
            for at in range(0, half, HIDDEN_STEP):
                place = slice(side * half + at, side * half + at + HIDDEN_STEP)
                inner = mul(low, d_ref[at : at + HIDDEN_STEP, :], 1, 1)
                pre = (inner * slope_ref[rows, place].astype(f32)).astype(bf16)
                pre_ref[rows, place] = pre
                bup_ref[:, place] += fold(pre.astype(f32))
                part = mul(pre, u_ref[:, at : at + HIDDEN_STEP], 1, 1)
                total = part if total is None else total + part
        hidden = second + total
        normed, spread = norm_parts(res_ref[rows, :])
        grad = norm_back(hidden * gain_one, normed, spread)
        gr_ref[rows, :] = grad
        mix_ref[rows, :] = grad.astype(bf16)
        sums_ref[0:8, :] += fold(hidden * normed)
        sums_ref[8:16, :] += fold(hidden)
        sums_ref[16:24, :] += fold(grad)

    over_tiles(step)
    for side, out in enumerate((gu_a, gu_b)):
        for at in range(0, half, 256):
            place = slice(side * half + at, side * half + at + 256)
            out[:, at : at + 256] = mul(hid_ref[...], pre_ref[:, place], 0, 0).astype(out.dtype)
    split = wo_a.shape[0]
    for side, (out, w_ref) in enumerate(((go_a, wo_a), (go_b, wo_b))):
        place = slice(side * split, (side + 1) * split)
        out[...] = mul(o_ref[place, :], mix_ref[...]).astype(out.dtype)
        for start in range(0, LANES, 512):
            lanes = slice(start, start + 512)
            grad = mul(w_ref[...], mix_ref[lanes, :], 1, 1).astype(bf16)
            g_ref[place, lanes] = grad
            prod = grad.astype(f32) * o_ref[place, lanes].astype(f32)
            for head in range(split // 64):
                at = (side * (split // 64) + head) * 16
                delta = jnp.sum(prod[head * 64 : head * 64 + 64], axis=0, keepdims=True)
                delta_ref[at : at + 16, lanes] = extra_rows(-delta)


def project_backward(x_ref, dq_ref, dk_ref, dv_ref, wa_ref, wb_ref, gr_ref, gi_ref, ga_ref, gb_ref, sums_ref, xt_ref, wt_ref):
    tail = jnp.zeros((LANES - SLOTS, x_ref.shape[1]), bf16)
    xt_ref[...] = jnp.concatenate([x_ref[...], tail], axis=0).T
    rows = wa_ref.shape[2]
    ones = jnp.ones((8, LANES), bf16)
    for side, (w_ref, g_ref) in enumerate(((wa_ref, ga_ref), (wb_ref, gb_ref))):
        place = slice(side * rows, (side + 1) * rows)
        for kind, d_ref in enumerate((dq_ref, dk_ref, dv_ref)):
            g_ref[kind] = mul(xt_ref[...], d_ref[place, :], 1, 1).astype(g_ref.dtype)
            wt_ref[kind, place, :] = w_ref[kind].T
            if kind != 1:
                sums_ref[kind // 2, :, place] = mul(ones, d_ref[place, :], 1, 1)
    for start in range(0, SLOTS, 256):
        size = min(256, SLOTS - start)
        lanes = slice(start, start + 256)
        total = mul(dq_ref[:, lanes], wt_ref[0], 0, 0)
        total = total + mul(dk_ref[:, lanes], wt_ref[1], 0, 0)
        total = total + mul(dv_ref[:, lanes], wt_ref[2], 0, 0)
        gi_ref[start : start + size, :] = gr_ref[start : start + size, :] + total[:size]


def shape(dims, kind=bf16):
    return jax.ShapeDtypeStruct(dims, kind)


smem = pl.BlockSpec(memory_space=pltpu.SMEM)


def specs(count):
    return [smem] + [pl.BlockSpec(memory_space=pltpu.VMEM)] * (count - 1)


def call_forward(number, x, wa, wb, ba, bb):
    width = 2 * wa.shape[2]
    big = shape((width, LANES))
    return pl.pallas_call(
        attend_forward, name="attend_forward",
        out_shape=[big, big, big, big, shape((width // 4, LANES))],
        in_specs=specs(6),
        scratch_shapes=[pltpu.VMEM((x.shape[1], LANES), bf16), pltpu.VMEM((CLASSES, LANES), bf16), pltpu.VMEM((64, LANES), bf16)],
        compiler_params=params(40),
    )(number, x, wa, wb, ba, bb)


def call_feed_forward(number, x, mixed, wo_a, wo_b, up_a, up_b, b_up, down_a, down_b, vecs, cot):
    rows, width = x.shape
    half = up_a.shape[1]
    return pl.pallas_call(
        feed_forward, name="feed_forward",
        out_shape=[
            shape((rows, width)), shape((rows, width)), shape((rows, width), f32), shape((rows, 2 * half)),
            shape((rows, width), f32), shape((half, width)), shape((half, width)), shape((24, width), f32),
        ],
        in_specs=specs(12),
        scratch_shapes=[pltpu.VMEM((rows, 2 * half), bf16), pltpu.VMEM((rows, width), bf16)],
        compiler_params=params(56),
    )(number, x, mixed, wo_a, wo_b, up_a, up_b, b_up, down_a, down_b, vecs, cot)


def call_feed_backward(second, slope, hidden, resid, mixed, wo_a, wo_b, up_a, up_b, down_a, down_b, vecs):
    rows, width = second.shape
    half = up_a.shape[1]
    split = wo_a.shape[0]
    return pl.pallas_call(
        feed_backward, name="feed_backward",
        out_shape=[
            shape((rows, width), f32), shape((2 * split, LANES)), shape((2 * split // 4, LANES)),
            shape((width, half)), shape((width, half)), shape((split, width)), shape((split, width)),
            shape((24, width), f32), shape((8, 2 * half), f32),
        ],
        scratch_shapes=[pltpu.VMEM((rows, 2 * half), bf16), pltpu.VMEM((LANES, width), bf16)],
        compiler_params=params(56),
    )(second, slope, hidden, resid, mixed, wo_a, wo_b, up_a, up_b, down_a, down_b, vecs)


def call_backward(number, q, k, v, grad, lse, delta):
    big = shape(q.shape)
    return pl.pallas_call(
        attend_backward, name="attend_backward",
        out_shape=[big, big, big],
        in_specs=specs(7),
        scratch_shapes=[
            pltpu.VMEM((CLASSES, LANES), bf16), pltpu.VMEM((64, LANES), bf16),
            pltpu.VMEM((2, 896, 896), bf16), pltpu.VMEM((2, 896, 896), bf16),
            pltpu.VMEM((64, LANES), f32), pltpu.VMEM((64, LANES), f32),
        ],
        compiler_params=params(40),
    )(number, q, k, v, grad, lse, delta)


def call_project(x, dq, dk, dv, wa, wb, resid):
    rows, width = x.shape
    return pl.pallas_call(
        project_backward, name="project_backward",
        out_shape=[shape((rows, width), f32), shape(wa.shape), shape(wb.shape), shape((2, 8, 2 * wa.shape[2]), f32)],
        scratch_shapes=[pltpu.VMEM((width, LANES), bf16), pltpu.VMEM((3, 2 * wa.shape[2], width), bf16)],
        compiler_params=params(40),
    )(x, dq, dk, dv, wa, wb, resid)


def swap(array):
    return lax.ppermute(array, "mp", [(0, 1), (1, 0)])


def per_device(
    variates, dataset, w_qkv, b_qv, w_out, b_out, gain_one, shift_one, w_up, b_up, w_down, b_down, gain_two, shift_two, cotangent,
):
    side = lax.axis_index("mp")
    number = lax.dynamic_slice_in_dim(dataset, side, 1, 0)
    width, half = w_up.shape
    small = swap(jnp.concatenate([b_qv.reshape(-1), b_up]).reshape(3, -1))
    other_b_qv = small[0:1].reshape(b_qv.shape) if small.shape[1] == b_qv.size else small.reshape(-1)[: b_qv.size].reshape(b_qv.shape)
    other_b_up = small.reshape(-1)[b_qv.size :]
    other_qkv = swap(w_qkv)
    other_out, other_up, other_down = swap(w_out), swap(w_up), swap(w_down)
    vecs = jnp.stack([b_out, gain_one, shift_one, b_down, gain_two, shift_two, b_out, b_out])
    b_up_all = jnp.concatenate([b_up, other_b_up])[None]
    q, k, v, mixed, lse = call_forward(number, variates, w_qkv, other_qkv, b_qv, other_b_qv)
    out, hidden, resid, slope, second, gd_a, gd_b, sums_two = call_feed_forward(
        number, variates, mixed, w_out, other_out, w_up, other_up, b_up_all, w_down, other_down, vecs, cotangent
    )
    own_down = lax.psum(gd_a + swap(gd_b), "dp")
    grad_res, grad_mix, delta, gu_a, gu_b, go_a, go_b, sums_one, bup_sum = call_feed_backward(
        second, slope, hidden, resid, mixed, w_out, other_out, w_up, other_up, w_down, other_down, vecs
    )
    vectors = jnp.concatenate(
        [jnp.sum(part.reshape(3, 8, width), axis=1).reshape(-1) for part in (sums_two, sums_one)]
    )
    bup_flat = jnp.sum(bup_sum, axis=0)
    own_up, own_out = lax.psum((gu_a + swap(gu_b), go_a + swap(go_b)), "dp")
    dq, dk, dv = call_backward(number, q, k, v, grad_mix, lse, delta)
    grad_in, gq_a, gq_b, bqv = call_project(variates, dq, dk, dv, w_qkv, other_qkv, grad_res)
    bqv = bqv[:, 0]
    split = b_qv.shape[1]
    mine = jnp.concatenate([bup_flat[:half], bqv[:, :split].reshape(-1)])
    theirs = jnp.concatenate([bup_flat[half:], bqv[:, split:].reshape(-1)])
    own_qkv = lax.psum(gq_a + swap(gq_b), "dp")
    vectors = vectors + swap(vectors)
    mine = mine + swap(theirs)
    count = vectors.shape[0]
    total = lax.psum(jnp.concatenate([vectors, mine]), "dp")
    vec = total[:count].reshape(6, width)
    rest = total[count:]
    return (
        out, grad_in, own_qkv.astype(f32), rest[half:].reshape(2, split), own_out.astype(f32),
        vec[5], vec[3], vec[4], own_up.astype(f32), rest[:half], own_down.astype(f32), vec[2], vec[0], vec[1],
    )


def solution(mesh):
    wide = P(("dp", "mp"), None)
    weights = (P(None, None, "mp"), P(None, "mp"), P("mp", None))
    placed = (wide, P("dp"), *weights, P(), P(), P(), P(None, "mp"), P("mp"), P("mp", None), P(), P(), P(), wide)
    given = (wide, wide, *weights, P(), P(), P(), P(None, "mp"), P("mp"), P("mp", None), P(), P(), P())
    return jax.shard_map(per_device, mesh=mesh, in_specs=placed, out_specs=given, check_vma=False)
```

```python
import jax
import jax.numpy as jnp
from jax import lax
from jax.experimental import pallas as pl
from jax.experimental.pallas import tpu as pltpu
from jax.sharding import PartitionSpec as P

HEAD_DIM = 64
SLOTS = 1424
WIDTHS = (7, 21, 321, 862)
LANES = 1536
CLASSES = 48
BIG = 1e30
EPS = 1e-05
MIB = 2**20

bf16 = jnp.bfloat16
f32 = jnp.float32


def mul(left, right, left_dim=1, right_dim=0):
    return lax.dot_general(
        left, right, (((left_dim,), (right_dim,)), ((), ())), preferred_element_type=f32
    )


def params(limit):
    return pltpu.CompilerParams(vmem_limit_bytes=limit * MIB)


def cover(width, start, stop, last):
    used = SLOTS // width * width
    low = start // width * width
    high = last if stop > used else -(-stop // width) * width
    return (low // 128 * 128, min(-(-min(high, last) // 128) * 128, LANES))


def groups_of(width, rows, step):
    found = []
    for start in range(0, rows, step):
        low, high = cover(width, start, min(start + step, rows), rows)
        if found and found[-1][2] == low and found[-1][2] + found[-1][3] == high:
            first, count = found[-1][:2]
            found[-1] = (first, count + step, low, high - low)
        else:
            found.append((start, step, low, high - low))
    return found


FORWARD = (
    [(128 * i, 128, max(128 * i - 128, 0), min(128 * i + 256, LANES) - max(128 * i - 128, 0)) for i in range(12)],
    groups_of(321, SLOTS, 128),
    [(768, 768, 768, 768), (0, 896, 0, 896)],
)
BACKWARD = (
    FORWARD[0],
    groups_of(321, 1284, 128),
    [(0, 896, 0, 896)],
)


def own_bucket(sets_ref):
    return sets_ref[lax.axis_index("mp")]


def token_class(width):
    token = lax.broadcasted_iota(jnp.int32, (CLASSES, LANES), 1)
    numbers = token.astype(f32)
    held = jnp.floor((numbers + 0.5) * (1.0 / width)).astype(jnp.int32)
    held = jnp.where(token < SLOTS, held, (SLOTS - 1) // width + 1)
    row = lax.broadcasted_iota(jnp.int32, (CLASSES, LANES), 0)
    return held % CLASSES == row


def write_masks(bucket, hot_ref, bar_ref):
    for number, width in enumerate(WIDTHS):

        @pl.when(bucket == number)
        def _():
            same = token_class(width)
            hot_ref[...] = jnp.where(same, 1.0, 0.0).astype(bf16)
            bar_ref[:CLASSES, :] = jnp.where(same, 0.0, -BIG).astype(bf16)

    row = lax.broadcasted_iota(jnp.int32, (16, LANES), 0)
    bar_ref[CLASSES:, :] = jnp.where(row < 3, 1.0, 0.0).astype(bf16)


def split_three(row):
    high = row.astype(bf16)
    rest = row - high.astype(f32)
    middle = rest.astype(bf16)
    low = (rest - middle.astype(f32)).astype(bf16)
    return high, middle, low


def extra_rows(row):
    parts = [p.astype(f32) for p in split_three(row)]
    number = lax.broadcasted_iota(jnp.int32, (16, row.shape[1]), 0)
    held = jnp.where(number == 0, parts[0], jnp.where(number == 1, parts[1], jnp.where(number == 2, parts[2], 0.0)))
    return held.astype(bf16)


def attend_forward(sets_ref, x_ref, wa_ref, wb_ref, ba_ref, bb_ref, q_ref, k_ref, v_ref, o_ref, lse_ref, xt_ref, hot_ref, bar_ref):
    bucket = own_bucket(sets_ref)
    write_masks(bucket, hot_ref, bar_ref)
    tail = jnp.zeros((LANES - SLOTS, x_ref.shape[1]), bf16)
    xt_ref[...] = jnp.concatenate([x_ref[...], tail], axis=0).T
    for side, (w_ref, b_ref) in enumerate(((wa_ref, ba_ref), (wb_ref, bb_ref))):
        for kind, out_ref in enumerate((q_ref, k_ref, v_ref)):
            weight = w_ref[kind].T
            rows = weight.shape[0]
            if kind != 1:
                row = b_ref[kind // 2 : kind // 2 + 1, :].astype(f32)
                column = jnp.broadcast_to(row, (128, rows)).T
                column = jnp.concatenate([column] * 4, axis=1)
            for start in range(0, LANES, 512):
                part = mul(weight, xt_ref[:, start : start + 512])
                if kind != 1:
                    part = part + column
                if kind == 0:
                    part = part * 0.125
                out_ref[side * rows : (side + 1) * rows, start : start + 512] = part.astype(bf16)

    def one_head(head, groups):
        rows = pl.ds(pl.multiple_of(head * 64, 64), 64)
        keep = None
        for q0, nq, k0, nk in groups:
            keys = jnp.concatenate([k_ref[rows, k0 : k0 + nk], bar_ref[:, k0 : k0 + nk]], axis=0).T
            ones = jnp.ones((16, nk), bf16)
            vals = jnp.concatenate([v_ref[rows, k0 : k0 + nk], ones], axis=0)
            for start in range(q0, q0 + nq, 256):
                size = min(256, q0 + nq - start)
                lanes = slice(start, start + size)
                zeros = jnp.zeros((16, size), bf16)
                quer = jnp.concatenate([q_ref[rows, lanes], hot_ref[:, lanes], zeros], axis=0)
                scores = mul(keys, quer)
                top = jnp.max(scores, axis=0, keepdims=True)
                raised = jnp.exp(scores - top).astype(bf16)
                total = mul(vals, raised)
                sums = total[64:65, :]
                mixed = (total[:64, :] * (1.0 / sums)).astype(bf16)
                logs = top + jnp.log(sums)
                if len(groups) == 2 and start == 768:
                    if q0 == 768:
                        keep = (mixed[:, :128], logs[:, :128])
                    else:
                        lane = lax.broadcasted_iota(jnp.int32, (64, 128), 1)
                        mixed = jnp.where(lane < WIDTHS[3] - 768, mixed.astype(f32), keep[0].astype(f32)).astype(bf16)
                        logs = jnp.where(lane[:1] < WIDTHS[3] - 768, logs, keep[1])
                o_ref[rows, lanes] = mixed
                lse_ref[pl.ds(pl.multiple_of(head * 16, 16), 16), lanes] = extra_rows(-logs)

    for group in range(3):
        chosen = (bucket < 2, bucket == 2, bucket == 3)[group]

        @pl.when(chosen)
        def _():
            def pair(number, carry):
                one_head(2 * number, FORWARD[group])
                one_head(2 * number + 1, FORWARD[group])
                return carry

            lax.fori_loop(0, q_ref.shape[0] // 128, pair, 0)


def attend_backward(sets_ref, q_ref, k_ref, v_ref, g_ref, lse_ref, delta_ref, dq_ref, dk_ref, dv_ref, hot_ref, bar_ref, p_ref, s_ref, ka_ref, va_ref):
    bucket = own_bucket(sets_ref)
    write_masks(bucket, hot_ref, bar_ref)

    def one_head(head, groups, slot):
        rows = pl.ds(pl.multiple_of(head * 64, 64), 64)
        more = pl.ds(pl.multiple_of(head * 16, 16), 16)
        single = len(groups) == 1
        if not single:
            ka_ref[...] = jnp.zeros_like(ka_ref)
            va_ref[...] = jnp.zeros_like(va_ref)
        for q0, nq, k0, nk in groups:
            span = slice(k0, k0 + nk)
            held = slice(q0, q0 + nq)
            keys = jnp.concatenate([k_ref[rows, span], bar_ref[:, span]], axis=0)
            vals = jnp.concatenate([v_ref[rows, span], bar_ref[CLASSES:, span]], axis=0)
            for start in range(q0, q0 + nq, 256):
                size = min(256, q0 + nq - start)
                lanes = slice(start, start + size)
                quer = jnp.concatenate(
                    [q_ref[rows, lanes], hot_ref[:, lanes], lse_ref[more, lanes]], axis=0
                )
                grad = jnp.concatenate([g_ref[rows, lanes], delta_ref[more, lanes]], axis=0)
                probs = jnp.exp(mul(quer, keys, 0, 0))
                slopes = probs * mul(grad, vals, 0, 0)
                p_ref[slot, start - q0 : start - q0 + size, :nk] = probs.astype(bf16)
                s_ref[slot, start - q0 : start - q0 + size, :nk] = slopes.astype(bf16)
            dv = mul(g_ref[rows, held], p_ref[slot, :nq, :nk])
            dk = mul(q_ref[rows, held], s_ref[slot, :nq, :nk])
            dq = mul(k_ref[rows, span], s_ref[slot, :nq, :nk], 1, 1)
            dq_ref[rows, held] = (dq * 0.125).astype(bf16)
            if single:
                dv_ref[rows, span] = dv.astype(bf16)
                dk_ref[rows, span] = dk.astype(bf16)
            else:
                va_ref[:, span] += dv
                ka_ref[:, span] += dk
        if single:
            rest = LANES - 896
            for out in (dq_ref, dk_ref, dv_ref):
                out[rows, 896:] = jnp.zeros((64, rest), bf16)
        else:
            dv_ref[rows, :] = va_ref[...].astype(bf16)
            dk_ref[rows, :] = ka_ref[...].astype(bf16)
            done = groups[-1][0] + groups[-1][1]
            if done < LANES:
                dq_ref[rows, done:] = jnp.zeros((64, LANES - done), bf16)

    for group in range(3):
        chosen = (bucket < 2, bucket == 2, bucket == 3)[group]

        @pl.when(chosen)
        def _():
            def pair(number, carry):
                one_head(2 * number, BACKWARD[group], 0)
                one_head(2 * number + 1, BACKWARD[group], 1)
                return carry

            lax.fori_loop(0, q_ref.shape[0] // 128, pair, 0)


TILES = [(i * 256, 256) for i in range(5)] + [(1280, 144)]


def over_tiles(step):
    def body(number, carry):
        step(pl.multiple_of(number * 256, 256), 256)
        return carry

    lax.fori_loop(0, 5, body, 0)
    step(1280, 144)


def mean_of(matrix):
    return jnp.sum(matrix, axis=1, keepdims=True) * (1.0 / matrix.shape[1])


def norm_parts(matrix):
    centre = matrix - mean_of(matrix)
    spread = lax.rsqrt(mean_of(centre * centre) + EPS)
    return centre * spread, spread


def norm_back(scaled, normed, spread):
    return spread * (scaled - mean_of(scaled) - normed * mean_of(scaled * normed))


def fold(matrix):
    return jnp.sum(matrix.reshape(matrix.shape[0] // 8, 8, matrix.shape[1]), axis=0)


def gelu_parts(pre):
    size = jnp.abs(pre)
    t = 1.0 / (1.0 + (0.3275911 * 2.0**-0.5) * size)
    bell = jnp.exp(-0.5 * pre * pre)
    poly = 0.5 * 1.061405429
    for factor in (-1.453152027, 1.421413741, -0.284496736, 0.254829592):
        poly = poly * t + 0.5 * factor
    tail = poly * t * bell
    phi = jnp.where(pre > 0, 1.0 - tail, tail)
    return pre * phi, phi + pre * (bell * (2.0 * jnp.pi) ** -0.5)


HIDDEN_STEP = 512


def row_of(ref):
    return ref[...].astype(f32).reshape(1, ref.shape[0])


def feed_forward(
    sets_ref, x_ref, o_ref, wo_a, wo_b, ua_ref, ub_ref, ba_ref, bb_ref, da_ref, db_ref,
    bo_ref, g1_ref, s1_ref, bd_ref, g2_ref, s2_ref, cot_ref,
    out_ref, hid_ref, res_ref, slope_ref, sec_ref, gd_a, gd_b, sums_ref, act_ref, low_ref,
):
    width = x_ref.shape[1]
    half = ua_ref.shape[1]
    bucket = own_bucket(sets_ref)
    used = SLOTS // WIDTHS[3] * WIDTHS[3]
    for number in range(3):
        used = jnp.where(bucket == number, SLOTS // WIDTHS[number] * WIDTHS[number], used)
    sums_ref[...] = jnp.zeros_like(sums_ref)
    b_out, gain_one, shift_one, b_down, gain_two, shift_two = (
        row_of(ref) for ref in (bo_ref, g1_ref, s1_ref, bd_ref, g2_ref, s2_ref)
    )
    b_up = [row_of(ref) for ref in (ba_ref, bb_ref)]

    def step(start, size):
        rows = pl.ds(start, size)
        lanes = pl.ds(start, 256)
        split = wo_a.shape[0]
        attn = mul(o_ref[:split, lanes], wo_a[...], 0, 0) + mul(o_ref[split:, lanes], wo_b[...], 0, 0)
        resid = x_ref[rows, :].astype(f32) + attn[:size] + b_out
        res_ref[rows, :] = resid
        normed, _ = norm_parts(resid)
        hidden = normed * gain_one + shift_one
        low = hidden.astype(bf16)
        hid_ref[rows, :] = low
        total = None
        for side, (u_ref, d_ref) in enumerate(((ua_ref, da_ref), (ub_ref, db_ref))):
            for at in range(0, half, HIDDEN_STEP):
                place = slice(side * half + at, side * half + at + HIDDEN_STEP)
                pre = mul(low, u_ref[:, at : at + HIDDEN_STEP]) + b_up[side][:, at : at + HIDDEN_STEP]
                active, slope = gelu_parts(pre)
                active = active.astype(bf16)
                act_ref[rows, place] = active
                slope_ref[rows, place] = slope.astype(bf16)
                part = mul(active, d_ref[at : at + HIDDEN_STEP, :])
                total = part if total is None else total + part
        second = hidden + total + b_down
        normed, spread = norm_parts(second)
        out_ref[rows, :] = (normed * gain_two + shift_two).astype(bf16)
        row = start + lax.broadcasted_iota(jnp.int32, (size, width), 0)
        top = jnp.where(row < used, cot_ref[rows, :].astype(f32), 0.0)
        grad = norm_back(top * gain_two, normed, spread)
        sec_ref[rows, :] = grad
        low_ref[rows, :] = grad.astype(bf16)
        sums_ref[0:8, :] += fold(top * normed)
        sums_ref[8:16, :] += fold(top)
        sums_ref[16:24, :] += fold(grad)

    over_tiles(step)
    for side, g_ref in enumerate((gd_a, gd_b)):
        for at in range(0, half, 256):
            place = slice(side * half + at, side * half + at + 256)
            g_ref[at : at + 256, :] = mul(act_ref[:, place], low_ref[...], 0, 0).astype(g_ref.dtype)


CHUNKS = 16
FEED_ROWS = 336
HEAD_ROWS = 208


def slots():
    own = lax.axis_index("dp") % CHUNKS

    def place(chunk):
        held = chunk ^ own
        return held % 4, held // 4

    return place


def feed_backward(
    sec_ref, slope_ref, hid_ref, res_ref, o_ref, wo_a, wo_b, ua_ref, ub_ref, da_ref, db_ref, g1_ref, two_ref,
    gr_ref, g_ref, delta_ref, mine_ref, theirs_ref, pre_ref, mix_ref, sums_ref, bup_ref,
):
    half = ua_ref.shape[1]
    width = hid_ref.shape[1]
    sums_ref[...] = jnp.zeros_like(sums_ref)
    bup_ref[...] = jnp.zeros_like(bup_ref)
    gain_one = row_of(g1_ref)
    mix_ref[SLOTS:, :] = jnp.zeros((LANES - SLOTS, mix_ref.shape[1]), bf16)
    place_of = slots()

    def step(start, size):
        rows = pl.ds(start, size)
        second = sec_ref[rows, :]
        low = second.astype(bf16)
        total = None
        for side, (u_ref, d_ref) in enumerate(((ua_ref, da_ref), (ub_ref, db_ref))):
            for at in range(0, half, HIDDEN_STEP):
                place = slice(side * half + at, side * half + at + HIDDEN_STEP)
                inner = mul(low, d_ref[at : at + HIDDEN_STEP, :], 1, 1)
                pre = (inner * slope_ref[rows, place].astype(f32)).astype(bf16)
                pre_ref[rows, place] = pre
                bup_ref[:, place] += fold(pre.astype(f32))
                part = mul(pre, u_ref[:, at : at + HIDDEN_STEP], 1, 1)
                total = part if total is None else total + part
        hidden = second + total
        normed, spread = norm_parts(res_ref[rows, :])
        grad = norm_back(hidden * gain_one, normed, spread)
        gr_ref[rows, :] = grad
        mix_ref[rows, :] = grad.astype(bf16)
        sums_ref[0:8, :] += fold(hidden * normed)
        sums_ref[8:16, :] += fold(hidden)
        sums_ref[16:24, :] += fold(grad)

    over_tiles(step)
    tall = width // CHUNKS
    for side, out in enumerate((mine_ref, theirs_ref)):
        for at in range(0, half, 256):
            place = slice(side * half + at, side * half + at + 256)
            part = mul(hid_ref[...], pre_ref[:, place], 0, 0).astype(bf16)
            for chunk in range(CHUNKS):
                xy, z = place_of(chunk)
                for block in range(2):
                    row = (at // 128 + block) * tall
                    out[xy, z, row : row + tall, :] = part[chunk * tall : (chunk + 1) * tall, block * 128 : block * 128 + 128]
    split = wo_a.shape[0]
    low = split // CHUNKS
    for side, (out, w_ref) in enumerate(((mine_ref, wo_a), (theirs_ref, wo_b))):
        place = slice(side * split, (side + 1) * split)
        part = mul(o_ref[place, :], mix_ref[...]).astype(bf16)
        for chunk in range(CHUNKS):
            xy, z = place_of(chunk)
            for block in range(width // 128):
                row = half // 128 * tall + block * low
                out[xy, z, row : row + low, :] = part[chunk * low : (chunk + 1) * low, block * 128 : block * 128 + 128]
        for start in range(0, LANES, 512):
            lanes = slice(start, start + 512)
            grad = mul(w_ref[...], mix_ref[lanes, :], 1, 1).astype(bf16)
            g_ref[place, lanes] = grad
            prod = grad.astype(f32) * o_ref[place, lanes].astype(f32)
            for head in range(split // 64):
                at = (side * (split // 64) + head) * 16
                delta = jnp.sum(prod[head * 64 : head * 64 + 64], axis=0, keepdims=True)
                delta_ref[at : at + 16, lanes] = extra_rows(-delta)
    vectors = []
    for ref in (two_ref, sums_ref):
        for kind in range(3):
            total = jnp.sum(ref[8 * kind : 8 * kind + 8, :], axis=0, keepdims=True)
            vectors += [total[:, at : at + 128] for at in range(0, width, 128)]
    number = lax.broadcasted_iota(jnp.int32, (16, 128), 0)
    for side, out in enumerate((mine_ref, theirs_ref)):
        total = jnp.sum(bup_ref[:, side * half : (side + 1) * half], axis=0, keepdims=True)
        held = vectors + [total[:, at : at + 128] for at in range(0, half, 128)]
        each = len(held) // CHUNKS
        for chunk in range(CHUNKS):
            xy, z = place_of(chunk)
            block = jnp.zeros((16, 128), f32)
            for row in range(each):
                block = jnp.where(number == row, held[chunk * each + row], block)
            out[xy, z, FEED_ROWS - 16 :, :] = block.astype(bf16)


def project_weights(x_ref, dqa_ref, dka_ref, dva_ref, dqb_ref, dkb_ref, dvb_ref, mine_ref, theirs_ref, xt_ref):
    tail = jnp.zeros((LANES - SLOTS, x_ref.shape[1]), bf16)
    xt_ref[...] = jnp.concatenate([x_ref[...], tail], axis=0).T
    width = x_ref.shape[1]
    tall = width // CHUNKS
    ones = jnp.ones((8, LANES), bf16)
    place_of = slots()
    for out, refs in ((mine_ref, (dqa_ref, dka_ref, dva_ref)), (theirs_ref, (dqb_ref, dkb_ref, dvb_ref))):
        sums = []
        for kind, d_ref in enumerate(refs):
            part = mul(xt_ref[...], d_ref[...], 1, 1).astype(bf16)
            blocks = part.shape[1] // 128
            for chunk in range(CHUNKS):
                xy, z = place_of(chunk)
                for block in range(blocks):
                    row = (kind * blocks + block) * tall
                    out[xy, z, row : row + tall, :] = part[chunk * tall : (chunk + 1) * tall, block * 128 : block * 128 + 128]
            if kind != 1:
                total = mul(ones, d_ref[...], 1, 1)[:1]
                sums += [total[:, block * 128 : block * 128 + 128] for block in range(blocks)]
        number = lax.broadcasted_iota(jnp.int32, (16, 128), 0)
        for chunk in range(CHUNKS):
            xy, z = place_of(chunk)
            held = jnp.where(number == 0, sums[chunk] if chunk < len(sums) else 0.0, 0.0)
            out[xy, z, HEAD_ROWS - 16 :, :] = held.astype(bf16)


def project_input(dqa_ref, dka_ref, dva_ref, dqb_ref, dkb_ref, dvb_ref, wa_ref, wb_ref, gr_ref, gi_ref, wt_ref):
    rows = wa_ref.shape[2]
    for side, w_ref in enumerate((wa_ref, wb_ref)):
        for kind in range(3):
            wt_ref[kind, side * rows : (side + 1) * rows, :] = w_ref[kind].T
    for start in range(0, SLOTS, 256):
        size = min(256, SLOTS - start)
        lanes = slice(start, start + 256)
        total = gr_ref[start : start + size, :]
        for side, refs in enumerate(((dqa_ref, dka_ref, dva_ref), (dqb_ref, dkb_ref, dvb_ref))):
            for kind, d_ref in enumerate(refs):
                total = total + mul(d_ref[:, lanes], wt_ref[kind, side * rows : (side + 1) * rows, :], 0, 0)[:size]
        gi_ref[start : start + size, :] = total


def add_pair(mine_ref, theirs_ref, *outs):
    for number, out in enumerate(outs):
        out[...] = (mine_ref[number].astype(f32) + theirs_ref[number].astype(f32)).astype(bf16)


def add_four(a_ref, b_ref, c_ref, d_ref, *outs):
    for number, out in enumerate(outs):
        held = slice(None) if len(outs) == 1 else number
        low = a_ref[held].astype(f32) + b_ref[held].astype(f32)
        out[...] = (low + (c_ref[held].astype(f32) + d_ref[held].astype(f32))).astype(bf16)


def lay_four(a_ref, b_ref, c_ref, d_ref, out_ref):
    for number, ref in enumerate((a_ref, b_ref, c_ref, d_ref)):
        out_ref[number] = ref[...]


def each_chunk(refs):
    own = lax.axis_index("dp") % CHUNKS
    for xy, ref in enumerate(refs):
        for z in range(4):
            yield (z * 4 + xy) ^ own, ref[z].astype(f32)


def spread_feed(a_ref, b_ref, c_ref, d_ref, up_ref, out_ref, g2_ref, s2_ref, bd_ref, g1_ref, s1_ref, bo_ref, bup_ref, keep_ref):
    width, half = up_ref.shape
    tall, low = width // CHUNKS, out_ref.shape[0] // CHUNKS
    for chunk, held in each_chunk((a_ref, b_ref, c_ref, d_ref)):
        rows = pl.ds(pl.multiple_of(chunk * tall, tall), tall)
        for block in range(half // 128):
            up_ref[rows, block * 128 : block * 128 + 128] = held[block * tall : (block + 1) * tall]
        rows = pl.ds(pl.multiple_of(chunk * low, low), low)
        base = half // 128 * tall
        for block in range(width // 128):
            out_ref[rows, block * 128 : block * 128 + 128] = held[base + block * low : base + (block + 1) * low]
        keep_ref[chunk] = held[FEED_ROWS - 16 :]
    refs = [(ref, at) for ref in (g2_ref, s2_ref, bd_ref, g1_ref, s1_ref, bo_ref, bup_ref) for at in range(0, ref.shape[0], 128)]
    each = len(refs) // CHUNKS
    for number, (ref, at) in enumerate(refs):
        ref[at : at + 128] = keep_ref[number // each, number % each, :]


def spread_heads(a_ref, b_ref, c_ref, d_ref, qkv_ref, bias_ref, keep_ref):
    kinds, width, half = qkv_ref.shape
    tall = width // CHUNKS
    for chunk, held in each_chunk((a_ref, b_ref, c_ref, d_ref)):
        rows = pl.ds(pl.multiple_of(chunk * tall, tall), tall)
        for kind in range(kinds):
            for block in range(half // 128):
                row = (kind * (half // 128) + block) * tall
                qkv_ref[kind, rows, block * 128 : block * 128 + 128] = held[row : row + tall]
        keep_ref[chunk] = held[HEAD_ROWS - 16 :]
    blocks = half // 128
    for number in range(2 * blocks):
        at = number % blocks * 128
        bias_ref[number // blocks : number // blocks + 1, at : at + 128] = keep_ref[number, 0:1, :]


def shape(dims, kind=bf16):
    return jax.ShapeDtypeStruct(dims, kind)


smem = pl.BlockSpec(memory_space=pltpu.SMEM)


def specs(count):
    return [smem] + [pl.BlockSpec(memory_space=pltpu.VMEM)] * (count - 1)


def cost(flops, moved, powers=0):
    return pl.CostEstimate(flops=int(flops), bytes_accessed=int(moved), transcendentals=int(powers))


def call_forward(sets, x, wa, wb, ba, bb):
    width = 2 * wa.shape[2]
    big = shape((width, LANES))
    return pl.pallas_call(
        attend_forward, name="attend_forward",
        out_shape=[big, big, big, big, shape((width // 4, LANES))],
        in_specs=specs(6),
        scratch_shapes=[pltpu.VMEM((x.shape[1], LANES), bf16), pltpu.VMEM((CLASSES, LANES), bf16), pltpu.VMEM((64, LANES), bf16)],
        compiler_params=params(40), cost_estimate=cost(14e9, 12e6),
    )(sets, x, wa, wb, ba, bb)


def call_feed_forward(sets, x, mixed, wo_a, wo_b, up_a, up_b, bu_a, bu_b, down_a, down_b, vecs, cot):
    rows, width = x.shape
    half = up_a.shape[1]
    return pl.pallas_call(
        feed_forward, name="feed_forward",
        out_shape=[
            shape((rows, width)), shape((rows, width)), shape((rows, width), f32), shape((rows, 2 * half)),
            shape((rows, width), f32), shape((half, width)), shape((half, width)), shape((24, width), f32),
        ],
        in_specs=specs(18),
        scratch_shapes=[pltpu.VMEM((rows, 2 * half), bf16), pltpu.VMEM((rows, width), bf16)],
        compiler_params=params(56), cost_estimate=cost(14e9, 20e6),
    )(sets, x, mixed, wo_a, wo_b, up_a, up_b, bu_a, bu_b, down_a, down_b, *vecs, cot)


def call_feed_backward(second, slope, hidden, resid, mixed, wo_a, wo_b, up_a, up_b, down_a, down_b, gain, sums):
    rows, width = second.shape
    half = up_a.shape[1]
    split = wo_a.shape[0]
    piece = shape((4, 4, FEED_ROWS, 128))
    return pl.pallas_call(
        feed_backward, name="feed_backward",
        out_shape=[shape((rows, width), f32), shape((2 * split, LANES)), shape((2 * split // 4, LANES)), piece, piece],
        scratch_shapes=[
            pltpu.VMEM((rows, 2 * half), bf16), pltpu.VMEM((LANES, width), bf16),
            pltpu.VMEM((24, width), f32), pltpu.VMEM((8, 2 * half), f32),
        ],
        compiler_params=params(56), cost_estimate=cost(14e9, 20e6),
    )(second, slope, hidden, resid, mixed, wo_a, wo_b, up_a, up_b, down_a, down_b, gain, sums)


def call_backward(part, sets, q, k, v, grad, lse, delta):
    rows = q.shape[0] // 2
    big = shape((rows, LANES))
    half = pl.BlockSpec((rows, LANES), lambda i: (part, 0))
    more = pl.BlockSpec((rows // 4, LANES), lambda i: (part, 0))
    return pl.pallas_call(
        attend_backward, name="attend_backward", grid=(1,),
        out_shape=[big, big, big],
        out_specs=[pl.BlockSpec((rows, LANES), lambda i: (0, 0))] * 3,
        in_specs=[smem, half, half, half, half, more, more],
        scratch_shapes=[
            pltpu.VMEM((CLASSES, LANES), bf16), pltpu.VMEM((64, LANES), bf16),
            pltpu.VMEM((2, 896, 896), bf16), pltpu.VMEM((2, 896, 896), bf16),
            pltpu.VMEM((64, LANES), f32), pltpu.VMEM((64, LANES), f32),
        ],
        compiler_params=params(40), cost_estimate=cost(8e9, 6e6),
    )(sets, q, k, v, grad, lse, delta)


def call_project_weights(x, own, other):
    width = x.shape[1]
    piece = shape((4, 4, HEAD_ROWS, 128))
    return pl.pallas_call(
        project_weights, name="project_weights", out_shape=[piece, piece],
        scratch_shapes=[pltpu.VMEM((width, LANES), bf16)],
        compiler_params=params(40), cost_estimate=cost(2.4e9, 8e6),
    )(x, *own, *other)


def call_project_input(own, other, wa, wb, resid):
    return pl.pallas_call(
        project_input, name="project_input", out_shape=shape(resid.shape, f32),
        scratch_shapes=[pltpu.VMEM((3, 2 * wa.shape[2], wa.shape[1]), bf16)],
        compiler_params=params(40), cost_estimate=cost(2.4e9, 12e6),
    )(*own, *other, wa, wb, resid)


def swap(array):
    return lax.ppermute(array, "mp", [(0, 1), (1, 0)])


def exchange(array, distance):
    count = lax.axis_size("dp")
    return lax.ppermute(array, "dp", [(i, i ^ distance) for i in range(count)])


def small(kernel, name, outs, scratch=()):
    moved = 2 * sum(o.size * o.dtype.itemsize for o in outs)
    return pl.pallas_call(
        kernel, name=name, out_shape=list(outs), scratch_shapes=list(scratch),
        compiler_params=params(24), cost_estimate=cost(1e6, moved),
    )


def reduce_piece(mine, theirs):
    _, _, rows, lanes = mine.shape
    group, one = shape((4, rows, lanes)), shape((rows, lanes))
    parts = small(add_pair, "add_pair", [group] * 4)(mine, swap(theirs))
    came = [exchange(parts[xy], xy) for xy in (1, 2, 3)]
    parts = small(add_four, "add_four", [one] * 4)(parts[0], *came)
    came = [exchange(parts[z], 4 * z) for z in (1, 2, 3)]
    (total,) = small(add_four, "add_four", [one])(parts[0], *came)
    distance = CHUNKS
    while distance < lax.axis_size("dp"):
        total = total + exchange(total, distance)
        distance *= 2
    (held,) = small(lay_four, "lay_four", [group])(total, *(exchange(total, 4 * z) for z in (1, 2, 3)))
    return [held, *(exchange(held, xy) for xy in (1, 2, 3))]


def per_device(
    variates, dataset, w_qkv, b_qv, w_out, b_out, gain_one, shift_one, w_up, b_up, w_down, b_down, gain_two, shift_two, cotangent,
):
    width, half = w_up.shape
    other_qkv, other_bias = swap(w_qkv), swap(b_qv)
    other_out, other_up, other_bup, other_down = swap(w_out), swap(w_up), swap(b_up), swap(w_down)
    q, k, v, mixed, lse = call_forward(dataset, variates, w_qkv, other_qkv, b_qv, other_bias)
    out, hidden, resid, slope, second, down_mine, down_theirs, sums = call_feed_forward(
        dataset, variates, mixed, w_out, other_out, w_up, other_up, b_up, other_bup, w_down, other_down,
        (b_out, gain_one, shift_one, b_down, gain_two, shift_two), cotangent,
    )
    grad_down = lax.psum(down_mine + swap(down_theirs), "dp")
    grad_res, grad_mix, delta, mine, theirs = call_feed_backward(
        second, slope, hidden, resid, mixed, w_out, other_out, w_up, other_up, w_down, other_down, gain_one, sums
    )
    feed = reduce_piece(mine, theirs)
    own = call_backward(0, dataset, q, k, v, grad_mix, lse, delta)
    other = call_backward(1, dataset, q, k, v, grad_mix, lse, delta)
    heads = reduce_piece(*call_project_weights(variates, own, other))
    grad_in = call_project_input(own, other, w_qkv, other_qkv, grad_res)
    vector = shape((width,), f32)
    outs = [shape((width, half), f32), shape(w_out.shape, f32)] + [vector] * 6 + [shape((half,), f32)]
    keep = [pltpu.VMEM((CHUNKS, 16, 128), f32)]
    grad_up, grad_out, two_gain, two_shift, down_bias, one_gain, one_shift, out_bias, up_bias = small(
        spread_feed, "spread_feed", outs, keep
    )(*feed)
    grad_qkv, bias = small(spread_heads, "spread_heads", [shape(w_qkv.shape, f32), shape(b_qv.shape, f32)], keep)(*heads)
    return (
        out, grad_in, grad_qkv, bias, grad_out, out_bias, one_gain, one_shift, grad_up, up_bias,
        grad_down.astype(f32), down_bias, two_gain, two_shift,
    )


def solution(mesh):
    wide = P(("dp", "mp"), None)
    weights = (P(None, None, "mp"), P(None, "mp"), P("mp", None))
    placed = (wide, P("dp"), *weights, P(), P(), P(), P(None, "mp"), P("mp"), P("mp", None), P(), P(), P(), wide)
    given = (wide, wide, *weights, P(), P(), P(), P(None, "mp"), P("mp"), P("mp", None), P(), P(), P())
    return jax.shard_map(per_device, mesh=mesh, in_specs=placed, out_specs=given, check_vma=False)
```

```python
import functools

import jax
import jax.numpy as jnp
from jax import lax
from jax.experimental import pallas as pl
from jax.experimental.pallas import tpu as pltpu
from jax.sharding import PartitionSpec as P

HEAD_DIM = 64
SLOTS = 1424
WIDTHS = (7, 21, 321, 862)
LANES = 1536
CLASSES = 80
BIG = 1e30
EPS = 1e-05
MIB = 2**20

bf16 = jnp.bfloat16
f32 = jnp.float32


def mul(left, right, left_dim=1, right_dim=0):
    return lax.dot_general(
        left, right, (((left_dim,), (right_dim,)), ((), ())), preferred_element_type=f32
    )


def params(limit):
    return pltpu.CompilerParams(vmem_limit_bytes=limit * MIB)


def cover(width, start, stop, last):
    used = SLOTS // width * width
    low = start // width * width
    high = last if stop > used else -(-stop // width) * width
    return (low // 128 * 128, min(-(-min(high, last) // 128) * 128, LANES))


def groups_of(width, rows, step):
    found = []
    for start in range(0, rows, step):
        low, high = cover(width, start, min(start + step, rows), rows)
        if found and found[-1][2] == low and found[-1][2] + found[-1][3] == high:
            first, count = found[-1][:2]
            found[-1] = (first, count + step, low, high - low)
        else:
            found.append((start, step, low, high - low))
    return found


FORWARD = (
    [(256 * i, 256, max(256 * i - 128, 0), min(256 * i + 384, LANES) - max(256 * i - 128, 0)) for i in range(6)],
    groups_of(321, SLOTS, 128),
    [(768, 768, 768, 768), (0, 896, 0, 896)],
)
BACKWARD = (
    FORWARD[0],
    groups_of(321, 1284, 128),
    [(0, 896, 0, 896)],
)


def own_bucket(sets_ref):
    return sets_ref[lax.axis_index("mp")]


def token_class(width):
    token = lax.broadcasted_iota(jnp.int32, (CLASSES, LANES), 1)
    numbers = token.astype(f32)
    held = jnp.floor((numbers + 0.5) * (1.0 / width)).astype(jnp.int32)
    held = jnp.where(token < SLOTS, held, (SLOTS - 1) // width + 1)
    row = lax.broadcasted_iota(jnp.int32, (CLASSES, LANES), 0)
    return held % CLASSES == row


def write_masks(bucket, hot_ref, bar_ref):
    for number, width in enumerate(WIDTHS):

        @pl.when(bucket == number)
        def _():
            same = token_class(width)
            hot_ref[...] = jnp.where(same, 1.0, 0.0).astype(bf16)
            bar_ref[:CLASSES, :] = jnp.where(same, 0.0, -BIG).astype(bf16)

    row = lax.broadcasted_iota(jnp.int32, (16, LANES), 0)
    bar_ref[CLASSES:, :] = jnp.where(row < 3, 1.0, 0.0).astype(bf16)


def split_three(row):
    high = row.astype(bf16)
    rest = row - high.astype(f32)
    middle = rest.astype(bf16)
    low = (rest - middle.astype(f32)).astype(bf16)
    return high, middle, low


def extra_rows(row):
    parts = [p.astype(f32) for p in split_three(row)]
    number = lax.broadcasted_iota(jnp.int32, (16, row.shape[1]), 0)
    held = jnp.where(number == 0, parts[0], jnp.where(number == 1, parts[1], jnp.where(number == 2, parts[2], 0.0)))
    return held.astype(bf16)


LOG_E = 1.4426950408889634
SAFE = 60.0
WITH = 2
TOGETHER = 1


def attend_forward(
    sets_ref, x_hbm, wa_hbm, wb_hbm, ba_ref, bb_ref, q_hbm, k_hbm, v_hbm, o_hbm, lse_hbm,
    x_ref, wa_ref, wb_ref, q_ref, k_ref, v_ref, o_ref, lse_ref, xt_ref, hot_ref, bar_ref, in_sems, out_sems,
):
    loads = [pltpu.make_async_copy(*pair, in_sems.at[i]) for i, pair in enumerate(((x_hbm, x_ref), (wa_hbm, wa_ref), (wb_hbm, wb_ref)))]
    for load in loads:
        load.start()
    pairs = ((q_ref, q_hbm), (k_ref, k_hbm), (v_ref, v_hbm), (o_ref, o_hbm), (lse_ref, lse_hbm))
    stores = [pltpu.make_async_copy(*pair, out_sems.at[i]) for i, pair in enumerate(pairs)]
    bucket = own_bucket(sets_ref)
    write_masks(bucket, hot_ref, bar_ref)
    tail = jnp.zeros((LANES - SLOTS, x_ref.shape[1]), bf16)
    loads[0].wait()
    xt_ref[...] = jnp.concatenate([x_ref[...], tail], axis=0).T
    worst = None
    for side, (w_ref, b_ref) in enumerate(((wa_ref, ba_ref), (wb_ref, bb_ref))):
        loads[1 + side].wait()
        for kind, out_ref in enumerate((q_ref, k_ref, v_ref)):
            weight = w_ref[kind].T
            rows = weight.shape[0]
            if kind != 1:
                row = b_ref[kind // 2 : kind // 2 + 1, :].astype(f32)
                column = jnp.broadcast_to(row, (128, rows)).T
                column = jnp.concatenate([column] * 4, axis=1)
            for start in range(0, LANES, 512):
                part = mul(weight, xt_ref[:, start : start + 512])
                if kind != 1:
                    part = part + column
                if kind == 0:
                    part = part * 0.125
                out_ref[side * rows : (side + 1) * rows, start : start + 512] = part.astype(bf16)
    for store in stores[:3]:
        store.start()
    heads = q_ref.shape[0] // 64
    for head in range(heads):
        norms = []
        for ref in (q_ref, k_ref):
            held = ref[head * 64 : head * 64 + 64, :].astype(f32)
            norms.append(jnp.max(jnp.sum(held * held, axis=0, keepdims=True), axis=1, keepdims=True))
        both = norms[0] * norms[1]
        worst = both if worst is None else jnp.maximum(worst, both)
    calm = worst[0, 0] < SAFE * SAFE

    def one_head(head, groups, plain):
        rows = pl.ds(pl.multiple_of(head * 64, 64), 64)
        keep = None
        jobs = []
        for q0, nq, k0, nk in groups:
            for start in range(q0, q0 + nq, 256):
                jobs.append((q0, start, min(256, q0 + nq - start), k0, nk))
        held = {}

        def scores_of(job):
            q0, start, size, k0, nk = job
            if (k0, nk) not in held:
                held[k0, nk] = jnp.concatenate([k_ref[rows, k0 : k0 + nk], bar_ref[:CLASSES, k0 : k0 + nk]], axis=0).T
            lanes = slice(start, start + size)
            quer = jnp.concatenate([q_ref[rows, lanes], hot_ref[:, lanes]], axis=0)
            return mul(held[k0, nk], quer)

        ahead = scores_of(jobs[0])
        for number, job in enumerate(jobs):
            q0, start, size, k0, nk = job
            lanes = slice(start, start + size)
            scores = ahead
            if number + 1 < len(jobs):
                ahead = scores_of(jobs[number + 1])
            if plain:
                raised = jnp.exp2(scores * LOG_E).astype(bf16)
            else:
                top = jnp.max(scores, axis=0, keepdims=True)
                raised = jnp.exp(scores - top).astype(bf16)
            vals = jnp.concatenate([v_ref[rows, k0 : k0 + nk], jnp.ones((16, nk), bf16)], axis=0)
            total = mul(vals, raised)
            sums = total[64:65, :]
            mixed = (total[:64, :] * (1.0 / sums)).astype(bf16)
            logs = jnp.log(sums)
            if not plain:
                logs = logs + top
            if len(groups) == 2 and start == 768:
                if q0 == 768:
                    keep = (mixed[:, :128], logs[:, :128])
                else:
                    lane = lax.broadcasted_iota(jnp.int32, (64, 128), 1)
                    mixed = jnp.where(lane < WIDTHS[3] - 768, mixed.astype(f32), keep[0].astype(f32)).astype(bf16)
                    logs = jnp.where(lane[:1] < WIDTHS[3] - 768, logs, keep[1])
            o_ref[rows, lanes] = mixed
            lse_ref[pl.ds(pl.multiple_of(head * 16, 16), 16), lanes] = extra_rows(-logs)

    def narrow(head, start, first, plain):
        rows = pl.ds(pl.multiple_of(head * 64, 64), 64)
        lanes, span = pl.ds(start, 256), pl.ds(first, 512)
        keys = jnp.concatenate([k_ref[rows, span], bar_ref[:CLASSES, span]], axis=0)
        quer = jnp.concatenate([q_ref[rows, lanes], hot_ref[:, lanes]], axis=0)
        return mul(keys, quer, 0, 0)

    def finish(head, start, first, scores, plain):
        rows = pl.ds(pl.multiple_of(head * 64, 64), 64)
        lanes, span = pl.ds(start, 256), pl.ds(first, 512)
        if plain:
            raised = jnp.exp2(scores * LOG_E).astype(bf16)
        else:
            top = jnp.max(scores, axis=0, keepdims=True)
            raised = jnp.exp(scores - top).astype(bf16)
        vals = jnp.concatenate([v_ref[rows, span], jnp.ones((16, 512), bf16)], axis=0)
        total = mul(vals, raised)
        sums = total[64:65, :]
        o_ref[rows, lanes] = (total[:64, :] * (1.0 / sums)).astype(bf16)
        logs = jnp.log(sums)
        if not plain:
            logs = logs + top
        lse_ref[pl.ds(pl.multiple_of(head * 16, 16), 16), lanes] = extra_rows(-logs)

    for group in range(3):
        chosen = (bucket < 2, bucket == 2, bucket == 3)[group]
        for plain in (True, False):

            @pl.when(jnp.logical_and(chosen, calm == plain))
            def _():
                if group == 0:

                    def turn(number, carry):
                        tile = number % 6
                        start = pl.multiple_of(tile * 256, 256)
                        first = pl.multiple_of(jnp.clip(tile * 256 - 128, 0, LANES - 512), 128)
                        heads_now = [number // 6 * WITH + i for i in range(WITH)]
                        held = [narrow(head, start, first, plain) for head in heads_now]
                        for head, scores in zip(heads_now, held):
                            finish(head, start, first, scores, plain)
                        return carry

                    lax.fori_loop(0, heads // WITH * 6, turn, 0)
                else:

                    def single(number, carry):
                        for i in range(TOGETHER):
                            one_head(TOGETHER * number + i, FORWARD[group], plain)
                        return carry

                    lax.fori_loop(0, heads // TOGETHER, single, 0)

    for store in stores[3:]:
        store.start()
    for store in stores:
        store.wait()


def copies(pairs, sems):
    return [pltpu.make_async_copy(*pair, sems.at[i]) for i, pair in enumerate(pairs)]


def attend_backward(
    part, sets_ref, q_hbm, k_hbm, v_hbm, g_hbm, lse_hbm, delta_hbm, x_hbm, dq_hbm, dk_hbm, dv_hbm, piece_ref,
    q_ref, k_ref, v_ref, g_ref, lse_ref, delta_ref, x_ref, dq_ref, dk_ref, dv_ref, xt_ref,
    hot_ref, bar_ref, p_ref, s_ref, ka_ref, va_ref, head_sems, in_sems, out_sems,
):
    half = q_ref.shape[0]

    def loads_of(number):
        there = pl.ds(part * half + number * 128, 128)
        here = pl.ds(number * 128, 128)
        pairs = [(far.at[there], near.at[here]) for far, near in ((q_hbm, q_ref), (k_hbm, k_ref), (v_hbm, v_ref), (g_hbm, g_ref))]
        there = pl.ds(part * (half // 4) + number * 32, 32)
        here = pl.ds(number * 32, 32)
        pairs += [(far.at[there], near.at[here]) for far, near in ((lse_hbm, lse_ref), (delta_hbm, delta_ref))]
        return copies(pairs, head_sems.at[number])

    def stores_of(number):
        here = pl.ds(number * 128, 128)
        return copies([(near.at[here], far.at[here]) for near, far in ((dq_ref, dq_hbm), (dk_ref, dk_hbm), (dv_ref, dv_hbm))], out_sems.at[number])

    for number in range(half // 128):
        for load in loads_of(number):
            load.start()
    given = copies([(x_hbm, x_ref)], in_sems)[0]
    given.start()
    bucket = own_bucket(sets_ref)
    write_masks(bucket, hot_ref, bar_ref)

    def one_head(head, groups, slot):
        rows = pl.ds(pl.multiple_of(head * 64, 64), 64)
        more = pl.ds(pl.multiple_of(head * 16, 16), 16)
        single = len(groups) == 1
        if not single:
            ka_ref[slot] = jnp.zeros(ka_ref.shape[1:], f32)
            va_ref[slot] = jnp.zeros(va_ref.shape[1:], f32)
        for q0, nq, k0, nk in groups:
            span = slice(k0, k0 + nk)
            held = slice(q0, q0 + nq)
            keys = jnp.concatenate([k_ref[rows, span], bar_ref[:, span]], axis=0)
            vals = jnp.concatenate([v_ref[rows, span], bar_ref[CLASSES:, span]], axis=0)
            for start in range(q0, q0 + nq, 256):
                size = min(256, q0 + nq - start)
                lanes = slice(start, start + size)
                quer = jnp.concatenate([q_ref[rows, lanes], hot_ref[:, lanes], lse_ref[more, lanes]], axis=0)
                grad = jnp.concatenate([g_ref[rows, lanes], delta_ref[more, lanes]], axis=0)
                probs = jnp.exp2(mul(quer, keys, 0, 0) * LOG_E)
                slopes = probs * mul(grad, vals, 0, 0)
                p_ref[slot, start - q0 : start - q0 + size, :nk] = probs.astype(bf16)
                s_ref[slot, start - q0 : start - q0 + size, :nk] = slopes.astype(bf16)
            dv = mul(g_ref[rows, held], p_ref[slot, :nq, :nk])
            dk = mul(q_ref[rows, held], s_ref[slot, :nq, :nk])
            dq = mul(k_ref[rows, span], s_ref[slot, :nq, :nk], 1, 1)
            dq_ref[rows, held] = (dq * 0.125).astype(bf16)
            if single:
                dv_ref[rows, span] = dv.astype(bf16)
                dk_ref[rows, span] = dk.astype(bf16)
            else:
                va_ref[slot, :, span] += dv
                ka_ref[slot, :, span] += dk
        if single:
            rest = LANES - 896
            for out in (dq_ref, dk_ref, dv_ref):
                out[rows, 896:] = jnp.zeros((64, rest), bf16)
        else:
            dv_ref[rows, :] = va_ref[slot].astype(bf16)
            dk_ref[rows, :] = ka_ref[slot].astype(bf16)
            done = groups[-1][0] + groups[-1][1]
            if done < LANES:
                dq_ref[rows, done:] = jnp.zeros((64, LANES - done), bf16)

    def narrow(head, start, first, slot):
        rows = pl.ds(pl.multiple_of(head * 64, 64), 64)
        more = pl.ds(pl.multiple_of(head * 16, 16), 16)
        lanes, span = pl.ds(start, 256), pl.ds(first, 512)
        keys = jnp.concatenate([k_ref[rows, span], bar_ref[:, span]], axis=0)
        vals = jnp.concatenate([v_ref[rows, span], bar_ref[CLASSES:, span]], axis=0)
        quer = jnp.concatenate([q_ref[rows, lanes], hot_ref[:, lanes], lse_ref[more, lanes]], axis=0)
        grad = jnp.concatenate([g_ref[rows, lanes], delta_ref[more, lanes]], axis=0)
        probs = jnp.exp2(mul(quer, keys, 0, 0) * LOG_E)
        slopes = (probs * mul(grad, vals, 0, 0)).astype(bf16)
        va_ref[slot, :, span] += mul(g_ref[rows, lanes], probs.astype(bf16))
        ka_ref[slot, :, span] += mul(q_ref[rows, lanes], slopes)
        dq_ref[rows, lanes] = (mul(k_ref[rows, span], slopes, 1, 1) * 0.125).astype(bf16)

    for group in range(3):
        chosen = (bucket < 2, bucket == 2, bucket == 3)[group]

        @pl.when(chosen)
        def _():
            def pair(number, carry):
                for load in loads_of(number):
                    load.wait()
                if group == 0:
                    ka_ref[...] = jnp.zeros_like(ka_ref)
                    va_ref[...] = jnp.zeros_like(va_ref)

                    def turn(tile, carry):
                        start = pl.multiple_of(tile * 256, 256)
                        first = pl.multiple_of(jnp.clip(tile * 256 - 128, 0, LANES - 512), 128)
                        for slot in range(2):
                            narrow(2 * number + slot, start, first, slot)
                        return carry

                    lax.fori_loop(0, 6, turn, 0)
                    for slot in range(2):
                        rows = pl.ds(pl.multiple_of((2 * number + slot) * 64, 64), 64)
                        dv_ref[rows, :] = va_ref[slot].astype(bf16)
                        dk_ref[rows, :] = ka_ref[slot].astype(bf16)
                else:
                    one_head(2 * number, BACKWARD[group], 0)
                    one_head(2 * number + 1, BACKWARD[group], 1)
                for store in stores_of(number):
                    store.start()
                return carry

            lax.fori_loop(0, half // 128, pair, 0)

    given.wait()
    width = x_ref.shape[1]
    tail = jnp.zeros((LANES - SLOTS, width), bf16)
    xt_ref[...] = jnp.concatenate([x_ref[...], tail], axis=0).T
    tall = width // CHUNKS
    ones = jnp.ones((8, LANES), bf16)
    place_of = slots()
    sums = []
    blocks = half // 128
    for kind, d_ref in enumerate((dq_ref, dk_ref, dv_ref)):
        product = mul(xt_ref[...], d_ref[...], 1, 1).astype(bf16)
        for chunk in range(CHUNKS):
            xy, z = place_of(chunk)
            for block in range(blocks):
                row = (kind * blocks + block) * tall
                piece_ref[xy, z, row : row + tall, :] = product[chunk * tall : (chunk + 1) * tall, block * 128 : block * 128 + 128]
        if kind != 1:
            total = mul(ones, d_ref[...], 1, 1)[:1]
            sums += [total[:, block * 128 : block * 128 + 128] for block in range(blocks)]
    number = lax.broadcasted_iota(jnp.int32, (16, 128), 0)
    for chunk in range(CHUNKS):
        xy, z = place_of(chunk)
        held = jnp.where(number == 0, sums[chunk] if chunk < len(sums) else 0.0, 0.0)
        piece_ref[xy, z, HEAD_ROWS - 16 :, :] = held.astype(bf16)
    for number in range(half // 128):
        for store in stores_of(number):
            store.wait()


TILES = [(i * 256, 256) for i in range(5)] + [(1280, 144)]


def over_tiles(step):
    def body(number, carry):
        step(number, pl.multiple_of(number * 256, 256), 256)
        return carry

    lax.fori_loop(0, 5, body, 0)
    step(5, *TILES[5])


def mean_of(matrix):
    return jnp.sum(matrix, axis=1, keepdims=True) * (1.0 / matrix.shape[1])


def norm_parts(matrix):
    centre = matrix - mean_of(matrix)
    spread = lax.rsqrt(mean_of(centre * centre) + EPS)
    return centre * spread, spread


def norm_back(scaled, normed, spread):
    return spread * (scaled - mean_of(scaled) - normed * mean_of(scaled * normed))


def fold(matrix):
    return jnp.sum(matrix.reshape(matrix.shape[0] // 8, 8, matrix.shape[1]), axis=0)


def gelu_parts(pre):
    size = jnp.abs(pre)
    t = pl.reciprocal(1.0 + (0.3275911 * 2.0**-0.5) * size)
    bell = jnp.exp2((-0.5 * LOG_E) * (pre * pre))
    poly = 0.5 * 1.061405429
    for factor in (-1.453152027, 1.421413741, -0.284496736, 0.254829592):
        poly = poly * t + 0.5 * factor
    tail = poly * t * bell
    phi = jnp.where(pre > 0, 1.0 - tail, tail)
    return pre * phi, phi + pre * (bell * (2.0 * jnp.pi) ** -0.5)


HIDDEN_STEP = 512


def row_of(ref):
    return ref[...].astype(f32).reshape(1, ref.shape[0])


def feed_forward(
    sets_ref, x_hbm, o_hbm, wo_a, wo_b, ua_hbm, ub_hbm, ba_ref, bb_ref, da_hbm, db_hbm,
    bo_ref, g1_ref, s1_ref, bd_ref, g2_ref, s2_ref, cot_hbm,
    out_hbm, hid_hbm, res_hbm, slope_hbm, sec_hbm, gd_a, gd_b, sums_ref,
    x_ref, o_ref, wo_ref, u_ref, d_ref, cot_ref, out_ref, hid_ref, res_ref, slope_ref, sec_ref, gd_ref, act_ref, low_ref,
    in_sems, row_sems, out_sems,
):
    half = ua_hbm.shape[1]
    split = wo_a.shape[0]
    pairs = [(o_hbm, o_ref), (wo_a, wo_ref.at[pl.ds(0, split)]), (wo_b, wo_ref.at[pl.ds(split, split)]), (x_hbm, x_ref)]
    pairs += [(ua_hbm, u_ref.at[0]), (ub_hbm, u_ref.at[1]), (da_hbm, d_ref.at[0]), (db_hbm, d_ref.at[1]), (cot_hbm, cot_ref)]
    loads = copies(pairs, in_sems)
    for load in loads:
        load.start()
    width = x_ref.shape[1]
    bucket = own_bucket(sets_ref)
    used = SLOTS // WIDTHS[3] * WIDTHS[3]
    for number in range(3):
        used = jnp.where(bucket == number, SLOTS // WIDTHS[number] * WIDTHS[number], used)
    sums_ref[...] = jnp.zeros_like(sums_ref)
    b_out, gain_one, shift_one, b_down, gain_two, shift_two = (
        row_of(ref) for ref in (bo_ref, g1_ref, s1_ref, bd_ref, g2_ref, s2_ref)
    )
    b_up = [row_of(ref) for ref in (ba_ref, bb_ref)]
    places = [(side, at) for side in range(2) for at in range(0, half, HIDDEN_STEP)]
    last = copies([(gd_ref.at[0], gd_a), (gd_ref.at[1], gd_b)], out_sems)

    def stores_of(number, start, size):
        rows = pl.ds(start, size)
        pairs = ((out_ref, out_hbm), (hid_ref, hid_hbm), (res_ref, res_hbm), (slope_ref, slope_hbm), (sec_ref, sec_hbm))
        return copies([(near.at[rows], far.at[rows]) for near, far in pairs], row_sems.at[number])

    def step(number, start, size):
        rows = pl.ds(start, size)
        lanes = pl.ds(start, 256)
        attn = mul(o_ref[:, lanes], wo_ref[...], 0, 0)
        resid = x_ref[rows, :].astype(f32) + attn[:size] + b_out
        res_ref[rows, :] = resid
        normed, _ = norm_parts(resid)
        hidden = normed * gain_one + shift_one
        low = hidden.astype(bf16)
        hid_ref[rows, :] = low

        @pl.when(number == 0)
        def _():
            for load in loads[4:]:
                load.wait()

        def lift(side, at):
            return mul(low, u_ref[side, :, at : at + HIDDEN_STEP]) + b_up[side][:, at : at + HIDDEN_STEP]

        total = None
        ahead = lift(*places[0])
        for turn, (side, at) in enumerate(places):
            pre = ahead
            if turn + 1 < len(places):
                ahead = lift(*places[turn + 1])
            place = slice(side * half + at, side * half + at + HIDDEN_STEP)
            active, slope = gelu_parts(pre)
            active = active.astype(bf16)
            act_ref[rows, place] = active
            slope_ref[rows, place] = slope.astype(bf16)
            part = mul(active, d_ref[side, at : at + HIDDEN_STEP, :])
            total = part if total is None else total + part
        second = hidden + total + b_down
        normed, spread = norm_parts(second)
        out_ref[rows, :] = (normed * gain_two + shift_two).astype(bf16)
        row = start + lax.broadcasted_iota(jnp.int32, (size, width), 0)
        top = jnp.where(row < used, cot_ref[rows, :].astype(f32), 0.0)
        grad = norm_back(top * gain_two, normed, spread)
        sec_ref[rows, :] = grad
        low_ref[rows, :] = grad.astype(bf16)
        sums_ref[0:8, :] += fold(top * normed)
        sums_ref[8:16, :] += fold(top)
        sums_ref[16:24, :] += fold(grad)
        for store in stores_of(number, start, size):
            store.start()

    for load in loads[:4]:
        load.wait()
    over_tiles(step)
    place_of = slots()
    tall = half // CHUNKS
    for side in range(2):
        for block in range(4):
            place = slice(side * half + block * 4 * tall, side * half + (block + 1) * 4 * tall)
            part = mul(act_ref[:, place], low_ref[...], 0, 0).astype(bf16)
            for z in range(4):
                xy, z_place = place_of(z * 4 + block)
                for lane in range(width // 128):
                    gd_ref[side, xy, z_place, lane * tall : (lane + 1) * tall, :] = part[z * tall : (z + 1) * tall, lane * 128 : lane * 128 + 128]
        last[side].start()
    for number, (start, size) in enumerate(TILES):
        for store in stores_of(number, start, size):
            store.wait()
    for store in last:
        store.wait()


CHUNKS = 16
FEED_ROWS = 336
DOWN_ROWS = 256
HEAD_ROWS = 208


def slots():
    own = lax.axis_index("dp") % CHUNKS

    def place(chunk):
        held = chunk ^ own
        return held % 4, held // 4

    return place


def feed_backward(
    sec_hbm, slope_hbm, hid_hbm, res_hbm, o_hbm, wo_a, wo_b, ua_hbm, ub_hbm, da_hbm, db_hbm, g1_ref, two_ref,
    gr_hbm, g_hbm, delta_hbm, mine_ref, theirs_ref,
    sec_ref, slope_ref, hid_ref, res_ref, o_ref, wo_ref, u_ref, d_ref, gr_ref, g_ref, delta_ref,
    pre_ref, mix_ref, sums_ref, bup_ref, row_in, in_sems, row_out, out_sems,
):
    half = ua_hbm.shape[1]
    width = hid_ref.shape[1]
    split = wo_a.shape[0]

    def loads_of(number, start, size):
        rows = pl.ds(start, size)
        pairs = ((sec_hbm, sec_ref), (slope_hbm, slope_ref), (res_hbm, res_ref))
        return copies([(far.at[rows], near.at[rows]) for far, near in pairs], row_in.at[number])

    def stores_of(number, start, size):
        rows = pl.ds(start, size)
        return copies([(gr_ref.at[rows], gr_hbm.at[rows])], row_out.at[number])

    pairs = [(da_hbm, d_ref.at[0]), (db_hbm, d_ref.at[1]), (ua_hbm, u_ref.at[0]), (ub_hbm, u_ref.at[1])]
    pairs += [(hid_hbm, hid_ref), (o_hbm, o_ref), (wo_a, wo_ref.at[pl.ds(0, split)]), (wo_b, wo_ref.at[pl.ds(split, split)])]
    loads = copies(pairs, in_sems)
    first = loads_of(0, *TILES[0])
    for load in first[:1] + loads[:1] + first[1:2] + loads[1:4] + first[2:]:
        load.start()
    for number, (start, size) in enumerate(TILES[1:]):
        for load in loads_of(number + 1, start, size):
            load.start()
    for load in loads[4:]:
        load.start()
    sums_ref[...] = jnp.zeros_like(sums_ref)
    bup_ref[...] = jnp.zeros_like(bup_ref)
    gain_one = row_of(g1_ref)
    mix_ref[SLOTS:, :] = jnp.zeros((LANES - SLOTS, mix_ref.shape[1]), bf16)
    place_of = slots()
    places = [(side, at) for side in range(2) for at in range(0, half, HIDDEN_STEP)]

    def step(number, start, size):
        for load in loads_of(number, start, size):
            load.wait()

        @pl.when(number == 0)
        def _():
            for load in loads[:4]:
                load.wait()

        rows = pl.ds(start, size)
        second = sec_ref[rows, :]
        low = second.astype(bf16)

        def sink(side, at):
            return mul(low, d_ref[side, at : at + HIDDEN_STEP, :], 1, 1)

        total = None
        ahead = sink(*places[0])
        for turn, (side, at) in enumerate(places):
            inner = ahead
            if turn + 1 < len(places):
                ahead = sink(*places[turn + 1])
            place = slice(side * half + at, side * half + at + HIDDEN_STEP)
            pre = (inner * slope_ref[rows, place].astype(f32)).astype(bf16)
            pre_ref[rows, place] = pre
            bup_ref[:, place] += fold(pre.astype(f32))
            part = mul(pre, u_ref[side, :, at : at + HIDDEN_STEP], 1, 1)
            total = part if total is None else total + part
        hidden = second + total
        normed, spread = norm_parts(res_ref[rows, :])
        grad = norm_back(hidden * gain_one, normed, spread)
        gr_ref[rows, :] = grad
        mix_ref[rows, :] = grad.astype(bf16)
        sums_ref[0:8, :] += fold(hidden * normed)
        sums_ref[8:16, :] += fold(hidden)
        sums_ref[16:24, :] += fold(grad)
        for store in stores_of(number, start, size):
            store.start()

    over_tiles(step)
    for load in loads[4:]:
        load.wait()
    tall = width // CHUNKS
    for side, out in enumerate((mine_ref, theirs_ref)):
        for at in range(0, half, 256):
            place = slice(side * half + at, side * half + at + 256)
            part = mul(hid_ref[...], pre_ref[:, place], 0, 0).astype(bf16)
            for chunk in range(CHUNKS):
                xy, z = place_of(chunk)
                for block in range(2):
                    row = (at // 128 + block) * tall
                    out[xy, z, row : row + tall, :] = part[chunk * tall : (chunk + 1) * tall, block * 128 : block * 128 + 128]
    low = split // CHUNKS
    for side, out in enumerate((mine_ref, theirs_ref)):
        place = slice(side * split, (side + 1) * split)
        part = mul(o_ref[place, :], mix_ref[...]).astype(bf16)
        for chunk in range(CHUNKS):
            xy, z = place_of(chunk)
            for block in range(width // 128):
                row = half // 128 * tall + block * low
                out[xy, z, row : row + low, :] = part[chunk * low : (chunk + 1) * low, block * 128 : block * 128 + 128]
        for start in range(0, LANES, 512):
            lanes = slice(start, start + 512)
            grad = mul(wo_ref[place, :], mix_ref[lanes, :], 1, 1).astype(bf16)
            g_ref[place, lanes] = grad
            prod = grad.astype(f32) * o_ref[place, lanes].astype(f32)
            for head in range(split // 64):
                at = (side * (split // 64) + head) * 16
                delta = jnp.sum(prod[head * 64 : head * 64 + 64], axis=0, keepdims=True)
                delta_ref[at : at + 16, lanes] = extra_rows(-delta)
    vectors = []
    for ref in (two_ref, sums_ref):
        for kind in range(3):
            total = jnp.sum(ref[8 * kind : 8 * kind + 8, :], axis=0, keepdims=True)
            vectors += [total[:, at : at + 128] for at in range(0, width, 128)]
    number = lax.broadcasted_iota(jnp.int32, (16, 128), 0)
    for side, out in enumerate((mine_ref, theirs_ref)):
        total = jnp.sum(bup_ref[:, side * half : (side + 1) * half], axis=0, keepdims=True)
        held = vectors + [total[:, at : at + 128] for at in range(0, half, 128)]
        each = len(held) // CHUNKS
        for chunk in range(CHUNKS):
            xy, z = place_of(chunk)
            block = jnp.zeros((16, 128), f32)
            for row in range(each):
                block = jnp.where(number == row, held[chunk * each + row], block)
            out[xy, z, FEED_ROWS - 16 :, :] = block.astype(bf16)
    last = copies([(g_ref, g_hbm), (delta_ref, delta_hbm)], out_sems)
    for store in last:
        store.start()
    for number, (start, size) in enumerate(TILES):
        for store in stores_of(number, start, size):
            store.wait()
    for store in last:
        store.wait()


def project_input(dqa_ref, dka_ref, dva_ref, dqb_ref, dkb_ref, dvb_ref, wa_ref, wb_ref, gr_ref, gi_ref, wt_ref):
    rows = wa_ref.shape[2]
    for side, w_ref in enumerate((wa_ref, wb_ref)):
        for kind in range(3):
            wt_ref[kind, side * rows : (side + 1) * rows, :] = w_ref[kind].T
    for start in range(0, SLOTS, 256):
        size = min(256, SLOTS - start)
        lanes = slice(start, start + 256)
        total = gr_ref[start : start + size, :]
        for side, refs in enumerate(((dqa_ref, dka_ref, dva_ref), (dqb_ref, dkb_ref, dvb_ref))):
            for kind, d_ref in enumerate(refs):
                total = total + mul(d_ref[:, lanes], wt_ref[kind, side * rows : (side + 1) * rows, :], 0, 0)[:size]
        gi_ref[start : start + size, :] = total


def add_pair(mine_ref, theirs_ref, *outs):
    for number, out in enumerate(outs):
        out[...] = (mine_ref[number].astype(f32) + theirs_ref[number].astype(f32)).astype(bf16)


def add_four(a_ref, b_ref, c_ref, d_ref, *outs):
    for number, out in enumerate(outs):
        held = slice(None) if len(outs) == 1 else number
        low = a_ref[held].astype(f32) + b_ref[held].astype(f32)
        out[...] = (low + (c_ref[held].astype(f32) + d_ref[held].astype(f32))).astype(bf16)


def join_four(*refs):
    first, second, outs = refs[:4], refs[4:8], refs[8:]
    for z, out in enumerate(outs):
        at = 0
        for a_ref, b_ref, c_ref, d_ref in (first, second):
            rows = a_ref.shape[1]
            low = a_ref[z].astype(f32) + b_ref[z].astype(f32)
            out[at : at + rows, :] = (low + (c_ref[z].astype(f32) + d_ref[z].astype(f32))).astype(bf16)
            at += rows


def lay_four(a_ref, b_ref, c_ref, d_ref, out_ref):
    for number, ref in enumerate((a_ref, b_ref, c_ref, d_ref)):
        out_ref[number] = ref[...]


def each_chunk(refs):
    own = lax.axis_index("dp") % CHUNKS
    for xy, ref in enumerate(refs):
        for z in range(4):
            yield (z * 4 + xy) ^ own, ref[z].astype(f32)


def spread_feed(
    a_ref, b_ref, c_ref, d_ref, up_ref, out_ref, g2_ref, s2_ref, bd_ref, g1_ref, s1_ref, bo_ref, bup_ref, down_ref, keep_ref,
):
    width, half = up_ref.shape
    tall, low = width // CHUNKS, out_ref.shape[0] // CHUNKS
    deep = half // CHUNKS
    for chunk, held in each_chunk((a_ref, b_ref, c_ref, d_ref)):
        rows = pl.ds(pl.multiple_of(chunk * tall, tall), tall)
        for block in range(half // 128):
            up_ref[rows, block * 128 : block * 128 + 128] = held[block * tall : (block + 1) * tall]
        rows = pl.ds(pl.multiple_of(chunk * low, low), low)
        base = half // 128 * tall
        for block in range(width // 128):
            out_ref[rows, block * 128 : block * 128 + 128] = held[base + block * low : base + (block + 1) * low]
        keep_ref[chunk] = held[FEED_ROWS - 16 : FEED_ROWS]
        rows = pl.ds(pl.multiple_of((chunk % 4 * 4 + chunk // 4) * deep, deep), deep)
        for block in range(width // 128):
            at = FEED_ROWS + block * deep
            down_ref[rows, block * 128 : block * 128 + 128] = held[at : at + deep]
    refs = [(ref, at) for ref in (g2_ref, s2_ref, bd_ref, g1_ref, s1_ref, bo_ref, bup_ref) for at in range(0, ref.shape[0], 128)]
    each = len(refs) // CHUNKS
    for number, (ref, at) in enumerate(refs):
        ref[at : at + 128] = keep_ref[number // each, number % each, :]


def spread_heads(a_ref, b_ref, c_ref, d_ref, qkv_ref, bias_ref, keep_ref):
    kinds, width, half = qkv_ref.shape
    tall = width // CHUNKS
    for chunk, held in each_chunk((a_ref, b_ref, c_ref, d_ref)):
        rows = pl.ds(pl.multiple_of(chunk * tall, tall), tall)
        for kind in range(kinds):
            for block in range(half // 128):
                row = (kind * (half // 128) + block) * tall
                qkv_ref[kind, rows, block * 128 : block * 128 + 128] = held[row : row + tall]
        keep_ref[chunk] = held[HEAD_ROWS - 16 :]
    blocks = half // 128
    for number in range(2 * blocks):
        at = number % blocks * 128
        bias_ref[number // blocks : number // blocks + 1, at : at + 128] = keep_ref[number, 0:1, :]


def shape(dims, kind=bf16):
    return jax.ShapeDtypeStruct(dims, kind)


smem = pl.BlockSpec(memory_space=pltpu.SMEM)


def specs(count):
    return [smem] + [pl.BlockSpec(memory_space=pltpu.VMEM)] * (count - 1)


def cost(flops, moved, powers=0):
    return pl.CostEstimate(flops=int(flops), bytes_accessed=int(moved), transcendentals=int(powers))


hbm = pl.BlockSpec(memory_space=pl.ANY)
vmem = pl.BlockSpec(memory_space=pltpu.VMEM)


def call_forward(sets, x, wa, wb, ba, bb):
    width = 2 * wa.shape[2]
    big, more = (width, LANES), (width // 4, LANES)
    return pl.pallas_call(
        attend_forward, name="attend_forward",
        out_shape=[shape(big), shape(big), shape(big), shape(big), shape(more)],
        in_specs=[smem, hbm, hbm, hbm, vmem, vmem], out_specs=[hbm] * 5,
        scratch_shapes=[pltpu.VMEM(a.shape, bf16) for a in (x, wa, wb)] + [pltpu.VMEM(big, bf16)] * 4 + [pltpu.VMEM(more, bf16)]
        + [pltpu.VMEM((x.shape[1], LANES), bf16), pltpu.VMEM((CLASSES, LANES), bf16), pltpu.VMEM((CLASSES + 16, LANES), bf16)]
        + [pltpu.SemaphoreType.DMA((3,)), pltpu.SemaphoreType.DMA((5,))],
        compiler_params=params(56), cost_estimate=cost(14e9, 12e6),
    )(sets, x, wa, wb, ba, bb)


def call_feed_forward(sets, x, mixed, wo_a, wo_b, up_a, up_b, bu_a, bu_b, down_a, down_b, vecs, cot):
    rows, width = x.shape
    half = up_a.shape[1]
    outs = [shape((rows, width)), shape((rows, width)), shape((rows, width), f32), shape((rows, 2 * half)), shape((rows, width), f32)]
    own = [x.shape, mixed.shape, (width, width), (2, width, half), (2, half, width), x.shape]
    piece = shape((4, 4, DOWN_ROWS, 128))
    return pl.pallas_call(
        feed_forward, name="feed_forward",
        out_shape=outs + [piece, piece, shape((24, width), f32)],
        in_specs=[smem] + [hbm] * 6 + [vmem] * 2 + [hbm] * 2 + [vmem] * 6 + [hbm], out_specs=[hbm] * 7 + [vmem],
        scratch_shapes=[pltpu.VMEM(a, bf16) for a in own] + [pltpu.VMEM(a.shape, a.dtype) for a in outs]
        + [pltpu.VMEM((2, *piece.shape), bf16), pltpu.VMEM((rows, 2 * half), bf16), pltpu.VMEM((rows, width), bf16)]
        + [pltpu.SemaphoreType.DMA((9,)), pltpu.SemaphoreType.DMA((6, 5)), pltpu.SemaphoreType.DMA((2,))],
        compiler_params=params(58), cost_estimate=cost(14e9, 20e6),
    )(sets, x, mixed, wo_a, wo_b, up_a, up_b, bu_a, bu_b, down_a, down_b, *vecs, cot)


def call_feed_backward(second, slope, hidden, resid, mixed, wo_a, wo_b, up_a, up_b, down_a, down_b, gain, sums):
    rows, width = second.shape
    half = up_a.shape[1]
    split = wo_a.shape[0]
    piece = shape((4, 4, FEED_ROWS, 128))
    outs = [shape((rows, width), f32), shape((2 * split, LANES)), shape((2 * split // 4, LANES))]
    given = [(a.shape, a.dtype) for a in (second, slope, hidden, resid, mixed)]
    given += [((width, width), bf16), ((2, width, half), bf16), ((2, half, width), bf16)]
    return pl.pallas_call(
        feed_backward, name="feed_backward",
        out_shape=outs + [piece, piece],
        in_specs=[hbm] * 11 + [vmem] * 2, out_specs=[hbm] * 3 + [vmem] * 2,
        scratch_shapes=[pltpu.VMEM(*a) for a in given] + [pltpu.VMEM(a.shape, a.dtype) for a in outs]
        + [
            pltpu.VMEM((rows, 2 * half), bf16), pltpu.VMEM((LANES, width), bf16),
            pltpu.VMEM((24, width), f32), pltpu.VMEM((8, 2 * half), f32),
        ]
        + [pltpu.SemaphoreType.DMA(a) for a in ((6, 3), (8,), (6, 1), (2,))],
        compiler_params=params(58), cost_estimate=cost(14e9, 20e6),
    )(second, slope, hidden, resid, mixed, wo_a, wo_b, up_a, up_b, down_a, down_b, gain, sums)


def call_backward(part, sets, q, k, v, grad, lse, delta, x):
    rows = q.shape[0] // 2
    big, more = (rows, LANES), (rows // 4, LANES)
    return pl.pallas_call(
        functools.partial(attend_backward, part), name="attend_backward",
        out_shape=[shape(big), shape(big), shape(big), shape((4, 4, HEAD_ROWS, 128))],
        in_specs=[smem] + [hbm] * 7, out_specs=[hbm] * 3 + [vmem],
        scratch_shapes=[pltpu.VMEM(a, bf16) for a in (big, big, big, big, more, more, x.shape, big, big, big, (x.shape[1], LANES))]
        + [
            pltpu.VMEM((CLASSES, LANES), bf16), pltpu.VMEM((CLASSES + 16, LANES), bf16),
            pltpu.VMEM((2, 896, 896), bf16), pltpu.VMEM((2, 896, 896), bf16),
            pltpu.VMEM((2, 64, LANES), f32), pltpu.VMEM((2, 64, LANES), f32),
        ]
        + [pltpu.SemaphoreType.DMA(a) for a in ((rows // 128, 6), (1,), (rows // 128, 3))],
        compiler_params=params(50), cost_estimate=cost(9e9, 6e6),
    )(sets, q, k, v, grad, lse, delta, x)


def call_project_input(own, other, wa, wb, resid):
    return pl.pallas_call(
        project_input, name="project_input", out_shape=shape(resid.shape, f32),
        scratch_shapes=[pltpu.VMEM((3, 2 * wa.shape[2], wa.shape[1]), bf16)],
        compiler_params=params(40), cost_estimate=cost(2.4e9, 12e6),
    )(*own, *other, wa, wb, resid)


def swap(array):
    return lax.ppermute(array, "mp", [(0, 1), (1, 0)])


def exchange(array, distance):
    count = lax.axis_size("dp")
    return lax.ppermute(array, "dp", [(i, i ^ distance) for i in range(count)])


def small(kernel, name, outs, scratch=()):
    moved = 2 * sum(o.size * o.dtype.itemsize for o in outs)
    return pl.pallas_call(
        kernel, name=name, out_shape=list(outs), scratch_shapes=list(scratch),
        compiler_params=params(24), cost_estimate=cost(1e6, moved),
    )


def after(array, *earlier):
    return lax.optimization_barrier((array, *earlier))[0]


def scatter_out(parts, *earlier):
    _, rows, lanes = parts[0].shape
    came = [exchange(parts[xy], xy) for xy in (1, 2, 3)]
    return small(add_four, "add_four", [shape((rows, lanes))] * 4)(after(parts[0], *earlier), *came)


def join_out(feed, down, *earlier):
    rows, lanes = feed[0].shape[1] + down[0].shape[1], feed[0].shape[2]
    feed = [after(feed[0], *earlier), *(exchange(feed[xy], xy) for xy in (1, 2, 3))]
    return small(join_four, "join_four", [shape((rows, lanes))] * 4)(*feed, *down)


def scatter_in(parts, *earlier):
    came = [exchange(parts[z], 4 * z) for z in (1, 2, 3)]
    (total,) = small(add_four, "add_four", [shape(parts[0].shape)])(after(parts[0], *earlier), *came)
    distance = CHUNKS
    while distance < lax.axis_size("dp"):
        total = total + exchange(total, distance)
        distance *= 2
    return total


def gather_in(total, *earlier):
    came = [exchange(total, 4 * z) for z in (1, 2, 3)]
    (held,) = small(lay_four, "lay_four", [shape((4, *total.shape))])(after(total, *earlier), *came)
    return held


def gather_out(held):
    return [held, *(exchange(held, xy) for xy in (1, 2, 3))]


def halves_added(mine, theirs):
    return small(add_pair, "add_pair", [shape(mine.shape[1:])] * 4)(mine, swap(theirs))


def per_device(
    variates, dataset, w_qkv, b_qv, w_out, b_out, gain_one, shift_one, w_up, b_up, w_down, b_down, gain_two, shift_two, cotangent,
):
    width, half = w_up.shape
    other_qkv, other_bias = swap(w_qkv), swap(b_qv)
    other_out, other_up, other_bup, other_down = swap(w_out), swap(w_up), swap(b_up), swap(w_down)
    q, k, v, mixed, lse = call_forward(dataset, variates, w_qkv, other_qkv, b_qv, other_bias)
    out, hidden, resid, slope, second, down_mine, down_theirs, sums = call_feed_forward(
        dataset, variates, mixed, w_out, other_out, w_up, other_up, b_up, other_bup, w_down, other_down,
        (b_out, gain_one, shift_one, b_down, gain_two, shift_two), cotangent,
    )
    down = halves_added(down_mine, down_theirs)
    sent = [exchange(down[xy], xy) for xy in (1, 2, 3)]
    grad_res, grad_mix, delta, mine, theirs = call_feed_backward(
        after(second, *down), slope, hidden, resid, mixed, w_out, other_out, w_up, other_up, w_down, other_down, gain_one, sums
    )
    feed = halves_added(mine, theirs)
    *other, theirs = call_backward(1, dataset, q, k, v, after(grad_mix, *feed, *sent), lse, delta, variates)
    feed = join_out(feed, [down[0], *sent], theirs)
    *own, mine = call_backward(0, dataset, q, k, v, after(grad_mix, theirs, *feed), lse, delta, variates)
    feed = scatter_in(feed, mine)
    heads = halves_added(mine, theirs)
    feed = gather_in(feed)
    grad_in = call_project_input(own, other, w_qkv, other_qkv, after(grad_res, feed, *heads))
    heads = scatter_out(heads, grad_in)
    feed = gather_out(after(feed, *heads))
    heads = scatter_in(heads)
    heads = gather_out(gather_in(heads))
    vector = shape((width,), f32)
    outs = [shape((width, half), f32), shape(w_out.shape, f32)] + [vector] * 6 + [shape((half,), f32), shape(w_down.shape, f32)]
    keep = [pltpu.VMEM((CHUNKS, 16, 128), f32)]
    grad_up, grad_out, two_gain, two_shift, down_bias, one_gain, one_shift, out_bias, up_bias, grad_down = small(
        spread_feed, "spread_feed", outs, keep
    )(*feed)
    grad_qkv, bias = small(spread_heads, "spread_heads", [shape(w_qkv.shape, f32), shape(b_qv.shape, f32)], keep)(*heads)
    return (
        out, grad_in, grad_qkv, bias, grad_out, out_bias, one_gain, one_shift, grad_up, up_bias,
        grad_down, down_bias, two_gain, two_shift,
    )


def solution(mesh):
    wide = P(("dp", "mp"), None)
    weights = (P(None, None, "mp"), P(None, "mp"), P("mp", None))
    placed = (wide, P("dp"), *weights, P(), P(), P(), P(None, "mp"), P("mp"), P("mp", None), P(), P(), P(), wide)
    given = (wide, wide, *weights, P(), P(), P(), P(None, "mp"), P("mp"), P("mp", None), P(), P(), P())
    return jax.shard_map(per_device, mesh=mesh, in_specs=placed, out_specs=given, check_vma=False)
```

```python
import functools

import jax
import jax.numpy as jnp
from jax import lax
from jax.experimental import pallas as pl
from jax.experimental.pallas import tpu as pltpu
from jax.sharding import PartitionSpec as P

HEAD_DIM = 64
SLOTS = 1424
WIDTHS = (7, 21, 321, 862)
LANES = 1536
CLASSES = 80
BIG = 1e30
EPS = 1e-05
MIB = 2**20

bf16 = jnp.bfloat16
f32 = jnp.float32


def mul(left, right, left_dim=1, right_dim=0):
    return lax.dot_general(
        left, right, (((left_dim,), (right_dim,)), ((), ())), preferred_element_type=f32
    )


def params(limit):
    return pltpu.CompilerParams(vmem_limit_bytes=limit * MIB)


def cover(width, start, stop, last):
    used = SLOTS // width * width
    low = start // width * width
    high = last if stop > used else -(-stop // width) * width
    return (low // 128 * 128, min(-(-min(high, last) // 128) * 128, LANES))


def groups_of(width, rows, step):
    found = []
    for start in range(0, rows, step):
        low, high = cover(width, start, min(start + step, rows), rows)
        if found and found[-1][2] == low and found[-1][2] + found[-1][3] == high:
            first, count = found[-1][:2]
            found[-1] = (first, count + step, low, high - low)
        else:
            found.append((start, step, low, high - low))
    return found


def near(tile):
    return jnp.clip(tile * 256 - 128, 0, LANES - 512)


def middle(tile):
    return jnp.where(tile < 2, 0, jnp.where(tile == 2, 256, jnp.where(tile == 3, 640, 768)))


FORWARD = (
    [(0, 6, 512, near, 8)],
    [(0, 6, 768, middle, 8)],
    [(0, 3, 896, lambda tile: 0 * tile, 8), (3, 4, 1536, lambda tile: 0 * tile, 2), (4, 6, 768, lambda tile: 0 * tile + 768, 8)],
    [(0, 6, 512, near, 1)],
    [(0, 6, LANES, lambda tile: 0 * tile, 1)],
)
BACKWARD = (
    [],
    groups_of(WIDTHS[2], SLOTS // WIDTHS[2] * WIDTHS[2], 128),
    [(0, 896, 0, 896)],
)


def own_bucket(sets_ref):
    return sets_ref[lax.axis_index("mp")]


def token_class(width):
    token = lax.broadcasted_iota(jnp.int32, (CLASSES, LANES), 1)
    numbers = token.astype(f32)
    held = jnp.floor((numbers + 0.5) * (1.0 / width)).astype(jnp.int32)
    held = jnp.where(token < SLOTS, held, (SLOTS - 1) // width + 1)
    row = lax.broadcasted_iota(jnp.int32, (CLASSES, LANES), 0)
    return held % CLASSES == row


def write_masks(bucket, hot_ref, bar_ref):
    for number, width in enumerate(WIDTHS):

        @pl.when(bucket == number)
        def _():
            same = token_class(width)
            hot_ref[...] = jnp.where(same, 1.0, 0.0).astype(bf16)
            bar_ref[:CLASSES, :] = jnp.where(same, 0.0, -BIG).astype(bf16)

    row = lax.broadcasted_iota(jnp.int32, (16, LANES), 0)
    bar_ref[CLASSES:, :] = jnp.where(row < 3, 1.0, 0.0).astype(bf16)


def split_three(row):
    high = row.astype(bf16)
    rest = row - high.astype(f32)
    middle = rest.astype(bf16)
    low = (rest - middle.astype(f32)).astype(bf16)
    return high, middle, low


def extra_rows(row):
    parts = [p.astype(f32) for p in split_three(row)]
    number = lax.broadcasted_iota(jnp.int32, (16, row.shape[1]), 0)
    held = jnp.where(number == 0, parts[0], jnp.where(number == 1, parts[1], jnp.where(number == 2, parts[2], 0.0)))
    return held.astype(bf16)


LOG_E = 1.4426950408889634
SAFE = 60.0


def attend_forward(
    sets_ref, x_hbm, wa_hbm, wb_hbm, ba_ref, bb_ref, q_hbm, k_hbm, v_hbm, o_hbm, lse_hbm,
    x_ref, wa_ref, wb_ref, q_ref, k_ref, v_ref, o_ref, lse_ref, xt_ref, hot_ref, bar_ref, in_sems, out_sems,
):
    loads = [pltpu.make_async_copy(*pair, in_sems.at[i]) for i, pair in enumerate(((x_hbm, x_ref), (wa_hbm, wa_ref), (wb_hbm, wb_ref)))]
    for load in loads:
        load.start()
    pairs = ((q_ref, q_hbm), (k_ref, k_hbm), (v_ref, v_hbm), (o_ref, o_hbm), (lse_ref, lse_hbm))
    stores = [pltpu.make_async_copy(*pair, out_sems.at[i]) for i, pair in enumerate(pairs)]
    bucket = own_bucket(sets_ref)
    write_masks(bucket, hot_ref, bar_ref)
    tail = jnp.zeros((LANES - SLOTS, x_ref.shape[1]), bf16)
    loads[0].wait()
    xt_ref[...] = jnp.concatenate([x_ref[...], tail], axis=0).T
    worst = None
    for side, (w_ref, b_ref) in enumerate(((wa_ref, ba_ref), (wb_ref, bb_ref))):
        loads[1 + side].wait()
        for kind, out_ref in enumerate((q_ref, k_ref, v_ref)):
            weight = w_ref[kind].T
            rows = weight.shape[0]
            if kind != 1:
                row = b_ref[kind // 2 : kind // 2 + 1, :].astype(f32)
                column = jnp.broadcast_to(row, (128, rows)).T
                column = jnp.concatenate([column] * 4, axis=1)
            for start in range(0, LANES, 512):
                part = mul(weight, xt_ref[:, start : start + 512])
                if kind != 1:
                    part = part + column
                if kind == 0:
                    part = part * 0.125
                out_ref[side * rows : (side + 1) * rows, start : start + 512] = part.astype(bf16)
    for store in stores[:3]:
        store.start()
    heads = q_ref.shape[0] // 64
    for head in range(heads):
        norms = []
        for ref in (q_ref, k_ref):
            held = ref[head * 64 : head * 64 + 64, :].astype(f32)
            norms.append(jnp.max(jnp.sum(held * held, axis=0, keepdims=True), axis=1, keepdims=True))
        both = norms[0] * norms[1]
        worst = both if worst is None else jnp.maximum(worst, both)
    calm = worst[0, 0] < SAFE * SAFE

    def score(head, start, first, span):
        rows = pl.ds(pl.multiple_of(head * 64, 64), 64)
        lanes, span = pl.ds(start, 256), pl.ds(first, span)
        keys = jnp.concatenate([k_ref[rows, span], bar_ref[:CLASSES, span]], axis=0)
        quer = jnp.concatenate([q_ref[rows, lanes], hot_ref[:, lanes]], axis=0)
        return mul(keys, quer, 0, 0)

    def finish(head, start, first, span, scores, plain):
        rows = pl.ds(pl.multiple_of(head * 64, 64), 64)
        lanes = pl.ds(start, 256)
        if plain:
            raised = jnp.exp2(scores * LOG_E).astype(bf16)
        else:
            top = jnp.max(scores, axis=0, keepdims=True)
            raised = jnp.exp(scores - top).astype(bf16)
        vals = jnp.concatenate([v_ref[rows, pl.ds(first, span)], jnp.ones((16, span), bf16)], axis=0)
        total = mul(vals, raised)
        sums = total[64:65, :]
        o_ref[rows, lanes] = (total[:64, :] * (1.0 / sums)).astype(bf16)
        logs = jnp.log(sums)
        if not plain:
            logs = logs + top
        lse_ref[pl.ds(pl.multiple_of(head * 16, 16), 16), lanes] = extra_rows(-logs)

    def over(begin, end, span, first_of, together, plain):
        def turn(number, carry):
            tile = begin + number % (end - begin)
            start = pl.multiple_of(tile * 256, 256)
            first = pl.multiple_of(first_of(tile), 128)
            own = [number // (end - begin) * together + i for i in range(together)]
            held = [score(head, start, first, span) for head in own]
            for head, scores in zip(own, held):
                finish(head, start, first, span, scores, plain)
            return carry

        lax.fori_loop(0, heads // together * (end - begin), turn, 0)

    for group in range(5):
        plain = group < 3
        chosen = (bucket < 2, bucket == 2, bucket == 3, bucket < 2, bucket >= 2)[group]

        @pl.when(jnp.logical_and(chosen, calm == plain))
        def _():
            for begin, end, span, first_of, together in FORWARD[group]:
                over(begin, end, span, first_of, together, plain)

    for store in stores[3:]:
        store.start()
    for store in stores:
        store.wait()


def copies(pairs, sems):
    return [pltpu.make_async_copy(*pair, sems.at[i]) for i, pair in enumerate(pairs)]


def attend_backward(
    part, sets_ref, q_hbm, k_hbm, v_hbm, g_hbm, lse_hbm, delta_hbm, x_hbm, dq_hbm, dk_hbm, dv_hbm, piece_ref,
    q_ref, k_ref, v_ref, g_ref, lse_ref, delta_ref, x_ref, dq_ref, dk_ref, dv_ref, xt_ref,
    hot_ref, bar_ref, p_ref, s_ref, ka_ref, va_ref, head_sems, in_sems, out_sems,
):
    half = q_ref.shape[0]

    def loads_of(number):
        there = pl.ds(part * half + number * 128, 128)
        here = pl.ds(number * 128, 128)
        pairs = [(far.at[there], near.at[here]) for far, near in ((q_hbm, q_ref), (k_hbm, k_ref), (v_hbm, v_ref), (g_hbm, g_ref))]
        there = pl.ds(part * (half // 4) + number * 32, 32)
        here = pl.ds(number * 32, 32)
        pairs += [(far.at[there], near.at[here]) for far, near in ((lse_hbm, lse_ref), (delta_hbm, delta_ref))]
        return copies(pairs, head_sems.at[number])

    def stores_of(number):
        here = pl.ds(number * 128, 128)
        return copies([(near.at[here], far.at[here]) for near, far in ((dq_ref, dq_hbm), (dk_ref, dk_hbm), (dv_ref, dv_hbm))], out_sems.at[number])

    for number in range(half // 128):
        for load in loads_of(number):
            load.start()
    given = copies([(x_hbm, x_ref)], in_sems)[0]
    bucket = own_bucket(sets_ref)
    write_masks(bucket, hot_ref, bar_ref)

    def one_head(head, groups, slot):
        rows = pl.ds(pl.multiple_of(head * 64, 64), 64)
        more = pl.ds(pl.multiple_of(head * 16, 16), 16)
        single = len(groups) == 1
        if not single:
            ka_ref[slot] = jnp.zeros(ka_ref.shape[1:], f32)
            va_ref[slot] = jnp.zeros(va_ref.shape[1:], f32)
        for q0, nq, k0, nk in groups:
            span = slice(k0, k0 + nk)
            held = slice(q0, q0 + nq)
            keys = jnp.concatenate([k_ref[rows, span], bar_ref[:, span]], axis=0)
            vals = jnp.concatenate([v_ref[rows, span], bar_ref[CLASSES:, span]], axis=0)
            for start in range(q0, q0 + nq, 256):
                size = min(256, q0 + nq - start)
                lanes = slice(start, start + size)
                quer = jnp.concatenate([q_ref[rows, lanes], hot_ref[:, lanes], lse_ref[more, lanes]], axis=0)
                grad = jnp.concatenate([g_ref[rows, lanes], delta_ref[more, lanes]], axis=0)
                probs = jnp.exp2(mul(quer, keys, 0, 0) * LOG_E)
                slopes = probs * mul(grad, vals, 0, 0)
                p_ref[slot, start - q0 : start - q0 + size, :nk] = probs.astype(bf16)
                s_ref[slot, start - q0 : start - q0 + size, :nk] = slopes.astype(bf16)
            dv = mul(g_ref[rows, held], p_ref[slot, :nq, :nk])
            dk = mul(q_ref[rows, held], s_ref[slot, :nq, :nk])
            dq = mul(k_ref[rows, span], s_ref[slot, :nq, :nk], 1, 1)
            dq_ref[rows, held] = (dq * 0.125).astype(bf16)
            if single:
                dv_ref[rows, span] = dv.astype(bf16)
                dk_ref[rows, span] = dk.astype(bf16)
            else:
                va_ref[slot, :, span] += dv
                ka_ref[slot, :, span] += dk
        if single:
            rest = LANES - 896
            for out in (dq_ref, dk_ref, dv_ref):
                out[rows, 896:] = jnp.zeros((64, rest), bf16)
        else:
            dv_ref[rows, :] = va_ref[slot].astype(bf16)
            dk_ref[rows, :] = ka_ref[slot].astype(bf16)
            done = groups[-1][0] + groups[-1][1]
            if done < LANES:
                dq_ref[rows, done:] = jnp.zeros((64, LANES - done), bf16)

    def tile_of(head, start, first, span):
        rows = pl.ds(head * 64, 64)
        more = pl.ds(head * 16, 16)
        lanes, span = pl.ds(start, 256), pl.ds(first, span)
        keys = jnp.concatenate([k_ref[rows, span], bar_ref[:, span]], axis=0)
        vals = jnp.concatenate([v_ref[rows, span], bar_ref[CLASSES:, span]], axis=0)
        quer = jnp.concatenate([q_ref[rows, lanes], hot_ref[:, lanes], lse_ref[more, lanes]], axis=0)
        grad = jnp.concatenate([g_ref[rows, lanes], delta_ref[more, lanes]], axis=0)
        probs = jnp.exp2(mul(quer, keys, 0, 0) * LOG_E)
        slopes = (probs * mul(grad, vals, 0, 0)).astype(bf16)
        return probs.astype(bf16), slopes

    def take(head, start, first, span, probs, slopes):
        rows = pl.ds(head * 64, 64)
        lanes, span = pl.ds(start, 256), pl.ds(first, span)
        va_ref[head, :, span] += mul(g_ref[rows, lanes], probs)
        ka_ref[head, :, span] += mul(q_ref[rows, lanes], slopes)
        dq_ref[rows, lanes] = (mul(k_ref[rows, span], slopes, 1, 1) * 0.125).astype(bf16)

    def by_tiles(span, first_of, together):
        for number in range(half // 128):
            for load in loads_of(number):
                load.wait()
        given.start()
        ka_ref[...] = jnp.zeros_like(ka_ref)
        va_ref[...] = jnp.zeros_like(va_ref)

        def turn(tile, carry):
            start = pl.multiple_of(tile * 256, 256)
            first = pl.multiple_of(first_of(tile), 128)
            for base in range(0, half // 64, together):
                own = range(base, base + together)
                held = [tile_of(head, start, first, span) for head in own]
                for head, (probs, slopes) in zip(own, held):
                    take(head, start, first, span, probs, slopes)
            return carry

        lax.fori_loop(0, 6, turn, 0)
        for head in range(half // 64):
            rows = pl.ds(head * 64, 64)
            dv_ref[rows, :] = va_ref[head].astype(bf16)
            dk_ref[rows, :] = ka_ref[head].astype(bf16)
        for number in range(half // 128):
            for store in stores_of(number):
                store.start()

    for group in range(3):
        chosen = (bucket < 2, bucket == 2, bucket == 3)[group]

        @pl.when(chosen)
        def _():
            if group == 0:
                by_tiles(512, near, 4)
            else:

                def pair(number, carry):
                    for load in loads_of(number):
                        load.wait()

                    @pl.when(number == 0)
                    def _():
                        given.start()

                    one_head(2 * number, BACKWARD[group], 0)
                    one_head(2 * number + 1, BACKWARD[group], 1)
                    for store in stores_of(number):
                        store.start()
                    return carry

                lax.fori_loop(0, half // 128, pair, 0)

    given.wait()
    width = x_ref.shape[1]
    tail = jnp.zeros((LANES - SLOTS, width), bf16)
    xt_ref[...] = jnp.concatenate([x_ref[...], tail], axis=0).T
    tall = width // CHUNKS
    ones = jnp.ones((8, LANES), bf16)
    place_of = slots()
    sums = []
    blocks = half // 128
    for kind, d_ref in enumerate((dq_ref, dk_ref, dv_ref)):
        product = mul(xt_ref[...], d_ref[...], 1, 1).astype(bf16)
        for chunk in range(CHUNKS):
            xy, z = place_of(chunk)
            for block in range(blocks):
                row = (kind * blocks + block) * tall
                piece_ref[xy, z, row : row + tall, :] = product[chunk * tall : (chunk + 1) * tall, block * 128 : block * 128 + 128]
        if kind != 1:
            total = mul(ones, d_ref[...], 1, 1)[:1]
            sums += [total[:, block * 128 : block * 128 + 128] for block in range(blocks)]
    number = lax.broadcasted_iota(jnp.int32, (16, 128), 0)
    for chunk in range(CHUNKS):
        xy, z = place_of(chunk)
        held = jnp.where(number == 0, sums[chunk] if chunk < len(sums) else 0.0, 0.0)
        piece_ref[xy, z, HEAD_ROWS - 16 :, :] = held.astype(bf16)
    for number in range(half // 128):
        for store in stores_of(number):
            store.wait()


TILES = [(i * 256, 256) for i in range(5)] + [(1280, 144)]


def over_tiles(step):
    def body(number, carry):
        step(number, pl.multiple_of(number * 256, 256), 256)
        return carry

    lax.fori_loop(0, 5, body, 0)
    step(5, *TILES[5])


def mean_of(matrix):
    return jnp.sum(matrix, axis=1, keepdims=True) * (1.0 / matrix.shape[1])


def norm_parts(matrix):
    centre = matrix - mean_of(matrix)
    spread = lax.rsqrt(mean_of(centre * centre) + EPS)
    return centre * spread, spread


def norm_back(scaled, normed, spread):
    return spread * (scaled - mean_of(scaled) - normed * mean_of(scaled * normed))


def fold(matrix):
    return jnp.sum(matrix.reshape(matrix.shape[0] // 8, 8, matrix.shape[1]), axis=0)


def gelu_parts(pre):
    size = jnp.abs(pre)
    t = pl.reciprocal(1.0 + (0.3275911 * 2.0**-0.5) * size)
    bell = jnp.exp2((-0.5 * LOG_E) * (pre * pre))
    poly = 0.5 * 1.061405429
    for factor in (-1.453152027, 1.421413741, -0.284496736, 0.254829592):
        poly = poly * t + 0.5 * factor
    tail = poly * t * bell
    phi = jnp.where(pre > 0, 1.0 - tail, tail)
    return pre * phi, phi + pre * (bell * (2.0 * jnp.pi) ** -0.5)


HIDDEN_STEP = 512


def row_of(ref):
    return ref[...].astype(f32).reshape(1, ref.shape[0])


def feed_forward(
    sets_ref, x_hbm, o_hbm, wo_a, wo_b, ua_hbm, ub_hbm, ba_ref, bb_ref, da_hbm, db_hbm,
    bo_ref, g1_ref, s1_ref, bd_ref, g2_ref, s2_ref, cot_hbm,
    out_hbm, hid_hbm, res_hbm, slope_hbm, sec_hbm, gd_a, gd_b, sums_ref,
    x_ref, o_ref, wo_ref, u_ref, d_ref, cot_ref, out_ref, hid_ref, res_ref, slope_ref, low_ref, gd_ref, act_ref,
    in_sems, row_sems, out_sems,
):
    half = ua_hbm.shape[1]
    split = wo_a.shape[0]
    pairs = [(o_hbm, o_ref), (wo_a, wo_ref.at[pl.ds(0, split)]), (wo_b, wo_ref.at[pl.ds(split, split)]), (x_hbm, x_ref)]
    pairs += [(ua_hbm, u_ref.at[0]), (ub_hbm, u_ref.at[1]), (da_hbm, d_ref.at[0]), (db_hbm, d_ref.at[1]), (cot_hbm, cot_ref)]
    loads = copies(pairs, in_sems)
    for load in loads:
        load.start()
    width = x_ref.shape[1]
    bucket = own_bucket(sets_ref)
    used = SLOTS // WIDTHS[3] * WIDTHS[3]
    for number in range(3):
        used = jnp.where(bucket == number, SLOTS // WIDTHS[number] * WIDTHS[number], used)
    sums_ref[...] = jnp.zeros_like(sums_ref)
    b_out, gain_one, shift_one, b_down, gain_two, shift_two = (
        row_of(ref) for ref in (bo_ref, g1_ref, s1_ref, bd_ref, g2_ref, s2_ref)
    )
    b_up = [row_of(ref) for ref in (ba_ref, bb_ref)]
    places = [(side, at) for side in range(2) for at in range(0, half, HIDDEN_STEP)]
    last = copies([(gd_ref.at[0], gd_a), (gd_ref.at[1], gd_b)], out_sems)

    def stores_of(number, start, size):
        rows = pl.ds(start, size)
        pairs = ((out_ref, out_hbm), (hid_ref, hid_hbm), (res_ref, res_hbm), (slope_ref, slope_hbm), (low_ref, sec_hbm))
        return copies([(near.at[rows], far.at[rows]) for near, far in pairs], row_sems.at[number])

    def step(number, start, size):
        rows = pl.ds(start, size)
        lanes = pl.ds(start, 256)
        attn = mul(o_ref[:, lanes], wo_ref[...], 0, 0)
        resid = x_ref[rows, :].astype(f32) + attn[:size] + b_out
        res_ref[rows, :] = resid
        normed, _ = norm_parts(resid)
        hidden = normed * gain_one + shift_one
        low = hidden.astype(bf16)
        hid_ref[rows, :] = low

        @pl.when(number == 0)
        def _():
            for load in loads[4:]:
                load.wait()

        def lift(side, at):
            return mul(low, u_ref[side, :, at : at + HIDDEN_STEP]) + b_up[side][:, at : at + HIDDEN_STEP]

        total = None
        ahead = lift(*places[0])
        for turn, (side, at) in enumerate(places):
            pre = ahead
            if turn + 1 < len(places):
                ahead = lift(*places[turn + 1])
            place = slice(side * half + at, side * half + at + HIDDEN_STEP)
            active, slope = gelu_parts(pre)
            active = active.astype(bf16)
            act_ref[rows, place] = active
            slope_ref[rows, place] = slope.astype(bf16)
            part = mul(active, d_ref[side, at : at + HIDDEN_STEP, :])
            total = part if total is None else total + part
        second = hidden + total + b_down
        normed, spread = norm_parts(second)
        out_ref[rows, :] = (normed * gain_two + shift_two).astype(bf16)
        row = start + lax.broadcasted_iota(jnp.int32, (size, width), 0)
        top = jnp.where(row < used, cot_ref[rows, :].astype(f32), 0.0)
        grad = norm_back(top * gain_two, normed, spread)
        low_ref[rows, :] = grad.astype(bf16)
        sums_ref[0:8, :] += fold(top * normed)
        sums_ref[8:16, :] += fold(top)
        sums_ref[16:24, :] += fold(grad)
        for store in stores_of(number, start, size):
            store.start()

    for load in loads[:4]:
        load.wait()
    over_tiles(step)
    place_of = slots()
    tall = half // CHUNKS
    for side in range(2):
        for block in range(4):
            place = slice(side * half + block * 4 * tall, side * half + (block + 1) * 4 * tall)
            part = mul(act_ref[:, place], low_ref[...], 0, 0).astype(bf16)
            for z in range(4):
                xy, z_place = place_of(z * 4 + block)
                for lane in range(width // 128):
                    gd_ref[side, xy, z_place, lane * tall : (lane + 1) * tall, :] = part[z * tall : (z + 1) * tall, lane * 128 : lane * 128 + 128]
        last[side].start()
    for number, (start, size) in enumerate(TILES):
        for store in stores_of(number, start, size):
            store.wait()
    for store in last:
        store.wait()


CHUNKS = 16
FEED_ROWS = 336
DOWN_ROWS = 256
HEAD_ROWS = 208


def slots():
    own = lax.axis_index("dp") % CHUNKS

    def place(chunk):
        held = chunk ^ own
        return held % 4, held // 4

    return place


def feed_backward(
    sec_hbm, slope_hbm, hid_hbm, res_hbm, o_hbm, wo_a, wo_b, ua_hbm, ub_hbm, da_hbm, db_hbm, g1_ref, two_ref,
    gr_hbm, g_hbm, delta_hbm, mine_ref, theirs_ref,
    sec_ref, slope_ref, hid_ref, res_ref, o_ref, wo_ref, u_ref, d_ref, gr_ref, g_ref, delta_ref,
    pre_ref, mix_ref, sums_ref, bup_ref, row_in, in_sems, row_out, out_sems,
):
    half = ua_hbm.shape[1]
    width = hid_ref.shape[1]
    split = wo_a.shape[0]

    def loads_of(number, start, size):
        rows = pl.ds(start, size)
        pairs = ((sec_hbm, sec_ref), (slope_hbm, slope_ref), (res_hbm, res_ref))
        return copies([(far.at[rows], near.at[rows]) for far, near in pairs], row_in.at[number])

    def stores_of(number, start, size):
        rows = pl.ds(start, size)
        return copies([(gr_ref.at[rows], gr_hbm.at[rows])], row_out.at[number])

    pairs = [(da_hbm, d_ref.at[0]), (db_hbm, d_ref.at[1]), (ua_hbm, u_ref.at[0]), (ub_hbm, u_ref.at[1])]
    pairs += [(hid_hbm, hid_ref), (o_hbm, o_ref), (wo_a, wo_ref.at[pl.ds(0, split)]), (wo_b, wo_ref.at[pl.ds(split, split)])]
    loads = copies(pairs, in_sems)
    for load in loads_of(0, *TILES[0]) + loads[:4]:
        load.start()
    sums_ref[...] = jnp.zeros_like(sums_ref)
    bup_ref[...] = jnp.zeros_like(bup_ref)
    gain_one = row_of(g1_ref)
    mix_ref[SLOTS:, :] = jnp.zeros((LANES - SLOTS, mix_ref.shape[1]), bf16)
    place_of = slots()
    places = [(side, at) for side in range(2) for at in range(0, half, HIDDEN_STEP)]

    def step(number, start, size):
        @pl.when(number < 4)
        def _():
            for load in loads_of(number + 1, start + 256, 256):
                load.start()

        @pl.when(number == 4)
        def _():
            for load in loads_of(5, *TILES[5]) + loads[4:]:
                load.start()

        for load in loads_of(number, start, size):
            load.wait()

        @pl.when(number == 0)
        def _():
            for load in loads[:4]:
                load.wait()

        rows = pl.ds(start, size)
        low = sec_ref[rows, :]
        second = low.astype(f32)

        def sink(side, at):
            return mul(low, d_ref[side, at : at + HIDDEN_STEP, :], 1, 1)

        total = None
        ahead = sink(*places[0])
        for turn, (side, at) in enumerate(places):
            inner = ahead
            if turn + 1 < len(places):
                ahead = sink(*places[turn + 1])
            place = slice(side * half + at, side * half + at + HIDDEN_STEP)
            pre = (inner * slope_ref[rows, place].astype(f32)).astype(bf16)
            pre_ref[rows, place] = pre
            bup_ref[:, place] += fold(pre.astype(f32))
            part = mul(pre, u_ref[side, :, at : at + HIDDEN_STEP], 1, 1)
            total = part if total is None else total + part
        hidden = second + total
        normed, spread = norm_parts(res_ref[rows, :])
        grad = norm_back(hidden * gain_one, normed, spread)
        gr_ref[rows, :] = grad
        mix_ref[rows, :] = grad.astype(bf16)
        sums_ref[0:8, :] += fold(hidden * normed)
        sums_ref[8:16, :] += fold(hidden)
        sums_ref[16:24, :] += fold(grad)
        for store in stores_of(number, start, size):
            store.start()

    over_tiles(step)
    for load in loads[4:]:
        load.wait()
    last = copies([(g_ref, g_hbm), (delta_ref, delta_hbm)], out_sems)
    for side in range(2):
        place = slice(side * split, (side + 1) * split)
        for start in range(0, LANES, 512):
            lanes = slice(start, start + 512)
            grad = mul(wo_ref[place, :], mix_ref[lanes, :], 1, 1).astype(bf16)
            g_ref[place, lanes] = grad
            prod = grad.astype(f32) * o_ref[place, lanes].astype(f32)
            for head in range(split // 64):
                at = (side * (split // 64) + head) * 16
                delta = jnp.sum(prod[head * 64 : head * 64 + 64], axis=0, keepdims=True)
                delta_ref[at : at + 16, lanes] = extra_rows(-delta)
    for store in last:
        store.start()
    tall = width // CHUNKS
    low = split // CHUNKS
    for side, out in enumerate((mine_ref, theirs_ref)):
        for at in range(0, half, 256):
            place = slice(side * half + at, side * half + at + 256)
            part = mul(hid_ref[...], pre_ref[:, place], 0, 0).astype(bf16)
            for chunk in range(CHUNKS):
                xy, z = place_of(chunk)
                for block in range(2):
                    row = (at // 128 + block) * tall
                    out[xy, z, row : row + tall, :] = part[chunk * tall : (chunk + 1) * tall, block * 128 : block * 128 + 128]
        part = mul(o_ref[side * split : (side + 1) * split, :], mix_ref[...]).astype(bf16)
        for chunk in range(CHUNKS):
            xy, z = place_of(chunk)
            for block in range(width // 128):
                row = half // 128 * tall + block * low
                out[xy, z, row : row + low, :] = part[chunk * low : (chunk + 1) * low, block * 128 : block * 128 + 128]
    vectors = []
    for ref in (two_ref, sums_ref):
        for kind in range(3):
            total = jnp.sum(ref[8 * kind : 8 * kind + 8, :], axis=0, keepdims=True)
            vectors += [total[:, at : at + 128] for at in range(0, width, 128)]
    number = lax.broadcasted_iota(jnp.int32, (16, 128), 0)
    for side, out in enumerate((mine_ref, theirs_ref)):
        total = jnp.sum(bup_ref[:, side * half : (side + 1) * half], axis=0, keepdims=True)
        held = vectors + [total[:, at : at + 128] for at in range(0, half, 128)]
        each = len(held) // CHUNKS
        for chunk in range(CHUNKS):
            xy, z = place_of(chunk)
            block = jnp.zeros((16, 128), f32)
            for row in range(each):
                block = jnp.where(number == row, held[chunk * each + row], block)
            out[xy, z, FEED_ROWS - 16 :, :] = block.astype(bf16)
    for number, (start, size) in enumerate(TILES):
        for store in stores_of(number, start, size):
            store.wait()
    for store in last:
        store.wait()


def project_input(dqa_ref, dka_ref, dva_ref, dqb_ref, dkb_ref, dvb_ref, wa_ref, wb_ref, gr_ref, gi_ref, wt_ref):
    rows = wa_ref.shape[2]
    for side, w_ref in enumerate((wa_ref, wb_ref)):
        for kind in range(3):
            wt_ref[kind, side * rows : (side + 1) * rows, :] = w_ref[kind].T
    for start in range(0, SLOTS, 256):
        size = min(256, SLOTS - start)
        lanes = slice(start, start + 256)
        total = gr_ref[start : start + size, :]
        for side, refs in enumerate(((dqa_ref, dka_ref, dva_ref), (dqb_ref, dkb_ref, dvb_ref))):
            for kind, d_ref in enumerate(refs):
                total = total + mul(d_ref[:, lanes], wt_ref[kind, side * rows : (side + 1) * rows, :], 0, 0)[:size]
        gi_ref[start : start + size, :] = total


def add_pair(mine_ref, theirs_ref, *outs):
    for number, out in enumerate(outs):
        out[...] = (mine_ref[number].astype(f32) + theirs_ref[number].astype(f32)).astype(bf16)


def add_four(a_ref, b_ref, c_ref, d_ref, *outs):
    for number, out in enumerate(outs):
        held = slice(None) if len(outs) == 1 else number
        low = a_ref[held].astype(f32) + b_ref[held].astype(f32)
        out[...] = (low + (c_ref[held].astype(f32) + d_ref[held].astype(f32))).astype(bf16)


def join_four(*refs):
    first, second, outs = refs[:4], refs[4:8], refs[8:]
    for z, out in enumerate(outs):
        at = 0
        for a_ref, b_ref, c_ref, d_ref in (first, second):
            rows = a_ref.shape[1]
            low = a_ref[z].astype(f32) + b_ref[z].astype(f32)
            out[at : at + rows, :] = (low + (c_ref[z].astype(f32) + d_ref[z].astype(f32))).astype(bf16)
            at += rows


def lay_four(a_ref, b_ref, c_ref, d_ref, out_ref):
    for number, ref in enumerate((a_ref, b_ref, c_ref, d_ref)):
        out_ref[number] = ref[...]


def each_chunk(refs):
    own = lax.axis_index("dp") % CHUNKS
    for xy, ref in enumerate(refs):
        for z in range(4):
            yield (z * 4 + xy) ^ own, ref[z].astype(f32)


def spread_feed(
    a_ref, b_ref, c_ref, d_ref, up_ref, out_ref, g2_ref, s2_ref, bd_ref, g1_ref, s1_ref, bo_ref, bup_ref, down_ref, keep_ref,
):
    width, half = up_ref.shape
    tall, low = width // CHUNKS, out_ref.shape[0] // CHUNKS
    deep = half // CHUNKS
    for chunk, held in each_chunk((a_ref, b_ref, c_ref, d_ref)):
        rows = pl.ds(pl.multiple_of(chunk * tall, tall), tall)
        for block in range(half // 128):
            up_ref[rows, block * 128 : block * 128 + 128] = held[block * tall : (block + 1) * tall]
        rows = pl.ds(pl.multiple_of(chunk * low, low), low)
        base = half // 128 * tall
        for block in range(width // 128):
            out_ref[rows, block * 128 : block * 128 + 128] = held[base + block * low : base + (block + 1) * low]
        keep_ref[chunk] = held[FEED_ROWS - 16 : FEED_ROWS]
        rows = pl.ds(pl.multiple_of((chunk % 4 * 4 + chunk // 4) * deep, deep), deep)
        for block in range(width // 128):
            at = FEED_ROWS + block * deep
            down_ref[rows, block * 128 : block * 128 + 128] = held[at : at + deep]
    refs = [(ref, at) for ref in (g2_ref, s2_ref, bd_ref, g1_ref, s1_ref, bo_ref, bup_ref) for at in range(0, ref.shape[0], 128)]
    each = len(refs) // CHUNKS
    for number, (ref, at) in enumerate(refs):
        ref[at : at + 128] = keep_ref[number // each, number % each, :]


def spread_heads(a_ref, b_ref, c_ref, d_ref, qkv_ref, bias_ref, keep_ref):
    kinds, width, half = qkv_ref.shape
    tall = width // CHUNKS
    for chunk, held in each_chunk((a_ref, b_ref, c_ref, d_ref)):
        rows = pl.ds(pl.multiple_of(chunk * tall, tall), tall)
        for kind in range(kinds):
            for block in range(half // 128):
                row = (kind * (half // 128) + block) * tall
                qkv_ref[kind, rows, block * 128 : block * 128 + 128] = held[row : row + tall]
        keep_ref[chunk] = held[HEAD_ROWS - 16 :]
    blocks = half // 128
    for number in range(2 * blocks):
        at = number % blocks * 128
        bias_ref[number // blocks : number // blocks + 1, at : at + 128] = keep_ref[number, 0:1, :]


def shape(dims, kind=bf16):
    return jax.ShapeDtypeStruct(dims, kind)


smem = pl.BlockSpec(memory_space=pltpu.SMEM)


def specs(count):
    return [smem] + [pl.BlockSpec(memory_space=pltpu.VMEM)] * (count - 1)


def cost(flops, moved, powers=0):
    return pl.CostEstimate(flops=int(flops), bytes_accessed=int(moved), transcendentals=int(powers))


hbm = pl.BlockSpec(memory_space=pl.ANY)
vmem = pl.BlockSpec(memory_space=pltpu.VMEM)


def call_forward(sets, x, wa, wb, ba, bb):
    width = 2 * wa.shape[2]
    big, more = (width, LANES), (width // 4, LANES)
    return pl.pallas_call(
        attend_forward, name="attend_forward",
        out_shape=[shape(big), shape(big), shape(big), shape(big), shape(more)],
        in_specs=[smem, hbm, hbm, hbm, vmem, vmem], out_specs=[hbm] * 5,
        scratch_shapes=[pltpu.VMEM(a.shape, bf16) for a in (x, wa, wb)] + [pltpu.VMEM(big, bf16)] * 4 + [pltpu.VMEM(more, bf16)]
        + [pltpu.VMEM((x.shape[1], LANES), bf16), pltpu.VMEM((CLASSES, LANES), bf16), pltpu.VMEM((CLASSES + 16, LANES), bf16)]
        + [pltpu.SemaphoreType.DMA((3,)), pltpu.SemaphoreType.DMA((5,))],
        compiler_params=params(56), cost_estimate=cost(14e9, 12e6),
    )(sets, x, wa, wb, ba, bb)


def call_feed_forward(sets, x, mixed, wo_a, wo_b, up_a, up_b, bu_a, bu_b, down_a, down_b, vecs, cot):
    rows, width = x.shape
    half = up_a.shape[1]
    outs = [shape((rows, width)), shape((rows, width)), shape((rows, width), f32), shape((rows, 2 * half)), shape((rows, width))]
    own = [x.shape, mixed.shape, (width, width), (2, width, half), (2, half, width), x.shape]
    piece = shape((4, 4, DOWN_ROWS, 128))
    return pl.pallas_call(
        feed_forward, name="feed_forward",
        out_shape=outs + [piece, piece, shape((24, width), f32)],
        in_specs=[smem] + [hbm] * 6 + [vmem] * 2 + [hbm] * 2 + [vmem] * 6 + [hbm], out_specs=[hbm] * 7 + [vmem],
        scratch_shapes=[pltpu.VMEM(a, bf16) for a in own] + [pltpu.VMEM(a.shape, a.dtype) for a in outs]
        + [pltpu.VMEM((2, *piece.shape), bf16), pltpu.VMEM((rows, 2 * half), bf16)]
        + [pltpu.SemaphoreType.DMA((9,)), pltpu.SemaphoreType.DMA((6, 5)), pltpu.SemaphoreType.DMA((2,))],
        compiler_params=params(58), cost_estimate=cost(14e9, 20e6),
    )(sets, x, mixed, wo_a, wo_b, up_a, up_b, bu_a, bu_b, down_a, down_b, *vecs, cot)


def call_feed_backward(second, slope, hidden, resid, mixed, wo_a, wo_b, up_a, up_b, down_a, down_b, gain, sums):
    rows, width = second.shape
    half = up_a.shape[1]
    split = wo_a.shape[0]
    piece = shape((4, 4, FEED_ROWS, 128))
    outs = [shape((rows, width), f32), shape((2 * split, LANES)), shape((2 * split // 4, LANES))]
    given = [(a.shape, a.dtype) for a in (second, slope, hidden, resid, mixed)]
    given += [((width, width), bf16), ((2, width, half), bf16), ((2, half, width), bf16)]
    return pl.pallas_call(
        feed_backward, name="feed_backward",
        out_shape=outs + [piece, piece],
        in_specs=[hbm] * 11 + [vmem] * 2, out_specs=[hbm] * 3 + [vmem] * 2,
        scratch_shapes=[pltpu.VMEM(*a) for a in given] + [pltpu.VMEM(a.shape, a.dtype) for a in outs]
        + [
            pltpu.VMEM((rows, 2 * half), bf16), pltpu.VMEM((LANES, width), bf16),
            pltpu.VMEM((24, width), f32), pltpu.VMEM((8, 2 * half), f32),
        ]
        + [pltpu.SemaphoreType.DMA(a) for a in ((6, 3), (8,), (6, 1), (2,))],
        compiler_params=params(58), cost_estimate=cost(14e9, 20e6),
    )(second, slope, hidden, resid, mixed, wo_a, wo_b, up_a, up_b, down_a, down_b, gain, sums)


def call_backward(part, sets, q, k, v, grad, lse, delta, x):
    rows = q.shape[0] // 2
    big, more = (rows, LANES), (rows // 4, LANES)
    return pl.pallas_call(
        functools.partial(attend_backward, part), name="attend_backward",
        out_shape=[shape(big), shape(big), shape(big), shape((4, 4, HEAD_ROWS, 128))],
        in_specs=[smem] + [hbm] * 7, out_specs=[hbm] * 3 + [vmem],
        scratch_shapes=[pltpu.VMEM(a, bf16) for a in (big, big, big, big, more, more, x.shape, big, big, big, (x.shape[1], LANES))]
        + [
            pltpu.VMEM((CLASSES, LANES), bf16), pltpu.VMEM((CLASSES + 16, LANES), bf16),
            pltpu.VMEM((2, 896, 896), bf16), pltpu.VMEM((2, 896, 896), bf16),
            pltpu.VMEM((rows // 64, 64, LANES), f32), pltpu.VMEM((rows // 64, 64, LANES), f32),
        ]
        + [pltpu.SemaphoreType.DMA(a) for a in ((rows // 128, 6), (1,), (rows // 128, 3))],
        compiler_params=params(50), cost_estimate=cost(9e9, 6e6),
    )(sets, q, k, v, grad, lse, delta, x)


def call_project_input(own, other, wa, wb, resid):
    return pl.pallas_call(
        project_input, name="project_input", out_shape=shape(resid.shape, f32),
        scratch_shapes=[pltpu.VMEM((3, 2 * wa.shape[2], wa.shape[1]), bf16)],
        compiler_params=params(40), cost_estimate=cost(2.4e9, 12e6),
    )(*own, *other, wa, wb, resid)


def swap(array):
    return lax.ppermute(array, "mp", [(0, 1), (1, 0)])


def exchange(array, distance):
    count = lax.axis_size("dp")
    return lax.ppermute(array, "dp", [(i, i ^ distance) for i in range(count)])


def small(kernel, name, outs, scratch=()):
    moved = 2 * sum(o.size * o.dtype.itemsize for o in outs)
    return pl.pallas_call(
        kernel, name=name, out_shape=list(outs), scratch_shapes=list(scratch),
        compiler_params=params(24), cost_estimate=cost(1e6, moved),
    )


def after(array, *earlier):
    return lax.optimization_barrier((array, *earlier))[0]


def to_plane(parts):
    return [exchange(parts[xy], xy) for xy in (1, 2, 3)]


def to_line(parts):
    return [exchange(parts[z], 4 * z) for z in (1, 2, 3)]


def plane_sum(parts, came, *earlier):
    _, rows, lanes = parts[0].shape
    return small(add_four, "add_four", [shape((rows, lanes))] * 4)(after(parts[0], *earlier), *came)


def plane_sum_joined(feed, feed_came, down, down_came, *earlier):
    rows, lanes = feed[0].shape[1] + down[0].shape[1], feed[0].shape[2]
    return small(join_four, "join_four", [shape((rows, lanes))] * 4)(after(feed[0], *earlier), *feed_came, down[0], *down_came)


def line_sum(parts, came, *earlier):
    (total,) = small(add_four, "add_four", [shape(parts[0].shape)])(after(parts[0], *earlier), *came)
    distance = CHUNKS
    while distance < lax.axis_size("dp"):
        total = total + exchange(total, distance)
        distance *= 2
    return total


def line_copies(total):
    return [exchange(total, 4 * z) for z in (1, 2, 3)]


def laid(total, came, *earlier):
    (held,) = small(lay_four, "lay_four", [shape((4, *total.shape))])(after(total, *earlier), *came)
    return held


def plane_copies(held):
    return [exchange(held, xy) for xy in (1, 2, 3)]


def halves_added(mine, came, *earlier):
    return small(add_pair, "add_pair", [shape(mine.shape[1:])] * 4)(after(mine, *earlier), came)


def per_device(
    variates, dataset, w_qkv, b_qv, w_out, b_out, gain_one, shift_one, w_up, b_up, w_down, b_down, gain_two, shift_two, cotangent,
):
    width, half = w_up.shape
    other_qkv, other_bias = swap(w_qkv), swap(b_qv)
    other_out, other_up, other_bup, other_down = swap(w_out), swap(w_up), swap(b_up), swap(w_down)
    q, k, v, mixed, lse = call_forward(dataset, variates, w_qkv, other_qkv, b_qv, other_bias)
    out, hidden, resid, slope, second, down_mine, down_theirs, sums = call_feed_forward(
        dataset, variates, mixed, w_out, other_out, w_up, other_up, b_up, other_bup, w_down, other_down,
        (b_out, gain_one, shift_one, b_down, gain_two, shift_two), cotangent,
    )
    down = halves_added(down_mine, swap(down_theirs))
    down_came = to_plane(down)
    grad_res, grad_mix, delta, mine, theirs = call_feed_backward(
        after(second, *down), slope, hidden, resid, mixed, w_out, other_out, w_up, other_up, w_down, other_down, gain_one, sums
    )
    feed = halves_added(mine, swap(after(theirs, *down_came)))
    feed_came = to_plane(feed)
    *other, theirs = call_backward(1, dataset, q, k, v, after(grad_mix, *feed), lse, delta, variates)
    feed = plane_sum_joined(feed, feed_came, down, down_came, theirs)
    heads_came = swap(after(theirs, *feed))
    feed_came = to_line(feed)
    *own, mine = call_backward(0, dataset, q, k, v, after(grad_mix, heads_came, *feed), lse, delta, variates)
    total = line_sum(feed, feed_came, mine)
    heads = halves_added(mine, heads_came, total)
    heads_plane = to_plane(heads)
    feed_came = line_copies(total)
    grad_in = call_project_input(own, other, w_qkv, other_qkv, after(grad_res, total, *heads))
    held = laid(total, feed_came, grad_in)
    heads = plane_sum(heads, heads_plane, grad_in)
    feed = [held, *plane_copies(after(held, *heads))]
    heads = line_sum(heads, to_line(heads))
    heads = laid(heads, line_copies(heads))
    heads = [heads, *plane_copies(heads)]
    vector = shape((width,), f32)
    outs = [shape((width, half), f32), shape(w_out.shape, f32)] + [vector] * 6 + [shape((half,), f32), shape(w_down.shape, f32)]
    keep = [pltpu.VMEM((CHUNKS, 16, 128), f32)]
    grad_up, grad_out, two_gain, two_shift, down_bias, one_gain, one_shift, out_bias, up_bias, grad_down = small(
        spread_feed, "spread_feed", outs, keep
    )(*feed)
    grad_qkv, bias = small(spread_heads, "spread_heads", [shape(w_qkv.shape, f32), shape(b_qv.shape, f32)], keep)(*heads)
    return (
        out, grad_in, grad_qkv, bias, grad_out, out_bias, one_gain, one_shift, grad_up, up_bias,
        grad_down, down_bias, two_gain, two_shift,
    )


def solution(mesh):
    wide = P(("dp", "mp"), None)
    weights = (P(None, None, "mp"), P(None, "mp"), P("mp", None))
    placed = (wide, P("dp"), *weights, P(), P(), P(), P(None, "mp"), P("mp"), P("mp", None), P(), P(), P(), wide)
    given = (wide, wide, *weights, P(), P(), P(), P(None, "mp"), P("mp"), P("mp", None), P(), P(), P())
    return jax.shard_map(per_device, mesh=mesh, in_specs=placed, out_specs=given, check_vma=False)
```

```python
import functools

import jax
import jax.numpy as jnp
from jax import lax
from jax.experimental import pallas as pl
from jax.experimental.pallas import tpu as pltpu
from jax.sharding import PartitionSpec as P

HEAD_DIM = 64
SLOTS = 1424
WIDTHS = (7, 21, 321, 862)
LANES = 1536
CLASSES = 80
BIG = 1e30
EPS = 1e-05
MIB = 2**20

bf16 = jnp.bfloat16
f32 = jnp.float32


def mul(left, right, left_dim=1, right_dim=0):
    return lax.dot_general(
        left, right, (((left_dim,), (right_dim,)), ((), ())), preferred_element_type=f32
    )


def params(limit):
    return pltpu.CompilerParams(vmem_limit_bytes=limit * MIB)


def cover(width, start, stop, last):
    used = SLOTS // width * width
    low = start // width * width
    high = last if stop > used else -(-stop // width) * width
    return (low // 128 * 128, min(-(-min(high, last) // 128) * 128, LANES))


def groups_of(width, rows, step):
    found = []
    for start in range(0, rows, step):
        low, high = cover(width, start, min(start + step, rows), rows)
        if found and found[-1][2] == low and found[-1][2] + found[-1][3] == high:
            first, count = found[-1][:2]
            found[-1] = (first, count + step, low, high - low)
        else:
            found.append((start, step, low, high - low))
    return found


def near(tile):
    return jnp.clip(tile * 256 - 128, 0, LANES - 512)


def middle(tile):
    return jnp.where(tile < 2, 0, jnp.where(tile == 2, 256, jnp.where(tile == 3, 640, 768)))


FORWARD = (
    [(0, 6, 512, near, 8)],
    [(0, 6, 768, middle, 8)],
    [(0, 3, 896, lambda tile: 0 * tile, 8), (3, 4, 1536, lambda tile: 0 * tile, 2), (4, 6, 768, lambda tile: 0 * tile + 768, 8)],
    [(0, 6, 512, near, 1)],
    [(0, 6, LANES, lambda tile: 0 * tile, 1)],
)
BACKWARD = (
    [],
    groups_of(WIDTHS[2], SLOTS // WIDTHS[2] * WIDTHS[2], 128),
    [(0, 896, 0, 896)],
)


def own_bucket(sets_ref):
    return sets_ref[lax.axis_index("mp")]


def token_class(width):
    token = lax.broadcasted_iota(jnp.int32, (CLASSES, LANES), 1)
    numbers = token.astype(f32)
    held = jnp.floor((numbers + 0.5) * (1.0 / width)).astype(jnp.int32)
    held = jnp.where(token < SLOTS, held, (SLOTS - 1) // width + 1)
    row = lax.broadcasted_iota(jnp.int32, (CLASSES, LANES), 0)
    return held % CLASSES == row


def write_masks(bucket, hot_ref, bar_ref):
    for number, width in enumerate(WIDTHS):

        @pl.when(bucket == number)
        def _():
            same = token_class(width)
            hot_ref[...] = jnp.where(same, 1.0, 0.0).astype(bf16)
            bar_ref[:CLASSES, :] = jnp.where(same, 0.0, -BIG).astype(bf16)

    row = lax.broadcasted_iota(jnp.int32, (16, LANES), 0)
    bar_ref[CLASSES:, :] = jnp.where(row < 3, 1.0, 0.0).astype(bf16)


def split_three(row):
    high = row.astype(bf16)
    rest = row - high.astype(f32)
    middle = rest.astype(bf16)
    low = (rest - middle.astype(f32)).astype(bf16)
    return high, middle, low


def extra_rows(row):
    parts = [p.astype(f32) for p in split_three(row)]
    number = lax.broadcasted_iota(jnp.int32, (16, row.shape[1]), 0)
    held = jnp.where(number == 0, parts[0], jnp.where(number == 1, parts[1], jnp.where(number == 2, parts[2], 0.0)))
    return held.astype(bf16)


LOG_E = 1.4426950408889634
SAFE = 60.0


def attend_forward(
    sets_ref, x_hbm, wa_hbm, wb_hbm, ba_ref, bb_ref, q_hbm, k_hbm, v_hbm, o_hbm, lse_hbm,
    x_ref, wa_ref, wb_ref, q_ref, k_ref, v_ref, o_ref, lse_ref, xt_ref, hot_ref, bar_ref, in_sems, out_sems,
):
    loads = [pltpu.make_async_copy(*pair, in_sems.at[i]) for i, pair in enumerate(((x_hbm, x_ref), (wa_hbm, wa_ref), (wb_hbm, wb_ref)))]
    for load in loads:
        load.start()
    pairs = ((q_ref, q_hbm), (k_ref, k_hbm), (v_ref, v_hbm), (o_ref, o_hbm), (lse_ref, lse_hbm))
    stores = [pltpu.make_async_copy(*pair, out_sems.at[i]) for i, pair in enumerate(pairs)]
    bucket = own_bucket(sets_ref)
    write_masks(bucket, hot_ref, bar_ref)
    tail = jnp.zeros((LANES - SLOTS, x_ref.shape[1]), bf16)
    loads[0].wait()
    xt_ref[...] = jnp.concatenate([x_ref[...], tail], axis=0).T
    worst = None
    for side, (w_ref, b_ref) in enumerate(((wa_ref, ba_ref), (wb_ref, bb_ref))):
        loads[1 + side].wait()
        for kind, out_ref in enumerate((q_ref, k_ref, v_ref)):
            weight = w_ref[kind].T
            rows = weight.shape[0]
            if kind != 1:
                row = b_ref[kind // 2 : kind // 2 + 1, :].astype(f32)
                column = jnp.broadcast_to(row, (128, rows)).T
                column = jnp.concatenate([column] * 4, axis=1)

            def project(number, carry):
                lanes = slice(number * 512, number * 512 + 512)
                part = mul(weight, xt_ref[:, lanes])
                if kind != 1:
                    part = part + column
                if kind == 0:
                    part = part * 0.125
                out_ref[side * rows : (side + 1) * rows, lanes] = part.astype(bf16)
                return carry

            for number in range(LANES // 512):
                project(number, 0)
    for store in stores[:3]:
        store.start()
    heads = q_ref.shape[0] // 64
    for head in range(heads):
        norms = []
        for ref in (q_ref, k_ref):
            held = ref[head * 64 : head * 64 + 64, :].astype(f32)
            norms.append(jnp.max(jnp.sum(held * held, axis=0, keepdims=True), axis=1, keepdims=True))
        both = norms[0] * norms[1]
        worst = both if worst is None else jnp.maximum(worst, both)
    calm = worst[0, 0] < SAFE * SAFE

    def score(head, start, first, span):
        rows = pl.ds(pl.multiple_of(head * 64, 64), 64)
        lanes, span = pl.ds(start, 256), pl.ds(first, span)
        keys = jnp.concatenate([k_ref[rows, span], bar_ref[:CLASSES, span]], axis=0)
        quer = jnp.concatenate([q_ref[rows, lanes], hot_ref[:, lanes]], axis=0)
        return mul(keys, quer, 0, 0)

    def finish(head, start, first, span, scores, plain):
        rows = pl.ds(pl.multiple_of(head * 64, 64), 64)
        lanes = pl.ds(start, 256)
        if plain:
            raised = jnp.exp2(scores * LOG_E).astype(bf16)
        else:
            top = jnp.max(scores, axis=0, keepdims=True)
            raised = jnp.exp(scores - top).astype(bf16)
        vals = jnp.concatenate([v_ref[rows, pl.ds(first, span)], jnp.ones((16, span), bf16)], axis=0)
        total = mul(vals, raised)
        sums = total[64:65, :]
        o_ref[rows, lanes] = (total[:64, :] * (1.0 / sums)).astype(bf16)
        logs = jnp.log(sums)
        if not plain:
            logs = logs + top
        lse_ref[pl.ds(pl.multiple_of(head * 16, 16), 16), lanes] = extra_rows(-logs)

    def over(begin, end, span, first_of, together, plain):
        def turn(number, carry):
            tile = begin + number % (end - begin)
            start = pl.multiple_of(tile * 256, 256)
            first = pl.multiple_of(first_of(tile), 128)
            own = [number // (end - begin) * together + i for i in range(together)]
            held = [score(head, start, first, span) for head in own]
            for head, scores in zip(own, held):
                finish(head, start, first, span, scores, plain)
            return carry

        lax.fori_loop(0, heads // together * (end - begin), turn, 0)

    for group in range(5):
        plain = group < 3
        chosen = (bucket < 2, bucket == 2, bucket == 3, bucket < 2, bucket >= 2)[group]

        @pl.when(jnp.logical_and(chosen, calm == plain))
        def _():
            for begin, end, span, first_of, together in FORWARD[group]:
                over(begin, end, span, first_of, together, plain)

    for store in stores[3:]:
        store.start()
    for store in stores:
        store.wait()


def copies(pairs, sems):
    return [pltpu.make_async_copy(*pair, sems.at[i]) for i, pair in enumerate(pairs)]


def attend_backward(
    part, sets_ref, q_hbm, k_hbm, v_hbm, g_hbm, lse_hbm, delta_hbm, x_hbm, dq_hbm, dk_hbm, dv_hbm, piece_ref,
    q_ref, k_ref, v_ref, g_ref, lse_ref, delta_ref, x_ref, grads_ref, xt_ref,
    hot_ref, bar_ref, p_ref, s_ref, ka_ref, va_ref, head_sems, in_sems, out_sems,
):
    half = q_ref.shape[0]
    dq_ref, dk_ref, dv_ref = (grads_ref.at[kind] for kind in range(3))

    def loads_of(number):
        there = pl.ds(part * half + number * 128, 128)
        here = pl.ds(number * 128, 128)
        pairs = [(far.at[there], near.at[here]) for far, near in ((q_hbm, q_ref), (k_hbm, k_ref), (v_hbm, v_ref), (g_hbm, g_ref))]
        there = pl.ds(part * (half // 4) + number * 32, 32)
        here = pl.ds(number * 32, 32)
        pairs += [(far.at[there], near.at[here]) for far, near in ((lse_hbm, lse_ref), (delta_hbm, delta_ref))]
        return copies(pairs, head_sems.at[number])

    def stores_of(number):
        here = pl.ds(number * 128, 128)
        return copies([(near.at[here], far.at[here]) for near, far in ((dq_ref, dq_hbm), (dk_ref, dk_hbm), (dv_ref, dv_hbm))], out_sems.at[number])

    for number in range(half // 128):
        for load in loads_of(number):
            load.start()
    given = copies([(x_hbm, x_ref)], in_sems)[0]
    bucket = own_bucket(sets_ref)
    write_masks(bucket, hot_ref, bar_ref)

    def one_head(head, groups, slot):
        rows = pl.ds(pl.multiple_of(head * 64, 64), 64)
        more = pl.ds(pl.multiple_of(head * 16, 16), 16)
        single = len(groups) == 1
        if not single:
            ka_ref[slot] = jnp.zeros(ka_ref.shape[1:], f32)
            va_ref[slot] = jnp.zeros(va_ref.shape[1:], f32)
        for q0, nq, k0, nk in groups:
            span = slice(k0, k0 + nk)
            held = slice(q0, q0 + nq)
            keys = jnp.concatenate([k_ref[rows, span], bar_ref[:, span]], axis=0)
            vals = jnp.concatenate([v_ref[rows, span], bar_ref[CLASSES:, span]], axis=0)
            for start in range(q0, q0 + nq, 256):
                size = min(256, q0 + nq - start)
                lanes = slice(start, start + size)
                quer = jnp.concatenate([q_ref[rows, lanes], hot_ref[:, lanes], lse_ref[more, lanes]], axis=0)
                grad = jnp.concatenate([g_ref[rows, lanes], delta_ref[more, lanes]], axis=0)
                probs = jnp.exp2(mul(quer, keys, 0, 0) * LOG_E)
                slopes = probs * mul(grad, vals, 0, 0)
                p_ref[slot, start - q0 : start - q0 + size, :nk] = probs.astype(bf16)
                s_ref[slot, start - q0 : start - q0 + size, :nk] = slopes.astype(bf16)
            dv = mul(g_ref[rows, held], p_ref[slot, :nq, :nk])
            dk = mul(q_ref[rows, held], s_ref[slot, :nq, :nk])
            dq = mul(k_ref[rows, span], s_ref[slot, :nq, :nk], 1, 1)
            dq_ref[rows, held] = (dq * 0.125).astype(bf16)
            if single:
                dv_ref[rows, span] = dv.astype(bf16)
                dk_ref[rows, span] = dk.astype(bf16)
            else:
                va_ref[slot, :, span] += dv
                ka_ref[slot, :, span] += dk
        if single:
            rest = LANES - 896
            for out in (dq_ref, dk_ref, dv_ref):
                out[rows, 896:] = jnp.zeros((64, rest), bf16)
        else:
            dv_ref[rows, :] = va_ref[slot].astype(bf16)
            dk_ref[rows, :] = ka_ref[slot].astype(bf16)
            done = groups[-1][0] + groups[-1][1]
            if done < LANES:
                dq_ref[rows, done:] = jnp.zeros((64, LANES - done), bf16)

    def tile_of(head, start, first, span):
        rows = pl.ds(head * 64, 64)
        more = pl.ds(head * 16, 16)
        lanes, span = pl.ds(start, 256), pl.ds(first, span)
        keys = jnp.concatenate([k_ref[rows, span], bar_ref[:, span]], axis=0)
        vals = jnp.concatenate([v_ref[rows, span], bar_ref[CLASSES:, span]], axis=0)
        quer = jnp.concatenate([q_ref[rows, lanes], hot_ref[:, lanes], lse_ref[more, lanes]], axis=0)
        grad = jnp.concatenate([g_ref[rows, lanes], delta_ref[more, lanes]], axis=0)
        probs = jnp.exp2(mul(quer, keys, 0, 0) * LOG_E)
        slopes = (probs * mul(grad, vals, 0, 0)).astype(bf16)
        return probs.astype(bf16), slopes

    def take(head, start, first, span, probs, slopes):
        rows = pl.ds(head * 64, 64)
        lanes, span = pl.ds(start, 256), pl.ds(first, span)
        va_ref[head, :, span] += mul(g_ref[rows, lanes], probs)
        ka_ref[head, :, span] += mul(q_ref[rows, lanes], slopes)
        dq_ref[rows, lanes] = (mul(k_ref[rows, span], slopes, 1, 1) * 0.125).astype(bf16)

    def by_tiles(span, first_of, together):
        for number in range(half // 128):
            for load in loads_of(number):
                load.wait()
        given.start()
        ka_ref[...] = jnp.zeros_like(ka_ref)
        va_ref[...] = jnp.zeros_like(va_ref)

        def turn(tile, carry):
            start = pl.multiple_of(tile * 256, 256)
            first = pl.multiple_of(first_of(tile), 128)
            for base in range(0, half // 64, together):
                own = range(base, base + together)
                held = [tile_of(head, start, first, span) for head in own]
                for head, (probs, slopes) in zip(own, held):
                    take(head, start, first, span, probs, slopes)
            return carry

        lax.fori_loop(0, 6, turn, 0)
        for head in range(half // 64):
            rows = pl.ds(head * 64, 64)
            dv_ref[rows, :] = va_ref[head].astype(bf16)
            dk_ref[rows, :] = ka_ref[head].astype(bf16)
        for number in range(half // 128):
            for store in stores_of(number):
                store.start()

    for group in range(3):
        chosen = (bucket < 2, bucket == 2, bucket == 3)[group]

        @pl.when(chosen)
        def _():
            if group == 0:
                by_tiles(512, near, 4)
            else:

                def pair(number, carry):
                    for load in loads_of(number):
                        load.wait()

                    @pl.when(number == 0)
                    def _():
                        given.start()

                    one_head(2 * number, BACKWARD[group], 0)
                    one_head(2 * number + 1, BACKWARD[group], 1)
                    for store in stores_of(number):
                        store.start()
                    return carry

                lax.fori_loop(0, half // 128, pair, 0)

    given.wait()
    width = x_ref.shape[1]
    tail = jnp.zeros((LANES - SLOTS, width), bf16)
    xt_ref[...] = jnp.concatenate([x_ref[...], tail], axis=0).T
    tall = width // CHUNKS
    ones = jnp.ones((8, LANES), bf16)
    place_of = slots()
    sums = []
    blocks = half // 128

    def product_of(kind, carry):
        product = mul(xt_ref[...], grads_ref[kind], 1, 1).astype(bf16)
        for chunk in range(CHUNKS):
            xy, z = place_of(chunk)
            for block in range(blocks):
                row = (kind * blocks + block) * tall
                piece_ref[xy, z, pl.ds(row, tall), :] = product[chunk * tall : (chunk + 1) * tall, block * 128 : block * 128 + 128]
        return carry

    for kind in range(3):
        product_of(kind, 0)
    for d_ref in (dq_ref, dv_ref):
        total = mul(ones, d_ref[...], 1, 1)[:1]
        sums += [total[:, block * 128 : block * 128 + 128] for block in range(blocks)]
    number = lax.broadcasted_iota(jnp.int32, (16, 128), 0)
    for chunk in range(CHUNKS):
        xy, z = place_of(chunk)
        held = jnp.where(number == 0, sums[chunk] if chunk < len(sums) else 0.0, 0.0)
        piece_ref[xy, z, HEAD_ROWS - 16 :, :] = held.astype(bf16)
    for number in range(half // 128):
        for store in stores_of(number):
            store.wait()


TILE = 240
TILES = 6
PADDED = TILE * TILES
LAST = SLOTS - TILE * (TILES - 1)


def over_tiles(step):
    def body(number, carry):
        step(number, pl.multiple_of(number * TILE, TILE))
        return carry

    lax.fori_loop(0, TILES, body, 0)


def rows_moved(number, start, begin):
    if isinstance(number, int):
        begin(start, LAST if number == TILES - 1 else TILE)
        return

    @pl.when(number < TILES - 1)
    def _():
        begin(start, TILE)

    @pl.when(number == TILES - 1)
    def _():
        begin(TILE * (TILES - 1), LAST)


def mean_of(matrix):
    return jnp.sum(matrix, axis=1, keepdims=True) * (1.0 / matrix.shape[1])


def norm_parts(matrix):
    centre = matrix - mean_of(matrix)
    spread = lax.rsqrt(mean_of(centre * centre) + EPS)
    return centre * spread, spread


def norm_back(scaled, normed, spread):
    return spread * (scaled - mean_of(scaled) - normed * mean_of(scaled * normed))


def fold(matrix):
    return jnp.sum(matrix.reshape(matrix.shape[0] // 8, 8, matrix.shape[1]), axis=0)


def gelu_parts(pre):
    size = jnp.abs(pre)
    t = pl.reciprocal(1.0 + (0.3275911 * 2.0**-0.5) * size)
    bell = jnp.exp2((-0.5 * LOG_E) * (pre * pre))
    poly = 0.5 * 1.061405429
    for factor in (-1.453152027, 1.421413741, -0.284496736, 0.254829592):
        poly = poly * t + 0.5 * factor
    tail = poly * t * bell
    phi = jnp.where(pre > 0, 1.0 - tail, tail)
    return pre * phi, phi + pre * (bell * (2.0 * jnp.pi) ** -0.5)


HIDDEN_STEP = 512


def row_of(ref):
    return ref[...].astype(f32).reshape(1, ref.shape[0])


def feed_forward(
    sets_ref, x_hbm, o_hbm, wo_a, wo_b, ua_hbm, ub_hbm, ba_ref, bb_ref, da_hbm, db_hbm,
    bo_ref, g1_ref, s1_ref, bd_ref, g2_ref, s2_ref, cot_hbm,
    out_hbm, hid_hbm, res_hbm, slope_hbm, sec_hbm, gd_a, gd_b, sums_ref,
    x_ref, o_ref, wo_ref, u_ref, d_ref, cot_ref, out_ref, hid_ref, res_ref, slope_ref, low_ref, gd_ref, act_ref,
    in_sems, row_sems, out_sems,
):
    half = ua_hbm.shape[1]
    split = wo_a.shape[0]
    width = x_ref.shape[1]
    true = pl.ds(0, SLOTS)
    pairs = [(o_hbm, o_ref), (wo_a, wo_ref.at[pl.ds(0, split)]), (wo_b, wo_ref.at[pl.ds(split, split)]), (x_hbm, x_ref.at[true])]
    pairs += [(ua_hbm, u_ref.at[0]), (ub_hbm, u_ref.at[1]), (da_hbm, d_ref.at[0]), (db_hbm, d_ref.at[1]), (cot_hbm, cot_ref.at[true])]
    loads = copies(pairs, in_sems)
    for load in loads:
        load.start()
    for ref in (x_ref, cot_ref):
        ref[SLOTS:, :] = jnp.zeros((PADDED - SLOTS, width), bf16)
    bucket = own_bucket(sets_ref)
    used = SLOTS // WIDTHS[3] * WIDTHS[3]
    for number in range(3):
        used = jnp.where(bucket == number, SLOTS // WIDTHS[number] * WIDTHS[number], used)
    sums_ref[...] = jnp.zeros_like(sums_ref)
    b_out, gain_one, shift_one, b_down, gain_two, shift_two = (
        row_of(ref) for ref in (bo_ref, g1_ref, s1_ref, bd_ref, g2_ref, s2_ref)
    )
    b_up = [row_of(ref) for ref in (ba_ref, bb_ref)]
    places = [(side, at) for side in range(2) for at in range(0, half, HIDDEN_STEP)]
    last = copies([(gd_ref.at[0], gd_a), (gd_ref.at[1], gd_b)], out_sems)

    def stores_of(number, start, size):
        rows = pl.ds(start, size)
        pairs = ((out_ref, out_hbm), (hid_ref, hid_hbm), (res_ref, res_hbm), (slope_ref, slope_hbm), (low_ref, sec_hbm))
        return copies([(near.at[rows], far.at[rows]) for near, far in pairs], row_sems.at[number])

    def step(number, start):
        rows = pl.ds(start, TILE)
        resid = res_ref[rows, :] + x_ref[rows, :].astype(f32) + b_out
        res_ref[rows, :] = resid
        normed, _ = norm_parts(resid)
        hidden = normed * gain_one + shift_one
        low = hidden.astype(bf16)
        hid_ref[rows, :] = low

        @pl.when(number == 0)
        def _():
            for load in loads[4:]:
                load.wait()

        def lift(side, at):
            return mul(low, u_ref[side, :, at : at + HIDDEN_STEP]) + b_up[side][:, at : at + HIDDEN_STEP]

        total = None
        ahead = lift(*places[0])
        for turn, (side, at) in enumerate(places):
            pre = ahead
            if turn + 1 < len(places):
                ahead = lift(*places[turn + 1])
            place = slice(side * half + at, side * half + at + HIDDEN_STEP)
            active, slope = gelu_parts(pre)
            active = active.astype(bf16)
            act_ref[rows, place] = active
            slope_ref[rows, place] = slope.astype(bf16)
            part = mul(active, d_ref[side, at : at + HIDDEN_STEP, :])
            total = part if total is None else total + part
        second = hidden + total + b_down
        normed, spread = norm_parts(second)
        out_ref[rows, :] = (normed * gain_two + shift_two).astype(bf16)
        row = start + lax.broadcasted_iota(jnp.int32, (TILE, width), 0)
        top = jnp.where(row < used, cot_ref[rows, :].astype(f32), 0.0)
        grad = norm_back(top * gain_two, normed, spread)
        low_ref[rows, :] = grad.astype(bf16)
        sums_ref[0:8, :] += fold(top * normed)
        sums_ref[8:16, :] += fold(top)
        sums_ref[16:24, :] += fold(grad)
        rows_moved(number, start, lambda at, size: [store.start() for store in stores_of(number, at, size)])

    for load in loads[:4]:
        load.wait()
    for start in range(0, PADDED, 512):
        size = min(512, PADDED - start)
        res_ref[start : start + size, :] = mul(o_ref[:, start : start + 512], wo_ref[...], 0, 0)[:size]
    over_tiles(step)
    place_of = slots()
    tall = half // CHUNKS

    def block_of(number, carry):
        side, block = number // 4, number % 4
        part = mul(act_ref[:, pl.ds(pl.multiple_of(number * 4 * tall, 4 * tall), 4 * tall)], low_ref[...], 0, 0).astype(bf16)
        for z in range(4):
            xy, z_place = place_of(z * 4 + block)
            for lane in range(width // 128):
                gd_ref[side, xy, z_place, lane * tall : (lane + 1) * tall, :] = part[z * tall : (z + 1) * tall, lane * 128 : lane * 128 + 128]

        @pl.when(number == 3)
        def _():
            last[0].start()

        return carry

    lax.fori_loop(0, 8, block_of, 0)
    last[1].start()
    for number in range(TILES):
        rows_moved(number, number * TILE, lambda at, size: [store.wait() for store in stores_of(number, at, size)])
    for store in last:
        store.wait()


CHUNKS = 16
FEED_ROWS = 336
DOWN_ROWS = 256
HEAD_ROWS = 208


def slots():
    own = lax.axis_index("dp") % CHUNKS

    def place(chunk):
        held = chunk ^ own
        return held % 4, held // 4

    return place


def feed_backward(
    sec_hbm, slope_hbm, hid_hbm, res_hbm, o_hbm, wo_a, wo_b, ua_hbm, ub_hbm, da_hbm, db_hbm, g1_ref, two_ref,
    gr_hbm, g_hbm, delta_hbm, mine_ref, theirs_ref,
    sec_ref, slope_ref, hid_ref, res_ref, o_ref, wo_ref, u_ref, d_ref, gr_ref, g_ref, delta_ref,
    pre_ref, mix_ref, sums_ref, bup_ref, row_in, in_sems, row_out, out_sems,
):
    half = ua_hbm.shape[1]
    width = hid_ref.shape[1]
    split = wo_a.shape[0]

    def loads_of(number, start, size):
        rows = pl.ds(start, size)
        pairs = ((sec_hbm, sec_ref), (slope_hbm, slope_ref), (res_hbm, res_ref))
        return copies([(far.at[rows], near.at[rows]) for far, near in pairs], row_in.at[number])

    def stores_of(number, start, size):
        rows = pl.ds(start, size)
        return copies([(gr_ref.at[rows], gr_hbm.at[rows])], row_out.at[number])

    pairs = [(da_hbm, d_ref.at[0]), (db_hbm, d_ref.at[1]), (ua_hbm, u_ref.at[0]), (ub_hbm, u_ref.at[1])]
    pairs += [(hid_hbm, hid_ref.at[pl.ds(0, SLOTS)]), (o_hbm, o_ref), (wo_a, wo_ref.at[pl.ds(0, split)]), (wo_b, wo_ref.at[pl.ds(split, split)])]
    loads = copies(pairs, in_sems)
    for load in loads_of(0, 0, TILE) + loads[:4]:
        load.start()
    for ref in (sec_ref, slope_ref, res_ref, hid_ref):
        ref[SLOTS:, :] = jnp.zeros((PADDED - SLOTS, ref.shape[1]), ref.dtype)
    sums_ref[...] = jnp.zeros_like(sums_ref)
    bup_ref[...] = jnp.zeros_like(bup_ref)
    gain_one = row_of(g1_ref)
    mix_ref[PADDED:, :] = jnp.zeros((LANES - PADDED, width), bf16)
    place_of = slots()
    places = [(side, at) for side in range(2) for at in range(0, half, HIDDEN_STEP)]

    def step(number, start):
        @pl.when(number < TILES - 1)
        def _():
            rows_moved(number + 1, start + TILE, lambda at, size: [load.start() for load in loads_of(number + 1, at, size)])

        @pl.when(number == TILES - 2)
        def _():
            for load in loads[4:]:
                load.start()

        rows_moved(number, start, lambda at, size: [load.wait() for load in loads_of(number, at, size)])

        @pl.when(number == 0)
        def _():
            for load in loads[:4]:
                load.wait()

        rows = pl.ds(start, TILE)
        low = sec_ref[rows, :]
        second = low.astype(f32)

        def sink(side, at):
            return mul(low, d_ref[side, at : at + HIDDEN_STEP, :], 1, 1)

        total = None
        ahead = sink(*places[0])
        for turn, (side, at) in enumerate(places):
            inner = ahead
            if turn + 1 < len(places):
                ahead = sink(*places[turn + 1])
            place = slice(side * half + at, side * half + at + HIDDEN_STEP)
            pre = (inner * slope_ref[rows, place].astype(f32)).astype(bf16)
            pre_ref[rows, place] = pre
            bup_ref[:, place] += fold(pre.astype(f32))
            part = mul(pre, u_ref[side, :, at : at + HIDDEN_STEP], 1, 1)
            total = part if total is None else total + part
        hidden = second + total
        normed, spread = norm_parts(res_ref[rows, :])
        grad = norm_back(hidden * gain_one, normed, spread)
        gr_ref[rows, :] = grad
        mix_ref[rows, :] = grad.astype(bf16)
        sums_ref[0:8, :] += fold(hidden * normed)
        sums_ref[8:16, :] += fold(hidden)
        sums_ref[16:24, :] += fold(grad)
        rows_moved(number, start, lambda at, size: [store.start() for store in stores_of(number, at, size)])

    over_tiles(step)
    for load in loads[4:]:
        load.wait()
    last = copies([(g_ref, g_hbm), (delta_ref, delta_hbm)], out_sems)

    def mixed_grad(number, carry):
        side = number // 3
        place = slice(side * split, (side + 1) * split)
        lanes = slice(number % 3 * 512, number % 3 * 512 + 512)
        grad = mul(wo_ref[place, :], mix_ref[lanes, :], 1, 1).astype(bf16)
        g_ref[place, lanes] = grad
        prod = grad.astype(f32) * o_ref[place, lanes].astype(f32)
        for head in range(split // 64):
            at = (side * (split // 64) + head) * 16
            delta = jnp.sum(prod[head * 64 : head * 64 + 64], axis=0, keepdims=True)
            delta_ref[pl.ds(at, 16), lanes] = extra_rows(-delta)
        return carry

    for number in range(6):
        mixed_grad(number, 0)
    for store in last:
        store.start()
    tall = width // CHUNKS
    low = split // CHUNKS
    for side, out in enumerate((mine_ref, theirs_ref)):

        def up_block(number, carry):
            at = side * half + number * 256
            part = mul(hid_ref[...], pre_ref[:, pl.ds(at, 256)], 0, 0).astype(bf16)
            for chunk in range(CHUNKS):
                xy, z = place_of(chunk)
                for block in range(2):
                    row = (2 * number + block) * tall
                    out[xy, z, pl.ds(row, tall), :] = part[chunk * tall : (chunk + 1) * tall, block * 128 : block * 128 + 128]
            return carry

        for number in range(half // 256):
            up_block(number, 0)
        part = mul(o_ref[side * split : (side + 1) * split, :], mix_ref[...]).astype(bf16)
        for chunk in range(CHUNKS):
            xy, z = place_of(chunk)
            for block in range(width // 128):
                row = half // 128 * tall + block * low
                out[xy, z, row : row + low, :] = part[chunk * low : (chunk + 1) * low, block * 128 : block * 128 + 128]
    vectors = []
    for ref in (two_ref, sums_ref):
        for kind in range(3):
            total = jnp.sum(ref[8 * kind : 8 * kind + 8, :], axis=0, keepdims=True)
            vectors += [total[:, at : at + 128] for at in range(0, width, 128)]
    number = lax.broadcasted_iota(jnp.int32, (16, 128), 0)
    for side, out in enumerate((mine_ref, theirs_ref)):
        total = jnp.sum(bup_ref[:, side * half : (side + 1) * half], axis=0, keepdims=True)
        held = vectors + [total[:, at : at + 128] for at in range(0, half, 128)]
        each = len(held) // CHUNKS
        for chunk in range(CHUNKS):
            xy, z = place_of(chunk)
            block = jnp.zeros((16, 128), f32)
            for row in range(each):
                block = jnp.where(number == row, held[chunk * each + row], block)
            out[xy, z, FEED_ROWS - 16 :, :] = block.astype(bf16)
    for number in range(TILES):
        rows_moved(number, number * TILE, lambda at, size: [store.wait() for store in stores_of(number, at, size)])
    for store in last:
        store.wait()


def project_input(dqa_ref, dka_ref, dva_ref, dqb_ref, dkb_ref, dvb_ref, wa_ref, wb_ref, gr_ref, gi_ref, wt_ref):
    rows = wa_ref.shape[2]
    for side, w_ref in enumerate((wa_ref, wb_ref)):
        for kind in range(3):
            wt_ref[kind, side * rows : (side + 1) * rows, :] = w_ref[kind].T
    for start in range(0, SLOTS, 256):
        size = min(256, SLOTS - start)
        lanes = slice(start, start + 256)
        total = gr_ref[start : start + size, :]
        for side, refs in enumerate(((dqa_ref, dka_ref, dva_ref), (dqb_ref, dkb_ref, dvb_ref))):
            for kind, d_ref in enumerate(refs):
                total = total + mul(d_ref[:, lanes], wt_ref[kind, side * rows : (side + 1) * rows, :], 0, 0)[:size]
        gi_ref[start : start + size, :] = total


def add_pair(mine_ref, theirs_ref, *outs):
    for number, out in enumerate(outs):
        out[...] = (mine_ref[number].astype(f32) + theirs_ref[number].astype(f32)).astype(bf16)


def add_four(a_ref, b_ref, c_ref, d_ref, *outs):
    for number, out in enumerate(outs):
        held = slice(None) if len(outs) == 1 else number
        low = a_ref[held].astype(f32) + b_ref[held].astype(f32)
        out[...] = (low + (c_ref[held].astype(f32) + d_ref[held].astype(f32))).astype(bf16)


def join_four(*refs):
    first, second, outs = refs[:4], refs[4:8], refs[8:]
    for z, out in enumerate(outs):
        at = 0
        for a_ref, b_ref, c_ref, d_ref in (first, second):
            rows = a_ref.shape[1]
            low = a_ref[z].astype(f32) + b_ref[z].astype(f32)
            out[at : at + rows, :] = (low + (c_ref[z].astype(f32) + d_ref[z].astype(f32))).astype(bf16)
            at += rows


def lay_four(a_ref, b_ref, c_ref, d_ref, out_ref):
    for number, ref in enumerate((a_ref, b_ref, c_ref, d_ref)):
        out_ref[number] = ref[...]


def each_chunk(refs):
    own = lax.axis_index("dp") % CHUNKS
    for xy, ref in enumerate(refs):
        for z in range(4):
            yield (z * 4 + xy) ^ own, ref[z].astype(f32)


def spread_feed(
    a_ref, b_ref, c_ref, d_ref, up_ref, out_ref, g2_ref, s2_ref, bd_ref, g1_ref, s1_ref, bo_ref, bup_ref, down_ref, keep_ref,
):
    width, half = up_ref.shape
    tall, low = width // CHUNKS, out_ref.shape[0] // CHUNKS
    deep = half // CHUNKS
    for chunk, held in each_chunk((a_ref, b_ref, c_ref, d_ref)):
        rows = pl.ds(pl.multiple_of(chunk * tall, tall), tall)
        for block in range(half // 128):
            up_ref[rows, block * 128 : block * 128 + 128] = held[block * tall : (block + 1) * tall]
        rows = pl.ds(pl.multiple_of(chunk * low, low), low)
        base = half // 128 * tall
        for block in range(width // 128):
            out_ref[rows, block * 128 : block * 128 + 128] = held[base + block * low : base + (block + 1) * low]
        keep_ref[chunk] = held[FEED_ROWS - 16 : FEED_ROWS]
        rows = pl.ds(pl.multiple_of((chunk % 4 * 4 + chunk // 4) * deep, deep), deep)
        for block in range(width // 128):
            at = FEED_ROWS + block * deep
            down_ref[rows, block * 128 : block * 128 + 128] = held[at : at + deep]
    refs = [(ref, at) for ref in (g2_ref, s2_ref, bd_ref, g1_ref, s1_ref, bo_ref, bup_ref) for at in range(0, ref.shape[0], 128)]
    each = len(refs) // CHUNKS
    for number, (ref, at) in enumerate(refs):
        ref[at : at + 128] = keep_ref[number // each, number % each, :]


def spread_heads(a_ref, b_ref, c_ref, d_ref, qkv_ref, bias_ref, keep_ref):
    kinds, width, half = qkv_ref.shape
    tall = width // CHUNKS
    for chunk, held in each_chunk((a_ref, b_ref, c_ref, d_ref)):
        rows = pl.ds(pl.multiple_of(chunk * tall, tall), tall)
        for kind in range(kinds):
            for block in range(half // 128):
                row = (kind * (half // 128) + block) * tall
                qkv_ref[kind, rows, block * 128 : block * 128 + 128] = held[row : row + tall]
        keep_ref[chunk] = held[HEAD_ROWS - 16 :]
    blocks = half // 128
    for number in range(2 * blocks):
        at = number % blocks * 128
        bias_ref[number // blocks : number // blocks + 1, at : at + 128] = keep_ref[number, 0:1, :]


def shape(dims, kind=bf16):
    return jax.ShapeDtypeStruct(dims, kind)


smem = pl.BlockSpec(memory_space=pltpu.SMEM)


def specs(count):
    return [smem] + [pl.BlockSpec(memory_space=pltpu.VMEM)] * (count - 1)


def cost(flops, moved, powers=0):
    return pl.CostEstimate(flops=int(flops), bytes_accessed=int(moved), transcendentals=int(powers))


hbm = pl.BlockSpec(memory_space=pl.ANY)
vmem = pl.BlockSpec(memory_space=pltpu.VMEM)


def call_forward(sets, x, wa, wb, ba, bb):
    width = 2 * wa.shape[2]
    big, more = (width, LANES), (width // 4, LANES)
    return pl.pallas_call(
        attend_forward, name="attend_forward",
        out_shape=[shape(big), shape(big), shape(big), shape(big), shape(more)],
        in_specs=[smem, hbm, hbm, hbm, vmem, vmem], out_specs=[hbm] * 5,
        scratch_shapes=[pltpu.VMEM(a.shape, bf16) for a in (x, wa, wb)] + [pltpu.VMEM(big, bf16)] * 4 + [pltpu.VMEM(more, bf16)]
        + [pltpu.VMEM((x.shape[1], LANES), bf16), pltpu.VMEM((CLASSES, LANES), bf16), pltpu.VMEM((CLASSES + 16, LANES), bf16)]
        + [pltpu.SemaphoreType.DMA((3,)), pltpu.SemaphoreType.DMA((5,))],
        compiler_params=params(54), cost_estimate=cost(14e9, 12e6),
    )(sets, x, wa, wb, ba, bb)


def call_feed_forward(sets, x, mixed, wo_a, wo_b, up_a, up_b, bu_a, bu_b, down_a, down_b, vecs, cot):
    rows, width = x.shape
    half = up_a.shape[1]
    outs = [shape((rows, width)), shape((rows, width)), shape((rows, width), f32), shape((rows, 2 * half)), shape((rows, width))]
    tall = (PADDED, width)
    own = [tall, mixed.shape, (width, width), (2, width, half), (2, half, width), tall]
    piece = shape((4, 4, DOWN_ROWS, 128))
    return pl.pallas_call(
        feed_forward, name="feed_forward",
        out_shape=outs + [piece, piece, shape((24, width), f32)],
        in_specs=[smem] + [hbm] * 6 + [vmem] * 2 + [hbm] * 2 + [vmem] * 6 + [hbm], out_specs=[hbm] * 7 + [vmem],
        scratch_shapes=[pltpu.VMEM(a, bf16) for a in own] + [pltpu.VMEM((PADDED, a.shape[1]), a.dtype) for a in outs]
        + [pltpu.VMEM((2, *piece.shape), bf16), pltpu.VMEM((PADDED, 2 * half), bf16)]
        + [pltpu.SemaphoreType.DMA((9,)), pltpu.SemaphoreType.DMA((6, 5)), pltpu.SemaphoreType.DMA((2,))],
        compiler_params=params(48), cost_estimate=cost(14e9, 20e6),
    )(sets, x, mixed, wo_a, wo_b, up_a, up_b, bu_a, bu_b, down_a, down_b, *vecs, cot)


def call_feed_backward(second, slope, hidden, resid, mixed, wo_a, wo_b, up_a, up_b, down_a, down_b, gain, sums):
    rows, width = second.shape
    half = up_a.shape[1]
    split = wo_a.shape[0]
    piece = shape((4, 4, FEED_ROWS, 128))
    outs = [shape((rows, width), f32), shape((2 * split, LANES)), shape((2 * split // 4, LANES))]
    given = [((PADDED, a.shape[1]), a.dtype) for a in (second, slope, hidden, resid)] + [(mixed.shape, bf16)]
    given += [((width, width), bf16), ((2, width, half), bf16), ((2, half, width), bf16)]
    return pl.pallas_call(
        feed_backward, name="feed_backward",
        out_shape=outs + [piece, piece],
        in_specs=[hbm] * 11 + [vmem] * 2, out_specs=[hbm] * 3 + [vmem] * 2,
        scratch_shapes=[pltpu.VMEM(*a) for a in given] + [pltpu.VMEM((PADDED, width), f32)] + [pltpu.VMEM(a.shape, a.dtype) for a in outs[1:]]
        + [
            pltpu.VMEM((PADDED, 2 * half), bf16), pltpu.VMEM((LANES, width), bf16),
            pltpu.VMEM((24, width), f32), pltpu.VMEM((8, 2 * half), f32),
        ]
        + [pltpu.SemaphoreType.DMA(a) for a in ((6, 3), (8,), (6, 1), (2,))],
        compiler_params=params(48), cost_estimate=cost(14e9, 20e6),
    )(second, slope, hidden, resid, mixed, wo_a, wo_b, up_a, up_b, down_a, down_b, gain, sums)


def call_backward(part, sets, q, k, v, grad, lse, delta, x):
    rows = q.shape[0] // 2
    big, more = (rows, LANES), (rows // 4, LANES)
    return pl.pallas_call(
        functools.partial(attend_backward, part), name="attend_backward",
        out_shape=[shape(big), shape(big), shape(big), shape((4, 4, HEAD_ROWS, 128))],
        in_specs=[smem] + [hbm] * 7, out_specs=[hbm] * 3 + [vmem],
        scratch_shapes=[pltpu.VMEM(a, bf16) for a in (big, big, big, big, more, more, x.shape, (3, *big), (x.shape[1], LANES))]
        + [
            pltpu.VMEM((CLASSES, LANES), bf16), pltpu.VMEM((CLASSES + 16, LANES), bf16),
            pltpu.VMEM((2, 896, 896), bf16), pltpu.VMEM((2, 896, 896), bf16),
            pltpu.VMEM((rows // 64, 64, LANES), f32), pltpu.VMEM((rows // 64, 64, LANES), f32),
        ]
        + [pltpu.SemaphoreType.DMA(a) for a in ((rows // 128, 6), (1,), (rows // 128, 3))],
        compiler_params=params(50), cost_estimate=cost(9e9, 6e6),
    )(sets, q, k, v, grad, lse, delta, x)


def call_project_input(own, other, wa, wb, resid):
    return pl.pallas_call(
        project_input, name="project_input", out_shape=shape(resid.shape, f32),
        scratch_shapes=[pltpu.VMEM((3, 2 * wa.shape[2], wa.shape[1]), bf16)],
        compiler_params=params(40), cost_estimate=cost(2.4e9, 12e6),
    )(*own, *other, wa, wb, resid)


def swap(array):
    return lax.ppermute(array, "mp", [(0, 1), (1, 0)])


def exchange(array, distance):
    count = lax.axis_size("dp")
    return lax.ppermute(array, "dp", [(i, i ^ distance) for i in range(count)])


def small(kernel, name, outs, scratch=()):
    moved = 2 * sum(o.size * o.dtype.itemsize for o in outs)
    return pl.pallas_call(
        kernel, name=name, out_shape=list(outs), scratch_shapes=list(scratch),
        compiler_params=params(24), cost_estimate=cost(1e6, moved),
    )


def after(array, *earlier):
    return lax.optimization_barrier((array, *earlier))[0]


def to_plane(parts):
    return [exchange(parts[xy], xy) for xy in (1, 2, 3)]


def to_line(parts):
    return [exchange(parts[z], 4 * z) for z in (1, 2, 3)]


def plane_sum(parts, came, *earlier):
    _, rows, lanes = parts[0].shape
    return small(add_four, "add_four", [shape((rows, lanes))] * 4)(after(parts[0], *earlier), *came)


def plane_sum_joined(feed, feed_came, down, down_came, *earlier):
    rows, lanes = feed[0].shape[1] + down[0].shape[1], feed[0].shape[2]
    return small(join_four, "join_four", [shape((rows, lanes))] * 4)(after(feed[0], *earlier), *feed_came, down[0], *down_came)


def line_sum(parts, came, *earlier):
    (total,) = small(add_four, "add_four", [shape(parts[0].shape)])(after(parts[0], *earlier), *came)
    distance = CHUNKS
    while distance < lax.axis_size("dp"):
        total = total + exchange(total, distance)
        distance *= 2
    return total


def line_copies(total):
    return [exchange(total, 4 * z) for z in (1, 2, 3)]


def laid(total, came, *earlier):
    (held,) = small(lay_four, "lay_four", [shape((4, *total.shape))])(after(total, *earlier), *came)
    return held


def plane_copies(held):
    return [exchange(held, xy) for xy in (1, 2, 3)]


def halves_added(mine, came, *earlier):
    return small(add_pair, "add_pair", [shape(mine.shape[1:])] * 4)(after(mine, *earlier), came)


def per_device(
    variates, dataset, w_qkv, b_qv, w_out, b_out, gain_one, shift_one, w_up, b_up, w_down, b_down, gain_two, shift_two, cotangent,
):
    width, half = w_up.shape
    other_qkv, other_bias = swap(w_qkv), swap(b_qv)
    other_out, other_up, other_bup, other_down = swap(w_out), swap(w_up), swap(b_up), swap(w_down)
    q, k, v, mixed, lse = call_forward(dataset, variates, w_qkv, other_qkv, b_qv, other_bias)
    out, hidden, resid, slope, second, down_mine, down_theirs, sums = call_feed_forward(
        dataset, variates, mixed, w_out, other_out, w_up, other_up, b_up, other_bup, w_down, other_down,
        (b_out, gain_one, shift_one, b_down, gain_two, shift_two), cotangent,
    )
    down = halves_added(down_mine, swap(down_theirs))
    down_came = to_plane(down)
    grad_res, grad_mix, delta, mine, theirs = call_feed_backward(
        after(second, *down), slope, hidden, resid, mixed, w_out, other_out, w_up, other_up, w_down, other_down, gain_one, sums
    )
    feed = halves_added(mine, swap(after(theirs, *down_came)))
    feed_came = to_plane(feed)
    *other, theirs = call_backward(1, dataset, q, k, v, after(grad_mix, *feed), lse, delta, variates)
    feed = plane_sum_joined(feed, feed_came, down, down_came, theirs)
    heads_came = swap(after(theirs, *feed))
    feed_came = to_line(feed)
    *own, mine = call_backward(0, dataset, q, k, v, after(grad_mix, heads_came, *feed), lse, delta, variates)
    total = line_sum(feed, feed_came, mine)
    heads = halves_added(mine, heads_came, total)
    heads_plane = to_plane(heads)
    feed_came = line_copies(total)
    grad_in = call_project_input(own, other, w_qkv, other_qkv, after(grad_res, total, *heads))
    held = laid(total, feed_came, grad_in)
    heads = plane_sum(heads, heads_plane, grad_in)
    feed = [held, *plane_copies(after(held, *heads))]
    heads = line_sum(heads, to_line(heads))
    heads = laid(heads, line_copies(heads))
    heads = [heads, *plane_copies(heads)]
    vector = shape((width,), f32)
    outs = [shape((width, half), f32), shape(w_out.shape, f32)] + [vector] * 6 + [shape((half,), f32), shape(w_down.shape, f32)]
    keep = [pltpu.VMEM((CHUNKS, 16, 128), f32)]
    grad_up, grad_out, two_gain, two_shift, down_bias, one_gain, one_shift, out_bias, up_bias, grad_down = small(
        spread_feed, "spread_feed", outs, keep
    )(*feed)
    grad_qkv, bias = small(spread_heads, "spread_heads", [shape(w_qkv.shape, f32), shape(b_qv.shape, f32)], keep)(*heads)
    return (
        out, grad_in, grad_qkv, bias, grad_out, out_bias, one_gain, one_shift, grad_up, up_bias,
        grad_down, down_bias, two_gain, two_shift,
    )


def solution(mesh):
    wide = P(("dp", "mp"), None)
    weights = (P(None, None, "mp"), P(None, "mp"), P("mp", None))
    placed = (wide, P("dp"), *weights, P(), P(), P(), P(None, "mp"), P("mp"), P("mp", None), P(), P(), P(), wide)
    given = (wide, wide, *weights, P(), P(), P(), P(None, "mp"), P("mp"), P("mp", None), P(), P(), P())
    return jax.shard_map(per_device, mesh=mesh, in_specs=placed, out_specs=given, check_vma=False)
```

```python
import functools

import jax
import jax.numpy as jnp
from jax import lax
from jax.experimental import pallas as pl
from jax.experimental.pallas import tpu as pltpu
from jax.sharding import PartitionSpec as P

HEAD_DIM = 64
SLOTS = 1424
WIDTHS = (7, 21, 321, 862)
LANES = 1536
CLASSES = 80
BIG = 1e30
EPS = 1e-05
MIB = 2**20

bf16 = jnp.bfloat16
f32 = jnp.float32


def mul(left, right, left_dim=1, right_dim=0):
    return lax.dot_general(
        left, right, (((left_dim,), (right_dim,)), ((), ())), preferred_element_type=f32
    )


def params(limit):
    return pltpu.CompilerParams(vmem_limit_bytes=limit * MIB)


def cover(width, start, stop, last):
    used = SLOTS // width * width
    low = start // width * width
    high = last if stop > used else -(-stop // width) * width
    return (low // 128 * 128, min(-(-min(high, last) // 128) * 128, LANES))


def groups_of(width, rows, step):
    found = []
    for start in range(0, rows, step):
        low, high = cover(width, start, min(start + step, rows), rows)
        if found and found[-1][2] == low and found[-1][2] + found[-1][3] == high:
            first, count = found[-1][:2]
            found[-1] = (first, count + step, low, high - low)
        else:
            found.append((start, step, low, high - low))
    return found


def near(tile):
    return jnp.clip(tile * 256 - 128, 0, LANES - 512)


def middle(tile):
    return jnp.where(tile < 2, 0, jnp.where(tile == 2, 256, jnp.where(tile == 3, 640, 768)))


FORWARD = (
    [(0, 6, 512, near, 8)],
    [(0, 6, 768, middle, 8)],
    [(0, 3, 896, lambda tile: 0 * tile, 8), (3, 4, 1536, lambda tile: 0 * tile, 2), (4, 6, 768, lambda tile: 0 * tile + 768, 8)],
    [(0, 6, 512, near, 1)],
    [(0, 6, LANES, lambda tile: 0 * tile, 1)],
)
BACKWARD = (
    [],
    groups_of(WIDTHS[2], SLOTS // WIDTHS[2] * WIDTHS[2], 128),
    [(0, 896, 0, 896)],
)


def own_bucket(sets_ref):
    return sets_ref[lax.axis_index("mp")]


def token_class(width):
    token = lax.broadcasted_iota(jnp.int32, (CLASSES, LANES), 1)
    numbers = token.astype(f32)
    held = jnp.floor((numbers + 0.5) * (1.0 / width)).astype(jnp.int32)
    held = jnp.where(token < SLOTS, held, (SLOTS - 1) // width + 1)
    row = lax.broadcasted_iota(jnp.int32, (CLASSES, LANES), 0)
    return held % CLASSES == row


def write_masks(bucket, hot_ref, bar_ref):
    for number, width in enumerate(WIDTHS):

        @pl.when(bucket == number)
        def _():
            same = token_class(width)
            hot_ref[...] = jnp.where(same, 1.0, 0.0).astype(bf16)
            bar_ref[:CLASSES, :] = jnp.where(same, 0.0, -BIG).astype(bf16)

    row = lax.broadcasted_iota(jnp.int32, (16, LANES), 0)
    bar_ref[CLASSES:, :] = jnp.where(row < 3, 1.0, 0.0).astype(bf16)


def split_three(row):
    high = row.astype(bf16)
    rest = row - high.astype(f32)
    middle = rest.astype(bf16)
    low = (rest - middle.astype(f32)).astype(bf16)
    return high, middle, low


def extra_rows(row):
    parts = [p.astype(f32) for p in split_three(row)]
    number = lax.broadcasted_iota(jnp.int32, (16, row.shape[1]), 0)
    held = jnp.where(number == 0, parts[0], jnp.where(number == 1, parts[1], jnp.where(number == 2, parts[2], 0.0)))
    return held.astype(bf16)


LOG_E = 1.4426950408889634
SAFE = 60.0


def attend_forward(
    sets_ref, x_hbm, wa_hbm, wb_ref, ba_ref, bb_ref, q_hbm, k_hbm, v_hbm, o_hbm, lse_hbm,
    x_ref, wa_ref, q_ref, k_ref, v_ref, o_ref, lse_ref, xt_ref, hot_ref, bar_ref, in_sems, out_sems,
):
    loads = [pltpu.make_async_copy(*pair, in_sems.at[i]) for i, pair in enumerate(((x_hbm, x_ref), (wa_hbm, wa_ref)))]
    for load in loads:
        load.start()
    pairs = ((q_ref, q_hbm), (k_ref, k_hbm), (v_ref, v_hbm), (o_ref, o_hbm), (lse_ref, lse_hbm))
    stores = [pltpu.make_async_copy(*pair, out_sems.at[i]) for i, pair in enumerate(pairs)]
    bucket = own_bucket(sets_ref)
    write_masks(bucket, hot_ref, bar_ref)
    tail = jnp.zeros((LANES - SLOTS, x_ref.shape[1]), bf16)
    loads[0].wait()
    xt_ref[...] = jnp.concatenate([x_ref[...], tail], axis=0).T
    worst = None
    for side, (w_ref, b_ref) in enumerate(((wa_ref, ba_ref), (wb_ref, bb_ref))):
        if side == 0:
            loads[1].wait()
        for kind, out_ref in enumerate((q_ref, k_ref, v_ref)):
            weight = w_ref[kind].T
            rows = weight.shape[0]
            if kind != 1:
                row = b_ref[kind // 2 : kind // 2 + 1, :].astype(f32)
                column = jnp.broadcast_to(row, (128, rows)).T
                column = jnp.concatenate([column] * 4, axis=1)

            def project(number, carry):
                lanes = slice(number * 512, number * 512 + 512)
                part = mul(weight, xt_ref[:, lanes])
                if kind != 1:
                    part = part + column
                if kind == 0:
                    part = part * 0.125
                out_ref[side * rows : (side + 1) * rows, lanes] = part.astype(bf16)
                return carry

            for number in range(LANES // 512):
                project(number, 0)
    for store in stores[:3]:
        store.start()
    heads = q_ref.shape[0] // 64
    for head in range(heads):
        norms = []
        for ref in (q_ref, k_ref):
            held = ref[head * 64 : head * 64 + 64, :].astype(f32)
            norms.append(jnp.max(jnp.sum(held * held, axis=0, keepdims=True), axis=1, keepdims=True))
        both = norms[0] * norms[1]
        worst = both if worst is None else jnp.maximum(worst, both)
    calm = worst[0, 0] < SAFE * SAFE

    def score(head, start, first, span):
        rows = pl.ds(pl.multiple_of(head * 64, 64), 64)
        lanes, span = pl.ds(start, 256), pl.ds(first, span)
        keys = jnp.concatenate([k_ref[rows, span], bar_ref[:CLASSES, span]], axis=0)
        quer = jnp.concatenate([q_ref[rows, lanes], hot_ref[:, lanes]], axis=0)
        return mul(keys, quer, 0, 0)

    def finish(head, start, first, span, scores, plain):
        rows = pl.ds(pl.multiple_of(head * 64, 64), 64)
        lanes = pl.ds(start, 256)
        if plain:
            raised = jnp.exp2(scores * LOG_E).astype(bf16)
        else:
            top = jnp.max(scores, axis=0, keepdims=True)
            raised = jnp.exp(scores - top).astype(bf16)
        vals = jnp.concatenate([v_ref[rows, pl.ds(first, span)], jnp.ones((16, span), bf16)], axis=0)
        total = mul(vals, raised)
        sums = total[64:65, :]
        o_ref[rows, lanes] = (total[:64, :] * (1.0 / sums)).astype(bf16)
        logs = jnp.log(sums)
        if not plain:
            logs = logs + top
        lse_ref[pl.ds(pl.multiple_of(head * 16, 16), 16), lanes] = extra_rows(-logs)

    def over(begin, end, span, first_of, together, plain):
        def turn(number, carry):
            tile = begin + number % (end - begin)
            start = pl.multiple_of(tile * 256, 256)
            first = pl.multiple_of(first_of(tile), 128)
            own = [number // (end - begin) * together + i for i in range(together)]
            held = [score(head, start, first, span) for head in own]
            for head, scores in zip(own, held):
                finish(head, start, first, span, scores, plain)
            return carry

        lax.fori_loop(0, heads // together * (end - begin), turn, 0)

    for group in range(5):
        plain = group < 3
        chosen = (bucket < 2, bucket == 2, bucket == 3, bucket < 2, bucket >= 2)[group]

        @pl.when(jnp.logical_and(chosen, calm == plain))
        def _():
            for begin, end, span, first_of, together in FORWARD[group]:
                over(begin, end, span, first_of, together, plain)

    for store in stores[3:]:
        store.start()
    for store in stores:
        store.wait()


def copies(pairs, sems):
    return [pltpu.make_async_copy(*pair, sems.at[i]) for i, pair in enumerate(pairs)]


def attend_backward(
    part, sets_ref, q_hbm, k_hbm, v_hbm, g_hbm, lse_hbm, delta_hbm, x_hbm, dq_hbm, dk_hbm, dv_hbm, piece_ref,
    q_ref, k_ref, v_ref, g_ref, lse_ref, delta_ref, x_ref, grads_ref, xt_ref,
    hot_ref, bar_ref, p_ref, s_ref, ka_ref, va_ref, head_sems, in_sems, out_sems,
):
    half = q_ref.shape[0]
    dq_ref, dk_ref, dv_ref = (grads_ref.at[kind] for kind in range(3))

    def loads_of(number):
        there = pl.ds(part * half + number * 128, 128)
        here = pl.ds(number * 128, 128)
        pairs = [(far.at[there], near.at[here]) for far, near in ((q_hbm, q_ref), (k_hbm, k_ref), (v_hbm, v_ref), (g_hbm, g_ref))]
        there = pl.ds(part * (half // 4) + number * 32, 32)
        here = pl.ds(number * 32, 32)
        pairs += [(far.at[there], near.at[here]) for far, near in ((lse_hbm, lse_ref), (delta_hbm, delta_ref))]
        return copies(pairs, head_sems.at[number])

    def stores_of(number):
        here = pl.ds(number * 128, 128)
        return copies([(near.at[here], far.at[here]) for near, far in ((dq_ref, dq_hbm), (dk_ref, dk_hbm), (dv_ref, dv_hbm))], out_sems.at[number])

    for number in range(half // 128):
        for load in loads_of(number):
            load.start()
    given = copies([(x_hbm, x_ref)], in_sems)[0]
    bucket = own_bucket(sets_ref)
    write_masks(bucket, hot_ref, bar_ref)

    def one_head(head, groups, slot):
        rows = pl.ds(pl.multiple_of(head * 64, 64), 64)
        more = pl.ds(pl.multiple_of(head * 16, 16), 16)
        single = len(groups) == 1
        if not single:
            ka_ref[slot] = jnp.zeros(ka_ref.shape[1:], f32)
            va_ref[slot] = jnp.zeros(va_ref.shape[1:], f32)
        for q0, nq, k0, nk in groups:
            span = slice(k0, k0 + nk)
            held = slice(q0, q0 + nq)
            keys = jnp.concatenate([k_ref[rows, span], bar_ref[:, span]], axis=0)
            vals = jnp.concatenate([v_ref[rows, span], bar_ref[CLASSES:, span]], axis=0)
            for start in range(q0, q0 + nq, 256):
                size = min(256, q0 + nq - start)
                lanes = slice(start, start + size)
                quer = jnp.concatenate([q_ref[rows, lanes], hot_ref[:, lanes], lse_ref[more, lanes]], axis=0)
                grad = jnp.concatenate([g_ref[rows, lanes], delta_ref[more, lanes]], axis=0)
                probs = jnp.exp2(mul(quer, keys, 0, 0) * LOG_E)
                slopes = probs * mul(grad, vals, 0, 0)
                p_ref[slot, start - q0 : start - q0 + size, :nk] = probs.astype(bf16)
                s_ref[slot, start - q0 : start - q0 + size, :nk] = slopes.astype(bf16)
            dv = mul(g_ref[rows, held], p_ref[slot, :nq, :nk])
            dk = mul(q_ref[rows, held], s_ref[slot, :nq, :nk])
            dq = mul(k_ref[rows, span], s_ref[slot, :nq, :nk], 1, 1)
            dq_ref[rows, held] = (dq * 0.125).astype(bf16)
            if single:
                dv_ref[rows, span] = dv.astype(bf16)
                dk_ref[rows, span] = dk.astype(bf16)
            else:
                va_ref[slot, :, span] += dv
                ka_ref[slot, :, span] += dk
        if single:
            rest = LANES - 896
            for out in (dq_ref, dk_ref, dv_ref):
                out[rows, 896:] = jnp.zeros((64, rest), bf16)
        else:
            dv_ref[rows, :] = va_ref[slot].astype(bf16)
            dk_ref[rows, :] = ka_ref[slot].astype(bf16)
            done = groups[-1][0] + groups[-1][1]
            if done < LANES:
                dq_ref[rows, done:] = jnp.zeros((64, LANES - done), bf16)

    def tile_of(head, start, first, span):
        rows = pl.ds(head * 64, 64)
        more = pl.ds(head * 16, 16)
        lanes, span = pl.ds(start, 256), pl.ds(first, span)
        keys = jnp.concatenate([k_ref[rows, span], bar_ref[:, span]], axis=0)
        vals = jnp.concatenate([v_ref[rows, span], bar_ref[CLASSES:, span]], axis=0)
        quer = jnp.concatenate([q_ref[rows, lanes], hot_ref[:, lanes], lse_ref[more, lanes]], axis=0)
        grad = jnp.concatenate([g_ref[rows, lanes], delta_ref[more, lanes]], axis=0)
        probs = jnp.exp2(mul(quer, keys, 0, 0) * LOG_E)
        slopes = (probs * mul(grad, vals, 0, 0)).astype(bf16)
        return probs.astype(bf16), slopes

    def take(head, start, first, span, probs, slopes):
        rows = pl.ds(head * 64, 64)
        lanes, span = pl.ds(start, 256), pl.ds(first, span)
        va_ref[head, :, span] += mul(g_ref[rows, lanes], probs)
        ka_ref[head, :, span] += mul(q_ref[rows, lanes], slopes)
        dq_ref[rows, lanes] = (mul(k_ref[rows, span], slopes, 1, 1) * 0.125).astype(bf16)

    def by_tiles(span, first_of, together):
        for number in range(half // 128):
            for load in loads_of(number):
                load.wait()
        given.start()
        ka_ref[...] = jnp.zeros_like(ka_ref)
        va_ref[...] = jnp.zeros_like(va_ref)

        def turn(tile, carry):
            start = pl.multiple_of(tile * 256, 256)
            first = pl.multiple_of(first_of(tile), 128)
            for base in range(0, half // 64, together):
                own = range(base, base + together)
                held = [tile_of(head, start, first, span) for head in own]
                for head, (probs, slopes) in zip(own, held):
                    take(head, start, first, span, probs, slopes)
            return carry

        lax.fori_loop(0, 6, turn, 0)
        for head in range(half // 64):
            rows = pl.ds(head * 64, 64)
            dv_ref[rows, :] = va_ref[head].astype(bf16)
            dk_ref[rows, :] = ka_ref[head].astype(bf16)
        for number in range(half // 128):
            for store in stores_of(number):
                store.start()

    for group in range(3):
        chosen = (bucket < 2, bucket == 2, bucket == 3)[group]

        @pl.when(chosen)
        def _():
            if group == 0:
                by_tiles(512, near, 4)
            else:

                def pair(number, carry):
                    for load in loads_of(number):
                        load.wait()

                    @pl.when(number == 0)
                    def _():
                        given.start()

                    one_head(2 * number, BACKWARD[group], 0)
                    one_head(2 * number + 1, BACKWARD[group], 1)
                    for store in stores_of(number):
                        store.start()
                    return carry

                lax.fori_loop(0, half // 128, pair, 0)

    given.wait()
    width = x_ref.shape[1]
    tail = jnp.zeros((LANES - SLOTS, width), bf16)
    xt_ref[...] = jnp.concatenate([x_ref[...], tail], axis=0).T
    tall = width // CHUNKS
    ones = jnp.ones((8, LANES), bf16)
    place_of = slots()
    sums = []
    blocks = half // 128

    def product_of(kind, carry):
        product = mul(xt_ref[...], grads_ref[kind], 1, 1).astype(bf16)
        for chunk in range(CHUNKS):
            xy, z = place_of(chunk)
            for block in range(blocks):
                row = (kind * blocks + block) * tall
                piece_ref[xy, z, pl.ds(row, tall), :] = product[chunk * tall : (chunk + 1) * tall, block * 128 : block * 128 + 128]
        return carry

    for kind in range(3):
        product_of(kind, 0)
    for d_ref in (dq_ref, dv_ref):
        total = mul(ones, d_ref[...], 1, 1)[:1]
        sums += [total[:, block * 128 : block * 128 + 128] for block in range(blocks)]
    number = lax.broadcasted_iota(jnp.int32, (16, 128), 0)
    for chunk in range(CHUNKS):
        xy, z = place_of(chunk)
        held = jnp.where(number == 0, sums[chunk] if chunk < len(sums) else 0.0, 0.0)
        piece_ref[xy, z, HEAD_ROWS - 16 :, :] = held.astype(bf16)
    for number in range(half // 128):
        for store in stores_of(number):
            store.wait()


TILE = 240
TILES = 6
PADDED = TILE * TILES
LAST = SLOTS - TILE * (TILES - 1)


def over_tiles(step):
    def body(number, carry):
        step(number, pl.multiple_of(number * TILE, TILE))
        return carry

    lax.fori_loop(0, TILES, body, 0)


def rows_moved(number, start, begin):
    if isinstance(number, int):
        begin(start, LAST if number == TILES - 1 else TILE)
        return

    @pl.when(number < TILES - 1)
    def _():
        begin(start, TILE)

    @pl.when(number == TILES - 1)
    def _():
        begin(TILE * (TILES - 1), LAST)


def mean_of(matrix):
    return jnp.sum(matrix, axis=1, keepdims=True) * (1.0 / matrix.shape[1])


def norm_parts(matrix):
    centre = matrix - mean_of(matrix)
    spread = lax.rsqrt(mean_of(centre * centre) + EPS)
    return centre * spread, spread


def norm_back(scaled, normed, spread):
    return spread * (scaled - mean_of(scaled) - normed * mean_of(scaled * normed))


def fold(matrix):
    return jnp.sum(matrix.reshape(matrix.shape[0] // 8, 8, matrix.shape[1]), axis=0)


def gelu_parts(pre):
    size = jnp.abs(pre)
    t = pl.reciprocal(1.0 + (0.3275911 * 2.0**-0.5) * size)
    bell = jnp.exp2((-0.5 * LOG_E) * (pre * pre))
    poly = 0.5 * 1.061405429
    for factor in (-1.453152027, 1.421413741, -0.284496736, 0.254829592):
        poly = poly * t + 0.5 * factor
    tail = poly * t * bell
    phi = jnp.where(pre > 0, 1.0 - tail, tail)
    return pre * phi, phi + pre * (bell * (2.0 * jnp.pi) ** -0.5)


HIDDEN_STEP = 512


def row_of(ref):
    return ref[...].astype(f32).reshape(1, ref.shape[0])


def feed_forward(
    sets_ref, x_hbm, o_hbm, wo_a, wo_b, ua_hbm, ub_hbm, ba_ref, bb_ref, da_hbm, db_hbm,
    bo_ref, g1_ref, s1_ref, bd_ref, g2_ref, s2_ref, cot_hbm,
    out_hbm, hid_hbm, res_hbm, slope_hbm, sec_hbm, gd_a, gd_b, sums_ref,
    x_ref, o_ref, wo_ref, u_ref, d_ref, cot_ref, out_ref, hid_ref, res_ref, slope_ref, low_ref, gd_ref, act_ref,
    in_sems, row_sems, out_sems,
):
    half = ua_hbm.shape[1]
    split = wo_a.shape[0]
    width = x_ref.shape[1]
    true = pl.ds(0, SLOTS)
    pairs = [(o_hbm, o_ref), (wo_a, wo_ref.at[pl.ds(0, split)]), (wo_b, wo_ref.at[pl.ds(split, split)]), (x_hbm, x_ref.at[true])]
    pairs += [(ua_hbm, u_ref.at[0]), (ub_hbm, u_ref.at[1]), (da_hbm, d_ref.at[0]), (db_hbm, d_ref.at[1]), (cot_hbm, cot_ref.at[true])]
    loads = copies(pairs, in_sems)
    for load in loads:
        load.start()
    for ref in (x_ref, cot_ref):
        ref[SLOTS:, :] = jnp.zeros((PADDED - SLOTS, width), bf16)
    bucket = own_bucket(sets_ref)
    used = SLOTS // WIDTHS[3] * WIDTHS[3]
    for number in range(3):
        used = jnp.where(bucket == number, SLOTS // WIDTHS[number] * WIDTHS[number], used)
    sums_ref[...] = jnp.zeros_like(sums_ref)
    b_out, gain_one, shift_one, b_down, gain_two, shift_two = (
        row_of(ref) for ref in (bo_ref, g1_ref, s1_ref, bd_ref, g2_ref, s2_ref)
    )
    b_up = [row_of(ref) for ref in (ba_ref, bb_ref)]
    places = [(side, at) for side in range(2) for at in range(0, half, HIDDEN_STEP)]
    last = copies([(gd_ref.at[0], gd_a), (gd_ref.at[1], gd_b)], out_sems)

    def stores_of(number, start, size):
        rows = pl.ds(start, size)
        pairs = ((out_ref, out_hbm), (hid_ref, hid_hbm), (res_ref, res_hbm), (slope_ref, slope_hbm), (low_ref, sec_hbm))
        return copies([(near.at[rows], far.at[rows]) for near, far in pairs], row_sems.at[number])

    def step(number, start):
        rows = pl.ds(start, TILE)
        resid = res_ref[rows, :] + x_ref[rows, :].astype(f32) + b_out
        res_ref[rows, :] = resid
        normed, _ = norm_parts(resid)
        hidden = normed * gain_one + shift_one
        low = hidden.astype(bf16)
        hid_ref[rows, :] = low

        @pl.when(number == 0)
        def _():
            for load in loads[4:]:
                load.wait()

        def lift(side, at):
            return mul(low, u_ref[side, :, at : at + HIDDEN_STEP]) + b_up[side][:, at : at + HIDDEN_STEP]

        total = None
        ahead = lift(*places[0])
        for turn, (side, at) in enumerate(places):
            pre = ahead
            if turn + 1 < len(places):
                ahead = lift(*places[turn + 1])
            place = slice(side * half + at, side * half + at + HIDDEN_STEP)
            active, slope = gelu_parts(pre)
            active = active.astype(bf16)
            act_ref[rows, place] = active
            slope_ref[rows, place] = slope.astype(bf16)
            part = mul(active, d_ref[side, at : at + HIDDEN_STEP, :])
            total = part if total is None else total + part
        second = hidden + total + b_down
        normed, spread = norm_parts(second)
        out_ref[rows, :] = (normed * gain_two + shift_two).astype(bf16)
        row = start + lax.broadcasted_iota(jnp.int32, (TILE, width), 0)
        top = jnp.where(row < used, cot_ref[rows, :].astype(f32), 0.0)
        grad = norm_back(top * gain_two, normed, spread)
        low_ref[rows, :] = grad.astype(bf16)
        sums_ref[0:8, :] += fold(top * normed)
        sums_ref[8:16, :] += fold(top)
        sums_ref[16:24, :] += fold(grad)
        rows_moved(number, start, lambda at, size: [store.start() for store in stores_of(number, at, size)])

    for load in loads[:4]:
        load.wait()
    for start in range(0, PADDED, 512):
        size = min(512, PADDED - start)
        res_ref[start : start + size, :] = mul(o_ref[:, start : start + 512], wo_ref[...], 0, 0)[:size]
    over_tiles(step)
    place_of = slots()
    tall = half // CHUNKS

    def block_of(number, carry):
        side, block = number // 4, number % 4
        part = mul(act_ref[:, pl.ds(pl.multiple_of(number * 4 * tall, 4 * tall), 4 * tall)], low_ref[...], 0, 0).astype(bf16)
        for z in range(4):
            xy, z_place = place_of(z * 4 + block)
            for lane in range(width // 128):
                gd_ref[side, xy, z_place, lane * tall : (lane + 1) * tall, :] = part[z * tall : (z + 1) * tall, lane * 128 : lane * 128 + 128]

        @pl.when(number == 3)
        def _():
            last[0].start()

        return carry

    lax.fori_loop(0, 8, block_of, 0)
    last[1].start()
    for number in range(TILES):
        rows_moved(number, number * TILE, lambda at, size: [store.wait() for store in stores_of(number, at, size)])
    for store in last:
        store.wait()


CHUNKS = 16
FEED_ROWS = 336
DOWN_ROWS = 256
HEAD_ROWS = 208


def slots():
    own = lax.axis_index("dp") % CHUNKS

    def place(chunk):
        held = chunk ^ own
        return held % 4, held // 4

    return place


def feed_backward(
    sec_hbm, slope_hbm, hid_hbm, res_hbm, o_hbm, wo_a, wo_b, ua_hbm, ub_hbm, da_hbm, db_hbm, g1_ref, two_ref,
    gr_hbm, g_hbm, delta_hbm, mine_ref, theirs_ref,
    sec_ref, slope_ref, hid_ref, res_ref, o_ref, wo_ref, u_ref, d_ref, gr_ref, g_ref, delta_ref,
    pre_ref, mix_ref, sums_ref, bup_ref, row_in, in_sems, row_out, out_sems,
):
    half = ua_hbm.shape[1]
    width = hid_ref.shape[1]
    split = wo_a.shape[0]

    def loads_of(number, start, size):
        rows = pl.ds(start, size)
        pairs = ((sec_hbm, sec_ref), (slope_hbm, slope_ref), (res_hbm, res_ref))
        return copies([(far.at[rows], near.at[rows]) for far, near in pairs], row_in.at[number])

    def stores_of(number, start, size):
        rows = pl.ds(start, size)
        return copies([(gr_ref.at[rows], gr_hbm.at[rows])], row_out.at[number])

    pairs = [(da_hbm, d_ref.at[0]), (db_hbm, d_ref.at[1]), (ua_hbm, u_ref.at[0]), (ub_hbm, u_ref.at[1])]
    pairs += [(hid_hbm, hid_ref.at[pl.ds(0, SLOTS)]), (o_hbm, o_ref), (wo_a, wo_ref.at[pl.ds(0, split)]), (wo_b, wo_ref.at[pl.ds(split, split)])]
    loads = copies(pairs, in_sems)
    for load in loads_of(0, 0, TILE) + loads[:4]:
        load.start()
    for ref in (sec_ref, slope_ref, res_ref, hid_ref):
        ref[SLOTS:, :] = jnp.zeros((PADDED - SLOTS, ref.shape[1]), ref.dtype)
    sums_ref[...] = jnp.zeros_like(sums_ref)
    bup_ref[...] = jnp.zeros_like(bup_ref)
    gain_one = row_of(g1_ref)
    mix_ref[PADDED:, :] = jnp.zeros((LANES - PADDED, width), bf16)
    place_of = slots()
    places = [(side, at) for side in range(2) for at in range(0, half, HIDDEN_STEP)]

    def step(number, start):
        @pl.when(number < TILES - 1)
        def _():
            rows_moved(number + 1, start + TILE, lambda at, size: [load.start() for load in loads_of(number + 1, at, size)])

        @pl.when(number == TILES - 2)
        def _():
            for load in loads[4:]:
                load.start()

        rows_moved(number, start, lambda at, size: [load.wait() for load in loads_of(number, at, size)])

        @pl.when(number == 0)
        def _():
            for load in loads[:4]:
                load.wait()

        rows = pl.ds(start, TILE)
        low = sec_ref[rows, :]
        second = low.astype(f32)

        def sink(side, at):
            return mul(low, d_ref[side, at : at + HIDDEN_STEP, :], 1, 1)

        total = None
        ahead = sink(*places[0])
        for turn, (side, at) in enumerate(places):
            inner = ahead
            if turn + 1 < len(places):
                ahead = sink(*places[turn + 1])
            place = slice(side * half + at, side * half + at + HIDDEN_STEP)
            pre = (inner * slope_ref[rows, place].astype(f32)).astype(bf16)
            pre_ref[rows, place] = pre
            bup_ref[:, place] += fold(pre.astype(f32))
            part = mul(pre, u_ref[side, :, at : at + HIDDEN_STEP], 1, 1)
            total = part if total is None else total + part
        hidden = second + total
        normed, spread = norm_parts(res_ref[rows, :])
        grad = norm_back(hidden * gain_one, normed, spread)
        gr_ref[rows, :] = grad
        mix_ref[rows, :] = grad.astype(bf16)
        sums_ref[0:8, :] += fold(hidden * normed)
        sums_ref[8:16, :] += fold(hidden)
        sums_ref[16:24, :] += fold(grad)
        rows_moved(number, start, lambda at, size: [store.start() for store in stores_of(number, at, size)])

    over_tiles(step)
    for load in loads[4:]:
        load.wait()
    last = copies([(g_ref, g_hbm), (delta_ref, delta_hbm)], out_sems)

    def mixed_grad(number, carry):
        side = number // 3
        place = slice(side * split, (side + 1) * split)
        lanes = slice(number % 3 * 512, number % 3 * 512 + 512)
        grad = mul(wo_ref[place, :], mix_ref[lanes, :], 1, 1).astype(bf16)
        g_ref[place, lanes] = grad
        prod = grad.astype(f32) * o_ref[place, lanes].astype(f32)
        for head in range(split // 64):
            at = (side * (split // 64) + head) * 16
            delta = jnp.sum(prod[head * 64 : head * 64 + 64], axis=0, keepdims=True)
            delta_ref[pl.ds(at, 16), lanes] = extra_rows(-delta)
        return carry

    for number in range(6):
        mixed_grad(number, 0)
    for store in last:
        store.start()
    tall = width // CHUNKS
    low = split // CHUNKS
    for side, out in enumerate((mine_ref, theirs_ref)):

        def up_block(number, carry):
            at = side * half + number * 256
            part = mul(hid_ref[...], pre_ref[:, pl.ds(at, 256)], 0, 0).astype(bf16)
            for chunk in range(CHUNKS):
                xy, z = place_of(chunk)
                for block in range(2):
                    row = (2 * number + block) * tall
                    out[xy, z, pl.ds(row, tall), :] = part[chunk * tall : (chunk + 1) * tall, block * 128 : block * 128 + 128]
            return carry

        for number in range(half // 256):
            up_block(number, 0)
        part = mul(o_ref[side * split : (side + 1) * split, :], mix_ref[...]).astype(bf16)
        for chunk in range(CHUNKS):
            xy, z = place_of(chunk)
            for block in range(width // 128):
                row = half // 128 * tall + block * low
                out[xy, z, row : row + low, :] = part[chunk * low : (chunk + 1) * low, block * 128 : block * 128 + 128]
    vectors = []
    for ref in (two_ref, sums_ref):
        for kind in range(3):
            total = jnp.sum(ref[8 * kind : 8 * kind + 8, :], axis=0, keepdims=True)
            vectors += [total[:, at : at + 128] for at in range(0, width, 128)]
    number = lax.broadcasted_iota(jnp.int32, (16, 128), 0)
    for side, out in enumerate((mine_ref, theirs_ref)):
        total = jnp.sum(bup_ref[:, side * half : (side + 1) * half], axis=0, keepdims=True)
        held = vectors + [total[:, at : at + 128] for at in range(0, half, 128)]
        each = len(held) // CHUNKS
        for chunk in range(CHUNKS):
            xy, z = place_of(chunk)
            block = jnp.zeros((16, 128), f32)
            for row in range(each):
                block = jnp.where(number == row, held[chunk * each + row], block)
            out[xy, z, FEED_ROWS - 16 :, :] = block.astype(bf16)
    for number in range(TILES):
        rows_moved(number, number * TILE, lambda at, size: [store.wait() for store in stores_of(number, at, size)])
    for store in last:
        store.wait()


def project_input(dqa_ref, dka_ref, dva_ref, dqb_ref, dkb_ref, dvb_ref, wa_ref, wb_ref, gr_ref, gi_ref, wt_ref):
    rows = wa_ref.shape[2]
    for side, w_ref in enumerate((wa_ref, wb_ref)):
        for kind in range(3):
            wt_ref[kind, side * rows : (side + 1) * rows, :] = w_ref[kind].T
    for start in range(0, SLOTS, 256):
        size = min(256, SLOTS - start)
        lanes = slice(start, start + 256)
        total = gr_ref[start : start + size, :]
        for side, refs in enumerate(((dqa_ref, dka_ref, dva_ref), (dqb_ref, dkb_ref, dvb_ref))):
            for kind, d_ref in enumerate(refs):
                total = total + mul(d_ref[:, lanes], wt_ref[kind, side * rows : (side + 1) * rows, :], 0, 0)[:size]
        gi_ref[start : start + size, :] = total


def add_pair(mine_ref, theirs_ref, *outs):
    for number, out in enumerate(outs):
        out[...] = (mine_ref[number].astype(f32) + theirs_ref[number].astype(f32)).astype(bf16)


def add_four(a_ref, b_ref, c_ref, d_ref, *outs):
    for number, out in enumerate(outs):
        held = slice(None) if len(outs) == 1 else number
        low = a_ref[held].astype(f32) + b_ref[held].astype(f32)
        out[...] = (low + (c_ref[held].astype(f32) + d_ref[held].astype(f32))).astype(bf16)


def join_four(*refs):
    first, second, outs = refs[:4], refs[4:8], refs[8:]
    for z, out in enumerate(outs):
        at = 0
        for a_ref, b_ref, c_ref, d_ref in (first, second):
            rows = a_ref.shape[1]
            low = a_ref[z].astype(f32) + b_ref[z].astype(f32)
            out[at : at + rows, :] = (low + (c_ref[z].astype(f32) + d_ref[z].astype(f32))).astype(bf16)
            at += rows


def lay_four(a_ref, b_ref, c_ref, d_ref, out_ref):
    for number, ref in enumerate((a_ref, b_ref, c_ref, d_ref)):
        out_ref[number] = ref[...]


def each_chunk(refs):
    own = lax.axis_index("dp") % CHUNKS
    for xy in range(4):
        for z in range(4):
            parts = [ref[z] for ref in (refs[3:] if xy == 3 else refs[xy : xy + 1])]
            yield (z * 4 + xy) ^ own, jnp.concatenate(parts, axis=0).astype(f32)


def spread_feed(
    a_ref, b_ref, c_ref, d_ref, e_ref, up_ref, out_ref, g2_ref, s2_ref, bd_ref, g1_ref, s1_ref, bo_ref, bup_ref, down_ref, keep_ref,
):
    width, half = up_ref.shape
    tall, low = width // CHUNKS, out_ref.shape[0] // CHUNKS
    deep = half // CHUNKS
    for chunk, held in each_chunk((a_ref, b_ref, c_ref, d_ref, e_ref)):
        rows = pl.ds(pl.multiple_of(chunk * tall, tall), tall)
        for block in range(half // 128):
            up_ref[rows, block * 128 : block * 128 + 128] = held[block * tall : (block + 1) * tall]
        rows = pl.ds(pl.multiple_of(chunk * low, low), low)
        base = half // 128 * tall
        for block in range(width // 128):
            out_ref[rows, block * 128 : block * 128 + 128] = held[base + block * low : base + (block + 1) * low]
        keep_ref[chunk] = held[FEED_ROWS - 16 : FEED_ROWS]
        rows = pl.ds(pl.multiple_of((chunk % 4 * 4 + chunk // 4) * deep, deep), deep)
        for block in range(width // 128):
            at = FEED_ROWS + block * deep
            down_ref[rows, block * 128 : block * 128 + 128] = held[at : at + deep]
    refs = [(ref, at) for ref in (g2_ref, s2_ref, bd_ref, g1_ref, s1_ref, bo_ref, bup_ref) for at in range(0, ref.shape[0], 128)]
    each = len(refs) // CHUNKS
    for number, (ref, at) in enumerate(refs):
        ref[at : at + 128] = keep_ref[number // each, number % each, :]


def spread_heads(a_ref, b_ref, c_ref, d_ref, qkv_ref, bias_ref, keep_ref):
    kinds, width, half = qkv_ref.shape
    tall = width // CHUNKS
    for chunk, held in each_chunk((a_ref, b_ref, c_ref, d_ref)):
        rows = pl.ds(pl.multiple_of(chunk * tall, tall), tall)
        for kind in range(kinds):
            for block in range(half // 128):
                row = (kind * (half // 128) + block) * tall
                qkv_ref[kind, rows, block * 128 : block * 128 + 128] = held[row : row + tall]
        keep_ref[chunk] = held[HEAD_ROWS - 16 :]
    blocks = half // 128
    for number in range(2 * blocks):
        at = number % blocks * 128
        bias_ref[number // blocks : number // blocks + 1, at : at + 128] = keep_ref[number, 0:1, :]


def shape(dims, kind=bf16):
    return jax.ShapeDtypeStruct(dims, kind)


smem = pl.BlockSpec(memory_space=pltpu.SMEM)


def specs(count):
    return [smem] + [pl.BlockSpec(memory_space=pltpu.VMEM)] * (count - 1)


def cost(flops, moved, powers=0):
    return pl.CostEstimate(flops=int(flops), bytes_accessed=int(moved), transcendentals=int(powers))


hbm = pl.BlockSpec(memory_space=pl.ANY)
vmem = pl.BlockSpec(memory_space=pltpu.VMEM)


def call_forward(sets, x, wa, wb, ba, bb):
    width = 2 * wa.shape[2]
    big, more = (width, LANES), (width // 4, LANES)
    return pl.pallas_call(
        attend_forward, name="attend_forward",
        out_shape=[shape(big), shape(big), shape(big), shape(big), shape(more)],
        in_specs=[smem, hbm, hbm, vmem, vmem, vmem], out_specs=[hbm] * 5,
        scratch_shapes=[pltpu.VMEM(a.shape, bf16) for a in (x, wa)] + [pltpu.VMEM(big, bf16)] * 4 + [pltpu.VMEM(more, bf16)]
        + [pltpu.VMEM((x.shape[1], LANES), bf16), pltpu.VMEM((CLASSES, LANES), bf16), pltpu.VMEM((CLASSES + 16, LANES), bf16)]
        + [pltpu.SemaphoreType.DMA((3,)), pltpu.SemaphoreType.DMA((5,))],
        compiler_params=params(54), cost_estimate=cost(14e9, 12e6),
    )(sets, x, wa, wb, ba, bb)


def call_feed_forward(sets, x, mixed, wo_a, wo_b, up_a, up_b, bu_a, bu_b, down_a, down_b, vecs, cot):
    rows, width = x.shape
    half = up_a.shape[1]
    outs = [shape((rows, width)), shape((rows, width)), shape((rows, width), f32), shape((rows, 2 * half)), shape((rows, width))]
    tall = (PADDED, width)
    own = [tall, mixed.shape, (width, width), (2, width, half), (2, half, width), tall]
    piece = shape((4, 4, DOWN_ROWS, 128))
    return pl.pallas_call(
        feed_forward, name="feed_forward",
        out_shape=outs + [piece, piece, shape((24, width), f32)],
        in_specs=[smem] + [hbm] * 6 + [vmem] * 2 + [hbm] * 2 + [vmem] * 6 + [hbm], out_specs=[hbm] * 7 + [vmem],
        scratch_shapes=[pltpu.VMEM(a, bf16) for a in own] + [pltpu.VMEM((PADDED, a.shape[1]), a.dtype) for a in outs]
        + [pltpu.VMEM((2, *piece.shape), bf16), pltpu.VMEM((PADDED, 2 * half), bf16)]
        + [pltpu.SemaphoreType.DMA((9,)), pltpu.SemaphoreType.DMA((6, 5)), pltpu.SemaphoreType.DMA((2,))],
        compiler_params=params(48), cost_estimate=cost(14e9, 20e6),
    )(sets, x, mixed, wo_a, wo_b, up_a, up_b, bu_a, bu_b, down_a, down_b, *vecs, cot)


def call_feed_backward(second, slope, hidden, resid, mixed, wo_a, wo_b, up_a, up_b, down_a, down_b, gain, sums):
    rows, width = second.shape
    half = up_a.shape[1]
    split = wo_a.shape[0]
    piece = shape((4, 4, FEED_ROWS, 128))
    outs = [shape((rows, width), f32), shape((2 * split, LANES)), shape((2 * split // 4, LANES))]
    given = [((PADDED, a.shape[1]), a.dtype) for a in (second, slope, hidden, resid)] + [(mixed.shape, bf16)]
    given += [((width, width), bf16), ((2, width, half), bf16), ((2, half, width), bf16)]
    return pl.pallas_call(
        feed_backward, name="feed_backward",
        out_shape=outs + [pltpu.VMEM(piece.shape, bf16)] * 2,
        in_specs=[hbm] * 11 + [vmem] * 2, out_specs=[hbm] * 3 + [vmem] * 2,
        scratch_shapes=[pltpu.VMEM(*a) for a in given] + [pltpu.VMEM((PADDED, width), f32)] + [pltpu.VMEM(a.shape, a.dtype) for a in outs[1:]]
        + [
            pltpu.VMEM((PADDED, 2 * half), bf16), pltpu.VMEM((LANES, width), bf16),
            pltpu.VMEM((24, width), f32), pltpu.VMEM((8, 2 * half), f32),
        ]
        + [pltpu.SemaphoreType.DMA(a) for a in ((6, 3), (8,), (6, 1), (2,))],
        compiler_params=params(48), cost_estimate=cost(14e9, 20e6),
    )(second, slope, hidden, resid, mixed, wo_a, wo_b, up_a, up_b, down_a, down_b, gain, sums)


def call_backward(part, sets, q, k, v, grad, lse, delta, x):
    rows = q.shape[0] // 2
    big, more = (rows, LANES), (rows // 4, LANES)
    return pl.pallas_call(
        functools.partial(attend_backward, part), name="attend_backward",
        out_shape=[shape(big), shape(big), shape(big), shape((4, 4, HEAD_ROWS, 128))],
        in_specs=[smem] + [hbm] * 7, out_specs=[hbm] * 3 + [vmem],
        scratch_shapes=[pltpu.VMEM(a, bf16) for a in (big, big, big, big, more, more, x.shape, (3, *big), (x.shape[1], LANES))]
        + [
            pltpu.VMEM((CLASSES, LANES), bf16), pltpu.VMEM((CLASSES + 16, LANES), bf16),
            pltpu.VMEM((2, 896, 896), bf16), pltpu.VMEM((2, 896, 896), bf16),
            pltpu.VMEM((rows // 64, 64, LANES), f32), pltpu.VMEM((rows // 64, 64, LANES), f32),
        ]
        + [pltpu.SemaphoreType.DMA(a) for a in ((rows // 128, 6), (1,), (rows // 128, 3))],
        compiler_params=params(50), cost_estimate=cost(9e9, 6e6),
    )(sets, q, k, v, grad, lse, delta, x)


def call_project_input(own, other, wa, wb, resid):
    return pl.pallas_call(
        project_input, name="project_input", out_shape=shape(resid.shape, f32),
        scratch_shapes=[pltpu.VMEM((3, 2 * wa.shape[2], wa.shape[1]), bf16)],
        compiler_params=params(40), cost_estimate=cost(2.4e9, 12e6),
    )(*own, *other, wa, wb, resid)


def swap(array):
    return lax.ppermute(array, "mp", [(0, 1), (1, 0)])


def exchange(array, distance):
    count = lax.axis_size("dp")
    return lax.ppermute(array, "dp", [(i, i ^ distance) for i in range(count)])


def small(kernel, name, outs, scratch=()):
    moved = 2 * sum(o.size * o.dtype.itemsize for o in outs)
    return pl.pallas_call(
        kernel, name=name, out_shape=list(outs), scratch_shapes=list(scratch),
        compiler_params=params(24), cost_estimate=cost(1e6, moved),
    )


def after(array, *earlier):
    return lax.optimization_barrier((array, *earlier))[0]


def to_plane(parts):
    return [exchange(parts[xy], xy) for xy in (1, 2, 3)]


def to_line(parts):
    return [exchange(parts[z], 4 * z) for z in (1, 2, 3)]


def plane_sum(parts, came, *earlier):
    _, rows, lanes = parts[0].shape
    return small(add_four, "add_four", [shape((rows, lanes))] * 4)(after(parts[0], *earlier), *came)


def plane_sum_joined(feed, feed_came, down, down_came, *earlier):
    rows, lanes = feed[0].shape[1] + down[0].shape[1], feed[0].shape[2]
    return small(join_four, "join_four", [shape((rows, lanes))] * 4)(after(feed[0], *earlier), *feed_came, down[0], *down_came)


def line_sum(parts, came, *earlier):
    (total,) = small(add_four, "add_four", [shape(parts[0].shape)])(after(parts[0], *earlier), *came)
    distance = CHUNKS
    while distance < lax.axis_size("dp"):
        total = total + exchange(total, distance)
        distance *= 2
    return total


def line_copies(total):
    return [exchange(total, 4 * z) for z in (1, 2, 3)]


def laid(total, came, *earlier):
    (held,) = small(lay_four, "lay_four", [shape((4, *total.shape))])(after(total, *earlier), *came)
    return held


def plane_copies(held):
    return [exchange(held, xy) for xy in (1, 2, 3)]


def across(beside, above, *earlier):
    cut = beside.shape[1] // 32 * 16
    return exchange(after(beside, *earlier)[:, :cut], 2), exchange(after(above, *earlier)[:, cut:], 1)


def halves_added(mine, came, *earlier):
    return small(add_pair, "add_pair", [shape(mine.shape[1:])] * 4)(after(mine, *earlier), came)


def per_device(
    variates, dataset, w_qkv, b_qv, w_out, b_out, gain_one, shift_one, w_up, b_up, w_down, b_down, gain_two, shift_two, cotangent,
):
    width, half = w_up.shape
    other_qkv, other_bias = swap(w_qkv), swap(b_qv)
    other_out, other_up, other_bup, other_down = swap(w_out), swap(w_up), swap(b_up), swap(w_down)
    q, k, v, mixed, lse = call_forward(dataset, variates, w_qkv, other_qkv, b_qv, other_bias)
    out, hidden, resid, slope, second, down_mine, down_theirs, sums = call_feed_forward(
        dataset, variates, mixed, w_out, other_out, w_up, other_up, b_up, other_bup, w_down, other_down,
        (b_out, gain_one, shift_one, b_down, gain_two, shift_two), cotangent,
    )
    down = halves_added(down_mine, swap(down_theirs))
    down_came = to_plane(down)
    grad_res, grad_mix, delta, mine, theirs = call_feed_backward(
        after(second, *down), slope, hidden, resid, mixed, w_out, other_out, w_up, other_up, w_down, other_down, gain_one, sums
    )
    feed = halves_added(mine, swap(after(theirs, *down_came)))
    feed_came = to_plane(feed)
    *other, theirs = call_backward(1, dataset, q, k, v, after(grad_mix, *feed), lse, delta, variates)
    feed = plane_sum_joined(feed, feed_came, down, down_came, theirs)
    heads_came = swap(after(theirs, *feed))
    feed_came = to_line(feed)
    *own, mine = call_backward(0, dataset, q, k, v, after(grad_mix, heads_came, *feed), lse, delta, variates)
    total = line_sum(feed, feed_came, mine)
    heads = halves_added(mine, heads_came, total)
    heads_plane = to_plane(heads)
    feed_came = line_copies(total)
    grad_in = call_project_input(own, other, w_qkv, other_qkv, after(grad_res, total, *heads))
    held = laid(total, feed_came, grad_in)
    heads = plane_sum(heads, heads_plane, grad_in)
    feed = plane_copies(after(held, *heads))[:2]
    heads = line_sum(heads, to_line(heads))
    line = line_copies(heads)
    feed = [held, *feed, *across(*feed, line[0])]
    heads = laid(heads, line)
    heads = [heads, *plane_copies(heads)]
    vector = shape((width,), f32)
    outs = [shape((width, half), f32), shape(w_out.shape, f32)] + [vector] * 6 + [shape((half,), f32), shape(w_down.shape, f32)]
    keep = [pltpu.VMEM((CHUNKS, 16, 128), f32)]
    grad_up, grad_out, two_gain, two_shift, down_bias, one_gain, one_shift, out_bias, up_bias, grad_down = small(
        spread_feed, "spread_feed", outs, keep
    )(*feed)
    grad_qkv, bias = small(spread_heads, "spread_heads", [shape(w_qkv.shape, f32), shape(b_qv.shape, f32)], keep)(*heads)
    return (
        out, grad_in, grad_qkv, bias, grad_out, out_bias, one_gain, one_shift, grad_up, up_bias,
        grad_down, down_bias, two_gain, two_shift,
    )


def solution(mesh):
    wide = P(("dp", "mp"), None)
    weights = (P(None, None, "mp"), P(None, "mp"), P("mp", None))
    placed = (wide, P("dp"), *weights, P(), P(), P(), P(None, "mp"), P("mp"), P("mp", None), P(), P(), P(), wide)
    given = (wide, wide, *weights, P(), P(), P(), P(None, "mp"), P("mp"), P("mp", None), P(), P(), P())
    return jax.shard_map(per_device, mesh=mesh, in_specs=placed, out_specs=given, check_vma=False)
```

```python
import functools

import jax
import jax.numpy as jnp
from jax import lax
from jax.experimental import pallas as pl
from jax.experimental.pallas import tpu as pltpu
from jax.sharding import PartitionSpec as P

HEAD_DIM = 64
SLOTS = 1424
WIDTHS = (7, 21, 321, 862)
LANES = 1536
CLASSES = 80
BIG = 1e30
EPS = 1e-05
MIB = 2**20

bf16 = jnp.bfloat16
f32 = jnp.float32


def mul(left, right, left_dim=1, right_dim=0):
    return lax.dot_general(
        left, right, (((left_dim,), (right_dim,)), ((), ())), preferred_element_type=f32
    )


def params(limit):
    return pltpu.CompilerParams(vmem_limit_bytes=limit * MIB)


def cover(width, start, stop, last):
    used = SLOTS // width * width
    low = start // width * width
    high = last if stop > used else -(-stop // width) * width
    return (low // 128 * 128, min(-(-min(high, last) // 128) * 128, LANES))


def groups_of(width, rows, step):
    found = []
    for start in range(0, rows, step):
        low, high = cover(width, start, min(start + step, rows), rows)
        if found and found[-1][2] == low and found[-1][2] + found[-1][3] == high:
            first, count = found[-1][:2]
            found[-1] = (first, count + step, low, high - low)
        else:
            found.append((start, step, low, high - low))
    return found


def near(tile):
    return jnp.clip(tile * 256 - 128, 0, LANES - 512)


def middle(tile):
    return jnp.where(tile < 2, 0, jnp.where(tile == 2, 256, jnp.where(tile == 3, 640, 768)))


FORWARD = (
    [(0, 6, 512, near, 8)],
    [(0, 6, 768, middle, 8)],
    [(0, 3, 896, lambda tile: 0 * tile, 8), (3, 4, 1536, lambda tile: 0 * tile, 2), (4, 6, 768, lambda tile: 0 * tile + 768, 8)],
    [(0, 6, 512, near, 1)],
    [(0, 6, LANES, lambda tile: 0 * tile, 1)],
)
BACKWARD = (
    [],
    groups_of(WIDTHS[2], SLOTS // WIDTHS[2] * WIDTHS[2], 256),
    [(0, 896, 0, 896)],
)


def own_bucket(sets_ref):
    return sets_ref[lax.axis_index("mp")]


def token_class(width):
    token = lax.broadcasted_iota(jnp.int32, (CLASSES, LANES), 1)
    numbers = token.astype(f32)
    held = jnp.floor((numbers + 0.5) * (1.0 / width)).astype(jnp.int32)
    held = jnp.where(token < SLOTS, held, (SLOTS - 1) // width + 1)
    row = lax.broadcasted_iota(jnp.int32, (CLASSES, LANES), 0)
    return held % CLASSES == row


def write_masks(bucket, hot_ref, bar_ref):
    for number, width in enumerate(WIDTHS):

        @pl.when(bucket == number)
        def _():
            same = token_class(width)
            hot_ref[...] = jnp.where(same, 1.0, 0.0).astype(bf16)
            bar_ref[:CLASSES, :] = jnp.where(same, 0.0, -BIG).astype(bf16)

    row = lax.broadcasted_iota(jnp.int32, (16, LANES), 0)
    bar_ref[CLASSES:, :] = jnp.where(row < 3, 1.0, 0.0).astype(bf16)


def split_three(row):
    high = row.astype(bf16)
    rest = row - high.astype(f32)
    middle = rest.astype(bf16)
    low = (rest - middle.astype(f32)).astype(bf16)
    return high, middle, low


def extra_rows(row):
    parts = [p.astype(f32) for p in split_three(row)]
    number = lax.broadcasted_iota(jnp.int32, (16, row.shape[1]), 0)
    held = jnp.where(number == 0, parts[0], jnp.where(number == 1, parts[1], jnp.where(number == 2, parts[2], 0.0)))
    return held.astype(bf16)


LOG_E = 1.4426950408889634
SAFE = 60.0


def attend_forward(
    sets_ref, x_hbm, wa_hbm, wb_ref, ba_ref, bb_ref, q_hbm, k_hbm, v_hbm, o_hbm, lse_hbm,
    x_ref, wa_ref, q_ref, k_ref, v_ref, o_ref, lse_ref, xt_ref, hot_ref, bar_ref, in_sems, out_sems,
):
    loads = [pltpu.make_async_copy(*pair, in_sems.at[i]) for i, pair in enumerate(((x_hbm, x_ref), (wa_hbm, wa_ref)))]
    for load in loads:
        load.start()
    pairs = ((q_ref, q_hbm), (k_ref, k_hbm), (v_ref, v_hbm), (o_ref, o_hbm), (lse_ref, lse_hbm))
    stores = [pltpu.make_async_copy(*pair, out_sems.at[i]) for i, pair in enumerate(pairs)]
    bucket = own_bucket(sets_ref)
    write_masks(bucket, hot_ref, bar_ref)
    tail = jnp.zeros((LANES - SLOTS, x_ref.shape[1]), bf16)
    loads[0].wait()
    xt_ref[...] = jnp.concatenate([x_ref[...], tail], axis=0).T
    worst = None
    for side, (w_ref, b_ref) in enumerate(((wa_ref, ba_ref), (wb_ref, bb_ref))):
        if side == 0:
            loads[1].wait()
        for kind, out_ref in enumerate((q_ref, k_ref, v_ref)):
            weight = w_ref[kind].T
            rows = weight.shape[0]
            if kind != 1:
                row = b_ref[kind // 2 : kind // 2 + 1, :].astype(f32)
                column = jnp.broadcast_to(row, (128, rows)).T
                column = jnp.concatenate([column] * 4, axis=1)

            def project(number, carry):
                lanes = slice(number * 512, number * 512 + 512)
                part = mul(weight, xt_ref[:, lanes])
                if kind != 1:
                    part = part + column
                if kind == 0:
                    part = part * 0.125
                out_ref[side * rows : (side + 1) * rows, lanes] = part.astype(bf16)
                return carry

            for number in range(LANES // 512):
                project(number, 0)
    for store in stores[:3]:
        store.start()
    heads = q_ref.shape[0] // 64
    for head in range(heads):
        norms = []
        for ref in (q_ref, k_ref):
            held = ref[head * 64 : head * 64 + 64, :].astype(f32)
            norms.append(jnp.max(jnp.sum(held * held, axis=0, keepdims=True), axis=1, keepdims=True))
        both = norms[0] * norms[1]
        worst = both if worst is None else jnp.maximum(worst, both)
    calm = worst[0, 0] < SAFE * SAFE

    def score(head, start, first, span):
        rows = pl.ds(pl.multiple_of(head * 64, 64), 64)
        lanes, span = pl.ds(start, 256), pl.ds(first, span)
        keys = jnp.concatenate([k_ref[rows, span], bar_ref[:CLASSES, span]], axis=0)
        quer = jnp.concatenate([q_ref[rows, lanes], hot_ref[:, lanes]], axis=0)
        return mul(keys, quer, 0, 0)

    def finish(head, start, first, span, scores, plain):
        rows = pl.ds(pl.multiple_of(head * 64, 64), 64)
        lanes = pl.ds(start, 256)
        if plain:
            raised = jnp.exp2(scores * LOG_E).astype(bf16)
        else:
            top = jnp.max(scores, axis=0, keepdims=True)
            raised = jnp.exp(scores - top).astype(bf16)
        vals = jnp.concatenate([v_ref[rows, pl.ds(first, span)], jnp.ones((16, span), bf16)], axis=0)
        total = mul(vals, raised)
        sums = total[64:65, :]
        o_ref[rows, lanes] = (total[:64, :] * (1.0 / sums)).astype(bf16)
        logs = jnp.log(sums)
        if not plain:
            logs = logs + top
        lse_ref[pl.ds(pl.multiple_of(head * 16, 16), 16), lanes] = extra_rows(-logs)

    def over(begin, end, span, first_of, together, plain):
        def turn(number, carry):
            tile = begin + number % (end - begin)
            start = pl.multiple_of(tile * 256, 256)
            first = pl.multiple_of(first_of(tile), 128)
            own = [number // (end - begin) * together + i for i in range(together)]
            held = [score(head, start, first, span) for head in own]
            for head, scores in zip(own, held):
                finish(head, start, first, span, scores, plain)
            return carry

        lax.fori_loop(0, heads // together * (end - begin), turn, 0)

    for group in range(5):
        plain = group < 3
        chosen = (bucket < 2, bucket == 2, bucket == 3, bucket < 2, bucket >= 2)[group]

        @pl.when(jnp.logical_and(chosen, calm == plain))
        def _():
            for begin, end, span, first_of, together in FORWARD[group]:
                over(begin, end, span, first_of, together, plain)

    for store in stores[3:]:
        store.start()
    for store in stores:
        store.wait()


def copies(pairs, sems):
    return [pltpu.make_async_copy(*pair, sems.at[i]) for i, pair in enumerate(pairs)]


def attend_backward(
    part, sets_ref, q_hbm, k_hbm, v_hbm, g_hbm, lse_hbm, delta_hbm, x_hbm, dq_hbm, dk_hbm, dv_hbm, piece_ref,
    q_ref, k_ref, v_ref, g_ref, lse_ref, delta_ref, x_ref, grads_ref, xt_ref,
    hot_ref, bar_ref, p_ref, s_ref, ka_ref, va_ref, head_sems, in_sems, out_sems,
):
    half = q_ref.shape[0]
    dq_ref, dk_ref, dv_ref = (grads_ref.at[kind] for kind in range(3))

    def loads_of(number):
        there = pl.ds(part * half + number * 128, 128)
        here = pl.ds(number * 128, 128)
        pairs = [(far.at[there], near.at[here]) for far, near in ((q_hbm, q_ref), (k_hbm, k_ref), (v_hbm, v_ref), (g_hbm, g_ref))]
        there = pl.ds(part * (half // 4) + number * 32, 32)
        here = pl.ds(number * 32, 32)
        pairs += [(far.at[there], near.at[here]) for far, near in ((lse_hbm, lse_ref), (delta_hbm, delta_ref))]
        return copies(pairs, head_sems.at[number])

    def stores_of(number):
        here = pl.ds(number * 128, 128)
        return copies([(near.at[here], far.at[here]) for near, far in ((dq_ref, dq_hbm), (dk_ref, dk_hbm), (dv_ref, dv_hbm))], out_sems.at[number])

    for number in range(half // 128):
        for load in loads_of(number):
            load.start()
    given = copies([(x_hbm, x_ref)], in_sems)[0]
    bucket = own_bucket(sets_ref)
    write_masks(bucket, hot_ref, bar_ref)

    def one_head(head, groups, slot):
        rows = pl.ds(pl.multiple_of(head * 64, 64), 64)
        more = pl.ds(pl.multiple_of(head * 16, 16), 16)
        single = len(groups) == 1
        if not single:
            ka_ref[slot] = jnp.zeros(ka_ref.shape[1:], f32)
            va_ref[slot] = jnp.zeros(va_ref.shape[1:], f32)
        for q0, nq, k0, nk in groups:
            span = slice(k0, k0 + nk)
            held = slice(q0, q0 + nq)
            keys = jnp.concatenate([k_ref[rows, span], bar_ref[:, span]], axis=0)
            vals = jnp.concatenate([v_ref[rows, span], bar_ref[CLASSES:, span]], axis=0)
            for start in range(q0, q0 + nq, 256):
                size = min(256, q0 + nq - start)
                lanes = slice(start, start + size)
                quer = jnp.concatenate([q_ref[rows, lanes], hot_ref[:, lanes], lse_ref[more, lanes]], axis=0)
                grad = jnp.concatenate([g_ref[rows, lanes], delta_ref[more, lanes]], axis=0)
                probs = jnp.exp2(mul(quer, keys, 0, 0) * LOG_E)
                slopes = probs * mul(grad, vals, 0, 0)
                p_ref[slot, start - q0 : start - q0 + size, :nk] = probs.astype(bf16)
                s_ref[slot, start - q0 : start - q0 + size, :nk] = slopes.astype(bf16)
            dv = mul(g_ref[rows, held], p_ref[slot, :nq, :nk])
            dk = mul(q_ref[rows, held], s_ref[slot, :nq, :nk])
            dq = mul(k_ref[rows, span], s_ref[slot, :nq, :nk], 1, 1)
            dq_ref[rows, held] = (dq * 0.125).astype(bf16)
            if single:
                dv_ref[rows, span] = dv.astype(bf16)
                dk_ref[rows, span] = dk.astype(bf16)
            else:
                va_ref[slot, :, span] += dv
                ka_ref[slot, :, span] += dk
        if single:
            rest = LANES - 896
            for out in (dq_ref, dk_ref, dv_ref):
                out[rows, 896:] = jnp.zeros((64, rest), bf16)
        else:
            dv_ref[rows, :] = va_ref[slot].astype(bf16)
            dk_ref[rows, :] = ka_ref[slot].astype(bf16)
            done = groups[-1][0] + groups[-1][1]
            if done < LANES:
                dq_ref[rows, done:] = jnp.zeros((64, LANES - done), bf16)

    def tile_of(head, start, first, span):
        rows = pl.ds(head * 64, 64)
        more = pl.ds(head * 16, 16)
        lanes, span = pl.ds(start, 256), pl.ds(first, span)
        keys = jnp.concatenate([k_ref[rows, span], bar_ref[:, span]], axis=0)
        vals = jnp.concatenate([v_ref[rows, span], bar_ref[CLASSES:, span]], axis=0)
        quer = jnp.concatenate([q_ref[rows, lanes], hot_ref[:, lanes], lse_ref[more, lanes]], axis=0)
        grad = jnp.concatenate([g_ref[rows, lanes], delta_ref[more, lanes]], axis=0)
        probs = jnp.exp2(mul(quer, keys, 0, 0) * LOG_E)
        slopes = (probs * mul(grad, vals, 0, 0)).astype(bf16)
        return probs.astype(bf16), slopes

    def take(head, start, first, span, probs, slopes):
        rows = pl.ds(head * 64, 64)
        lanes, span = pl.ds(start, 256), pl.ds(first, span)
        va_ref[head, :, span] += mul(g_ref[rows, lanes], probs)
        ka_ref[head, :, span] += mul(q_ref[rows, lanes], slopes)
        dq_ref[rows, lanes] = (mul(k_ref[rows, span], slopes, 1, 1) * 0.125).astype(bf16)

    def by_tiles(span, first_of, together):
        for number in range(half // 128):
            for load in loads_of(number):
                load.wait()
        given.start()
        ka_ref[...] = jnp.zeros_like(ka_ref)
        va_ref[...] = jnp.zeros_like(va_ref)

        def turn(tile, carry):
            start = pl.multiple_of(tile * 256, 256)
            first = pl.multiple_of(first_of(tile), 128)
            for base in range(0, half // 64, together):
                own = range(base, base + together)
                held = [tile_of(head, start, first, span) for head in own]
                for head, (probs, slopes) in zip(own, held):
                    take(head, start, first, span, probs, slopes)
            return carry

        lax.fori_loop(0, 6, turn, 0)
        for head in range(half // 64):
            rows = pl.ds(head * 64, 64)
            dv_ref[rows, :] = va_ref[head].astype(bf16)
            dk_ref[rows, :] = ka_ref[head].astype(bf16)
        for number in range(half // 128):
            for store in stores_of(number):
                store.start()

    for group in range(3):
        chosen = (bucket < 2, bucket == 2, bucket == 3)[group]

        @pl.when(chosen)
        def _():
            if group == 0:
                by_tiles(512, near, 4)
            else:

                def pair(number, carry):
                    for load in loads_of(number):
                        load.wait()

                    @pl.when(number == 0)
                    def _():
                        given.start()

                    one_head(2 * number, BACKWARD[group], 0)
                    one_head(2 * number + 1, BACKWARD[group], 1)
                    for store in stores_of(number):
                        store.start()
                    return carry

                lax.fori_loop(0, half // 128, pair, 0)

    given.wait()
    width = x_ref.shape[1]
    tail = jnp.zeros((LANES - SLOTS, width), bf16)
    xt_ref[...] = jnp.concatenate([x_ref[...], tail], axis=0).T
    tall = width // CHUNKS
    ones = jnp.ones((8, LANES), bf16)
    place_of = slots()
    sums = []
    blocks = half // 128

    def product_of(kind, carry):
        product = mul(xt_ref[...], grads_ref[kind], 1, 1).astype(bf16)
        for chunk in range(CHUNKS):
            xy, z = place_of(chunk)
            for block in range(blocks):
                row = (kind * blocks + block) * tall
                piece_ref[xy, z, pl.ds(row, tall), :] = product[chunk * tall : (chunk + 1) * tall, block * 128 : block * 128 + 128]
        return carry

    for kind in range(3):
        product_of(kind, 0)
    for d_ref in (dq_ref, dv_ref):
        total = mul(ones, d_ref[...], 1, 1)[:1]
        sums += [total[:, block * 128 : block * 128 + 128] for block in range(blocks)]
    number = lax.broadcasted_iota(jnp.int32, (16, 128), 0)
    for chunk in range(CHUNKS):
        xy, z = place_of(chunk)
        held = jnp.where(number == 0, sums[chunk] if chunk < len(sums) else 0.0, 0.0)
        piece_ref[xy, z, HEAD_ROWS - 16 :, :] = held.astype(bf16)
    for number in range(half // 128):
        for store in stores_of(number):
            store.wait()


TILE = 240
TILES = 6
PADDED = TILE * TILES
LAST = SLOTS - TILE * (TILES - 1)


def over_tiles(step):
    def body(number, carry):
        step(number, pl.multiple_of(number * TILE, TILE))
        return carry

    lax.fori_loop(0, TILES, body, 0)


def rows_moved(number, start, begin):
    if isinstance(number, int):
        begin(start, LAST if number == TILES - 1 else TILE)
        return

    @pl.when(number < TILES - 1)
    def _():
        begin(start, TILE)

    @pl.when(number == TILES - 1)
    def _():
        begin(TILE * (TILES - 1), LAST)


def mean_of(matrix):
    return jnp.sum(matrix, axis=1, keepdims=True) * (1.0 / matrix.shape[1])


def norm_parts(matrix):
    centre = matrix - mean_of(matrix)
    spread = lax.rsqrt(mean_of(centre * centre) + EPS)
    return centre * spread, spread


def norm_back(scaled, normed, spread):
    return spread * (scaled - mean_of(scaled) - normed * mean_of(scaled * normed))


def fold(matrix):
    return jnp.sum(matrix.reshape(matrix.shape[0] // 8, 8, matrix.shape[1]), axis=0)


def gelu_parts(pre):
    size = jnp.abs(pre)
    t = pl.reciprocal(1.0 + (0.3275911 * 2.0**-0.5) * size)
    bell = jnp.exp2((-0.5 * LOG_E) * (pre * pre))
    poly = 0.5 * 1.061405429
    for factor in (-1.453152027, 1.421413741, -0.284496736, 0.254829592):
        poly = poly * t + 0.5 * factor
    tail = poly * t * bell
    phi = jnp.where(pre > 0, 1.0 - tail, tail)
    return pre * phi, phi + pre * (bell * (2.0 * jnp.pi) ** -0.5)


HIDDEN_STEP = 512


def row_of(ref):
    return ref[...].astype(f32).reshape(1, ref.shape[0])


def feed_forward(
    sets_ref, x_hbm, o_hbm, wo_a, wo_b, ua_hbm, ub_hbm, ba_ref, bb_ref, da_hbm, db_hbm,
    bo_ref, g1_ref, s1_ref, bd_ref, g2_ref, s2_ref, cot_hbm,
    out_hbm, hid_hbm, res_hbm, slope_hbm, sec_hbm, gd_a, gd_b, sums_ref,
    x_ref, o_ref, wo_ref, u_ref, d_ref, cot_ref, out_ref, hid_ref, res_ref, slope_ref, low_ref, gd_ref, act_ref,
    in_sems, row_sems, out_sems,
):
    half = ua_hbm.shape[1]
    split = wo_a.shape[0]
    width = x_ref.shape[1]
    true = pl.ds(0, SLOTS)
    pairs = [(o_hbm, o_ref), (wo_a, wo_ref.at[pl.ds(0, split)]), (wo_b, wo_ref.at[pl.ds(split, split)]), (x_hbm, x_ref.at[true])]
    pairs += [(ua_hbm, u_ref.at[0]), (ub_hbm, u_ref.at[1]), (da_hbm, d_ref.at[0]), (db_hbm, d_ref.at[1]), (cot_hbm, cot_ref.at[true])]
    loads = copies(pairs, in_sems)
    for load in loads:
        load.start()
    for ref in (x_ref, cot_ref):
        ref[SLOTS:, :] = jnp.zeros((PADDED - SLOTS, width), bf16)
    bucket = own_bucket(sets_ref)
    used = SLOTS // WIDTHS[3] * WIDTHS[3]
    for number in range(3):
        used = jnp.where(bucket == number, SLOTS // WIDTHS[number] * WIDTHS[number], used)
    sums_ref[...] = jnp.zeros_like(sums_ref)
    b_out, gain_one, shift_one, b_down, gain_two, shift_two = (
        row_of(ref) for ref in (bo_ref, g1_ref, s1_ref, bd_ref, g2_ref, s2_ref)
    )
    b_up = [row_of(ref) for ref in (ba_ref, bb_ref)]
    places = [(side, at) for side in range(2) for at in range(0, half, HIDDEN_STEP)]
    last = copies([(gd_ref.at[0], gd_a), (gd_ref.at[1], gd_b)], out_sems)

    def stores_of(number, start, size):
        rows = pl.ds(start, size)
        pairs = ((out_ref, out_hbm), (hid_ref, hid_hbm), (res_ref, res_hbm), (slope_ref, slope_hbm), (low_ref, sec_hbm))
        return copies([(near.at[rows], far.at[rows]) for near, far in pairs], row_sems.at[number])

    def step(number, start):
        rows = pl.ds(start, TILE)
        resid = res_ref[rows, :] + x_ref[rows, :].astype(f32) + b_out
        res_ref[rows, :] = resid
        normed, _ = norm_parts(resid)
        hidden = normed * gain_one + shift_one
        low = hidden.astype(bf16)
        hid_ref[rows, :] = low

        @pl.when(number == 0)
        def _():
            for load in loads[4:]:
                load.wait()

        def lift(side, at):
            return mul(low, u_ref[side, :, at : at + HIDDEN_STEP]) + b_up[side][:, at : at + HIDDEN_STEP]

        total = None
        ahead = lift(*places[0])
        for turn, (side, at) in enumerate(places):
            pre = ahead
            if turn + 1 < len(places):
                ahead = lift(*places[turn + 1])
            place = slice(side * half + at, side * half + at + HIDDEN_STEP)
            active, slope = gelu_parts(pre)
            active = active.astype(bf16)
            act_ref[rows, place] = active
            slope_ref[rows, place] = slope.astype(bf16)
            part = mul(active, d_ref[side, at : at + HIDDEN_STEP, :])
            total = part if total is None else total + part
        second = hidden + total + b_down
        normed, spread = norm_parts(second)
        out_ref[rows, :] = (normed * gain_two + shift_two).astype(bf16)
        row = start + lax.broadcasted_iota(jnp.int32, (TILE, width), 0)
        top = jnp.where(row < used, cot_ref[rows, :].astype(f32), 0.0)
        grad = norm_back(top * gain_two, normed, spread)
        low_ref[rows, :] = grad.astype(bf16)
        sums_ref[0:8, :] += fold(top * normed)
        sums_ref[8:16, :] += fold(top)
        sums_ref[16:24, :] += fold(grad)
        rows_moved(number, start, lambda at, size: [store.start() for store in stores_of(number, at, size)])

    for load in loads[:4]:
        load.wait()
    for start in range(0, PADDED, 512):
        size = min(512, PADDED - start)
        res_ref[start : start + size, :] = mul(o_ref[:, start : start + 512], wo_ref[...], 0, 0)[:size]
    over_tiles(step)
    place_of = slots()
    tall = half // CHUNKS

    def block_of(number, carry):
        side, block = number // 4, number % 4
        part = mul(act_ref[:, pl.ds(pl.multiple_of(number * 4 * tall, 4 * tall), 4 * tall)], low_ref[...], 0, 0).astype(bf16)
        for z in range(4):
            xy, z_place = place_of(z * 4 + block)
            for lane in range(width // 128):
                gd_ref[side, xy, z_place, lane * tall : (lane + 1) * tall, :] = part[z * tall : (z + 1) * tall, lane * 128 : lane * 128 + 128]

        @pl.when(number == 3)
        def _():
            last[0].start()

        return carry

    lax.fori_loop(0, 8, block_of, 0)
    last[1].start()
    for number in range(TILES):
        rows_moved(number, number * TILE, lambda at, size: [store.wait() for store in stores_of(number, at, size)])
    for store in last:
        store.wait()


CHUNKS = 16
FEED_ROWS = 336
DOWN_ROWS = 256
HEAD_ROWS = 208


def slots():
    own = lax.axis_index("dp") % CHUNKS

    def place(chunk):
        held = chunk ^ own
        return held % 4, held // 4

    return place


def feed_backward(
    sec_hbm, slope_hbm, hid_hbm, res_hbm, o_hbm, wo_a, wo_b, ua_hbm, ub_hbm, da_hbm, db_hbm, g1_ref, two_ref,
    gr_hbm, g_hbm, delta_hbm, mine_ref, theirs_ref,
    sec_ref, slope_ref, hid_ref, res_ref, o_ref, wo_ref, u_ref, d_ref, gr_ref, g_ref, delta_ref,
    pre_ref, mix_ref, sums_ref, bup_ref, row_in, in_sems, row_out, out_sems,
):
    half = ua_hbm.shape[1]
    width = hid_ref.shape[1]
    split = wo_a.shape[0]

    def loads_of(number, start, size):
        rows = pl.ds(start, size)
        pairs = ((sec_hbm, sec_ref), (slope_hbm, slope_ref), (res_hbm, res_ref))
        return copies([(far.at[rows], near.at[rows]) for far, near in pairs], row_in.at[number])

    def stores_of(number, start, size):
        rows = pl.ds(start, size)
        return copies([(gr_ref.at[rows], gr_hbm.at[rows])], row_out.at[number])

    pairs = [(da_hbm, d_ref.at[0]), (db_hbm, d_ref.at[1]), (ua_hbm, u_ref.at[0]), (ub_hbm, u_ref.at[1])]
    pairs += [(hid_hbm, hid_ref.at[pl.ds(0, SLOTS)]), (o_hbm, o_ref), (wo_a, wo_ref.at[pl.ds(0, split)]), (wo_b, wo_ref.at[pl.ds(split, split)])]
    loads = copies(pairs, in_sems)
    for load in loads_of(0, 0, TILE) + loads[:4]:
        load.start()
    for ref in (sec_ref, slope_ref, res_ref, hid_ref):
        ref[SLOTS:, :] = jnp.zeros((PADDED - SLOTS, ref.shape[1]), ref.dtype)
    sums_ref[...] = jnp.zeros_like(sums_ref)
    bup_ref[...] = jnp.zeros_like(bup_ref)
    gain_one = row_of(g1_ref)
    mix_ref[PADDED:, :] = jnp.zeros((LANES - PADDED, width), bf16)
    place_of = slots()
    places = [(side, at) for side in range(2) for at in range(0, half, HIDDEN_STEP)]

    def step(number, start):
        @pl.when(number < TILES - 1)
        def _():
            rows_moved(number + 1, start + TILE, lambda at, size: [load.start() for load in loads_of(number + 1, at, size)])

        @pl.when(number == TILES - 2)
        def _():
            for load in loads[4:]:
                load.start()

        rows_moved(number, start, lambda at, size: [load.wait() for load in loads_of(number, at, size)])

        @pl.when(number == 0)
        def _():
            for load in loads[:4]:
                load.wait()

        rows = pl.ds(start, TILE)
        low = sec_ref[rows, :]
        second = low.astype(f32)

        def sink(side, at):
            return mul(low, d_ref[side, at : at + HIDDEN_STEP, :], 1, 1)

        total = None
        ahead = sink(*places[0])
        for turn, (side, at) in enumerate(places):
            inner = ahead
            if turn + 1 < len(places):
                ahead = sink(*places[turn + 1])
            place = slice(side * half + at, side * half + at + HIDDEN_STEP)
            pre = (inner * slope_ref[rows, place].astype(f32)).astype(bf16)
            pre_ref[rows, place] = pre
            bup_ref[:, place] += fold(pre.astype(f32))
            part = mul(pre, u_ref[side, :, at : at + HIDDEN_STEP], 1, 1)
            total = part if total is None else total + part
        hidden = second + total
        normed, spread = norm_parts(res_ref[rows, :])
        grad = norm_back(hidden * gain_one, normed, spread)
        gr_ref[rows, :] = grad
        mix_ref[rows, :] = grad.astype(bf16)
        sums_ref[0:8, :] += fold(hidden * normed)
        sums_ref[8:16, :] += fold(hidden)
        sums_ref[16:24, :] += fold(grad)
        rows_moved(number, start, lambda at, size: [store.start() for store in stores_of(number, at, size)])

    over_tiles(step)
    for load in loads[4:]:
        load.wait()
    last = copies([(g_ref, g_hbm), (delta_ref, delta_hbm)], out_sems)

    def mixed_grad(number, carry):
        side = number // 3
        place = slice(side * split, (side + 1) * split)
        lanes = slice(number % 3 * 512, number % 3 * 512 + 512)
        grad = mul(wo_ref[place, :], mix_ref[lanes, :], 1, 1).astype(bf16)
        g_ref[place, lanes] = grad
        prod = grad.astype(f32) * o_ref[place, lanes].astype(f32)
        for head in range(split // 64):
            at = (side * (split // 64) + head) * 16
            delta = jnp.sum(prod[head * 64 : head * 64 + 64], axis=0, keepdims=True)
            delta_ref[pl.ds(at, 16), lanes] = extra_rows(-delta)
        return carry

    for number in range(6):
        mixed_grad(number, 0)
    for store in last:
        store.start()
    tall = width // CHUNKS
    low = split // CHUNKS
    for side, out in enumerate((mine_ref, theirs_ref)):

        def up_block(number, carry):
            at = side * half + number * 256
            part = mul(hid_ref[...], pre_ref[:, pl.ds(at, 256)], 0, 0).astype(bf16)
            for chunk in range(CHUNKS):
                xy, z = place_of(chunk)
                for block in range(2):
                    row = (2 * number + block) * tall
                    out[xy, z, pl.ds(row, tall), :] = part[chunk * tall : (chunk + 1) * tall, block * 128 : block * 128 + 128]
            return carry

        for number in range(half // 256):
            up_block(number, 0)
        part = mul(o_ref[side * split : (side + 1) * split, :], mix_ref[...]).astype(bf16)
        for chunk in range(CHUNKS):
            xy, z = place_of(chunk)
            for block in range(width // 128):
                row = half // 128 * tall + block * low
                out[xy, z, row : row + low, :] = part[chunk * low : (chunk + 1) * low, block * 128 : block * 128 + 128]
    vectors = []
    for ref in (two_ref, sums_ref):
        for kind in range(3):
            total = jnp.sum(ref[8 * kind : 8 * kind + 8, :], axis=0, keepdims=True)
            vectors += [total[:, at : at + 128] for at in range(0, width, 128)]
    number = lax.broadcasted_iota(jnp.int32, (16, 128), 0)
    for side, out in enumerate((mine_ref, theirs_ref)):
        total = jnp.sum(bup_ref[:, side * half : (side + 1) * half], axis=0, keepdims=True)
        held = vectors + [total[:, at : at + 128] for at in range(0, half, 128)]
        each = len(held) // CHUNKS
        for chunk in range(CHUNKS):
            xy, z = place_of(chunk)
            block = jnp.zeros((16, 128), f32)
            for row in range(each):
                block = jnp.where(number == row, held[chunk * each + row], block)
            out[xy, z, FEED_ROWS - 16 :, :] = block.astype(bf16)
    for number in range(TILES):
        rows_moved(number, number * TILE, lambda at, size: [store.wait() for store in stores_of(number, at, size)])
    for store in last:
        store.wait()


def project_input(dqa_ref, dka_ref, dva_ref, dqb_ref, dkb_ref, dvb_ref, wa_ref, wb_ref, gr_ref, gi_ref, wt_ref):
    rows = wa_ref.shape[2]
    for side, w_ref in enumerate((wa_ref, wb_ref)):
        for kind in range(3):
            wt_ref[kind, side * rows : (side + 1) * rows, :] = w_ref[kind].T
    for start in range(0, SLOTS, 256):
        size = min(256, SLOTS - start)
        lanes = slice(start, start + 256)
        total = gr_ref[start : start + size, :]
        for side, refs in enumerate(((dqa_ref, dka_ref, dva_ref), (dqb_ref, dkb_ref, dvb_ref))):
            for kind, d_ref in enumerate(refs):
                total = total + mul(d_ref[:, lanes], wt_ref[kind, side * rows : (side + 1) * rows, :], 0, 0)[:size]
        gi_ref[start : start + size, :] = total


def add_pair(mine_ref, theirs_ref, *outs):
    for number, out in enumerate(outs):
        out[...] = (mine_ref[number].astype(f32) + theirs_ref[number].astype(f32)).astype(bf16)


def add_four(a_ref, b_ref, c_ref, d_ref, *outs):
    for number, out in enumerate(outs):
        held = slice(None) if len(outs) == 1 else number
        low = a_ref[held].astype(f32) + b_ref[held].astype(f32)
        out[...] = (low + (c_ref[held].astype(f32) + d_ref[held].astype(f32))).astype(bf16)


def join_four(*refs):
    first, second, outs = refs[:4], refs[4:8], refs[8:]
    for z, out in enumerate(outs):
        at = 0
        for a_ref, b_ref, c_ref, d_ref in (first, second):
            rows = a_ref.shape[1]
            low = a_ref[z].astype(f32) + b_ref[z].astype(f32)
            out[at : at + rows, :] = (low + (c_ref[z].astype(f32) + d_ref[z].astype(f32))).astype(bf16)
            at += rows


def lay_four(a_ref, b_ref, c_ref, d_ref, out_ref):
    for number, ref in enumerate((a_ref, b_ref, c_ref, d_ref)):
        out_ref[number] = ref[...]


def each_chunk(refs):
    own = lax.axis_index("dp") % CHUNKS
    for xy in range(4):
        for z in range(4):
            parts = [ref[z] for ref in (refs[3:] if xy == 3 else refs[xy : xy + 1])]
            yield (z * 4 + xy) ^ own, jnp.concatenate(parts, axis=0).astype(f32)


def spread_feed(
    a_ref, b_ref, c_ref, d_ref, e_ref, up_ref, out_ref, g2_ref, s2_ref, bd_ref, g1_ref, s1_ref, bo_ref, bup_ref, down_ref, keep_ref,
):
    width, half = up_ref.shape
    tall, low = width // CHUNKS, out_ref.shape[0] // CHUNKS
    deep = half // CHUNKS
    for chunk, held in each_chunk((a_ref, b_ref, c_ref, d_ref, e_ref)):
        rows = pl.ds(pl.multiple_of(chunk * tall, tall), tall)
        for block in range(half // 128):
            up_ref[rows, block * 128 : block * 128 + 128] = held[block * tall : (block + 1) * tall]
        rows = pl.ds(pl.multiple_of(chunk * low, low), low)
        base = half // 128 * tall
        for block in range(width // 128):
            out_ref[rows, block * 128 : block * 128 + 128] = held[base + block * low : base + (block + 1) * low]
        keep_ref[chunk] = held[FEED_ROWS - 16 : FEED_ROWS]
        rows = pl.ds(pl.multiple_of((chunk % 4 * 4 + chunk // 4) * deep, deep), deep)
        for block in range(width // 128):
            at = FEED_ROWS + block * deep
            down_ref[rows, block * 128 : block * 128 + 128] = held[at : at + deep]
    refs = [(ref, at) for ref in (g2_ref, s2_ref, bd_ref, g1_ref, s1_ref, bo_ref, bup_ref) for at in range(0, ref.shape[0], 128)]
    each = len(refs) // CHUNKS
    for number, (ref, at) in enumerate(refs):
        ref[at : at + 128] = keep_ref[number // each, number % each, :]


def spread_heads(a_ref, b_ref, c_ref, d_ref, qkv_ref, bias_ref, keep_ref):
    kinds, width, half = qkv_ref.shape
    tall = width // CHUNKS
    for chunk, held in each_chunk((a_ref, b_ref, c_ref, d_ref)):
        rows = pl.ds(pl.multiple_of(chunk * tall, tall), tall)
        for kind in range(kinds):
            for block in range(half // 128):
                row = (kind * (half // 128) + block) * tall
                qkv_ref[kind, rows, block * 128 : block * 128 + 128] = held[row : row + tall]
        keep_ref[chunk] = held[HEAD_ROWS - 16 :]
    blocks = half // 128
    for number in range(2 * blocks):
        at = number % blocks * 128
        bias_ref[number // blocks : number // blocks + 1, at : at + 128] = keep_ref[number, 0:1, :]


def shape(dims, kind=bf16):
    return jax.ShapeDtypeStruct(dims, kind)


smem = pl.BlockSpec(memory_space=pltpu.SMEM)


def specs(count):
    return [smem] + [pl.BlockSpec(memory_space=pltpu.VMEM)] * (count - 1)


def cost(flops, moved, powers=0):
    return pl.CostEstimate(flops=int(flops), bytes_accessed=int(moved), transcendentals=int(powers))


hbm = pl.BlockSpec(memory_space=pl.ANY)
vmem = pl.BlockSpec(memory_space=pltpu.VMEM)


def call_forward(sets, x, wa, wb, ba, bb):
    width = 2 * wa.shape[2]
    big, more = (width, LANES), (width // 4, LANES)
    return pl.pallas_call(
        attend_forward, name="attend_forward",
        out_shape=[shape(big), shape(big), shape(big), shape(big), shape(more)],
        in_specs=[smem, hbm, hbm, vmem, vmem, vmem], out_specs=[hbm] * 5,
        scratch_shapes=[pltpu.VMEM(a.shape, bf16) for a in (x, wa)] + [pltpu.VMEM(big, bf16)] * 4 + [pltpu.VMEM(more, bf16)]
        + [pltpu.VMEM((x.shape[1], LANES), bf16), pltpu.VMEM((CLASSES, LANES), bf16), pltpu.VMEM((CLASSES + 16, LANES), bf16)]
        + [pltpu.SemaphoreType.DMA((3,)), pltpu.SemaphoreType.DMA((5,))],
        compiler_params=params(54), cost_estimate=cost(14e9, 12e6),
    )(sets, x, wa, wb, ba, bb)


def call_feed_forward(sets, x, mixed, wo_a, wo_b, up_a, up_b, bu_a, bu_b, down_a, down_b, vecs, cot):
    rows, width = x.shape
    half = up_a.shape[1]
    outs = [shape((rows, width)), shape((rows, width)), shape((rows, width), f32), shape((rows, 2 * half)), shape((rows, width))]
    tall = (PADDED, width)
    own = [tall, mixed.shape, (width, width), (2, width, half), (2, half, width), tall]
    piece = shape((4, 4, DOWN_ROWS, 128))
    return pl.pallas_call(
        feed_forward, name="feed_forward",
        out_shape=outs + [piece, piece, shape((24, width), f32)],
        in_specs=[smem] + [hbm] * 6 + [vmem] * 2 + [hbm] * 2 + [vmem] * 6 + [hbm], out_specs=[hbm] * 7 + [vmem],
        scratch_shapes=[pltpu.VMEM(a, bf16) for a in own] + [pltpu.VMEM((PADDED, a.shape[1]), a.dtype) for a in outs]
        + [pltpu.VMEM((2, *piece.shape), bf16), pltpu.VMEM((PADDED, 2 * half), bf16)]
        + [pltpu.SemaphoreType.DMA((9,)), pltpu.SemaphoreType.DMA((6, 5)), pltpu.SemaphoreType.DMA((2,))],
        compiler_params=params(48), cost_estimate=cost(14e9, 20e6),
    )(sets, x, mixed, wo_a, wo_b, up_a, up_b, bu_a, bu_b, down_a, down_b, *vecs, cot)


def call_feed_backward(second, slope, hidden, resid, mixed, wo_a, wo_b, up_a, up_b, down_a, down_b, gain, sums):
    rows, width = second.shape
    half = up_a.shape[1]
    split = wo_a.shape[0]
    piece = shape((4, 4, FEED_ROWS, 128))
    outs = [shape((rows, width), f32), shape((2 * split, LANES)), shape((2 * split // 4, LANES))]
    given = [((PADDED, a.shape[1]), a.dtype) for a in (second, slope, hidden, resid)] + [(mixed.shape, bf16)]
    given += [((width, width), bf16), ((2, width, half), bf16), ((2, half, width), bf16)]
    return pl.pallas_call(
        feed_backward, name="feed_backward",
        out_shape=outs + [pltpu.VMEM(piece.shape, bf16)] * 2,
        in_specs=[hbm] * 11 + [vmem] * 2, out_specs=[hbm] * 3 + [vmem] * 2,
        scratch_shapes=[pltpu.VMEM(*a) for a in given] + [pltpu.VMEM((PADDED, width), f32)] + [pltpu.VMEM(a.shape, a.dtype) for a in outs[1:]]
        + [
            pltpu.VMEM((PADDED, 2 * half), bf16), pltpu.VMEM((LANES, width), bf16),
            pltpu.VMEM((24, width), f32), pltpu.VMEM((8, 2 * half), f32),
        ]
        + [pltpu.SemaphoreType.DMA(a) for a in ((6, 3), (8,), (6, 1), (2,))],
        compiler_params=params(48), cost_estimate=cost(14e9, 20e6),
    )(second, slope, hidden, resid, mixed, wo_a, wo_b, up_a, up_b, down_a, down_b, gain, sums)


def call_backward(part, sets, q, k, v, grad, lse, delta, x):
    rows = q.shape[0] // 2
    big, more = (rows, LANES), (rows // 4, LANES)
    return pl.pallas_call(
        functools.partial(attend_backward, part), name="attend_backward",
        out_shape=[shape(big), shape(big), shape(big), shape((4, 4, HEAD_ROWS, 128))],
        in_specs=[smem] + [hbm] * 7, out_specs=[hbm] * 3 + [vmem],
        scratch_shapes=[pltpu.VMEM(a, bf16) for a in (big, big, big, big, more, more, x.shape, (3, *big), (x.shape[1], LANES))]
        + [
            pltpu.VMEM((CLASSES, LANES), bf16), pltpu.VMEM((CLASSES + 16, LANES), bf16),
            pltpu.VMEM((2, 896, 896), bf16), pltpu.VMEM((2, 896, 896), bf16),
            pltpu.VMEM((rows // 64, 64, LANES), f32), pltpu.VMEM((rows // 64, 64, LANES), f32),
        ]
        + [pltpu.SemaphoreType.DMA(a) for a in ((rows // 128, 6), (1,), (rows // 128, 3))],
        compiler_params=params(50), cost_estimate=cost(9e9, 6e6),
    )(sets, q, k, v, grad, lse, delta, x)


def call_project_input(own, other, wa, wb, resid):
    return pl.pallas_call(
        project_input, name="project_input", out_shape=shape(resid.shape, f32),
        scratch_shapes=[pltpu.VMEM((3, 2 * wa.shape[2], wa.shape[1]), bf16)],
        compiler_params=params(40), cost_estimate=cost(2.4e9, 12e6),
    )(*own, *other, wa, wb, resid)


def swap(array):
    return lax.ppermute(array, "mp", [(0, 1), (1, 0)])


def exchange(array, distance):
    count = lax.axis_size("dp")
    return lax.ppermute(array, "dp", [(i, i ^ distance) for i in range(count)])


def small(kernel, name, outs, scratch=()):
    moved = 2 * sum(o.size * o.dtype.itemsize for o in outs)
    return pl.pallas_call(
        kernel, name=name, out_shape=list(outs), scratch_shapes=list(scratch),
        compiler_params=params(24), cost_estimate=cost(1e6, moved),
    )


def after(array, *earlier):
    return lax.optimization_barrier((array, *earlier))[0]


def to_plane(parts):
    return [exchange(parts[xy], xy) for xy in (1, 2, 3)]


def to_line(parts):
    return [exchange(parts[z], 4 * z) for z in (1, 2, 3)]


def plane_sum(parts, came, *earlier):
    _, rows, lanes = parts[0].shape
    return small(add_four, "add_four", [shape((rows, lanes))] * 4)(after(parts[0], *earlier), *came)


def plane_sum_joined(feed, feed_came, down, down_came, *earlier):
    rows, lanes = feed[0].shape[1] + down[0].shape[1], feed[0].shape[2]
    return small(join_four, "join_four", [shape((rows, lanes))] * 4)(after(feed[0], *earlier), *feed_came, down[0], *down_came)


def line_sum(parts, came, *earlier):
    (total,) = small(add_four, "add_four", [shape(parts[0].shape)])(after(parts[0], *earlier), *came)
    distance = CHUNKS
    while distance < lax.axis_size("dp"):
        total = total + exchange(total, distance)
        distance *= 2
    return total


def line_copies(total):
    return [exchange(total, 4 * z) for z in (1, 2, 3)]


def laid(total, came, *earlier):
    (held,) = small(lay_four, "lay_four", [shape((4, *total.shape))])(after(total, *earlier), *came)
    return held


def plane_copies(held):
    return [exchange(held, xy) for xy in (1, 2, 3)]


def across(beside, above, *earlier):
    cut = beside.shape[1] // 32 * 16
    return exchange(after(beside, *earlier)[:, :cut], 2), exchange(after(above, *earlier)[:, cut:], 1)


def halves_added(mine, came, *earlier):
    return small(add_pair, "add_pair", [shape(mine.shape[1:])] * 4)(after(mine, *earlier), came)


def per_device(
    variates, dataset, w_qkv, b_qv, w_out, b_out, gain_one, shift_one, w_up, b_up, w_down, b_down, gain_two, shift_two, cotangent,
):
    width, half = w_up.shape
    other_qkv, other_bias = pltpu.with_memory_space_constraint(swap(w_qkv), pltpu.VMEM), swap(b_qv)
    other_out, other_up, other_bup, other_down = swap(w_out), swap(w_up), swap(b_up), swap(w_down)
    q, k, v, mixed, lse = call_forward(dataset, variates, w_qkv, other_qkv, b_qv, other_bias)
    out, hidden, resid, slope, second, down_mine, down_theirs, sums = call_feed_forward(
        dataset, variates, mixed, w_out, other_out, w_up, other_up, b_up, other_bup, w_down, other_down,
        (b_out, gain_one, shift_one, b_down, gain_two, shift_two), cotangent,
    )
    down = halves_added(down_mine, swap(down_theirs))
    down_came = to_plane(down)
    grad_res, grad_mix, delta, mine, theirs = call_feed_backward(
        after(second, *down), slope, hidden, resid, mixed, w_out, other_out, w_up, other_up, w_down, other_down, gain_one, sums
    )
    feed = halves_added(mine, swap(after(theirs, *down_came)))
    feed_came = to_plane(feed)
    *other, theirs = call_backward(1, dataset, q, k, v, after(grad_mix, *feed), lse, delta, variates)
    feed = plane_sum_joined(feed, feed_came, down, down_came, theirs)
    heads_came = swap(after(theirs, *feed))
    feed_came = to_line(feed)
    *own, mine = call_backward(0, dataset, q, k, v, after(grad_mix, heads_came, *feed), lse, delta, variates)
    total = line_sum(feed, feed_came, mine)
    heads = halves_added(mine, heads_came, total)
    heads_plane = to_plane(heads)
    feed_came = line_copies(total)
    grad_in = call_project_input(own, other, w_qkv, other_qkv, after(grad_res, total, *heads))
    held = laid(total, feed_came, grad_in)
    heads = plane_sum(heads, heads_plane, grad_in)
    feed = plane_copies(after(held, *heads))[:2]
    heads = line_sum(heads, to_line(heads))
    line = line_copies(heads)
    feed = [held, *feed, *across(*feed, line[0])]
    heads = laid(heads, line)
    plane = plane_copies(heads)
    vector = shape((width,), f32)
    outs = [shape((width, half), f32), shape(w_out.shape, f32)] + [vector] * 6 + [shape((half,), f32), shape(w_down.shape, f32)]
    keep = [pltpu.VMEM((CHUNKS, 16, 128), f32)]
    grad_up, grad_out, two_gain, two_shift, down_bias, one_gain, one_shift, out_bias, up_bias, grad_down = small(
        spread_feed, "spread_feed", outs, keep
    )(*feed)
    heads = [after(heads, grad_up), *plane]
    grad_qkv, bias = small(spread_heads, "spread_heads", [shape(w_qkv.shape, f32), shape(b_qv.shape, f32)], keep)(*heads)
    return (
        out, grad_in, grad_qkv, bias, grad_out, out_bias, one_gain, one_shift, grad_up, up_bias,
        grad_down, down_bias, two_gain, two_shift,
    )


def solution(mesh):
    wide = P(("dp", "mp"), None)
    weights = (P(None, None, "mp"), P(None, "mp"), P("mp", None))
    placed = (wide, P("dp"), *weights, P(), P(), P(), P(None, "mp"), P("mp"), P("mp", None), P(), P(), P(), wide)
    given = (wide, wide, *weights, P(), P(), P(), P(None, "mp"), P("mp"), P("mp", None), P(), P(), P())
    return jax.shard_map(per_device, mesh=mesh, in_specs=placed, out_specs=given, check_vma=False)
```

```python
import functools

import jax
import jax.numpy as jnp
from jax import lax
from jax.experimental import pallas as pl
from jax.experimental.pallas import tpu as pltpu
from jax.sharding import PartitionSpec as P

HEAD_DIM = 64
SLOTS = 1424
WIDTHS = (7, 21, 321, 862)
LANES = 1536
CLASSES = 80
BIG = 1e30
EPS = 1e-05
MIB = 2**20

bf16 = jnp.bfloat16
f32 = jnp.float32


def mul(left, right, left_dim=1, right_dim=0):
    return lax.dot_general(
        left, right, (((left_dim,), (right_dim,)), ((), ())), preferred_element_type=f32
    )


def params(limit):
    return pltpu.CompilerParams(vmem_limit_bytes=limit * MIB)


def cover(width, start, stop, last):
    used = SLOTS // width * width
    low = start // width * width
    high = last if stop > used else -(-stop // width) * width
    return (low // 128 * 128, min(-(-min(high, last) // 128) * 128, LANES))


def groups_of(width, rows, step):
    found = []
    for start in range(0, rows, step):
        low, high = cover(width, start, min(start + step, rows), rows)
        if found and found[-1][2] == low and found[-1][2] + found[-1][3] == high:
            first, count = found[-1][:2]
            found[-1] = (first, count + step, low, high - low)
        else:
            found.append((start, step, low, high - low))
    return found


def near(tile):
    return jnp.clip(tile * 256 - 128, 0, LANES - 512)


def middle(tile):
    return jnp.where(tile < 2, 0, jnp.where(tile == 2, 256, jnp.where(tile == 3, 640, 768)))


FORWARD = (
    [(0, 6, 512, near, 8)],
    [(0, 6, 768, middle, 8)],
    [(0, 3, 896, lambda tile: 0 * tile, 8), (3, 4, 1536, lambda tile: 0 * tile, 2), (4, 6, 768, lambda tile: 0 * tile + 768, 8)],
    [(0, 6, 512, near, 1)],
    [(0, 6, LANES, lambda tile: 0 * tile, 1)],
)
BACKWARD = (
    [],
    groups_of(WIDTHS[2], SLOTS // WIDTHS[2] * WIDTHS[2], 256),
    [(0, 896, 0, 896)],
)


def own_bucket(sets_ref):
    return sets_ref[lax.axis_index("mp")]


def token_class(width):
    token = lax.broadcasted_iota(jnp.int32, (CLASSES, LANES), 1)
    numbers = token.astype(f32)
    held = jnp.floor((numbers + 0.5) * (1.0 / width)).astype(jnp.int32)
    held = jnp.where(token < SLOTS, held, (SLOTS - 1) // width + 1)
    row = lax.broadcasted_iota(jnp.int32, (CLASSES, LANES), 0)
    return held % CLASSES == row


def write_masks(bucket, hot_ref, bar_ref):
    for number, width in enumerate(WIDTHS):

        @pl.when(bucket == number)
        def _():
            same = token_class(width)
            hot_ref[...] = jnp.where(same, 1.0, 0.0).astype(bf16)
            bar_ref[:CLASSES, :] = jnp.where(same, 0.0, -BIG).astype(bf16)

    row = lax.broadcasted_iota(jnp.int32, (16, LANES), 0)
    bar_ref[CLASSES:, :] = jnp.where(row < 3, 1.0, 0.0).astype(bf16)


def split_three(row):
    high = row.astype(bf16)
    rest = row - high.astype(f32)
    middle = rest.astype(bf16)
    low = (rest - middle.astype(f32)).astype(bf16)
    return high, middle, low


def extra_rows(row):
    parts = [p.astype(f32) for p in split_three(row)]
    number = lax.broadcasted_iota(jnp.int32, (16, row.shape[1]), 0)
    held = jnp.where(number == 0, parts[0], jnp.where(number == 1, parts[1], jnp.where(number == 2, parts[2], 0.0)))
    return held.astype(bf16)


LOG_E = 1.4426950408889634
SAFE = 60.0


def attend_forward(
    sets_ref, x_hbm, wa_hbm, wb_ref, ba_ref, bb_ref, q_hbm, k_hbm, v_hbm, o_hbm, lse_hbm,
    x_ref, wa_ref, q_ref, k_ref, v_ref, o_ref, lse_ref, xt_ref, hot_ref, bar_ref, in_sems, out_sems,
):
    loads = [pltpu.make_async_copy(*pair, in_sems.at[i]) for i, pair in enumerate(((x_hbm, x_ref), (wa_hbm, wa_ref)))]
    for load in loads:
        load.start()
    pairs = ((q_ref, q_hbm), (k_ref, k_hbm), (v_ref, v_hbm), (o_ref, o_hbm), (lse_ref, lse_hbm))
    stores = [pltpu.make_async_copy(*pair, out_sems.at[i]) for i, pair in enumerate(pairs)]
    bucket = own_bucket(sets_ref)
    write_masks(bucket, hot_ref, bar_ref)
    tail = jnp.zeros((LANES - SLOTS, x_ref.shape[1]), bf16)
    loads[0].wait()
    xt_ref[...] = jnp.concatenate([x_ref[...], tail], axis=0).T
    worst = None
    for side, (w_ref, b_ref) in enumerate(((wa_ref, ba_ref), (wb_ref, bb_ref))):
        if side == 0:
            loads[1].wait()
        for kind, out_ref in enumerate((q_ref, k_ref, v_ref)):
            weight = w_ref[kind].T
            rows = weight.shape[0]
            if kind != 1:
                row = b_ref[kind // 2 : kind // 2 + 1, :].astype(f32)
                column = jnp.broadcast_to(row, (128, rows)).T
                column = jnp.concatenate([column] * 4, axis=1)

            def project(number, carry):
                lanes = slice(number * 512, number * 512 + 512)
                part = mul(weight, xt_ref[:, lanes])
                if kind != 1:
                    part = part + column
                if kind == 0:
                    part = part * 0.125
                out_ref[side * rows : (side + 1) * rows, lanes] = part.astype(bf16)
                return carry

            for number in range(LANES // 512):
                project(number, 0)
    for store in stores[:3]:
        store.start()
    heads = q_ref.shape[0] // 64
    for head in range(heads):
        norms = []
        for ref in (q_ref, k_ref):
            held = ref[head * 64 : head * 64 + 64, :].astype(f32)
            norms.append(jnp.max(jnp.sum(held * held, axis=0, keepdims=True), axis=1, keepdims=True))
        both = norms[0] * norms[1]
        worst = both if worst is None else jnp.maximum(worst, both)
    calm = worst[0, 0] < SAFE * SAFE

    def score(head, start, first, span):
        rows = pl.ds(pl.multiple_of(head * 64, 64), 64)
        lanes, span = pl.ds(start, 256), pl.ds(first, span)
        keys = jnp.concatenate([k_ref[rows, span], bar_ref[:CLASSES, span]], axis=0)
        quer = jnp.concatenate([q_ref[rows, lanes], hot_ref[:, lanes]], axis=0)
        return mul(keys, quer, 0, 0)

    def finish(head, start, first, span, scores, plain):
        rows = pl.ds(pl.multiple_of(head * 64, 64), 64)
        lanes = pl.ds(start, 256)
        if plain:
            raised = jnp.exp2(scores * LOG_E).astype(bf16)
        else:
            top = jnp.max(scores, axis=0, keepdims=True)
            raised = jnp.exp(scores - top).astype(bf16)
        vals = jnp.concatenate([v_ref[rows, pl.ds(first, span)], jnp.ones((16, span), bf16)], axis=0)
        total = mul(vals, raised)
        sums = total[64:65, :]
        o_ref[rows, lanes] = (total[:64, :] * (1.0 / sums)).astype(bf16)
        logs = jnp.log(sums)
        if not plain:
            logs = logs + top
        lse_ref[pl.ds(pl.multiple_of(head * 16, 16), 16), lanes] = extra_rows(-logs)

    def over(begin, end, span, first_of, together, plain):
        def turn(number, carry):
            tile = begin + number % (end - begin)
            start = pl.multiple_of(tile * 256, 256)
            first = pl.multiple_of(first_of(tile), 128)
            own = [number // (end - begin) * together + i for i in range(together)]
            held = [score(head, start, first, span) for head in own]
            for head, scores in zip(own, held):
                finish(head, start, first, span, scores, plain)
            return carry

        lax.fori_loop(0, heads // together * (end - begin), turn, 0)

    for group in range(5):
        plain = group < 3
        chosen = (bucket < 2, bucket == 2, bucket == 3, bucket < 2, bucket >= 2)[group]

        @pl.when(jnp.logical_and(chosen, calm == plain))
        def _():
            for begin, end, span, first_of, together in FORWARD[group]:
                over(begin, end, span, first_of, together, plain)

    for store in stores[3:]:
        store.start()
    for store in stores:
        store.wait()


def copies(pairs, sems):
    return [pltpu.make_async_copy(*pair, sems.at[i]) for i, pair in enumerate(pairs)]


def attend_backward(
    part, sets_ref, q_hbm, k_hbm, v_hbm, g_hbm, lse_hbm, delta_hbm, x_hbm, dq_hbm, dk_hbm, dv_hbm, piece_ref,
    q_ref, k_ref, v_ref, g_ref, lse_ref, delta_ref, x_ref, grads_ref, xt_ref,
    hot_ref, bar_ref, p_ref, s_ref, ka_ref, va_ref, head_sems, in_sems, out_sems,
):
    half = q_ref.shape[0]
    dq_ref, dk_ref, dv_ref = (grads_ref.at[kind] for kind in range(3))

    def loads_of(number):
        there = pl.ds(part * half + number * 128, 128)
        here = pl.ds(number * 128, 128)
        pairs = [(far.at[there], near.at[here]) for far, near in ((q_hbm, q_ref), (k_hbm, k_ref), (v_hbm, v_ref), (g_hbm, g_ref))]
        there = pl.ds(part * (half // 4) + number * 32, 32)
        here = pl.ds(number * 32, 32)
        pairs += [(far.at[there], near.at[here]) for far, near in ((lse_hbm, lse_ref), (delta_hbm, delta_ref))]
        return copies(pairs, head_sems.at[number])

    def stores_of(number):
        here = pl.ds(number * 128, 128)
        return copies([(near.at[here], far.at[here]) for near, far in ((dq_ref, dq_hbm), (dk_ref, dk_hbm), (dv_ref, dv_hbm))], out_sems.at[number])

    for number in range(half // 128):
        for load in loads_of(number):
            load.start()
    given = copies([(x_hbm, x_ref)], in_sems)[0]
    bucket = own_bucket(sets_ref)
    write_masks(bucket, hot_ref, bar_ref)

    def one_head(head, groups, slot):
        rows = pl.ds(pl.multiple_of(head * 64, 64), 64)
        more = pl.ds(pl.multiple_of(head * 16, 16), 16)
        single = len(groups) == 1
        if not single:
            ka_ref[slot] = jnp.zeros(ka_ref.shape[1:], f32)
            va_ref[slot] = jnp.zeros(va_ref.shape[1:], f32)
        for q0, nq, k0, nk in groups:
            span = slice(k0, k0 + nk)
            held = slice(q0, q0 + nq)
            keys = jnp.concatenate([k_ref[rows, span], bar_ref[:, span]], axis=0)
            vals = jnp.concatenate([v_ref[rows, span], bar_ref[CLASSES:, span]], axis=0)
            for start in range(q0, q0 + nq, 256):
                size = min(256, q0 + nq - start)
                lanes = slice(start, start + size)
                quer = jnp.concatenate([q_ref[rows, lanes], hot_ref[:, lanes], lse_ref[more, lanes]], axis=0)
                grad = jnp.concatenate([g_ref[rows, lanes], delta_ref[more, lanes]], axis=0)
                probs = jnp.exp2(mul(quer, keys, 0, 0) * LOG_E)
                slopes = probs * mul(grad, vals, 0, 0)
                p_ref[slot, start - q0 : start - q0 + size, :nk] = probs.astype(bf16)
                s_ref[slot, start - q0 : start - q0 + size, :nk] = slopes.astype(bf16)
            dv = mul(g_ref[rows, held], p_ref[slot, :nq, :nk])
            dk = mul(q_ref[rows, held], s_ref[slot, :nq, :nk])
            dq = mul(k_ref[rows, span], s_ref[slot, :nq, :nk], 1, 1)
            dq_ref[rows, held] = (dq * 0.125).astype(bf16)
            if single:
                dv_ref[rows, span] = dv.astype(bf16)
                dk_ref[rows, span] = dk.astype(bf16)
            else:
                va_ref[slot, :, span] += dv
                ka_ref[slot, :, span] += dk
        if single:
            rest = LANES - 896
            for out in (dq_ref, dk_ref, dv_ref):
                out[rows, 896:] = jnp.zeros((64, rest), bf16)
        else:
            dv_ref[rows, :] = va_ref[slot].astype(bf16)
            dk_ref[rows, :] = ka_ref[slot].astype(bf16)
            done = groups[-1][0] + groups[-1][1]
            if done < LANES:
                dq_ref[rows, done:] = jnp.zeros((64, LANES - done), bf16)

    def tile_of(head, start, first, span):
        rows = pl.ds(head * 64, 64)
        more = pl.ds(head * 16, 16)
        lanes, span = pl.ds(start, 256), pl.ds(first, span)
        keys = jnp.concatenate([k_ref[rows, span], bar_ref[:, span]], axis=0)
        vals = jnp.concatenate([v_ref[rows, span], bar_ref[CLASSES:, span]], axis=0)
        quer = jnp.concatenate([q_ref[rows, lanes], hot_ref[:, lanes], lse_ref[more, lanes]], axis=0)
        grad = jnp.concatenate([g_ref[rows, lanes], delta_ref[more, lanes]], axis=0)
        probs = jnp.exp2(mul(quer, keys, 0, 0) * LOG_E)
        slopes = (probs * mul(grad, vals, 0, 0)).astype(bf16)
        return probs.astype(bf16), slopes

    def take(head, start, first, span, probs, slopes):
        rows = pl.ds(head * 64, 64)
        lanes, span = pl.ds(start, 256), pl.ds(first, span)
        va_ref[head, :, span] += mul(g_ref[rows, lanes], probs)
        ka_ref[head, :, span] += mul(q_ref[rows, lanes], slopes)
        dq_ref[rows, lanes] = (mul(k_ref[rows, span], slopes, 1, 1) * 0.125).astype(bf16)

    def by_tiles(span, first_of, together):
        for number in range(half // 128):
            for load in loads_of(number):
                load.wait()
        given.start()
        ka_ref[...] = jnp.zeros_like(ka_ref)
        va_ref[...] = jnp.zeros_like(va_ref)

        def turn(tile, carry):
            start = pl.multiple_of(tile * 256, 256)
            first = pl.multiple_of(first_of(tile), 128)
            for base in range(0, half // 64, together):
                own = range(base, base + together)
                held = [tile_of(head, start, first, span) for head in own]
                for head, (probs, slopes) in zip(own, held):
                    take(head, start, first, span, probs, slopes)
            return carry

        lax.fori_loop(0, 6, turn, 0)
        for head in range(half // 64):
            rows = pl.ds(head * 64, 64)
            dv_ref[rows, :] = va_ref[head].astype(bf16)
            dk_ref[rows, :] = ka_ref[head].astype(bf16)
        for number in range(half // 128):
            for store in stores_of(number):
                store.start()

    for group in range(3):
        chosen = (bucket < 2, bucket == 2, bucket == 3)[group]

        @pl.when(chosen)
        def _():
            if group == 0:
                by_tiles(512, near, 4)
            else:

                def pair(number, carry):
                    for load in loads_of(number):
                        load.wait()

                    @pl.when(number == 0)
                    def _():
                        given.start()

                    one_head(2 * number, BACKWARD[group], 0)
                    one_head(2 * number + 1, BACKWARD[group], 1)
                    for store in stores_of(number):
                        store.start()
                    return carry

                lax.fori_loop(0, half // 128, pair, 0)

    given.wait()
    width = x_ref.shape[1]
    tail = jnp.zeros((LANES - SLOTS, width), bf16)
    xt_ref[...] = jnp.concatenate([x_ref[...], tail], axis=0).T
    tall = width // CHUNKS
    ones = jnp.ones((8, LANES), bf16)
    place_of = slots()
    sums = []
    blocks = half // 128

    def product_of(kind, carry):
        product = mul(xt_ref[...], grads_ref[kind], 1, 1).astype(bf16)
        for chunk in range(CHUNKS):
            xy, z = place_of(chunk)
            for block in range(blocks):
                row = (kind * blocks + block) * tall
                piece_ref[xy, z, pl.ds(row, tall), :] = product[chunk * tall : (chunk + 1) * tall, block * 128 : block * 128 + 128]
        return carry

    for kind in range(3):
        product_of(kind, 0)
    for d_ref in (dq_ref, dv_ref):
        total = mul(ones, d_ref[...], 1, 1)[:1]
        sums += [total[:, block * 128 : block * 128 + 128] for block in range(blocks)]
    number = lax.broadcasted_iota(jnp.int32, (16, 128), 0)
    for chunk in range(CHUNKS):
        xy, z = place_of(chunk)
        held = jnp.where(number == 0, sums[chunk] if chunk < len(sums) else 0.0, 0.0)
        piece_ref[xy, z, HEAD_ROWS - 16 :, :] = held.astype(bf16)
    for number in range(half // 128):
        for store in stores_of(number):
            store.wait()


TILE = 240
TILES = 6
PADDED = TILE * TILES
LAST = SLOTS - TILE * (TILES - 1)


def over_tiles(step):
    def body(number, carry):
        step(number, pl.multiple_of(number * TILE, TILE))
        return carry

    lax.fori_loop(0, TILES, body, 0)


def rows_moved(number, start, begin):
    if isinstance(number, int):
        begin(start, LAST if number == TILES - 1 else TILE)
        return

    @pl.when(number < TILES - 1)
    def _():
        begin(start, TILE)

    @pl.when(number == TILES - 1)
    def _():
        begin(TILE * (TILES - 1), LAST)


def mean_of(matrix):
    return jnp.sum(matrix, axis=1, keepdims=True) * (1.0 / matrix.shape[1])


def norm_parts(matrix):
    centre = matrix - mean_of(matrix)
    spread = lax.rsqrt(mean_of(centre * centre) + EPS)
    return centre * spread, spread


def norm_back(scaled, normed, spread):
    return spread * (scaled - mean_of(scaled) - normed * mean_of(scaled * normed))


def fold(matrix):
    return jnp.sum(matrix.reshape(matrix.shape[0] // 8, 8, matrix.shape[1]), axis=0)


def gelu_parts(pre):
    size = jnp.abs(pre)
    t = pl.reciprocal(1.0 + (0.3275911 * 2.0**-0.5) * size)
    bell = jnp.exp2((-0.5 * LOG_E) * (pre * pre))
    poly = 0.5 * 1.061405429
    for factor in (-1.453152027, 1.421413741, -0.284496736, 0.254829592):
        poly = poly * t + 0.5 * factor
    tail = poly * t * bell
    phi = jnp.where(pre > 0, 1.0 - tail, tail)
    return pre * phi, phi + pre * (bell * (2.0 * jnp.pi) ** -0.5)


HIDDEN_STEP = 512


def row_of(ref):
    return ref[...].astype(f32).reshape(1, ref.shape[0])


def feed_forward(
    sets_ref, x_hbm, o_hbm, wo_a, wo_b, ua_hbm, ub_hbm, ba_ref, bb_ref, da_hbm, db_hbm,
    bo_ref, g1_ref, s1_ref, bd_ref, g2_ref, s2_ref, cot_hbm,
    out_hbm, hid_hbm, res_hbm, slope_hbm, sec_hbm, gd_a, gd_b, sums_ref,
    x_ref, o_ref, wo_ref, u_ref, d_ref, cot_ref, out_ref, hid_ref, res_ref, slope_ref, low_ref, gd_ref, act_ref,
    in_sems, row_sems, out_sems,
):
    half = ua_hbm.shape[1]
    split = wo_a.shape[0]
    width = x_ref.shape[1]
    true = pl.ds(0, SLOTS)
    pairs = [(o_hbm, o_ref), (wo_a, wo_ref.at[pl.ds(0, split)]), (wo_b, wo_ref.at[pl.ds(split, split)]), (x_hbm, x_ref.at[true])]
    pairs += [(ua_hbm, u_ref.at[0]), (ub_hbm, u_ref.at[1]), (da_hbm, d_ref.at[0]), (db_hbm, d_ref.at[1]), (cot_hbm, cot_ref.at[true])]
    loads = copies(pairs, in_sems)
    for load in loads:
        load.start()
    for ref in (x_ref, cot_ref):
        ref[SLOTS:, :] = jnp.zeros((PADDED - SLOTS, width), bf16)
    bucket = own_bucket(sets_ref)
    used = SLOTS // WIDTHS[3] * WIDTHS[3]
    for number in range(3):
        used = jnp.where(bucket == number, SLOTS // WIDTHS[number] * WIDTHS[number], used)
    sums_ref[...] = jnp.zeros_like(sums_ref)
    b_out, gain_one, shift_one, b_down, gain_two, shift_two = (
        row_of(ref) for ref in (bo_ref, g1_ref, s1_ref, bd_ref, g2_ref, s2_ref)
    )
    b_up = [row_of(ref) for ref in (ba_ref, bb_ref)]
    places = [(side, at) for side in range(2) for at in range(0, half, HIDDEN_STEP)]
    last = copies([(gd_ref.at[0], gd_a), (gd_ref.at[1], gd_b)], out_sems)

    def stores_of(number, start, size):
        rows = pl.ds(start, size)
        pairs = ((out_ref, out_hbm), (hid_ref, hid_hbm), (res_ref, res_hbm), (slope_ref, slope_hbm), (low_ref, sec_hbm))
        return copies([(near.at[rows], far.at[rows]) for near, far in pairs], row_sems.at[number])

    def step(number, start):
        rows = pl.ds(start, TILE)
        resid = res_ref[rows, :] + x_ref[rows, :].astype(f32) + b_out
        res_ref[rows, :] = resid
        normed, _ = norm_parts(resid)
        hidden = normed * gain_one + shift_one
        low = hidden.astype(bf16)
        hid_ref[rows, :] = low

        @pl.when(number == 0)
        def _():
            for load in loads[4:]:
                load.wait()

        def lift(side, at):
            return mul(low, u_ref[side, :, at : at + HIDDEN_STEP]) + b_up[side][:, at : at + HIDDEN_STEP]

        total = None
        ahead = lift(*places[0])
        for turn, (side, at) in enumerate(places):
            pre = ahead
            if turn + 1 < len(places):
                ahead = lift(*places[turn + 1])
            place = slice(side * half + at, side * half + at + HIDDEN_STEP)
            active, slope = gelu_parts(pre)
            active = active.astype(bf16)
            act_ref[rows, place] = active
            slope_ref[rows, place] = slope.astype(bf16)
            part = mul(active, d_ref[side, at : at + HIDDEN_STEP, :])
            total = part if total is None else total + part
        second = hidden + total + b_down
        normed, spread = norm_parts(second)
        out_ref[rows, :] = (normed * gain_two + shift_two).astype(bf16)
        row = start + lax.broadcasted_iota(jnp.int32, (TILE, width), 0)
        top = jnp.where(row < used, cot_ref[rows, :].astype(f32), 0.0)
        grad = norm_back(top * gain_two, normed, spread)
        low_ref[rows, :] = grad.astype(bf16)
        sums_ref[0:8, :] += fold(top * normed)
        sums_ref[8:16, :] += fold(top)
        sums_ref[16:24, :] += fold(grad)
        rows_moved(number, start, lambda at, size: [store.start() for store in stores_of(number, at, size)])

    for load in loads[:4]:
        load.wait()
    for start in range(0, PADDED, 512):
        size = min(512, PADDED - start)
        res_ref[start : start + size, :] = mul(o_ref[:, start : start + 512], wo_ref[...], 0, 0)[:size]
    over_tiles(step)
    place_of = slots()
    tall = half // CHUNKS

    def block_of(number, carry):
        side, block = number // 4, number % 4
        part = mul(act_ref[:, pl.ds(pl.multiple_of(number * 4 * tall, 4 * tall), 4 * tall)], low_ref[...], 0, 0).astype(bf16)
        for z in range(4):
            xy, z_place = place_of(z * 4 + block)
            for lane in range(width // 128):
                gd_ref[side, xy, z_place, lane * tall : (lane + 1) * tall, :] = part[z * tall : (z + 1) * tall, lane * 128 : lane * 128 + 128]

        @pl.when(number == 3)
        def _():
            last[0].start()

        return carry

    lax.fori_loop(0, 8, block_of, 0)
    last[1].start()
    for number in range(TILES):
        rows_moved(number, number * TILE, lambda at, size: [store.wait() for store in stores_of(number, at, size)])
    for store in last:
        store.wait()


CHUNKS = 16
FEED_ROWS = 336
DOWN_ROWS = 256
HEAD_ROWS = 208


def slots():
    own = lax.axis_index("dp") % CHUNKS

    def place(chunk):
        held = chunk ^ own
        return held % 4, held // 4

    return place


def feed_backward(
    sec_hbm, slope_hbm, hid_hbm, res_hbm, o_hbm, wo_a, wo_b, ua_hbm, ub_hbm, da_hbm, db_hbm, g1_ref, two_ref,
    gr_hbm, g_hbm, delta_hbm, mine_ref, theirs_ref,
    sec_ref, slope_ref, hid_ref, res_ref, o_ref, wo_ref, u_ref, d_ref, gr_ref, g_ref, delta_ref,
    pre_ref, mix_ref, sums_ref, bup_ref, row_in, in_sems, row_out, out_sems,
):
    half = ua_hbm.shape[1]
    width = hid_ref.shape[1]
    split = wo_a.shape[0]

    def loads_of(number, start, size):
        rows = pl.ds(start, size)
        pairs = ((sec_hbm, sec_ref), (slope_hbm, slope_ref), (res_hbm, res_ref))
        return copies([(far.at[rows], near.at[rows]) for far, near in pairs], row_in.at[number])

    def stores_of(number, start, size):
        rows = pl.ds(start, size)
        return copies([(gr_ref.at[rows], gr_hbm.at[rows])], row_out.at[number])

    pairs = [(da_hbm, d_ref.at[0]), (db_hbm, d_ref.at[1]), (ua_hbm, u_ref.at[0]), (ub_hbm, u_ref.at[1])]
    pairs += [(hid_hbm, hid_ref.at[pl.ds(0, SLOTS)]), (o_hbm, o_ref), (wo_a, wo_ref.at[pl.ds(0, split)]), (wo_b, wo_ref.at[pl.ds(split, split)])]
    loads = copies(pairs, in_sems)
    for load in loads_of(0, 0, TILE) + loads[:4]:
        load.start()
    for ref in (sec_ref, slope_ref, res_ref, hid_ref):
        ref[SLOTS:, :] = jnp.zeros((PADDED - SLOTS, ref.shape[1]), ref.dtype)
    sums_ref[...] = jnp.zeros_like(sums_ref)
    bup_ref[...] = jnp.zeros_like(bup_ref)
    gain_one = row_of(g1_ref)
    mix_ref[PADDED:, :] = jnp.zeros((LANES - PADDED, width), bf16)
    place_of = slots()
    places = [(side, at) for side in range(2) for at in range(0, half, HIDDEN_STEP)]

    def step(number, start):
        @pl.when(number < TILES - 1)
        def _():
            rows_moved(number + 1, start + TILE, lambda at, size: [load.start() for load in loads_of(number + 1, at, size)])

        @pl.when(number == TILES - 2)
        def _():
            for load in loads[4:]:
                load.start()

        rows_moved(number, start, lambda at, size: [load.wait() for load in loads_of(number, at, size)])

        @pl.when(number == 0)
        def _():
            for load in loads[:4]:
                load.wait()

        rows = pl.ds(start, TILE)
        low = sec_ref[rows, :]
        second = low.astype(f32)

        def sink(side, at):
            return mul(low, d_ref[side, at : at + HIDDEN_STEP, :], 1, 1)

        total = None
        ahead = sink(*places[0])
        for turn, (side, at) in enumerate(places):
            inner = ahead
            if turn + 1 < len(places):
                ahead = sink(*places[turn + 1])
            place = slice(side * half + at, side * half + at + HIDDEN_STEP)
            pre = (inner * slope_ref[rows, place].astype(f32)).astype(bf16)
            pre_ref[rows, place] = pre
            bup_ref[:, place] += fold(pre.astype(f32))
            part = mul(pre, u_ref[side, :, at : at + HIDDEN_STEP], 1, 1)
            total = part if total is None else total + part
        hidden = second + total
        normed, spread = norm_parts(res_ref[rows, :])
        grad = norm_back(hidden * gain_one, normed, spread)
        gr_ref[rows, :] = grad
        mix_ref[rows, :] = grad.astype(bf16)
        sums_ref[0:8, :] += fold(hidden * normed)
        sums_ref[8:16, :] += fold(hidden)
        sums_ref[16:24, :] += fold(grad)
        rows_moved(number, start, lambda at, size: [store.start() for store in stores_of(number, at, size)])

    over_tiles(step)
    for load in loads[4:]:
        load.wait()
    last = copies([(g_ref, g_hbm), (delta_ref, delta_hbm)], out_sems)

    def mixed_grad(number, carry):
        side = number // 3
        place = slice(side * split, (side + 1) * split)
        lanes = slice(number % 3 * 512, number % 3 * 512 + 512)
        grad = mul(wo_ref[place, :], mix_ref[lanes, :], 1, 1).astype(bf16)
        g_ref[place, lanes] = grad
        prod = grad.astype(f32) * o_ref[place, lanes].astype(f32)
        for head in range(split // 64):
            at = (side * (split // 64) + head) * 16
            delta = jnp.sum(prod[head * 64 : head * 64 + 64], axis=0, keepdims=True)
            delta_ref[pl.ds(at, 16), lanes] = extra_rows(-delta)
        return carry

    for number in range(6):
        mixed_grad(number, 0)
    for store in last:
        store.start()
    tall = width // CHUNKS
    low = split // CHUNKS
    for side, out in enumerate((mine_ref, theirs_ref)):

        def up_block(number, carry):
            at = side * half + number * 256
            part = mul(hid_ref[...], pre_ref[:, pl.ds(at, 256)], 0, 0).astype(bf16)
            for chunk in range(CHUNKS):
                xy, z = place_of(chunk)
                for block in range(2):
                    row = (2 * number + block) * tall
                    out[xy, z, pl.ds(row, tall), :] = part[chunk * tall : (chunk + 1) * tall, block * 128 : block * 128 + 128]
            return carry

        for number in range(half // 256):
            up_block(number, 0)
        part = mul(o_ref[side * split : (side + 1) * split, :], mix_ref[...]).astype(bf16)
        for chunk in range(CHUNKS):
            xy, z = place_of(chunk)
            for block in range(width // 128):
                row = half // 128 * tall + block * low
                out[xy, z, row : row + low, :] = part[chunk * low : (chunk + 1) * low, block * 128 : block * 128 + 128]
    vectors = []
    for ref in (two_ref, sums_ref):
        for kind in range(3):
            total = jnp.sum(ref[8 * kind : 8 * kind + 8, :], axis=0, keepdims=True)
            vectors += [total[:, at : at + 128] for at in range(0, width, 128)]
    number = lax.broadcasted_iota(jnp.int32, (16, 128), 0)
    for side, out in enumerate((mine_ref, theirs_ref)):
        total = jnp.sum(bup_ref[:, side * half : (side + 1) * half], axis=0, keepdims=True)
        held = vectors + [total[:, at : at + 128] for at in range(0, half, 128)]
        each = len(held) // CHUNKS
        for chunk in range(CHUNKS):
            xy, z = place_of(chunk)
            block = jnp.zeros((16, 128), f32)
            for row in range(each):
                block = jnp.where(number == row, held[chunk * each + row], block)
            out[xy, z, FEED_ROWS - 16 :, :] = block.astype(bf16)
    for number in range(TILES):
        rows_moved(number, number * TILE, lambda at, size: [store.wait() for store in stores_of(number, at, size)])
    for store in last:
        store.wait()


def project_input(dqa_ref, dka_ref, dva_ref, dqb_ref, dkb_ref, dvb_ref, wa_ref, wb_ref, gr_ref, gi_ref, wt_ref):
    rows = wa_ref.shape[2]
    for side, w_ref in enumerate((wa_ref, wb_ref)):
        for kind in range(3):
            wt_ref[kind, side * rows : (side + 1) * rows, :] = w_ref[kind].T
    for start in range(0, SLOTS, 256):
        size = min(256, SLOTS - start)
        lanes = slice(start, start + 256)
        total = gr_ref[start : start + size, :]
        for side, refs in enumerate(((dqa_ref, dka_ref, dva_ref), (dqb_ref, dkb_ref, dvb_ref))):
            for kind, d_ref in enumerate(refs):
                total = total + mul(d_ref[:, lanes], wt_ref[kind, side * rows : (side + 1) * rows, :], 0, 0)[:size]
        gi_ref[start : start + size, :] = total


def add_pair(mine_ref, theirs_ref, *outs):
    for number, out in enumerate(outs):
        out[...] = (mine_ref[number].astype(f32) + theirs_ref[number].astype(f32)).astype(bf16)


def add_four(a_ref, b_ref, c_ref, d_ref, *outs):
    for number, out in enumerate(outs):
        held = slice(None) if len(outs) == 1 else number
        low = a_ref[held].astype(f32) + b_ref[held].astype(f32)
        out[...] = (low + (c_ref[held].astype(f32) + d_ref[held].astype(f32))).astype(bf16)


def join_four(*refs):
    first, second, outs = refs[:4], refs[4:8], refs[8:]
    for z, out in enumerate(outs):
        at = 0
        for a_ref, b_ref, c_ref, d_ref in (first, second):
            rows = a_ref.shape[1]
            low = a_ref[z].astype(f32) + b_ref[z].astype(f32)
            out[at : at + rows, :] = (low + (c_ref[z].astype(f32) + d_ref[z].astype(f32))).astype(bf16)
            at += rows


def lay_four(a_ref, b_ref, c_ref, d_ref, out_ref):
    for number, ref in enumerate((a_ref, b_ref, c_ref, d_ref)):
        out_ref[number] = ref[...]


def each_chunk(refs):
    own = lax.axis_index("dp") % CHUNKS
    for xy in range(4):
        for z in range(4):
            parts = [ref[z] for ref in (refs[3:] if xy == 3 else refs[xy : xy + 1])]
            yield (z * 4 + xy) ^ own, jnp.concatenate(parts, axis=0).astype(f32)


def spread_feed(
    a_ref, b_ref, c_ref, d_ref, e_ref, up_ref, out_ref, g2_ref, s2_ref, bd_ref, g1_ref, s1_ref, bo_ref, bup_ref, down_ref, keep_ref,
):
    width, half = up_ref.shape
    tall, low = width // CHUNKS, out_ref.shape[0] // CHUNKS
    deep = half // CHUNKS
    for chunk, held in each_chunk((a_ref, b_ref, c_ref, d_ref, e_ref)):
        rows = pl.ds(pl.multiple_of(chunk * tall, tall), tall)
        for block in range(half // 128):
            up_ref[rows, block * 128 : block * 128 + 128] = held[block * tall : (block + 1) * tall]
        rows = pl.ds(pl.multiple_of(chunk * low, low), low)
        base = half // 128 * tall
        for block in range(width // 128):
            out_ref[rows, block * 128 : block * 128 + 128] = held[base + block * low : base + (block + 1) * low]
        keep_ref[chunk] = held[FEED_ROWS - 16 : FEED_ROWS]
        rows = pl.ds(pl.multiple_of((chunk % 4 * 4 + chunk // 4) * deep, deep), deep)
        for block in range(width // 128):
            at = FEED_ROWS + block * deep
            down_ref[rows, block * 128 : block * 128 + 128] = held[at : at + deep]
    refs = [(ref, at) for ref in (g2_ref, s2_ref, bd_ref, g1_ref, s1_ref, bo_ref, bup_ref) for at in range(0, ref.shape[0], 128)]
    each = len(refs) // CHUNKS
    for number, (ref, at) in enumerate(refs):
        ref[at : at + 128] = keep_ref[number // each, number % each, :]


def spread_heads(a_ref, b_ref, c_ref, d_ref, qkv_ref, bias_ref, keep_ref):
    kinds, width, half = qkv_ref.shape
    tall = width // CHUNKS
    for chunk, held in each_chunk((a_ref, b_ref, c_ref, d_ref)):
        rows = pl.ds(pl.multiple_of(chunk * tall, tall), tall)
        for kind in range(kinds):
            for block in range(half // 128):
                row = (kind * (half // 128) + block) * tall
                qkv_ref[kind, rows, block * 128 : block * 128 + 128] = held[row : row + tall]
        keep_ref[chunk] = held[HEAD_ROWS - 16 :]
    blocks = half // 128
    for number in range(2 * blocks):
        at = number % blocks * 128
        bias_ref[number // blocks : number // blocks + 1, at : at + 128] = keep_ref[number, 0:1, :]


def shape(dims, kind=bf16):
    return jax.ShapeDtypeStruct(dims, kind)


smem = pl.BlockSpec(memory_space=pltpu.SMEM)


def specs(count):
    return [smem] + [pl.BlockSpec(memory_space=pltpu.VMEM)] * (count - 1)


def cost(flops, moved, powers=0):
    return pl.CostEstimate(flops=int(flops), bytes_accessed=int(moved), transcendentals=int(powers))


hbm = pl.BlockSpec(memory_space=pl.ANY)
vmem = pl.BlockSpec(memory_space=pltpu.VMEM)


def call_forward(sets, x, wa, wb, ba, bb):
    width = 2 * wa.shape[2]
    big, more = (width, LANES), (width // 4, LANES)
    return pl.pallas_call(
        attend_forward, name="attend_forward",
        out_shape=[shape(big), shape(big), shape(big), shape(big), shape(more)],
        in_specs=[smem, hbm, hbm, vmem, vmem, vmem], out_specs=[hbm] * 5,
        scratch_shapes=[pltpu.VMEM(a.shape, bf16) for a in (x, wa)] + [pltpu.VMEM(big, bf16)] * 4 + [pltpu.VMEM(more, bf16)]
        + [pltpu.VMEM((x.shape[1], LANES), bf16), pltpu.VMEM((CLASSES, LANES), bf16), pltpu.VMEM((CLASSES + 16, LANES), bf16)]
        + [pltpu.SemaphoreType.DMA((3,)), pltpu.SemaphoreType.DMA((5,))],
        compiler_params=params(54), cost_estimate=cost(14e9, 12e6),
    )(sets, x, wa, wb, ba, bb)


def call_feed_forward(sets, x, mixed, wo_a, wo_b, up_a, up_b, bu_a, bu_b, down_a, down_b, vecs, cot):
    rows, width = x.shape
    half = up_a.shape[1]
    outs = [shape((rows, width)), shape((rows, width)), shape((rows, width), f32), shape((rows, 2 * half)), shape((rows, width))]
    tall = (PADDED, width)
    own = [tall, mixed.shape, (width, width), (2, width, half), (2, half, width), tall]
    piece = shape((4, 4, DOWN_ROWS, 128))
    return pl.pallas_call(
        feed_forward, name="feed_forward",
        out_shape=outs + [piece, piece, shape((24, width), f32)],
        in_specs=[smem] + [hbm] * 6 + [vmem] * 2 + [hbm] * 2 + [vmem] * 6 + [hbm], out_specs=[hbm] * 7 + [vmem],
        scratch_shapes=[pltpu.VMEM(a, bf16) for a in own] + [pltpu.VMEM((PADDED, a.shape[1]), a.dtype) for a in outs]
        + [pltpu.VMEM((2, *piece.shape), bf16), pltpu.VMEM((PADDED, 2 * half), bf16)]
        + [pltpu.SemaphoreType.DMA((9,)), pltpu.SemaphoreType.DMA((6, 5)), pltpu.SemaphoreType.DMA((2,))],
        compiler_params=params(48), cost_estimate=cost(14e9, 20e6),
    )(sets, x, mixed, wo_a, wo_b, up_a, up_b, bu_a, bu_b, down_a, down_b, *vecs, cot)


def call_feed_backward(second, slope, hidden, resid, mixed, wo_a, wo_b, up_a, up_b, down_a, down_b, gain, sums):
    rows, width = second.shape
    half = up_a.shape[1]
    split = wo_a.shape[0]
    piece = shape((4, 4, FEED_ROWS, 128))
    outs = [shape((rows, width), f32), shape((2 * split, LANES)), shape((2 * split // 4, LANES))]
    given = [((PADDED, a.shape[1]), a.dtype) for a in (second, slope, hidden, resid)] + [(mixed.shape, bf16)]
    given += [((width, width), bf16), ((2, width, half), bf16), ((2, half, width), bf16)]
    return pl.pallas_call(
        feed_backward, name="feed_backward",
        out_shape=outs + [pltpu.VMEM(piece.shape, bf16)] * 2,
        in_specs=[hbm] * 11 + [vmem] * 2, out_specs=[hbm] * 3 + [vmem] * 2,
        scratch_shapes=[pltpu.VMEM(*a) for a in given] + [pltpu.VMEM((PADDED, width), f32)] + [pltpu.VMEM(a.shape, a.dtype) for a in outs[1:]]
        + [
            pltpu.VMEM((PADDED, 2 * half), bf16), pltpu.VMEM((LANES, width), bf16),
            pltpu.VMEM((24, width), f32), pltpu.VMEM((8, 2 * half), f32),
        ]
        + [pltpu.SemaphoreType.DMA(a) for a in ((6, 3), (8,), (6, 1), (2,))],
        compiler_params=params(48), cost_estimate=cost(14e9, 20e6),
    )(second, slope, hidden, resid, mixed, wo_a, wo_b, up_a, up_b, down_a, down_b, gain, sums)


def call_backward(part, sets, q, k, v, grad, lse, delta, x):
    rows = q.shape[0] // 2
    big, more = (rows, LANES), (rows // 4, LANES)
    return pl.pallas_call(
        functools.partial(attend_backward, part), name="attend_backward",
        out_shape=[shape(big), shape(big), shape(big), shape((4, 4, HEAD_ROWS, 128))],
        in_specs=[smem] + [hbm] * 7, out_specs=[hbm] * 3 + [vmem],
        scratch_shapes=[pltpu.VMEM(a, bf16) for a in (big, big, big, big, more, more, x.shape, (3, *big), (x.shape[1], LANES))]
        + [
            pltpu.VMEM((CLASSES, LANES), bf16), pltpu.VMEM((CLASSES + 16, LANES), bf16),
            pltpu.VMEM((2, 896, 896), bf16), pltpu.VMEM((2, 896, 896), bf16),
            pltpu.VMEM((rows // 64, 64, LANES), f32), pltpu.VMEM((rows // 64, 64, LANES), f32),
        ]
        + [pltpu.SemaphoreType.DMA(a) for a in ((rows // 128, 6), (1,), (rows // 128, 3))],
        compiler_params=params(50), cost_estimate=cost(9e9, 6e6),
    )(sets, q, k, v, grad, lse, delta, x)


def call_project_input(own, other, wa, wb, resid):
    return pl.pallas_call(
        project_input, name="project_input", out_shape=shape(resid.shape, f32),
        scratch_shapes=[pltpu.VMEM((3, 2 * wa.shape[2], wa.shape[1]), bf16)],
        compiler_params=params(40), cost_estimate=cost(2.4e9, 12e6),
    )(*own, *other, wa, wb, resid)


def swap(array):
    return lax.ppermute(array, "mp", [(0, 1), (1, 0)])


def exchange(array, distance):
    count = lax.axis_size("dp")
    return lax.ppermute(array, "dp", [(i, i ^ distance) for i in range(count)])


def small(kernel, name, outs, scratch=()):
    moved = 2 * sum(o.size * o.dtype.itemsize for o in outs)
    return pl.pallas_call(
        kernel, name=name, out_shape=list(outs), scratch_shapes=list(scratch),
        compiler_params=params(24), cost_estimate=cost(1e6, moved),
    )


def after(array, *earlier):
    return lax.optimization_barrier((array, *earlier))[0]


def to_plane(parts):
    return [exchange(parts[xy], xy) for xy in (1, 2, 3)]


def to_line(parts):
    return [exchange(parts[z], 4 * z) for z in (1, 2, 3)]


def plane_sum(parts, came, *earlier):
    _, rows, lanes = parts[0].shape
    return small(add_four, "add_four", [shape((rows, lanes))] * 4)(after(parts[0], *earlier), *came)


def plane_sum_joined(feed, feed_came, down, down_came, *earlier):
    rows, lanes = feed[0].shape[1] + down[0].shape[1], feed[0].shape[2]
    return small(join_four, "join_four", [shape((rows, lanes))] * 4)(after(feed[0], *earlier), *feed_came, down[0], *down_came)


def line_sum(parts, came, *earlier):
    (total,) = small(add_four, "add_four", [shape(parts[0].shape)])(after(parts[0], *earlier), *came)
    distance = CHUNKS
    while distance < lax.axis_size("dp"):
        total = total + exchange(total, distance)
        distance *= 2
    return total


def line_copies(total):
    return [exchange(total, 4 * z) for z in (1, 2, 3)]


def laid(total, came, *earlier):
    (held,) = small(lay_four, "lay_four", [shape((4, *total.shape))])(after(total, *earlier), *came)
    return held


def plane_copies(held):
    return [exchange(held, xy) for xy in (1, 2, 3)]


def across(beside, above, *earlier):
    cut = beside.shape[1] // 32 * 16
    return exchange(after(beside, *earlier)[:, :cut], 2), exchange(after(above, *earlier)[:, cut:], 1)


def halves_added(mine, came, *earlier):
    return small(add_pair, "add_pair", [shape(mine.shape[1:])] * 4)(after(mine, *earlier), came)


def per_device(
    variates, dataset, w_qkv, b_qv, w_out, b_out, gain_one, shift_one, w_up, b_up, w_down, b_down, gain_two, shift_two, cotangent,
):
    width, half = w_up.shape
    other_qkv, other_bias = pltpu.with_memory_space_constraint(swap(w_qkv), pltpu.VMEM), swap(b_qv)
    other_out, other_up, other_bup, other_down = swap(w_out), swap(w_up), swap(b_up), swap(w_down)
    q, k, v, mixed, lse = call_forward(dataset, variates, w_qkv, other_qkv, b_qv, other_bias)
    out, hidden, resid, slope, second, down_mine, down_theirs, sums = call_feed_forward(
        dataset, variates, mixed, w_out, other_out, w_up, other_up, b_up, other_bup, w_down, other_down,
        (b_out, gain_one, shift_one, b_down, gain_two, shift_two), cotangent,
    )
    down = halves_added(down_mine, swap(down_theirs))
    down_came = to_plane(down)
    grad_res, grad_mix, delta, mine, theirs = call_feed_backward(
        after(second, *down), slope, hidden, resid, mixed, w_out, other_out, w_up, other_up, w_down, other_down, gain_one, sums
    )
    feed = halves_added(mine, swap(after(theirs, *down_came)))
    feed_came = to_plane(feed)
    *other, theirs = call_backward(1, dataset, q, k, v, after(grad_mix, *feed), lse, delta, variates)
    feed = plane_sum_joined(feed, feed_came, down, down_came, theirs)
    heads_came = swap(after(theirs, *feed))
    feed_came = to_line(feed)
    *own, mine = call_backward(0, dataset, q, k, v, after(grad_mix, heads_came, *feed), lse, delta, variates)
    total = line_sum(feed, feed_came, mine)
    heads = halves_added(mine, heads_came, total)
    heads_plane = to_plane(heads)
    feed_came = line_copies(total)
    grad_in = call_project_input(own, other, w_qkv, other_qkv, after(grad_res, total, *heads))
    held = laid(total, feed_came, grad_in)
    heads = plane_sum(heads, heads_plane, grad_in)
    line = to_line(heads)
    feed = plane_copies(after(held, line[0]))[:2]
    heads = line_sum(heads, line)
    line = line_copies(heads)
    heads = laid(heads, line)
    feed = [held, *feed, *across(*feed, heads)]
    plane = plane_copies(heads)
    vector = shape((width,), f32)
    outs = [shape((width, half), f32), shape(w_out.shape, f32)] + [vector] * 6 + [shape((half,), f32), shape(w_down.shape, f32)]
    keep = [pltpu.VMEM((CHUNKS, 16, 128), f32)]
    grad_up, grad_out, two_gain, two_shift, down_bias, one_gain, one_shift, out_bias, up_bias, grad_down = small(
        spread_feed, "spread_feed", outs, keep
    )(*feed)
    heads = [after(heads, grad_up), *plane]
    grad_qkv, bias = small(spread_heads, "spread_heads", [shape(w_qkv.shape, f32), shape(b_qv.shape, f32)], keep)(*heads)
    return (
        out, grad_in, grad_qkv, bias, grad_out, out_bias, one_gain, one_shift, grad_up, up_bias,
        grad_down, down_bias, two_gain, two_shift,
    )


def solution(mesh):
    wide = P(("dp", "mp"), None)
    weights = (P(None, None, "mp"), P(None, "mp"), P("mp", None))
    placed = (wide, P("dp"), *weights, P(), P(), P(), P(None, "mp"), P("mp"), P("mp", None), P(), P(), P(), wide)
    given = (wide, wide, *weights, P(), P(), P(), P(None, "mp"), P("mp"), P("mp", None), P(), P(), P())
    return jax.shard_map(per_device, mesh=mesh, in_specs=placed, out_specs=given, check_vma=False)
```

```python
import functools

import jax
import jax.numpy as jnp
from jax import lax
from jax.experimental import pallas as pl
from jax.experimental.pallas import tpu as pltpu
from jax.sharding import PartitionSpec as P

HEAD_DIM = 64
SLOTS = 1424
WIDTHS = (7, 21, 321, 862)
LANES = 1536
CLASSES = 80
BIG = 1e30
EPS = 1e-05
MIB = 2**20

bf16 = jnp.bfloat16
f32 = jnp.float32


def mul(left, right, left_dim=1, right_dim=0):
    return lax.dot_general(
        left, right, (((left_dim,), (right_dim,)), ((), ())), preferred_element_type=f32
    )


def params(limit):
    return pltpu.CompilerParams(vmem_limit_bytes=limit * MIB)


def cover(width, start, stop, last):
    used = SLOTS // width * width
    low = start // width * width
    high = last if stop > used else -(-stop // width) * width
    return (low // 128 * 128, min(-(-min(high, last) // 128) * 128, LANES))


def groups_of(width, rows, step):
    found = []
    for start in range(0, rows, step):
        low, high = cover(width, start, min(start + step, rows), rows)
        if found and found[-1][2] == low and found[-1][2] + found[-1][3] == high:
            first, count = found[-1][:2]
            found[-1] = (first, count + step, low, high - low)
        else:
            found.append((start, step, low, high - low))
    return found


def near(tile):
    return jnp.clip(tile * 256 - 128, 0, LANES - 512)


def middle(tile):
    return jnp.where(tile < 2, 0, jnp.where(tile == 2, 256, jnp.where(tile == 3, 640, 768)))


FORWARD = (
    [(0, 6, 512, near, 8)],
    [(0, 6, 768, middle, 8)],
    [(0, 3, 896, lambda tile: 0 * tile, 8), (3, 4, 1536, lambda tile: 0 * tile, 4), (4, 6, 768, lambda tile: 0 * tile + 768, 8)],
    [(0, 6, 512, near, 1)],
    [(0, 6, LANES, lambda tile: 0 * tile, 1)],
)
BACKWARD = (
    [],
    groups_of(WIDTHS[2], SLOTS // WIDTHS[2] * WIDTHS[2], 256),
    [(0, 896, 0, 896)],
)


def own_bucket(sets_ref):
    return sets_ref[lax.axis_index("mp")]


def token_class(width):
    token = lax.broadcasted_iota(jnp.int32, (CLASSES, LANES), 1)
    numbers = token.astype(f32)
    held = jnp.floor((numbers + 0.5) * (1.0 / width)).astype(jnp.int32)
    held = jnp.where(token < SLOTS, held, (SLOTS - 1) // width + 1)
    row = lax.broadcasted_iota(jnp.int32, (CLASSES, LANES), 0)
    return held % CLASSES == row


def write_masks(bucket, hot_ref, bar_ref):
    for number, width in enumerate(WIDTHS):

        @pl.when(bucket == number)
        def _():
            same = token_class(width)
            hot_ref[...] = jnp.where(same, 1.0, 0.0).astype(bf16)
            bar_ref[:CLASSES, :] = jnp.where(same, 0.0, -BIG).astype(bf16)

    row = lax.broadcasted_iota(jnp.int32, (16, LANES), 0)
    bar_ref[CLASSES:, :] = jnp.where(row < 3, 1.0, 0.0).astype(bf16)


def split_three(row):
    high = row.astype(bf16)
    rest = row - high.astype(f32)
    middle = rest.astype(bf16)
    low = (rest - middle.astype(f32)).astype(bf16)
    return high, middle, low


def extra_rows(row):
    parts = [p.astype(f32) for p in split_three(row)]
    number = lax.broadcasted_iota(jnp.int32, (16, row.shape[1]), 0)
    held = jnp.where(number == 0, parts[0], jnp.where(number == 1, parts[1], jnp.where(number == 2, parts[2], 0.0)))
    return held.astype(bf16)


LOG_E = 1.4426950408889634
SAFE = 60.0


def attend_forward(
    sets_ref, x_hbm, wa_hbm, wb_ref, ba_ref, bb_ref, q_hbm, k_hbm, v_hbm, o_hbm, lse_hbm,
    x_ref, wa_ref, q_ref, k_ref, v_ref, o_ref, lse_ref, xt_ref, hot_ref, bar_ref, in_sems, out_sems,
):
    loads = [pltpu.make_async_copy(*pair, in_sems.at[i]) for i, pair in enumerate(((x_hbm, x_ref), (wa_hbm, wa_ref)))]
    for load in loads:
        load.start()
    pairs = ((q_ref, q_hbm), (k_ref, k_hbm), (v_ref, v_hbm), (o_ref, o_hbm), (lse_ref, lse_hbm))
    stores = [pltpu.make_async_copy(*pair, out_sems.at[i]) for i, pair in enumerate(pairs)]
    bucket = own_bucket(sets_ref)
    write_masks(bucket, hot_ref, bar_ref)
    tail = jnp.zeros((LANES - SLOTS, x_ref.shape[1]), bf16)
    loads[0].wait()
    xt_ref[...] = jnp.concatenate([x_ref[...], tail], axis=0).T
    worst = None
    for side, (w_ref, b_ref) in enumerate(((wa_ref, ba_ref), (wb_ref, bb_ref))):
        if side == 0:
            loads[1].wait()
        for kind, out_ref in enumerate((q_ref, k_ref, v_ref)):
            weight = w_ref[kind].T
            rows = weight.shape[0]
            if kind != 1:
                row = b_ref[kind // 2 : kind // 2 + 1, :].astype(f32)
                column = jnp.broadcast_to(row, (128, rows)).T
                column = jnp.concatenate([column] * 4, axis=1)

            def project(number, carry):
                lanes = slice(number * 512, number * 512 + 512)
                part = mul(weight, xt_ref[:, lanes])
                if kind != 1:
                    part = part + column
                if kind == 0:
                    part = part * 0.125
                out_ref[side * rows : (side + 1) * rows, lanes] = part.astype(bf16)
                return carry

            for number in range(LANES // 512):
                project(number, 0)
    for store in stores[:3]:
        store.start()
    heads = q_ref.shape[0] // 64
    for head in range(heads):
        norms = []
        for ref in (q_ref, k_ref):
            held = ref[head * 64 : head * 64 + 64, :].astype(f32)
            norms.append(jnp.max(jnp.sum(held * held, axis=0, keepdims=True), axis=1, keepdims=True))
        both = norms[0] * norms[1]
        worst = both if worst is None else jnp.maximum(worst, both)
    calm = worst[0, 0] < SAFE * SAFE

    def score(head, start, first, span):
        rows = pl.ds(pl.multiple_of(head * 64, 64), 64)
        lanes, span = pl.ds(start, 256), pl.ds(first, span)
        keys = jnp.concatenate([k_ref[rows, span], bar_ref[:CLASSES, span]], axis=0)
        quer = jnp.concatenate([q_ref[rows, lanes], hot_ref[:, lanes]], axis=0)
        return mul(keys, quer, 0, 0)

    def finish(head, start, first, span, scores, plain):
        rows = pl.ds(pl.multiple_of(head * 64, 64), 64)
        lanes = pl.ds(start, 256)
        if plain:
            raised = jnp.exp2(scores * LOG_E).astype(bf16)
        else:
            top = jnp.max(scores, axis=0, keepdims=True)
            raised = jnp.exp(scores - top).astype(bf16)
        vals = jnp.concatenate([v_ref[rows, pl.ds(first, span)], jnp.ones((16, span), bf16)], axis=0)
        total = mul(vals, raised)
        sums = total[64:65, :]
        o_ref[rows, lanes] = (total[:64, :] * (1.0 / sums)).astype(bf16)
        logs = jnp.log(sums)
        if not plain:
            logs = logs + top
        lse_ref[pl.ds(pl.multiple_of(head * 16, 16), 16), lanes] = extra_rows(-logs)

    def over(begin, end, span, first_of, together, plain):
        def turn(number, carry):
            tile = begin + number % (end - begin)
            start = pl.multiple_of(tile * 256, 256)
            first = pl.multiple_of(first_of(tile), 128)
            own = [number // (end - begin) * together + i for i in range(together)]
            held = [score(head, start, first, span) for head in own]
            for head, scores in zip(own, held):
                finish(head, start, first, span, scores, plain)
            return carry

        lax.fori_loop(0, heads // together * (end - begin), turn, 0)

    for group in range(5):
        plain = group < 3
        chosen = (bucket < 2, bucket == 2, bucket == 3, bucket < 2, bucket >= 2)[group]

        @pl.when(jnp.logical_and(chosen, calm == plain))
        def _():
            for begin, end, span, first_of, together in FORWARD[group]:
                over(begin, end, span, first_of, together, plain)

    for store in stores[3:]:
        store.start()
    for store in stores:
        store.wait()


def copies(pairs, sems):
    return [pltpu.make_async_copy(*pair, sems.at[i]) for i, pair in enumerate(pairs)]


def attend_backward(
    part, sets_ref, q_hbm, k_hbm, v_hbm, g_hbm, lse_hbm, delta_hbm, x_hbm, dq_hbm, dk_hbm, dv_hbm, piece_ref,
    q_ref, k_ref, v_ref, g_ref, lse_ref, delta_ref, x_ref, grads_ref, xt_ref,
    hot_ref, bar_ref, p_ref, s_ref, ka_ref, va_ref, head_sems, in_sems, out_sems,
):
    half = q_ref.shape[0]
    dq_ref, dk_ref, dv_ref = (grads_ref.at[kind] for kind in range(3))

    def loads_of(number):
        there = pl.ds(part * half + number * 128, 128)
        here = pl.ds(number * 128, 128)
        pairs = [(far.at[there], near.at[here]) for far, near in ((q_hbm, q_ref), (k_hbm, k_ref), (v_hbm, v_ref), (g_hbm, g_ref))]
        there = pl.ds(part * (half // 4) + number * 32, 32)
        here = pl.ds(number * 32, 32)
        pairs += [(far.at[there], near.at[here]) for far, near in ((lse_hbm, lse_ref), (delta_hbm, delta_ref))]
        return copies(pairs, head_sems.at[number])

    def stores_of(number):
        here = pl.ds(number * 128, 128)
        return copies([(near.at[here], far.at[here]) for near, far in ((dq_ref, dq_hbm), (dk_ref, dk_hbm), (dv_ref, dv_hbm))], out_sems.at[number])

    for number in range(half // 128):
        for load in loads_of(number):
            load.start()
    given = copies([(x_hbm, x_ref)], in_sems)[0]
    bucket = own_bucket(sets_ref)
    write_masks(bucket, hot_ref, bar_ref)

    def one_head(head, groups, slot):
        rows = pl.ds(pl.multiple_of(head * 64, 64), 64)
        more = pl.ds(pl.multiple_of(head * 16, 16), 16)
        single = len(groups) == 1
        if not single:
            ka_ref[slot] = jnp.zeros(ka_ref.shape[1:], f32)
            va_ref[slot] = jnp.zeros(va_ref.shape[1:], f32)
        for q0, nq, k0, nk in groups:
            span = slice(k0, k0 + nk)
            held = slice(q0, q0 + nq)
            keys = jnp.concatenate([k_ref[rows, span], bar_ref[:, span]], axis=0)
            vals = jnp.concatenate([v_ref[rows, span], bar_ref[CLASSES:, span]], axis=0)
            for start in range(q0, q0 + nq, 256):
                size = min(256, q0 + nq - start)
                lanes = slice(start, start + size)
                quer = jnp.concatenate([q_ref[rows, lanes], hot_ref[:, lanes], lse_ref[more, lanes]], axis=0)
                grad = jnp.concatenate([g_ref[rows, lanes], delta_ref[more, lanes]], axis=0)
                probs = jnp.exp2(mul(quer, keys, 0, 0) * LOG_E)
                slopes = probs * mul(grad, vals, 0, 0)
                p_ref[slot, start - q0 : start - q0 + size, :nk] = probs.astype(bf16)
                s_ref[slot, start - q0 : start - q0 + size, :nk] = slopes.astype(bf16)
            dv = mul(g_ref[rows, held], p_ref[slot, :nq, :nk])
            dk = mul(q_ref[rows, held], s_ref[slot, :nq, :nk])
            dq = mul(k_ref[rows, span], s_ref[slot, :nq, :nk], 1, 1)
            dq_ref[rows, held] = (dq * 0.125).astype(bf16)
            if single:
                dv_ref[rows, span] = dv.astype(bf16)
                dk_ref[rows, span] = dk.astype(bf16)
            else:
                va_ref[slot, :, span] += dv
                ka_ref[slot, :, span] += dk
        if single:
            rest = LANES - 896
            for out in (dq_ref, dk_ref, dv_ref):
                out[rows, 896:] = jnp.zeros((64, rest), bf16)
        else:
            dv_ref[rows, :] = va_ref[slot].astype(bf16)
            dk_ref[rows, :] = ka_ref[slot].astype(bf16)
            done = groups[-1][0] + groups[-1][1]
            if done < LANES:
                dq_ref[rows, done:] = jnp.zeros((64, LANES - done), bf16)

    def tile_of(head, start, first, span):
        rows = pl.ds(head * 64, 64)
        more = pl.ds(head * 16, 16)
        lanes, span = pl.ds(start, 256), pl.ds(first, span)
        keys = jnp.concatenate([k_ref[rows, span], bar_ref[:, span]], axis=0)
        vals = jnp.concatenate([v_ref[rows, span], bar_ref[CLASSES:, span]], axis=0)
        quer = jnp.concatenate([q_ref[rows, lanes], hot_ref[:, lanes], lse_ref[more, lanes]], axis=0)
        grad = jnp.concatenate([g_ref[rows, lanes], delta_ref[more, lanes]], axis=0)
        probs = jnp.exp2(mul(quer, keys, 0, 0) * LOG_E)
        slopes = (probs * mul(grad, vals, 0, 0)).astype(bf16)
        return probs.astype(bf16), slopes

    def take(head, start, first, span, probs, slopes):
        rows = pl.ds(head * 64, 64)
        lanes, span = pl.ds(start, 256), pl.ds(first, span)
        va_ref[head, :, span] += mul(g_ref[rows, lanes], probs)
        ka_ref[head, :, span] += mul(q_ref[rows, lanes], slopes)
        dq_ref[rows, lanes] = (mul(k_ref[rows, span], slopes, 1, 1) * 0.125).astype(bf16)

    def by_tiles(span, first_of, together):
        for number in range(half // 128):
            for load in loads_of(number):
                load.wait()
        given.start()
        ka_ref[...] = jnp.zeros_like(ka_ref)
        va_ref[...] = jnp.zeros_like(va_ref)

        def turn(tile, carry):
            start = pl.multiple_of(tile * 256, 256)
            first = pl.multiple_of(first_of(tile), 128)
            for base in range(0, half // 64, together):
                own = range(base, base + together)
                held = [tile_of(head, start, first, span) for head in own]
                for head, (probs, slopes) in zip(own, held):
                    take(head, start, first, span, probs, slopes)
            return carry

        lax.fori_loop(0, 6, turn, 0)
        for head in range(half // 64):
            rows = pl.ds(head * 64, 64)
            dv_ref[rows, :] = va_ref[head].astype(bf16)
            dk_ref[rows, :] = ka_ref[head].astype(bf16)
        for number in range(half // 128):
            for store in stores_of(number):
                store.start()

    for group in range(3):
        chosen = (bucket < 2, bucket == 2, bucket == 3)[group]

        @pl.when(chosen)
        def _():
            if group == 0:
                by_tiles(512, near, 4)
            else:

                def pair(number, carry):
                    for load in loads_of(number):
                        load.wait()

                    @pl.when(number == 0)
                    def _():
                        given.start()

                    one_head(2 * number, BACKWARD[group], 0)
                    one_head(2 * number + 1, BACKWARD[group], 1)
                    for store in stores_of(number):
                        store.start()
                    return carry

                lax.fori_loop(0, half // 128, pair, 0)

    given.wait()
    width = x_ref.shape[1]
    tail = jnp.zeros((LANES - SLOTS, width), bf16)
    xt_ref[...] = jnp.concatenate([x_ref[...], tail], axis=0).T
    tall = width // CHUNKS
    ones = jnp.ones((8, LANES), bf16)
    place_of = slots()
    sums = []
    blocks = half // 128

    def product_of(kind, carry):
        product = mul(xt_ref[...], grads_ref[kind], 1, 1).astype(bf16)
        for chunk in range(CHUNKS):
            xy, z = place_of(chunk)
            for block in range(blocks):
                row = (kind * blocks + block) * tall
                piece_ref[xy, z, pl.ds(row, tall), :] = product[chunk * tall : (chunk + 1) * tall, block * 128 : block * 128 + 128]
        return carry

    for kind in range(3):
        product_of(kind, 0)
    for d_ref in (dq_ref, dv_ref):
        total = mul(ones, d_ref[...], 1, 1)[:1]
        sums += [total[:, block * 128 : block * 128 + 128] for block in range(blocks)]
    number = lax.broadcasted_iota(jnp.int32, (16, 128), 0)
    for chunk in range(CHUNKS):
        xy, z = place_of(chunk)
        held = jnp.where(number == 0, sums[chunk] if chunk < len(sums) else 0.0, 0.0)
        piece_ref[xy, z, HEAD_ROWS - 16 :, :] = held.astype(bf16)
    for number in range(half // 128):
        for store in stores_of(number):
            store.wait()


TILE = 240
TILES = 6
PADDED = TILE * TILES
LAST = SLOTS - TILE * (TILES - 1)


def over_tiles(step):
    def body(number, carry):
        step(number, pl.multiple_of(number * TILE, TILE))
        return carry

    lax.fori_loop(0, TILES, body, 0)


def rows_moved(number, start, begin):
    if isinstance(number, int):
        begin(start, LAST if number == TILES - 1 else TILE)
        return

    @pl.when(number < TILES - 1)
    def _():
        begin(start, TILE)

    @pl.when(number == TILES - 1)
    def _():
        begin(TILE * (TILES - 1), LAST)


def mean_of(matrix):
    return jnp.sum(matrix, axis=1, keepdims=True) * (1.0 / matrix.shape[1])


def norm_parts(matrix):
    centre = matrix - mean_of(matrix)
    spread = lax.rsqrt(mean_of(centre * centre) + EPS)
    return centre * spread, spread


def norm_back(scaled, normed, spread):
    return spread * (scaled - mean_of(scaled) - normed * mean_of(scaled * normed))


def fold(matrix):
    return jnp.sum(matrix.reshape(matrix.shape[0] // 8, 8, matrix.shape[1]), axis=0)


def gelu_parts(pre):
    size = jnp.abs(pre)
    t = pl.reciprocal(1.0 + (0.3275911 * 2.0**-0.5) * size)
    bell = jnp.exp2((-0.5 * LOG_E) * (pre * pre))
    poly = 0.5 * 1.061405429
    for factor in (-1.453152027, 1.421413741, -0.284496736, 0.254829592):
        poly = poly * t + 0.5 * factor
    tail = poly * t * bell
    phi = jnp.where(pre > 0, 1.0 - tail, tail)
    return pre * phi, phi + pre * (bell * (2.0 * jnp.pi) ** -0.5)


HIDDEN_STEP = 512


def row_of(ref):
    return ref[...].astype(f32).reshape(1, ref.shape[0])


def feed_forward(
    sets_ref, x_hbm, o_hbm, wo_a, wo_b, ua_hbm, ub_hbm, ba_ref, bb_ref, da_hbm, db_hbm,
    bo_ref, g1_ref, s1_ref, bd_ref, g2_ref, s2_ref, cot_hbm,
    out_hbm, hid_hbm, res_hbm, slope_hbm, sec_hbm, gd_a, gd_b, sums_ref,
    x_ref, o_ref, wo_ref, u_ref, d_ref, cot_ref, out_ref, hid_ref, res_ref, slope_ref, low_ref, gd_ref, act_ref,
    in_sems, row_sems, out_sems,
):
    half = ua_hbm.shape[1]
    split = wo_a.shape[0]
    width = x_ref.shape[1]
    true = pl.ds(0, SLOTS)
    pairs = [(o_hbm, o_ref), (wo_a, wo_ref.at[pl.ds(0, split)]), (wo_b, wo_ref.at[pl.ds(split, split)]), (x_hbm, x_ref.at[true])]
    pairs += [(ua_hbm, u_ref.at[0]), (ub_hbm, u_ref.at[1]), (da_hbm, d_ref.at[0]), (db_hbm, d_ref.at[1]), (cot_hbm, cot_ref.at[true])]
    loads = copies(pairs, in_sems)
    for load in loads:
        load.start()
    for ref in (x_ref, cot_ref):
        ref[SLOTS:, :] = jnp.zeros((PADDED - SLOTS, width), bf16)
    bucket = own_bucket(sets_ref)
    used = SLOTS // WIDTHS[3] * WIDTHS[3]
    for number in range(3):
        used = jnp.where(bucket == number, SLOTS // WIDTHS[number] * WIDTHS[number], used)
    sums_ref[...] = jnp.zeros_like(sums_ref)
    b_out, gain_one, shift_one, b_down, gain_two, shift_two = (
        row_of(ref) for ref in (bo_ref, g1_ref, s1_ref, bd_ref, g2_ref, s2_ref)
    )
    b_up = [row_of(ref) for ref in (ba_ref, bb_ref)]
    places = [(side, at) for side in range(2) for at in range(0, half, HIDDEN_STEP)]
    last = copies([(gd_ref.at[0], gd_a), (gd_ref.at[1], gd_b)], out_sems)

    def stores_of(number, start, size):
        rows = pl.ds(start, size)
        pairs = ((out_ref, out_hbm), (hid_ref, hid_hbm), (res_ref, res_hbm), (slope_ref, slope_hbm), (low_ref, sec_hbm))
        return copies([(near.at[rows], far.at[rows]) for near, far in pairs], row_sems.at[number])

    def step(number, start):
        rows = pl.ds(start, TILE)
        resid = res_ref[rows, :] + x_ref[rows, :].astype(f32) + b_out
        res_ref[rows, :] = resid
        normed, _ = norm_parts(resid)
        hidden = normed * gain_one + shift_one
        low = hidden.astype(bf16)
        hid_ref[rows, :] = low

        @pl.when(number == 0)
        def _():
            for load in loads[4:]:
                load.wait()

        def lift(side, at):
            return mul(low, u_ref[side, :, at : at + HIDDEN_STEP]) + b_up[side][:, at : at + HIDDEN_STEP]

        total = None
        ahead = lift(*places[0])
        for turn, (side, at) in enumerate(places):
            pre = ahead
            if turn + 1 < len(places):
                ahead = lift(*places[turn + 1])
            place = slice(side * half + at, side * half + at + HIDDEN_STEP)
            active, slope = gelu_parts(pre)
            active = active.astype(bf16)
            act_ref[rows, place] = active
            slope_ref[rows, place] = slope.astype(bf16)
            part = mul(active, d_ref[side, at : at + HIDDEN_STEP, :])
            total = part if total is None else total + part
        second = hidden + total + b_down
        normed, spread = norm_parts(second)
        out_ref[rows, :] = (normed * gain_two + shift_two).astype(bf16)
        row = start + lax.broadcasted_iota(jnp.int32, (TILE, width), 0)
        top = jnp.where(row < used, cot_ref[rows, :].astype(f32), 0.0)
        grad = norm_back(top * gain_two, normed, spread)
        low_ref[rows, :] = grad.astype(bf16)
        sums_ref[0:8, :] += fold(top * normed)
        sums_ref[8:16, :] += fold(top)
        sums_ref[16:24, :] += fold(grad)
        rows_moved(number, start, lambda at, size: [store.start() for store in stores_of(number, at, size)])

    for load in loads[:4]:
        load.wait()
    for start in range(0, PADDED, 512):
        size = min(512, PADDED - start)
        res_ref[start : start + size, :] = mul(o_ref[:, start : start + 512], wo_ref[...], 0, 0)[:size]
    over_tiles(step)
    place_of = slots()
    tall = half // CHUNKS

    def block_of(number, carry):
        side, block = number // 4, number % 4
        part = mul(act_ref[:, pl.ds(pl.multiple_of(number * 4 * tall, 4 * tall), 4 * tall)], low_ref[...], 0, 0).astype(bf16)
        for z in range(4):
            xy, z_place = place_of(z * 4 + block)
            for lane in range(width // 128):
                gd_ref[side, xy, z_place, lane * tall : (lane + 1) * tall, :] = part[z * tall : (z + 1) * tall, lane * 128 : lane * 128 + 128]

        @pl.when(number == 3)
        def _():
            last[0].start()

        return carry

    lax.fori_loop(0, 8, block_of, 0)
    last[1].start()
    for number in range(TILES):
        rows_moved(number, number * TILE, lambda at, size: [store.wait() for store in stores_of(number, at, size)])
    for store in last:
        store.wait()


CHUNKS = 16
FEED_ROWS = 336
DOWN_ROWS = 256
HEAD_ROWS = 208


def slots():
    own = lax.axis_index("dp") % CHUNKS

    def place(chunk):
        held = chunk ^ own
        return held % 4, held // 4

    return place


def feed_backward(
    sec_hbm, slope_hbm, hid_hbm, res_hbm, o_hbm, wo_a, wo_b, ua_hbm, ub_hbm, da_hbm, db_hbm, g1_ref, two_ref,
    gr_hbm, g_hbm, delta_hbm, mine_ref, theirs_ref,
    sec_ref, slope_ref, hid_ref, res_ref, o_ref, wo_ref, u_ref, d_ref, gr_ref, g_ref, delta_ref,
    pre_ref, mix_ref, sums_ref, bup_ref, row_in, in_sems, row_out, out_sems,
):
    half = ua_hbm.shape[1]
    width = hid_ref.shape[1]
    split = wo_a.shape[0]

    def loads_of(number, start, size):
        rows = pl.ds(start, size)
        pairs = ((sec_hbm, sec_ref), (slope_hbm, slope_ref), (res_hbm, res_ref))
        return copies([(far.at[rows], near.at[rows]) for far, near in pairs], row_in.at[number])

    def stores_of(number, start, size):
        rows = pl.ds(start, size)
        return copies([(gr_ref.at[rows], gr_hbm.at[rows])], row_out.at[number])

    pairs = [(da_hbm, d_ref.at[0]), (db_hbm, d_ref.at[1]), (ua_hbm, u_ref.at[0]), (ub_hbm, u_ref.at[1])]
    pairs += [(hid_hbm, hid_ref.at[pl.ds(0, SLOTS)]), (o_hbm, o_ref), (wo_a, wo_ref.at[pl.ds(0, split)]), (wo_b, wo_ref.at[pl.ds(split, split)])]
    loads = copies(pairs, in_sems)
    for load in loads_of(0, 0, TILE) + loads[:4]:
        load.start()
    for ref in (sec_ref, slope_ref, res_ref, hid_ref):
        ref[SLOTS:, :] = jnp.zeros((PADDED - SLOTS, ref.shape[1]), ref.dtype)
    sums_ref[...] = jnp.zeros_like(sums_ref)
    bup_ref[...] = jnp.zeros_like(bup_ref)
    gain_one = row_of(g1_ref)
    mix_ref[PADDED:, :] = jnp.zeros((LANES - PADDED, width), bf16)
    place_of = slots()
    places = [(side, at) for side in range(2) for at in range(0, half, HIDDEN_STEP)]

    def step(number, start):
        @pl.when(number < TILES - 1)
        def _():
            rows_moved(number + 1, start + TILE, lambda at, size: [load.start() for load in loads_of(number + 1, at, size)])

        @pl.when(number == TILES - 2)
        def _():
            for load in loads[4:]:
                load.start()

        rows_moved(number, start, lambda at, size: [load.wait() for load in loads_of(number, at, size)])

        @pl.when(number == 0)
        def _():
            for load in loads[:4]:
                load.wait()

        rows = pl.ds(start, TILE)
        low = sec_ref[rows, :]
        second = low.astype(f32)

        def sink(side, at):
            return mul(low, d_ref[side, at : at + HIDDEN_STEP, :], 1, 1)

        total = None
        ahead = sink(*places[0])
        for turn, (side, at) in enumerate(places):
            inner = ahead
            if turn + 1 < len(places):
                ahead = sink(*places[turn + 1])
            place = slice(side * half + at, side * half + at + HIDDEN_STEP)
            pre = (inner * slope_ref[rows, place].astype(f32)).astype(bf16)
            pre_ref[rows, place] = pre
            bup_ref[:, place] += fold(pre.astype(f32))
            part = mul(pre, u_ref[side, :, at : at + HIDDEN_STEP], 1, 1)
            total = part if total is None else total + part
        hidden = second + total
        normed, spread = norm_parts(res_ref[rows, :])
        grad = norm_back(hidden * gain_one, normed, spread)
        gr_ref[rows, :] = grad
        mix_ref[rows, :] = grad.astype(bf16)
        sums_ref[0:8, :] += fold(hidden * normed)
        sums_ref[8:16, :] += fold(hidden)
        sums_ref[16:24, :] += fold(grad)
        rows_moved(number, start, lambda at, size: [store.start() for store in stores_of(number, at, size)])

    over_tiles(step)
    for load in loads[4:]:
        load.wait()
    last = copies([(g_ref, g_hbm), (delta_ref, delta_hbm)], out_sems)

    def mixed_grad(number, carry):
        side = number // 3
        place = slice(side * split, (side + 1) * split)
        lanes = slice(number % 3 * 512, number % 3 * 512 + 512)
        grad = mul(wo_ref[place, :], mix_ref[lanes, :], 1, 1).astype(bf16)
        g_ref[place, lanes] = grad
        prod = grad.astype(f32) * o_ref[place, lanes].astype(f32)
        for head in range(split // 64):
            at = (side * (split // 64) + head) * 16
            delta = jnp.sum(prod[head * 64 : head * 64 + 64], axis=0, keepdims=True)
            delta_ref[pl.ds(at, 16), lanes] = extra_rows(-delta)
        return carry

    for number in range(6):
        mixed_grad(number, 0)
    for store in last:
        store.start()
    tall = width // CHUNKS
    low = split // CHUNKS
    for side, out in enumerate((mine_ref, theirs_ref)):

        def up_block(number, carry):
            at = side * half + number * 256
            part = mul(hid_ref[...], pre_ref[:, pl.ds(at, 256)], 0, 0).astype(bf16)
            for chunk in range(CHUNKS):
                xy, z = place_of(chunk)
                for block in range(2):
                    row = (2 * number + block) * tall
                    out[xy, z, pl.ds(row, tall), :] = part[chunk * tall : (chunk + 1) * tall, block * 128 : block * 128 + 128]
            return carry

        for number in range(half // 256):
            up_block(number, 0)
        part = mul(o_ref[side * split : (side + 1) * split, :], mix_ref[...]).astype(bf16)
        for chunk in range(CHUNKS):
            xy, z = place_of(chunk)
            for block in range(width // 128):
                row = half // 128 * tall + block * low
                out[xy, z, row : row + low, :] = part[chunk * low : (chunk + 1) * low, block * 128 : block * 128 + 128]
    vectors = []
    for ref in (two_ref, sums_ref):
        for kind in range(3):
            total = jnp.sum(ref[8 * kind : 8 * kind + 8, :], axis=0, keepdims=True)
            vectors += [total[:, at : at + 128] for at in range(0, width, 128)]
    number = lax.broadcasted_iota(jnp.int32, (16, 128), 0)
    for side, out in enumerate((mine_ref, theirs_ref)):
        total = jnp.sum(bup_ref[:, side * half : (side + 1) * half], axis=0, keepdims=True)
        held = vectors + [total[:, at : at + 128] for at in range(0, half, 128)]
        each = len(held) // CHUNKS
        for chunk in range(CHUNKS):
            xy, z = place_of(chunk)
            block = jnp.zeros((16, 128), f32)
            for row in range(each):
                block = jnp.where(number == row, held[chunk * each + row], block)
            out[xy, z, FEED_ROWS - 16 :, :] = block.astype(bf16)
    for number in range(TILES):
        rows_moved(number, number * TILE, lambda at, size: [store.wait() for store in stores_of(number, at, size)])
    for store in last:
        store.wait()


def project_input(dqa_ref, dka_ref, dva_ref, dqb_ref, dkb_ref, dvb_ref, wa_ref, wb_ref, gr_ref, gi_ref, wt_ref):
    rows = wa_ref.shape[2]
    for side, w_ref in enumerate((wa_ref, wb_ref)):
        for kind in range(3):
            wt_ref[kind, side * rows : (side + 1) * rows, :] = w_ref[kind].T
    for start in range(0, SLOTS, 256):
        size = min(256, SLOTS - start)
        lanes = slice(start, start + 256)
        total = gr_ref[start : start + size, :]
        for side, refs in enumerate(((dqa_ref, dka_ref, dva_ref), (dqb_ref, dkb_ref, dvb_ref))):
            for kind, d_ref in enumerate(refs):
                total = total + mul(d_ref[:, lanes], wt_ref[kind, side * rows : (side + 1) * rows, :], 0, 0)[:size]
        gi_ref[start : start + size, :] = total


def add_pair(mine_ref, theirs_ref, *outs):
    for number, out in enumerate(outs):
        out[...] = (mine_ref[number].astype(f32) + theirs_ref[number].astype(f32)).astype(bf16)


def add_four(a_ref, b_ref, c_ref, d_ref, *outs):
    for number, out in enumerate(outs):
        held = slice(None) if len(outs) == 1 else number
        low = a_ref[held].astype(f32) + b_ref[held].astype(f32)
        out[...] = (low + (c_ref[held].astype(f32) + d_ref[held].astype(f32))).astype(bf16)


def join_four(*refs):
    first, second, outs = refs[:4], refs[4:8], refs[8:]
    for z, out in enumerate(outs):
        at = 0
        for a_ref, b_ref, c_ref, d_ref in (first, second):
            rows = a_ref.shape[1]
            low = a_ref[z].astype(f32) + b_ref[z].astype(f32)
            out[at : at + rows, :] = (low + (c_ref[z].astype(f32) + d_ref[z].astype(f32))).astype(bf16)
            at += rows


def lay_four(a_ref, b_ref, c_ref, d_ref, out_ref):
    for number, ref in enumerate((a_ref, b_ref, c_ref, d_ref)):
        out_ref[number] = ref[...]


def each_chunk(refs):
    own = lax.axis_index("dp") % CHUNKS
    for xy in range(4):
        for z in range(4):
            parts = [ref[z] for ref in (refs[3:] if xy == 3 else refs[xy : xy + 1])]
            yield (z * 4 + xy) ^ own, jnp.concatenate(parts, axis=0).astype(f32)


def spread_feed(
    a_ref, b_ref, c_ref, d_ref, e_ref, up_ref, out_ref, g2_ref, s2_ref, bd_ref, g1_ref, s1_ref, bo_ref, bup_ref, down_ref, keep_ref,
):
    width, half = up_ref.shape
    tall, low = width // CHUNKS, out_ref.shape[0] // CHUNKS
    deep = half // CHUNKS
    for chunk, held in each_chunk((a_ref, b_ref, c_ref, d_ref, e_ref)):
        rows = pl.ds(pl.multiple_of(chunk * tall, tall), tall)
        for block in range(half // 128):
            up_ref[rows, block * 128 : block * 128 + 128] = held[block * tall : (block + 1) * tall]
        rows = pl.ds(pl.multiple_of(chunk * low, low), low)
        base = half // 128 * tall
        for block in range(width // 128):
            out_ref[rows, block * 128 : block * 128 + 128] = held[base + block * low : base + (block + 1) * low]
        keep_ref[chunk] = held[FEED_ROWS - 16 : FEED_ROWS]
        rows = pl.ds(pl.multiple_of((chunk % 4 * 4 + chunk // 4) * deep, deep), deep)
        for block in range(width // 128):
            at = FEED_ROWS + block * deep
            down_ref[rows, block * 128 : block * 128 + 128] = held[at : at + deep]
    refs = [(ref, at) for ref in (g2_ref, s2_ref, bd_ref, g1_ref, s1_ref, bo_ref, bup_ref) for at in range(0, ref.shape[0], 128)]
    each = len(refs) // CHUNKS
    for number, (ref, at) in enumerate(refs):
        ref[at : at + 128] = keep_ref[number // each, number % each, :]


def spread_heads(a_ref, b_ref, c_ref, d_ref, qkv_ref, bias_ref, keep_ref):
    kinds, width, half = qkv_ref.shape
    tall = width // CHUNKS
    for chunk, held in each_chunk((a_ref, b_ref, c_ref, d_ref)):
        rows = pl.ds(pl.multiple_of(chunk * tall, tall), tall)
        for kind in range(kinds):
            for block in range(half // 128):
                row = (kind * (half // 128) + block) * tall
                qkv_ref[kind, rows, block * 128 : block * 128 + 128] = held[row : row + tall]
        keep_ref[chunk] = held[HEAD_ROWS - 16 :]
    blocks = half // 128
    for number in range(2 * blocks):
        at = number % blocks * 128
        bias_ref[number // blocks : number // blocks + 1, at : at + 128] = keep_ref[number, 0:1, :]


def shape(dims, kind=bf16):
    return jax.ShapeDtypeStruct(dims, kind)


smem = pl.BlockSpec(memory_space=pltpu.SMEM)


def specs(count):
    return [smem] + [pl.BlockSpec(memory_space=pltpu.VMEM)] * (count - 1)


def cost(flops, moved, powers=0):
    return pl.CostEstimate(flops=int(flops), bytes_accessed=int(moved), transcendentals=int(powers))


hbm = pl.BlockSpec(memory_space=pl.ANY)
vmem = pl.BlockSpec(memory_space=pltpu.VMEM)


def call_forward(sets, x, wa, wb, ba, bb):
    width = 2 * wa.shape[2]
    big, more = (width, LANES), (width // 4, LANES)
    return pl.pallas_call(
        attend_forward, name="attend_forward",
        out_shape=[shape(big), shape(big), shape(big), shape(big), shape(more)],
        in_specs=[smem, hbm, hbm, vmem, vmem, vmem], out_specs=[hbm] * 5,
        scratch_shapes=[pltpu.VMEM(a.shape, bf16) for a in (x, wa)] + [pltpu.VMEM(big, bf16)] * 4 + [pltpu.VMEM(more, bf16)]
        + [pltpu.VMEM((x.shape[1], LANES), bf16), pltpu.VMEM((CLASSES, LANES), bf16), pltpu.VMEM((CLASSES + 16, LANES), bf16)]
        + [pltpu.SemaphoreType.DMA((3,)), pltpu.SemaphoreType.DMA((5,))],
        compiler_params=params(54), cost_estimate=cost(14e9, 12e6),
    )(sets, x, wa, wb, ba, bb)


def call_feed_forward(sets, x, mixed, wo_a, wo_b, up_a, up_b, bu_a, bu_b, down_a, down_b, vecs, cot):
    rows, width = x.shape
    half = up_a.shape[1]
    outs = [shape((rows, width)), shape((rows, width)), shape((rows, width), f32), shape((rows, 2 * half)), shape((rows, width))]
    tall = (PADDED, width)
    own = [tall, mixed.shape, (width, width), (2, width, half), (2, half, width), tall]
    piece = shape((4, 4, DOWN_ROWS, 128))
    return pl.pallas_call(
        feed_forward, name="feed_forward",
        out_shape=outs + [piece, piece, shape((24, width), f32)],
        in_specs=[smem] + [hbm] * 6 + [vmem] * 2 + [hbm] * 2 + [vmem] * 6 + [hbm], out_specs=[hbm] * 7 + [vmem],
        scratch_shapes=[pltpu.VMEM(a, bf16) for a in own] + [pltpu.VMEM((PADDED, a.shape[1]), a.dtype) for a in outs]
        + [pltpu.VMEM((2, *piece.shape), bf16), pltpu.VMEM((PADDED, 2 * half), bf16)]
        + [pltpu.SemaphoreType.DMA((9,)), pltpu.SemaphoreType.DMA((6, 5)), pltpu.SemaphoreType.DMA((2,))],
        compiler_params=params(48), cost_estimate=cost(14e9, 20e6),
    )(sets, x, mixed, wo_a, wo_b, up_a, up_b, bu_a, bu_b, down_a, down_b, *vecs, cot)


def call_feed_backward(second, slope, hidden, resid, mixed, wo_a, wo_b, up_a, up_b, down_a, down_b, gain, sums):
    rows, width = second.shape
    half = up_a.shape[1]
    split = wo_a.shape[0]
    piece = shape((4, 4, FEED_ROWS, 128))
    outs = [shape((rows, width), f32), shape((2 * split, LANES)), shape((2 * split // 4, LANES))]
    given = [((PADDED, a.shape[1]), a.dtype) for a in (second, slope, hidden, resid)] + [(mixed.shape, bf16)]
    given += [((width, width), bf16), ((2, width, half), bf16), ((2, half, width), bf16)]
    return pl.pallas_call(
        feed_backward, name="feed_backward",
        out_shape=outs + [pltpu.VMEM(piece.shape, bf16)] * 2,
        in_specs=[hbm] * 11 + [vmem] * 2, out_specs=[hbm] * 3 + [vmem] * 2,
        scratch_shapes=[pltpu.VMEM(*a) for a in given] + [pltpu.VMEM((PADDED, width), f32)] + [pltpu.VMEM(a.shape, a.dtype) for a in outs[1:]]
        + [
            pltpu.VMEM((PADDED, 2 * half), bf16), pltpu.VMEM((LANES, width), bf16),
            pltpu.VMEM((24, width), f32), pltpu.VMEM((8, 2 * half), f32),
        ]
        + [pltpu.SemaphoreType.DMA(a) for a in ((6, 3), (8,), (6, 1), (2,))],
        compiler_params=params(48), cost_estimate=cost(14e9, 20e6),
    )(second, slope, hidden, resid, mixed, wo_a, wo_b, up_a, up_b, down_a, down_b, gain, sums)


def call_backward(part, sets, q, k, v, grad, lse, delta, x):
    rows = q.shape[0] // 2
    big, more = (rows, LANES), (rows // 4, LANES)
    return pl.pallas_call(
        functools.partial(attend_backward, part), name="attend_backward",
        out_shape=[shape(big), shape(big), shape(big), shape((4, 4, HEAD_ROWS, 128))],
        in_specs=[smem] + [hbm] * 7, out_specs=[hbm] * 3 + [vmem],
        scratch_shapes=[pltpu.VMEM(a, bf16) for a in (big, big, big, big, more, more, x.shape, (3, *big), (x.shape[1], LANES))]
        + [
            pltpu.VMEM((CLASSES, LANES), bf16), pltpu.VMEM((CLASSES + 16, LANES), bf16),
            pltpu.VMEM((2, 896, 896), bf16), pltpu.VMEM((2, 896, 896), bf16),
            pltpu.VMEM((rows // 64, 64, LANES), f32), pltpu.VMEM((rows // 64, 64, LANES), f32),
        ]
        + [pltpu.SemaphoreType.DMA(a) for a in ((rows // 128, 6), (1,), (rows // 128, 3))],
        compiler_params=params(50), cost_estimate=cost(9e9, 6e6),
    )(sets, q, k, v, grad, lse, delta, x)


def call_project_input(own, other, wa, wb, resid):
    return pl.pallas_call(
        project_input, name="project_input", out_shape=shape(resid.shape, f32),
        scratch_shapes=[pltpu.VMEM((3, 2 * wa.shape[2], wa.shape[1]), bf16)],
        compiler_params=params(40), cost_estimate=cost(2.4e9, 12e6),
    )(*own, *other, wa, wb, resid)


def swap(array):
    return lax.ppermute(array, "mp", [(0, 1), (1, 0)])


def exchange(array, distance):
    count = lax.axis_size("dp")
    return lax.ppermute(array, "dp", [(i, i ^ distance) for i in range(count)])


def small(kernel, name, outs, scratch=()):
    moved = 2 * sum(o.size * o.dtype.itemsize for o in outs)
    return pl.pallas_call(
        kernel, name=name, out_shape=list(outs), scratch_shapes=list(scratch),
        compiler_params=params(24), cost_estimate=cost(1e6, moved),
    )


def after(array, *earlier):
    return lax.optimization_barrier((array, *earlier))[0]


def to_plane(parts):
    return [exchange(parts[xy], xy) for xy in (1, 2, 3)]


def to_line(parts):
    return [exchange(parts[z], 4 * z) for z in (1, 2, 3)]


def plane_sum(parts, came, *earlier):
    _, rows, lanes = parts[0].shape
    return small(add_four, "add_four", [shape((rows, lanes))] * 4)(after(parts[0], *earlier), *came)


def plane_sum_joined(feed, feed_came, down, down_came, *earlier):
    rows, lanes = feed[0].shape[1] + down[0].shape[1], feed[0].shape[2]
    return small(join_four, "join_four", [shape((rows, lanes))] * 4)(after(feed[0], *earlier), *feed_came, down[0], *down_came)


def line_sum(parts, came, *earlier):
    (total,) = small(add_four, "add_four", [shape(parts[0].shape)])(after(parts[0], *earlier), *came)
    distance = CHUNKS
    while distance < lax.axis_size("dp"):
        total = total + exchange(total, distance)
        distance *= 2
    return total


def line_copies(total):
    return [exchange(total, 4 * z) for z in (1, 2, 3)]


def laid(total, came, *earlier):
    (held,) = small(lay_four, "lay_four", [shape((4, *total.shape))])(after(total, *earlier), *came)
    return held


def plane_copies(held):
    return [exchange(held, xy) for xy in (1, 2, 3)]


def across(beside, above, *earlier):
    cut = beside.shape[1] // 32 * 16
    return exchange(after(beside, *earlier)[:, :cut], 2), exchange(after(above, *earlier)[:, cut:], 1)


def halves_added(mine, came, *earlier):
    return small(add_pair, "add_pair", [shape(mine.shape[1:])] * 4)(after(mine, *earlier), came)


def per_device(
    variates, dataset, w_qkv, b_qv, w_out, b_out, gain_one, shift_one, w_up, b_up, w_down, b_down, gain_two, shift_two, cotangent,
):
    width, half = w_up.shape
    other_qkv, other_bias = pltpu.with_memory_space_constraint(swap(w_qkv), pltpu.VMEM), swap(b_qv)
    other_out, other_up, other_bup, other_down = swap(w_out), swap(w_up), swap(b_up), pltpu.with_memory_space_constraint(swap(w_down), pltpu.VMEM)
    q, k, v, mixed, lse = call_forward(dataset, variates, w_qkv, other_qkv, b_qv, other_bias)
    out, hidden, resid, slope, second, down_mine, down_theirs, sums = call_feed_forward(
        dataset, variates, mixed, w_out, other_out, w_up, other_up, b_up, other_bup, w_down, other_down,
        (b_out, gain_one, shift_one, b_down, gain_two, shift_two), cotangent,
    )
    down = halves_added(down_mine, swap(down_theirs))
    down_came = to_plane(down)
    grad_res, grad_mix, delta, mine, theirs = call_feed_backward(
        after(second, *down), slope, hidden, resid, mixed, w_out, other_out, w_up, other_up, w_down, other_down, gain_one, sums
    )
    feed = halves_added(mine, swap(after(theirs, *down_came)))
    feed_came = to_plane(feed)
    *other, theirs = call_backward(1, dataset, q, k, v, after(grad_mix, *feed), lse, delta, variates)
    feed = plane_sum_joined(feed, feed_came, down, down_came, theirs)
    heads_came = swap(after(theirs, *feed))
    feed_came = to_line(feed)
    *own, mine = call_backward(0, dataset, q, k, v, after(grad_mix, heads_came, *feed), lse, delta, variates)
    total = line_sum(feed, feed_came, mine)
    heads = halves_added(mine, heads_came, total)
    heads_plane = to_plane(heads)
    feed_came = line_copies(total)
    grad_in = call_project_input(own, other, w_qkv, other_qkv, after(grad_res, total, *heads))
    held = laid(total, feed_came, grad_in)
    heads = plane_sum(heads, heads_plane, grad_in)
    line = to_line(heads)
    feed = plane_copies(after(held, line[0]))[:2]
    heads = line_sum(heads, line)
    line = line_copies(heads)
    heads = laid(heads, line)
    feed = [held, *feed, *across(*feed, heads)]
    plane = plane_copies(heads)
    vector = shape((width,), f32)
    outs = [shape((width, half), f32), shape(w_out.shape, f32)] + [vector] * 6 + [shape((half,), f32), shape(w_down.shape, f32)]
    keep = [pltpu.VMEM((CHUNKS, 16, 128), f32)]
    grad_up, grad_out, two_gain, two_shift, down_bias, one_gain, one_shift, out_bias, up_bias, grad_down = small(
        spread_feed, "spread_feed", outs, keep
    )(*feed)
    heads = [after(heads, grad_up), *plane]
    grad_qkv, bias = small(spread_heads, "spread_heads", [shape(w_qkv.shape, f32), shape(b_qv.shape, f32)], keep)(*heads)
    return (
        out, grad_in, grad_qkv, bias, grad_out, out_bias, one_gain, one_shift, grad_up, up_bias,
        grad_down, down_bias, two_gain, two_shift,
    )


def solution(mesh):
    wide = P(("dp", "mp"), None)
    weights = (P(None, None, "mp"), P(None, "mp"), P("mp", None))
    placed = (wide, P("dp"), *weights, P(), P(), P(), P(None, "mp"), P("mp"), P("mp", None), P(), P(), P(), wide)
    given = (wide, wide, *weights, P(), P(), P(), P(None, "mp"), P("mp"), P("mp", None), P(), P(), P())
    return jax.shard_map(per_device, mesh=mesh, in_specs=placed, out_specs=given, check_vma=False)
```

```python
import functools

import jax
import jax.numpy as jnp
from jax import lax
from jax.experimental import pallas as pl
from jax.experimental.pallas import tpu as pltpu
from jax.sharding import PartitionSpec as P

HEAD_DIM = 64
SLOTS = 1424
WIDTHS = (7, 21, 321, 862)
LANES = 1536
CLASSES = 80
BIG = 1e30
EPS = 1e-05
MIB = 2**20

bf16 = jnp.bfloat16
f32 = jnp.float32


def mul(left, right, left_dim=1, right_dim=0):
    return lax.dot_general(
        left, right, (((left_dim,), (right_dim,)), ((), ())), preferred_element_type=f32
    )


def params(limit):
    return pltpu.CompilerParams(vmem_limit_bytes=limit * MIB)


def cover(width, start, stop, last):
    used = SLOTS // width * width
    low = start // width * width
    high = last if stop > used else -(-stop // width) * width
    return (low // 128 * 128, min(-(-min(high, last) // 128) * 128, LANES))


def groups_of(width, rows, step):
    found = []
    for start in range(0, rows, step):
        low, high = cover(width, start, min(start + step, rows), rows)
        if found and found[-1][2] == low and found[-1][2] + found[-1][3] == high:
            first, count = found[-1][:2]
            found[-1] = (first, count + step, low, high - low)
        else:
            found.append((start, step, low, high - low))
    return found


def near(tile):
    return jnp.clip(tile * 256 - 128, 0, LANES - 512)


def middle(tile):
    return jnp.where(tile < 2, 0, jnp.where(tile == 2, 256, jnp.where(tile == 3, 640, 768)))


FORWARD = (
    [(0, 6, 512, near, 8)],
    [(0, 6, 768, middle, 8)],
    [(0, 3, 896, lambda tile: 0 * tile, 8), (3, 4, 1536, lambda tile: 0 * tile, 4), (4, 6, 768, lambda tile: 0 * tile + 768, 8)],
    [(0, 6, 512, near, 1)],
    [(0, 6, LANES, lambda tile: 0 * tile, 1)],
)
BACKWARD = (
    [],
    groups_of(WIDTHS[2], SLOTS // WIDTHS[2] * WIDTHS[2], 256),
    [(0, 896, 0, 896)],
)


def own_bucket(sets_ref):
    return sets_ref[lax.axis_index("mp")]


def token_class(width):
    token = lax.broadcasted_iota(jnp.int32, (CLASSES, LANES), 1)
    numbers = token.astype(f32)
    held = jnp.floor((numbers + 0.5) * (1.0 / width)).astype(jnp.int32)
    held = jnp.where(token < SLOTS, held, (SLOTS - 1) // width + 1)
    row = lax.broadcasted_iota(jnp.int32, (CLASSES, LANES), 0)
    return held % CLASSES == row


def write_masks(bucket, hot_ref, bar_ref):
    for number, width in enumerate(WIDTHS):

        @pl.when(bucket == number)
        def _():
            same = token_class(width)
            hot_ref[...] = jnp.where(same, 1.0, 0.0).astype(bf16)
            bar_ref[:CLASSES, :] = jnp.where(same, 0.0, -BIG).astype(bf16)

    row = lax.broadcasted_iota(jnp.int32, (16, LANES), 0)
    bar_ref[CLASSES:, :] = jnp.where(row < 3, 1.0, 0.0).astype(bf16)


def split_three(row):
    high = row.astype(bf16)
    rest = row - high.astype(f32)
    middle = rest.astype(bf16)
    low = (rest - middle.astype(f32)).astype(bf16)
    return high, middle, low


def extra_rows(row):
    parts = [p.astype(f32) for p in split_three(row)]
    number = lax.broadcasted_iota(jnp.int32, (16, row.shape[1]), 0)
    held = jnp.where(number == 0, parts[0], jnp.where(number == 1, parts[1], jnp.where(number == 2, parts[2], 0.0)))
    return held.astype(bf16)


LOG_E = 1.4426950408889634
SAFE = 60.0


def attend_forward(
    sets_ref, x_hbm, wa_hbm, wb_ref, ba_ref, bb_ref, q_hbm, k_hbm, v_hbm, o_hbm, lse_hbm,
    x_ref, wa_ref, q_ref, k_ref, v_ref, o_ref, lse_ref, xt_ref, hot_ref, bar_ref, in_sems, out_sems,
):
    loads = [pltpu.make_async_copy(*pair, in_sems.at[i]) for i, pair in enumerate(((x_hbm, x_ref), (wa_hbm, wa_ref)))]
    for load in loads:
        load.start()
    pairs = ((q_ref, q_hbm), (k_ref, k_hbm), (v_ref, v_hbm), (o_ref, o_hbm), (lse_ref, lse_hbm))
    stores = [pltpu.make_async_copy(*pair, out_sems.at[i]) for i, pair in enumerate(pairs)]
    bucket = own_bucket(sets_ref)
    write_masks(bucket, hot_ref, bar_ref)
    tail = jnp.zeros((LANES - SLOTS, x_ref.shape[1]), bf16)
    loads[0].wait()
    xt_ref[...] = jnp.concatenate([x_ref[...], tail], axis=0).T
    worst = None
    for side, (w_ref, b_ref) in enumerate(((wa_ref, ba_ref), (wb_ref, bb_ref))):
        if side == 0:
            loads[1].wait()
        for kind, out_ref in enumerate((q_ref, k_ref, v_ref)):
            weight = w_ref[kind].T
            rows = weight.shape[0]
            if kind != 1:
                row = b_ref[kind // 2 : kind // 2 + 1, :].astype(f32)
                column = jnp.broadcast_to(row, (128, rows)).T
                column = jnp.concatenate([column] * 4, axis=1)

            def project(number, carry):
                lanes = slice(number * 512, number * 512 + 512)
                part = mul(weight, xt_ref[:, lanes])
                if kind != 1:
                    part = part + column
                if kind == 0:
                    part = part * 0.125
                out_ref[side * rows : (side + 1) * rows, lanes] = part.astype(bf16)
                return carry

            for number in range(LANES // 512):
                project(number, 0)
    for store in stores[:3]:
        store.start()
    heads = q_ref.shape[0] // 64
    for head in range(heads):
        norms = []
        for ref in (q_ref, k_ref):
            held = ref[head * 64 : head * 64 + 64, :].astype(f32)
            norms.append(jnp.max(jnp.sum(held * held, axis=0, keepdims=True), axis=1, keepdims=True))
        both = norms[0] * norms[1]
        worst = both if worst is None else jnp.maximum(worst, both)
    calm = worst[0, 0] < SAFE * SAFE

    def score(head, start, first, span):
        rows = pl.ds(pl.multiple_of(head * 64, 64), 64)
        lanes, span = pl.ds(start, 256), pl.ds(first, span)
        keys = jnp.concatenate([k_ref[rows, span], bar_ref[:CLASSES, span]], axis=0)
        quer = jnp.concatenate([q_ref[rows, lanes], hot_ref[:, lanes]], axis=0)
        return mul(keys, quer, 0, 0)

    def finish(head, start, first, span, scores, plain):
        rows = pl.ds(pl.multiple_of(head * 64, 64), 64)
        lanes = pl.ds(start, 256)
        if plain:
            raised = jnp.exp2(scores * LOG_E).astype(bf16)
        else:
            top = jnp.max(scores, axis=0, keepdims=True)
            raised = jnp.exp(scores - top).astype(bf16)
        vals = jnp.concatenate([v_ref[rows, pl.ds(first, span)], jnp.ones((16, span), bf16)], axis=0)
        total = mul(vals, raised)
        sums = total[64:65, :]
        o_ref[rows, lanes] = (total[:64, :] * (1.0 / sums)).astype(bf16)
        logs = jnp.log(sums)
        if not plain:
            logs = logs + top
        lse_ref[pl.ds(pl.multiple_of(head * 16, 16), 16), lanes] = extra_rows(-logs)

    def over(begin, end, span, first_of, together, plain):
        def turn(number, carry):
            tile = begin + number % (end - begin)
            start = pl.multiple_of(tile * 256, 256)
            first = pl.multiple_of(first_of(tile), 128)
            own = [number // (end - begin) * together + i for i in range(together)]
            held = [score(head, start, first, span) for head in own]
            for head, scores in zip(own, held):
                finish(head, start, first, span, scores, plain)
            return carry

        lax.fori_loop(0, heads // together * (end - begin), turn, 0)

    for group in range(5):
        plain = group < 3
        chosen = (bucket < 2, bucket == 2, bucket == 3, bucket < 2, bucket >= 2)[group]

        @pl.when(jnp.logical_and(chosen, calm == plain))
        def _():
            for begin, end, span, first_of, together in FORWARD[group]:
                over(begin, end, span, first_of, together, plain)

    for store in stores[3:]:
        store.start()
    for store in stores:
        store.wait()


def copies(pairs, sems):
    return [pltpu.make_async_copy(*pair, sems.at[i]) for i, pair in enumerate(pairs)]


def attend_backward(
    part, sets_ref, q_hbm, k_hbm, v_hbm, g_hbm, lse_hbm, delta_hbm, x_hbm, dq_hbm, dk_hbm, dv_hbm, piece_ref,
    q_ref, k_ref, v_ref, g_ref, lse_ref, delta_ref, x_ref, grads_ref, xt_ref,
    hot_ref, bar_ref, p_ref, s_ref, ka_ref, va_ref, head_sems, in_sems, out_sems,
):
    half = q_ref.shape[0]
    dq_ref, dk_ref, dv_ref = (grads_ref.at[kind] for kind in range(3))

    def loads_of(number):
        there = pl.ds(part * half + number * 128, 128)
        here = pl.ds(number * 128, 128)
        pairs = [(far.at[there], near.at[here]) for far, near in ((q_hbm, q_ref), (k_hbm, k_ref), (v_hbm, v_ref), (g_hbm, g_ref))]
        there = pl.ds(part * (half // 4) + number * 32, 32)
        here = pl.ds(number * 32, 32)
        pairs += [(far.at[there], near.at[here]) for far, near in ((lse_hbm, lse_ref), (delta_hbm, delta_ref))]
        return copies(pairs, head_sems.at[number])

    def stores_of(number):
        here = pl.ds(number * 128, 128)
        return copies([(near.at[here], far.at[here]) for near, far in ((dq_ref, dq_hbm), (dk_ref, dk_hbm), (dv_ref, dv_hbm))], out_sems.at[number])

    for number in range(half // 128):
        for load in loads_of(number):
            load.start()
    given = copies([(x_hbm, x_ref)], in_sems)[0]
    bucket = own_bucket(sets_ref)
    write_masks(bucket, hot_ref, bar_ref)

    def one_head(head, groups, slot):
        rows = pl.ds(pl.multiple_of(head * 64, 64), 64)
        more = pl.ds(pl.multiple_of(head * 16, 16), 16)
        single = len(groups) == 1
        if not single:
            ka_ref[slot] = jnp.zeros(ka_ref.shape[1:], f32)
            va_ref[slot] = jnp.zeros(va_ref.shape[1:], f32)
        for q0, nq, k0, nk in groups:
            span = slice(k0, k0 + nk)
            held = slice(q0, q0 + nq)
            keys = jnp.concatenate([k_ref[rows, span], bar_ref[:, span]], axis=0)
            vals = jnp.concatenate([v_ref[rows, span], bar_ref[CLASSES:, span]], axis=0)
            for start in range(q0, q0 + nq, 256):
                size = min(256, q0 + nq - start)
                lanes = slice(start, start + size)
                quer = jnp.concatenate([q_ref[rows, lanes], hot_ref[:, lanes], lse_ref[more, lanes]], axis=0)
                grad = jnp.concatenate([g_ref[rows, lanes], delta_ref[more, lanes]], axis=0)
                probs = jnp.exp2(mul(quer, keys, 0, 0) * LOG_E)
                slopes = probs * mul(grad, vals, 0, 0)
                p_ref[slot, start - q0 : start - q0 + size, :nk] = probs.astype(bf16)
                s_ref[slot, start - q0 : start - q0 + size, :nk] = slopes.astype(bf16)
            dv = mul(g_ref[rows, held], p_ref[slot, :nq, :nk])
            dk = mul(q_ref[rows, held], s_ref[slot, :nq, :nk])
            dq = mul(k_ref[rows, span], s_ref[slot, :nq, :nk], 1, 1)
            dq_ref[rows, held] = (dq * 0.125).astype(bf16)
            if single:
                dv_ref[rows, span] = dv.astype(bf16)
                dk_ref[rows, span] = dk.astype(bf16)
            else:
                va_ref[slot, :, span] += dv
                ka_ref[slot, :, span] += dk
        if single:
            rest = LANES - 896
            for out in (dq_ref, dk_ref, dv_ref):
                out[rows, 896:] = jnp.zeros((64, rest), bf16)
        else:
            dv_ref[rows, :] = va_ref[slot].astype(bf16)
            dk_ref[rows, :] = ka_ref[slot].astype(bf16)
            done = groups[-1][0] + groups[-1][1]
            if done < LANES:
                dq_ref[rows, done:] = jnp.zeros((64, LANES - done), bf16)

    def tile_of(head, start, first, span):
        rows = pl.ds(head * 64, 64)
        more = pl.ds(head * 16, 16)
        lanes, span = pl.ds(start, 256), pl.ds(first, span)
        keys = jnp.concatenate([k_ref[rows, span], bar_ref[:, span]], axis=0)
        vals = jnp.concatenate([v_ref[rows, span], bar_ref[CLASSES:, span]], axis=0)
        quer = jnp.concatenate([q_ref[rows, lanes], hot_ref[:, lanes], lse_ref[more, lanes]], axis=0)
        grad = jnp.concatenate([g_ref[rows, lanes], delta_ref[more, lanes]], axis=0)
        probs = jnp.exp2(mul(quer, keys, 0, 0) * LOG_E)
        slopes = (probs * mul(grad, vals, 0, 0)).astype(bf16)
        return probs.astype(bf16), slopes

    def take(head, start, first, span, probs, slopes):
        rows = pl.ds(head * 64, 64)
        lanes, span = pl.ds(start, 256), pl.ds(first, span)
        va_ref[head, :, span] += mul(g_ref[rows, lanes], probs)
        ka_ref[head, :, span] += mul(q_ref[rows, lanes], slopes)
        dq_ref[rows, lanes] = (mul(k_ref[rows, span], slopes, 1, 1) * 0.125).astype(bf16)

    def by_tiles(span, first_of, together):
        for number in range(half // 128):
            for load in loads_of(number):
                load.wait()
        given.start()
        ka_ref[...] = jnp.zeros_like(ka_ref)
        va_ref[...] = jnp.zeros_like(va_ref)

        def turn(tile, carry):
            start = pl.multiple_of(tile * 256, 256)
            first = pl.multiple_of(first_of(tile), 128)
            for base in range(0, half // 64, together):
                own = range(base, base + together)
                held = [tile_of(head, start, first, span) for head in own]
                for head, (probs, slopes) in zip(own, held):
                    take(head, start, first, span, probs, slopes)
            return carry

        lax.fori_loop(0, 6, turn, 0)
        for head in range(half // 64):
            rows = pl.ds(head * 64, 64)
            dv_ref[rows, :] = va_ref[head].astype(bf16)
            dk_ref[rows, :] = ka_ref[head].astype(bf16)
        for number in range(half // 128):
            for store in stores_of(number):
                store.start()

    for group in range(3):
        chosen = (bucket < 2, bucket == 2, bucket == 3)[group]

        @pl.when(chosen)
        def _():
            if group == 0:
                by_tiles(512, near, 4)
            else:

                def pair(number, carry):
                    for load in loads_of(number):
                        load.wait()

                    @pl.when(number == 0)
                    def _():
                        given.start()

                    one_head(2 * number, BACKWARD[group], 0)
                    one_head(2 * number + 1, BACKWARD[group], 1)
                    for store in stores_of(number):
                        store.start()
                    return carry

                lax.fori_loop(0, half // 128, pair, 0)

    given.wait()
    width = x_ref.shape[1]
    tail = jnp.zeros((LANES - SLOTS, width), bf16)
    xt_ref[...] = jnp.concatenate([x_ref[...], tail], axis=0).T
    tall = width // CHUNKS
    ones = jnp.ones((8, LANES), bf16)
    place_of = slots()
    sums = []
    blocks = half // 128

    def product_of(kind, carry):
        product = mul(xt_ref[...], grads_ref[kind], 1, 1).astype(bf16)
        for chunk in range(CHUNKS):
            xy, z = place_of(chunk)
            for block in range(blocks):
                row = (kind * blocks + block) * tall
                piece_ref[xy, z, pl.ds(row, tall), :] = product[chunk * tall : (chunk + 1) * tall, block * 128 : block * 128 + 128]
        return carry

    for kind in range(3):
        product_of(kind, 0)
    for d_ref in (dq_ref, dv_ref):
        total = mul(ones, d_ref[...], 1, 1)[:1]
        sums += [total[:, block * 128 : block * 128 + 128] for block in range(blocks)]
    number = lax.broadcasted_iota(jnp.int32, (16, 128), 0)
    for chunk in range(CHUNKS):
        xy, z = place_of(chunk)
        held = jnp.where(number == 0, sums[chunk] if chunk < len(sums) else 0.0, 0.0)
        piece_ref[xy, z, HEAD_ROWS - 16 :, :] = held.astype(bf16)
    for number in range(half // 128):
        for store in stores_of(number):
            store.wait()


TILE = 240
TILES = 6
PADDED = TILE * TILES
LAST = SLOTS - TILE * (TILES - 1)


def over_tiles(step):
    def body(number, carry):
        step(number, pl.multiple_of(number * TILE, TILE))
        return carry

    lax.fori_loop(0, TILES, body, 0)


def rows_moved(number, start, begin):
    if isinstance(number, int):
        begin(start, LAST if number == TILES - 1 else TILE)
        return

    @pl.when(number < TILES - 1)
    def _():
        begin(start, TILE)

    @pl.when(number == TILES - 1)
    def _():
        begin(TILE * (TILES - 1), LAST)


def mean_of(matrix):
    return jnp.sum(matrix, axis=1, keepdims=True) * (1.0 / matrix.shape[1])


def norm_parts(matrix):
    centre = matrix - mean_of(matrix)
    spread = lax.rsqrt(mean_of(centre * centre) + EPS)
    return centre * spread, spread


def norm_back(scaled, normed, spread):
    return spread * (scaled - mean_of(scaled) - normed * mean_of(scaled * normed))


def fold(matrix):
    return jnp.sum(matrix.reshape(matrix.shape[0] // 8, 8, matrix.shape[1]), axis=0)


def gelu_parts(pre):
    size = jnp.abs(pre)
    t = pl.reciprocal(1.0 + (0.3275911 * 2.0**-0.5) * size)
    bell = jnp.exp2((-0.5 * LOG_E) * (pre * pre))
    poly = 0.5 * 1.061405429
    for factor in (-1.453152027, 1.421413741, -0.284496736, 0.254829592):
        poly = poly * t + 0.5 * factor
    tail = poly * t * bell
    phi = jnp.where(pre > 0, 1.0 - tail, tail)
    return pre * phi, phi + pre * (bell * (2.0 * jnp.pi) ** -0.5)


HIDDEN_STEP = 512


def row_of(ref):
    return ref[...].astype(f32).reshape(1, ref.shape[0])


def feed_forward(
    sets_ref, x_hbm, o_hbm, wo_a, wo_b, ua_hbm, ub_hbm, ba_ref, bb_ref, da_hbm, db_hbm,
    bo_ref, g1_ref, s1_ref, bd_ref, g2_ref, s2_ref, cot_hbm,
    out_hbm, hid_hbm, res_hbm, slope_hbm, sec_hbm, gd_a, gd_b, sums_ref,
    x_ref, o_ref, wo_ref, u_ref, d_ref, cot_ref, out_ref, hid_ref, res_ref, slope_ref, low_ref, gd_ref, act_ref,
    in_sems, row_sems, out_sems,
):
    half = ua_hbm.shape[1]
    split = wo_a.shape[0]
    width = x_ref.shape[1]
    true = pl.ds(0, SLOTS)
    pairs = [(o_hbm, o_ref), (wo_a, wo_ref.at[pl.ds(0, split)]), (wo_b, wo_ref.at[pl.ds(split, split)]), (x_hbm, x_ref.at[true])]
    pairs += [(ua_hbm, u_ref.at[0]), (ub_hbm, u_ref.at[1]), (da_hbm, d_ref.at[0]), (db_hbm, d_ref.at[1]), (cot_hbm, cot_ref.at[true])]
    loads = copies(pairs, in_sems)
    for load in loads:
        load.start()
    for ref in (x_ref, cot_ref):
        ref[SLOTS:, :] = jnp.zeros((PADDED - SLOTS, width), bf16)
    bucket = own_bucket(sets_ref)
    used = SLOTS // WIDTHS[3] * WIDTHS[3]
    for number in range(3):
        used = jnp.where(bucket == number, SLOTS // WIDTHS[number] * WIDTHS[number], used)
    sums_ref[...] = jnp.zeros_like(sums_ref)
    b_out, gain_one, shift_one, b_down, gain_two, shift_two = (
        row_of(ref) for ref in (bo_ref, g1_ref, s1_ref, bd_ref, g2_ref, s2_ref)
    )
    b_up = [row_of(ref) for ref in (ba_ref, bb_ref)]
    places = [(side, at) for side in range(2) for at in range(0, half, HIDDEN_STEP)]
    last = copies([(gd_ref.at[0], gd_a), (gd_ref.at[1], gd_b)], out_sems)

    def stores_of(number, start, size):
        rows = pl.ds(start, size)
        pairs = ((out_ref, out_hbm), (hid_ref, hid_hbm), (res_ref, res_hbm), (slope_ref, slope_hbm), (low_ref, sec_hbm))
        return copies([(near.at[rows], far.at[rows]) for near, far in pairs], row_sems.at[number])

    def step(number, start):
        rows = pl.ds(start, TILE)
        resid = res_ref[rows, :] + x_ref[rows, :].astype(f32) + b_out
        res_ref[rows, :] = resid
        normed, _ = norm_parts(resid)
        hidden = normed * gain_one + shift_one
        low = hidden.astype(bf16)
        hid_ref[rows, :] = low

        @pl.when(number == 0)
        def _():
            for load in loads[4:]:
                load.wait()

        def lift(side, at):
            return mul(low, u_ref[side, :, at : at + HIDDEN_STEP]) + b_up[side][:, at : at + HIDDEN_STEP]

        total = None
        ahead = lift(*places[0])
        for turn, (side, at) in enumerate(places):
            pre = ahead
            if turn + 1 < len(places):
                ahead = lift(*places[turn + 1])
            place = slice(side * half + at, side * half + at + HIDDEN_STEP)
            active, slope = gelu_parts(pre)
            active = active.astype(bf16)
            act_ref[rows, place] = active
            slope_ref[rows, place] = slope.astype(bf16)
            part = mul(active, d_ref[side, at : at + HIDDEN_STEP, :])
            total = part if total is None else total + part
        second = hidden + total + b_down
        normed, spread = norm_parts(second)
        out_ref[rows, :] = (normed * gain_two + shift_two).astype(bf16)
        row = start + lax.broadcasted_iota(jnp.int32, (TILE, width), 0)
        top = jnp.where(row < used, cot_ref[rows, :].astype(f32), 0.0)
        grad = norm_back(top * gain_two, normed, spread)
        low_ref[rows, :] = grad.astype(bf16)
        sums_ref[0:8, :] += fold(top * normed)
        sums_ref[8:16, :] += fold(top)
        sums_ref[16:24, :] += fold(grad)
        rows_moved(number, start, lambda at, size: [store.start() for store in stores_of(number, at, size)])

    for load in loads[:4]:
        load.wait()
    for start in range(0, PADDED, 512):
        size = min(512, PADDED - start)
        res_ref[start : start + size, :] = mul(o_ref[:, start : start + 512], wo_ref[...], 0, 0)[:size]
    over_tiles(step)
    place_of = slots()
    tall = half // CHUNKS

    def block_of(number, carry):
        side, block = number // 4, number % 4
        part = mul(act_ref[:, pl.ds(pl.multiple_of(number * 4 * tall, 4 * tall), 4 * tall)], low_ref[...], 0, 0).astype(bf16)
        for z in range(4):
            xy, z_place = place_of(z * 4 + block)
            for lane in range(width // 128):
                gd_ref[side, xy, z_place, lane * tall : (lane + 1) * tall, :] = part[z * tall : (z + 1) * tall, lane * 128 : lane * 128 + 128]

        @pl.when(number == 3)
        def _():
            last[0].start()

        return carry

    lax.fori_loop(0, 8, block_of, 0)
    last[1].start()
    for number in range(TILES):
        rows_moved(number, number * TILE, lambda at, size: [store.wait() for store in stores_of(number, at, size)])
    for store in last:
        store.wait()


CHUNKS = 16
FEED_ROWS = 336
DOWN_ROWS = 256
HEAD_ROWS = 208


def slots():
    own = lax.axis_index("dp") % CHUNKS

    def place(chunk):
        held = chunk ^ own
        return held % 4, held // 4

    return place


def feed_backward(
    sec_hbm, slope_hbm, hid_hbm, res_hbm, o_hbm, wo_a, wo_b, ua_hbm, ub_hbm, da_hbm, db_hbm, g1_ref, two_ref,
    gr_hbm, g_hbm, delta_hbm, mine_ref, theirs_ref,
    sec_ref, slope_ref, hid_ref, res_ref, o_ref, wo_ref, u_ref, d_ref, gr_ref, g_ref, delta_ref,
    pre_ref, mix_ref, sums_ref, bup_ref, row_in, in_sems, row_out, out_sems,
):
    half = ua_hbm.shape[1]
    width = hid_ref.shape[1]
    split = wo_a.shape[0]

    def loads_of(number, start, size):
        rows = pl.ds(start, size)
        pairs = ((sec_hbm, sec_ref), (slope_hbm, slope_ref), (res_hbm, res_ref))
        return copies([(far.at[rows], near.at[rows]) for far, near in pairs], row_in.at[number])

    def stores_of(number, start, size):
        rows = pl.ds(start, size)
        return copies([(gr_ref.at[rows], gr_hbm.at[rows])], row_out.at[number])

    pairs = [(da_hbm, d_ref.at[0]), (db_hbm, d_ref.at[1]), (ua_hbm, u_ref.at[0]), (ub_hbm, u_ref.at[1])]
    pairs += [(hid_hbm, hid_ref.at[pl.ds(0, SLOTS)]), (o_hbm, o_ref), (wo_a, wo_ref.at[pl.ds(0, split)]), (wo_b, wo_ref.at[pl.ds(split, split)])]
    loads = copies(pairs, in_sems)
    for load in loads_of(0, 0, TILE) + loads[:4]:
        load.start()
    for ref in (sec_ref, slope_ref, res_ref, hid_ref):
        ref[SLOTS:, :] = jnp.zeros((PADDED - SLOTS, ref.shape[1]), ref.dtype)
    sums_ref[...] = jnp.zeros_like(sums_ref)
    bup_ref[...] = jnp.zeros_like(bup_ref)
    gain_one = row_of(g1_ref)
    mix_ref[PADDED:, :] = jnp.zeros((LANES - PADDED, width), bf16)
    place_of = slots()
    places = [(side, at) for side in range(2) for at in range(0, half, HIDDEN_STEP)]

    def step(number, start):
        @pl.when(number < TILES - 1)
        def _():
            rows_moved(number + 1, start + TILE, lambda at, size: [load.start() for load in loads_of(number + 1, at, size)])

        @pl.when(number == TILES - 2)
        def _():
            for load in loads[4:]:
                load.start()

        rows_moved(number, start, lambda at, size: [load.wait() for load in loads_of(number, at, size)])

        @pl.when(number == 0)
        def _():
            for load in loads[:4]:
                load.wait()

        rows = pl.ds(start, TILE)
        low = sec_ref[rows, :]
        second = low.astype(f32)

        def sink(side, at):
            return mul(low, d_ref[side, at : at + HIDDEN_STEP, :], 1, 1)

        total = None
        ahead = sink(*places[0])
        for turn, (side, at) in enumerate(places):
            inner = ahead
            if turn + 1 < len(places):
                ahead = sink(*places[turn + 1])
            place = slice(side * half + at, side * half + at + HIDDEN_STEP)
            pre = (inner * slope_ref[rows, place].astype(f32)).astype(bf16)
            pre_ref[rows, place] = pre
            bup_ref[:, place] += fold(pre.astype(f32))
            part = mul(pre, u_ref[side, :, at : at + HIDDEN_STEP], 1, 1)
            total = part if total is None else total + part
        hidden = second + total
        normed, spread = norm_parts(res_ref[rows, :])
        grad = norm_back(hidden * gain_one, normed, spread)
        gr_ref[rows, :] = grad
        mix_ref[rows, :] = grad.astype(bf16)
        sums_ref[0:8, :] += fold(hidden * normed)
        sums_ref[8:16, :] += fold(hidden)
        sums_ref[16:24, :] += fold(grad)
        rows_moved(number, start, lambda at, size: [store.start() for store in stores_of(number, at, size)])

    over_tiles(step)
    for load in loads[4:]:
        load.wait()
    last = copies([(g_ref, g_hbm), (delta_ref, delta_hbm)], out_sems)

    def mixed_grad(number, carry):
        side = number // 3
        place = slice(side * split, (side + 1) * split)
        lanes = slice(number % 3 * 512, number % 3 * 512 + 512)
        grad = mul(wo_ref[place, :], mix_ref[lanes, :], 1, 1).astype(bf16)
        g_ref[place, lanes] = grad
        prod = grad.astype(f32) * o_ref[place, lanes].astype(f32)
        for head in range(split // 64):
            at = (side * (split // 64) + head) * 16
            delta = jnp.sum(prod[head * 64 : head * 64 + 64], axis=0, keepdims=True)
            delta_ref[pl.ds(at, 16), lanes] = extra_rows(-delta)
        return carry

    for number in range(6):
        mixed_grad(number, 0)
    for store in last:
        store.start()
    tall = width // CHUNKS
    low = split // CHUNKS
    for side, out in enumerate((mine_ref, theirs_ref)):

        def up_block(number, carry):
            at = side * half + number * 256
            part = mul(hid_ref[...], pre_ref[:, pl.ds(at, 256)], 0, 0).astype(bf16)
            for chunk in range(CHUNKS):
                xy, z = place_of(chunk)
                for block in range(2):
                    row = (2 * number + block) * tall
                    out[xy, z, pl.ds(row, tall), :] = part[chunk * tall : (chunk + 1) * tall, block * 128 : block * 128 + 128]
            return carry

        for number in range(half // 256):
            up_block(number, 0)
        part = mul(o_ref[side * split : (side + 1) * split, :], mix_ref[...]).astype(bf16)
        for chunk in range(CHUNKS):
            xy, z = place_of(chunk)
            for block in range(width // 128):
                row = half // 128 * tall + block * low
                out[xy, z, row : row + low, :] = part[chunk * low : (chunk + 1) * low, block * 128 : block * 128 + 128]
    vectors = []
    for ref in (two_ref, sums_ref):
        for kind in range(3):
            total = jnp.sum(ref[8 * kind : 8 * kind + 8, :], axis=0, keepdims=True)
            vectors += [total[:, at : at + 128] for at in range(0, width, 128)]
    number = lax.broadcasted_iota(jnp.int32, (16, 128), 0)
    for side, out in enumerate((mine_ref, theirs_ref)):
        total = jnp.sum(bup_ref[:, side * half : (side + 1) * half], axis=0, keepdims=True)
        held = vectors + [total[:, at : at + 128] for at in range(0, half, 128)]
        each = len(held) // CHUNKS
        for chunk in range(CHUNKS):
            xy, z = place_of(chunk)
            block = jnp.zeros((16, 128), f32)
            for row in range(each):
                block = jnp.where(number == row, held[chunk * each + row], block)
            out[xy, z, FEED_ROWS - 16 :, :] = block.astype(bf16)
    for number in range(TILES):
        rows_moved(number, number * TILE, lambda at, size: [store.wait() for store in stores_of(number, at, size)])
    for store in last:
        store.wait()


def project_input(dqa_ref, dka_ref, dva_ref, dqb_ref, dkb_ref, dvb_ref, wa_ref, wb_ref, gr_ref, gi_ref, wt_ref):
    rows = wa_ref.shape[2]
    for side, w_ref in enumerate((wa_ref, wb_ref)):
        for kind in range(3):
            wt_ref[kind, side * rows : (side + 1) * rows, :] = w_ref[kind].T
    for start in range(0, SLOTS, 256):
        size = min(256, SLOTS - start)
        lanes = slice(start, start + 256)
        total = gr_ref[start : start + size, :]
        for side, refs in enumerate(((dqa_ref, dka_ref, dva_ref), (dqb_ref, dkb_ref, dvb_ref))):
            for kind, d_ref in enumerate(refs):
                total = total + mul(d_ref[:, lanes], wt_ref[kind, side * rows : (side + 1) * rows, :], 0, 0)[:size]
        gi_ref[start : start + size, :] = total


def add_pair(mine_ref, theirs_ref, *outs):
    for number, out in enumerate(outs):
        out[...] = (mine_ref[number].astype(f32) + theirs_ref[number].astype(f32)).astype(bf16)


def add_four(a_ref, b_ref, c_ref, d_ref, *outs):
    for number, out in enumerate(outs):
        held = slice(None) if len(outs) == 1 else number
        low = a_ref[held].astype(f32) + b_ref[held].astype(f32)
        out[...] = (low + (c_ref[held].astype(f32) + d_ref[held].astype(f32))).astype(bf16)


def join_four(*refs):
    first, second, outs = refs[:4], refs[4:8], refs[8:]
    for z, out in enumerate(outs):
        at = 0
        for a_ref, b_ref, c_ref, d_ref in (first, second):
            rows = a_ref.shape[1]
            low = a_ref[z].astype(f32) + b_ref[z].astype(f32)
            out[at : at + rows, :] = (low + (c_ref[z].astype(f32) + d_ref[z].astype(f32))).astype(bf16)
            at += rows


def lay_four(a_ref, b_ref, c_ref, d_ref, out_ref):
    for number, ref in enumerate((a_ref, b_ref, c_ref, d_ref)):
        out_ref[number] = ref[...]


def each_chunk(refs):
    own = lax.axis_index("dp") % CHUNKS
    for xy in range(4):
        for z in range(4):
            parts = [ref[z] for ref in (refs[3:] if xy == 3 else refs[xy : xy + 1])]
            yield (z * 4 + xy) ^ own, jnp.concatenate(parts, axis=0).astype(f32)


def spread_feed(
    a_ref, b_ref, c_ref, d_ref, e_ref, up_ref, out_ref, g2_ref, s2_ref, bd_ref, g1_ref, s1_ref, bo_ref, bup_ref, down_ref, keep_ref,
):
    width, half = up_ref.shape
    tall, low = width // CHUNKS, out_ref.shape[0] // CHUNKS
    deep = half // CHUNKS
    for chunk, held in each_chunk((a_ref, b_ref, c_ref, d_ref, e_ref)):
        rows = pl.ds(pl.multiple_of(chunk * tall, tall), tall)
        for block in range(half // 128):
            up_ref[rows, block * 128 : block * 128 + 128] = held[block * tall : (block + 1) * tall]
        rows = pl.ds(pl.multiple_of(chunk * low, low), low)
        base = half // 128 * tall
        for block in range(width // 128):
            out_ref[rows, block * 128 : block * 128 + 128] = held[base + block * low : base + (block + 1) * low]
        keep_ref[chunk] = held[FEED_ROWS - 16 : FEED_ROWS]
        rows = pl.ds(pl.multiple_of((chunk % 4 * 4 + chunk // 4) * deep, deep), deep)
        for block in range(width // 128):
            at = FEED_ROWS + block * deep
            down_ref[rows, block * 128 : block * 128 + 128] = held[at : at + deep]
    refs = [(ref, at) for ref in (g2_ref, s2_ref, bd_ref, g1_ref, s1_ref, bo_ref, bup_ref) for at in range(0, ref.shape[0], 128)]
    each = len(refs) // CHUNKS
    for number, (ref, at) in enumerate(refs):
        ref[at : at + 128] = keep_ref[number // each, number % each, :]


def spread_heads(a_ref, b_ref, c_ref, d_ref, qkv_ref, bias_ref, keep_ref):
    kinds, width, half = qkv_ref.shape
    tall = width // CHUNKS
    for chunk, held in each_chunk((a_ref, b_ref, c_ref, d_ref)):
        rows = pl.ds(pl.multiple_of(chunk * tall, tall), tall)
        for kind in range(kinds):
            for block in range(half // 128):
                row = (kind * (half // 128) + block) * tall
                qkv_ref[kind, rows, block * 128 : block * 128 + 128] = held[row : row + tall]
        keep_ref[chunk] = held[HEAD_ROWS - 16 :]
    blocks = half // 128
    for number in range(2 * blocks):
        at = number % blocks * 128
        bias_ref[number // blocks : number // blocks + 1, at : at + 128] = keep_ref[number, 0:1, :]


def shape(dims, kind=bf16):
    return jax.ShapeDtypeStruct(dims, kind)


smem = pl.BlockSpec(memory_space=pltpu.SMEM)


def specs(count):
    return [smem] + [pl.BlockSpec(memory_space=pltpu.VMEM)] * (count - 1)


def cost(flops, moved, powers=0):
    return pl.CostEstimate(flops=int(flops), bytes_accessed=int(moved), transcendentals=int(powers))


hbm = pl.BlockSpec(memory_space=pl.ANY)
vmem = pl.BlockSpec(memory_space=pltpu.VMEM)


def call_forward(sets, x, wa, wb, ba, bb):
    width = 2 * wa.shape[2]
    big, more = (width, LANES), (width // 4, LANES)
    return pl.pallas_call(
        attend_forward, name="attend_forward",
        out_shape=[shape(big), shape(big), shape(big), shape(big), shape(more)],
        in_specs=[smem, hbm, hbm, vmem, vmem, vmem], out_specs=[hbm] * 5,
        scratch_shapes=[pltpu.VMEM(a.shape, bf16) for a in (x, wa)] + [pltpu.VMEM(big, bf16)] * 4 + [pltpu.VMEM(more, bf16)]
        + [pltpu.VMEM((x.shape[1], LANES), bf16), pltpu.VMEM((CLASSES, LANES), bf16), pltpu.VMEM((CLASSES + 16, LANES), bf16)]
        + [pltpu.SemaphoreType.DMA((3,)), pltpu.SemaphoreType.DMA((5,))],
        compiler_params=params(54), cost_estimate=cost(14e9, 12e6),
    )(sets, x, wa, wb, ba, bb)


def call_feed_forward(sets, x, mixed, wo_a, wo_b, up_a, up_b, bu_a, bu_b, down_a, down_b, vecs, cot):
    rows, width = x.shape
    half = up_a.shape[1]
    outs = [shape((rows, width)), shape((rows, width)), shape((rows, width), f32), shape((rows, 2 * half)), shape((rows, width))]
    tall = (PADDED, width)
    own = [tall, mixed.shape, (width, width), (2, width, half), (2, half, width), tall]
    piece = shape((4, 4, DOWN_ROWS, 128))
    return pl.pallas_call(
        feed_forward, name="feed_forward",
        out_shape=outs + [piece, piece, shape((24, width), f32)],
        in_specs=[smem] + [hbm] * 6 + [vmem] * 2 + [hbm] * 2 + [vmem] * 6 + [hbm], out_specs=[hbm] * 7 + [vmem],
        scratch_shapes=[pltpu.VMEM(a, bf16) for a in own] + [pltpu.VMEM((PADDED, a.shape[1]), a.dtype) for a in outs]
        + [pltpu.VMEM((2, *piece.shape), bf16), pltpu.VMEM((PADDED, 2 * half), bf16)]
        + [pltpu.SemaphoreType.DMA((9,)), pltpu.SemaphoreType.DMA((6, 5)), pltpu.SemaphoreType.DMA((2,))],
        compiler_params=params(48), cost_estimate=cost(14e9, 20e6),
    )(sets, x, mixed, wo_a, wo_b, up_a, up_b, bu_a, bu_b, down_a, down_b, *vecs, cot)


def call_feed_backward(second, slope, hidden, resid, mixed, wo_a, wo_b, up_a, up_b, down_a, down_b, gain, sums):
    rows, width = second.shape
    half = up_a.shape[1]
    split = wo_a.shape[0]
    piece = shape((4, 4, FEED_ROWS, 128))
    outs = [shape((rows, width), f32), shape((2 * split, LANES)), shape((2 * split // 4, LANES))]
    given = [((PADDED, a.shape[1]), a.dtype) for a in (second, slope, hidden, resid)] + [(mixed.shape, bf16)]
    given += [((width, width), bf16), ((2, width, half), bf16), ((2, half, width), bf16)]
    return pl.pallas_call(
        feed_backward, name="feed_backward",
        out_shape=outs + [pltpu.VMEM(piece.shape, bf16)] * 2,
        in_specs=[hbm] * 11 + [vmem] * 2, out_specs=[hbm] * 3 + [vmem] * 2,
        scratch_shapes=[pltpu.VMEM(*a) for a in given] + [pltpu.VMEM((PADDED, width), f32)] + [pltpu.VMEM(a.shape, a.dtype) for a in outs[1:]]
        + [
            pltpu.VMEM((PADDED, 2 * half), bf16), pltpu.VMEM((LANES, width), bf16),
            pltpu.VMEM((24, width), f32), pltpu.VMEM((8, 2 * half), f32),
        ]
        + [pltpu.SemaphoreType.DMA(a) for a in ((6, 3), (8,), (6, 1), (2,))],
        compiler_params=params(48), cost_estimate=cost(14e9, 20e6),
    )(second, slope, hidden, resid, mixed, wo_a, wo_b, up_a, up_b, down_a, down_b, gain, sums)


def call_backward(part, sets, q, k, v, grad, lse, delta, x):
    rows = q.shape[0] // 2
    big, more = (rows, LANES), (rows // 4, LANES)
    return pl.pallas_call(
        functools.partial(attend_backward, part), name="attend_backward",
        out_shape=[shape(big), shape(big), shape(big), shape((4, 4, HEAD_ROWS, 128))],
        in_specs=[smem] + [hbm] * 7, out_specs=[hbm] * 3 + [vmem],
        scratch_shapes=[pltpu.VMEM(a, bf16) for a in (big, big, big, big, more, more, x.shape, (3, *big), (x.shape[1], LANES))]
        + [
            pltpu.VMEM((CLASSES, LANES), bf16), pltpu.VMEM((CLASSES + 16, LANES), bf16),
            pltpu.VMEM((2, 896, 896), bf16), pltpu.VMEM((2, 896, 896), bf16),
            pltpu.VMEM((rows // 64, 64, LANES), f32), pltpu.VMEM((rows // 64, 64, LANES), f32),
        ]
        + [pltpu.SemaphoreType.DMA(a) for a in ((rows // 128, 6), (1,), (rows // 128, 3))],
        compiler_params=params(50), cost_estimate=cost(9e9, 6e6),
    )(sets, q, k, v, grad, lse, delta, x)


def call_project_input(own, other, wa, wb, resid):
    return pl.pallas_call(
        project_input, name="project_input", out_shape=shape(resid.shape, f32),
        scratch_shapes=[pltpu.VMEM((3, 2 * wa.shape[2], wa.shape[1]), bf16)],
        compiler_params=params(40), cost_estimate=cost(2.4e9, 12e6),
    )(*own, *other, wa, wb, resid)


def swap(array):
    return lax.ppermute(array, "mp", [(0, 1), (1, 0)])


def exchange(array, distance):
    count = lax.axis_size("dp")
    return lax.ppermute(array, "dp", [(i, i ^ distance) for i in range(count)])


def small(kernel, name, outs, scratch=()):
    moved = 2 * sum(o.size * o.dtype.itemsize for o in outs)
    return pl.pallas_call(
        kernel, name=name, out_shape=list(outs), scratch_shapes=list(scratch),
        compiler_params=params(24), cost_estimate=cost(1e6, moved),
    )


def after(array, *earlier):
    return lax.optimization_barrier((array, *earlier))[0]


def to_plane(parts):
    return [exchange(parts[xy], xy) for xy in (1, 2, 3)]


def to_line(parts):
    return [exchange(parts[z], 4 * z) for z in (1, 2, 3)]


def plane_sum(parts, came, *earlier):
    _, rows, lanes = parts[0].shape
    return small(add_four, "add_four", [shape((rows, lanes))] * 4)(after(parts[0], *earlier), *came)


def plane_sum_joined(feed, feed_came, down, down_came, *earlier):
    rows, lanes = feed[0].shape[1] + down[0].shape[1], feed[0].shape[2]
    return small(join_four, "join_four", [shape((rows, lanes))] * 4)(after(feed[0], *earlier), *feed_came, down[0], *down_came)


def line_sum(parts, came, *earlier):
    (total,) = small(add_four, "add_four", [shape(parts[0].shape)])(after(parts[0], *earlier), *came)
    distance = CHUNKS
    while distance < lax.axis_size("dp"):
        total = total + exchange(total, distance)
        distance *= 2
    return total


def line_copies(total):
    return [exchange(total, 4 * z) for z in (1, 2, 3)]


def laid(total, came, *earlier):
    (held,) = small(lay_four, "lay_four", [shape((4, *total.shape))])(after(total, *earlier), *came)
    return held


def plane_copies(held):
    return [exchange(held, xy) for xy in (1, 2, 3)]


def across(beside, above, *earlier):
    cut = beside.shape[1] // 32 * 16
    return exchange(after(beside, *earlier)[:, :cut], 2), exchange(after(above, *earlier)[:, cut:], 1)


def halves_added(mine, came, *earlier):
    return small(add_pair, "add_pair", [shape(mine.shape[1:])] * 4)(after(mine, *earlier), came)


def per_device(
    variates, dataset, w_qkv, b_qv, w_out, b_out, gain_one, shift_one, w_up, b_up, w_down, b_down, gain_two, shift_two, cotangent,
):
    width, half = w_up.shape
    other_qkv, other_bias = (pltpu.with_memory_space_constraint(swap(a), pltpu.VMEM) for a in (w_qkv, b_qv))
    other_out, other_up, other_bup, other_down = swap(w_out), swap(w_up), swap(b_up), pltpu.with_memory_space_constraint(swap(w_down), pltpu.VMEM)
    q, k, v, mixed, lse = call_forward(dataset, variates, w_qkv, other_qkv, b_qv, other_bias)
    out, hidden, resid, slope, second, down_mine, down_theirs, sums = call_feed_forward(
        dataset, variates, mixed, w_out, other_out, w_up, other_up, b_up, other_bup, w_down, other_down,
        (b_out, gain_one, shift_one, b_down, gain_two, shift_two), cotangent,
    )
    down = halves_added(down_mine, swap(down_theirs))
    down_came = to_plane(down)
    grad_res, grad_mix, delta, mine, theirs = call_feed_backward(
        after(second, *down), slope, hidden, resid, mixed, w_out, other_out, w_up, other_up, w_down, other_down, gain_one, sums
    )
    feed = halves_added(mine, swap(after(theirs, *down_came)))
    feed_came = to_plane(feed)
    *other, theirs = call_backward(1, dataset, q, k, v, after(grad_mix, *feed), lse, delta, variates)
    feed = plane_sum_joined(feed, feed_came, down, down_came, theirs)
    heads_came = swap(after(theirs, *feed))
    feed_came = to_line(feed)
    *own, mine = call_backward(0, dataset, q, k, v, after(grad_mix, heads_came, *feed), lse, delta, variates)
    total = line_sum(feed, feed_came, mine)
    heads = halves_added(mine, heads_came, total)
    heads_plane = to_plane(heads)
    feed_came = line_copies(total)
    grad_in = call_project_input(own, other, w_qkv, other_qkv, after(grad_res, total, *heads))
    held = laid(total, feed_came, grad_in)
    heads = plane_sum(heads, heads_plane, grad_in)
    line = to_line(heads)
    feed = plane_copies(after(held, line[0]))[:2]
    heads = line_sum(heads, line)
    line = line_copies(heads)
    heads = laid(heads, line)
    feed = [held, *feed, *across(*feed, heads)]
    plane = plane_copies(heads)
    vector = shape((width,), f32)
    outs = [shape((width, half), f32), shape(w_out.shape, f32)] + [vector] * 6 + [shape((half,), f32), shape(w_down.shape, f32)]
    keep = [pltpu.VMEM((CHUNKS, 16, 128), f32)]
    grad_up, grad_out, two_gain, two_shift, down_bias, one_gain, one_shift, out_bias, up_bias, grad_down = small(
        spread_feed, "spread_feed", outs, keep
    )(*feed)
    heads = [after(heads, grad_up), *plane]
    grad_qkv, bias = small(spread_heads, "spread_heads", [shape(w_qkv.shape, f32), shape(b_qv.shape, f32)], keep)(*heads)
    return (
        out, grad_in, grad_qkv, bias, grad_out, out_bias, one_gain, one_shift, grad_up, up_bias,
        grad_down, down_bias, two_gain, two_shift,
    )


def solution(mesh):
    wide = P(("dp", "mp"), None)
    weights = (P(None, None, "mp"), P(None, "mp"), P("mp", None))
    placed = (wide, P("dp"), *weights, P(), P(), P(), P(None, "mp"), P("mp"), P("mp", None), P(), P(), P(), wide)
    given = (wide, wide, *weights, P(), P(), P(), P(None, "mp"), P("mp"), P("mp", None), P(), P(), P())
    return jax.shard_map(per_device, mesh=mesh, in_specs=placed, out_specs=given, check_vma=False)
```
